32 devices in a mesh: dp: 16 (over z, y, core), tensor: 2 (over x).
Axes of the slice: x: 2, y: 2, z: 4, core: 2. Of those that a mesh axis runs over, the one named last changes fastest.
Arguments:
- tokens: bfloat16 [7680, 1536], P(('dp', 'tensor')), may hold values from -6 to 6
- teacher: bfloat16 [7680, 1536], P(('dp', 'tensor')), may hold values from -6 to 6
- valid: int32 [7680], P(('dp', 'tensor')), may hold values from 0 to 1
- mixer_gain: bfloat16 [1536], P(('dp', 'tensor')), may hold values from 0.099609375 to 1.8984375
- in_weight: bfloat16 [1536, 3, 1536], P('dp', None, 'tensor'), may hold values from -0.15625 to 0.15625
- conv_weight: bfloat16 [3, 1536], P(None, ('dp', 'tensor')), may hold values from -3.5 to 3.5
- out_weight: bfloat16 [1536, 1536], P('dp', 'tensor'), may hold values from -0.15625 to 0.15625
- ffn_gain: bfloat16 [1536], P(('dp', 'tensor')), may hold values from 0.099609375 to 1.8984375
- gate_weight: bfloat16 [1536, 6912], P('dp', 'tensor'), may hold values from -0.15625 to 0.15625
- up_weight: bfloat16 [1536, 6912], P('dp', 'tensor'), may hold values from -0.15625 to 0.15625
- down_weight: bfloat16 [1536, 6912], P('dp', 'tensor'), may hold values from -0.078125 to 0.078125
Outputs:
- loss: float32 [], replicated
- block_output: float32 [7680, 1536], P(('dp', 'tensor'))
- tokens_grad: float32 [7680, 1536], P(('dp', 'tensor'))
- mixer_gain_grad: float32 [1536], P(('dp', 'tensor'))
- in_weight_grad: float32 [1536, 3, 1536], P('dp', None, 'tensor')
- conv_weight_grad: float32 [3, 1536], P(None, ('dp', 'tensor'))
- out_weight_grad: float32 [1536, 1536], P('dp', 'tensor')
- ffn_gain_grad: float32 [1536], P(('dp', 'tensor'))
- gate_weight_grad: float32 [1536, 6912], P('dp', 'tensor')
- up_weight_grad: float32 [1536, 6912], P('dp', 'tensor')
- down_weight_grad: float32 [1536, 6912], P('dp', 'tensor')
The draws below stay inside these ranges and needn't reach their ends.
All inputs are finite; a program needn't handle non-finite values.
Results may differ from the reference program's by a relative error of at most 0.0088.
Values may be sent and summed in bfloat16 or wider, within the bound.
A program may use at most 192 MiB of HBM per device.

```python
import jax
import jax.numpy as jnp
from jax import lax

D = 1536
FF = 6912
KERNEL = 3
SEQ_LEN = 480
SEQS = 16
TOKENS = 7680


def draw_valid(key, part):
    key = jax.random.fold_in(key, 11)
    picks = jax.random.randint(key, (TOKENS,), 0, 4 * SEQS)
    sequence = jnp.arange(TOKENS, dtype=jnp.int32) // SEQ_LEN
    return (picks < SEQS + 2 * sequence).astype(jnp.int32)


def block_scale(own_key, extent, cuts, smallest, high):
    factor_of, own = 1.0, jax.random.fold_in(own_key, 6)
    for axis_at, blocks in cuts:
        steps = jnp.exp(jax.random.uniform(jax.random.fold_in(own, axis_at), (blocks,), jnp.float32, smallest / len(cuts), high / len(cuts)))
        factor_of = factor_of * jnp.repeat(steps, extent[axis_at] // blocks).reshape([-1 if axis == axis_at else 1 for axis in range(len(extent))])
    return factor_of


def centred(rng, extent, deviation, reach, cuts=(), kind=jnp.bfloat16):
    factor_of = block_scale(rng, extent, cuts, -0.22, 0.18) if cuts else 1.0
    drawn = jax.random.normal(rng, extent, jnp.float32) * deviation * factor_of
    return jnp.minimum(jnp.maximum(drawn, -reach), reach).astype(kind)


def setup_inputs(seed: int = 0) -> dict:
    seeds = jax.random.split(jax.random.key(seed), 12)
    tokens = centred(seeds[0], (TOKENS, D), 1.0, 6.0, ((0, 32),))
    teacher = centred(seeds[1], (TOKENS, D), 1.0, 6.0, ((0, 32),))
    valid = draw_valid(jax.random.fold_in(seeds[11], 71), 0)
    mixer_gain = jnp.clip(1.0 + 0.18 * jax.random.normal(seeds[3], (D,), jnp.float32), 0.099609375, 1.8984375).astype(jnp.bfloat16)
    in_weight = centred(seeds[4], (D, 3, D), D ** -0.5, 0.15625, ((0, 16), (2, 2)))
    conv_weight = centred(seeds[5], (KERNEL, D), KERNEL ** -0.5, 3.5, ((1, 32),))
    out_weight = centred(seeds[6], (D, D), D ** -0.5, 0.15625, ((0, 16), (1, 2)))
    ffn_gain = jnp.clip(1.0 + 0.18 * jax.random.normal(seeds[7], (D,), jnp.float32), 0.099609375, 1.8984375).astype(jnp.bfloat16)
    gate_weight = centred(seeds[8], (D, FF), D ** -0.5, 0.15625, ((0, 16), (1, 2)))
    up_weight = centred(seeds[9], (D, FF), D ** -0.5, 0.15625, ((0, 16), (1, 2)))
    down_weight = centred(seeds[10], (D, FF), FF ** -0.5, 0.078125, ((0, 16), (1, 2)))
    return {"tokens": tokens, "teacher": teacher, "valid": valid, "mixer_gain": mixer_gain, "in_weight": in_weight, "conv_weight": conv_weight, "out_weight": out_weight, "ffn_gain": ffn_gain, "gate_weight": gate_weight, "up_weight": up_weight, "down_weight": down_weight}


norm_eps = 1e-05
highest_mode = lax.Precision.HIGHEST

@jax.custom_vjp
def low(v):
    return lax.optimization_barrier(v.astype(jnp.bfloat16)).astype(jnp.float32)

@jax.custom_vjp
def low_back(v):
    return v

def low_keep(v):
    return (low(v), None)

def low_pass(kept, grad):
    return (grad,)

def back_keep(v):
    return (v, None)

def back_low(kept, grad):
    return (low(grad),)
low.defvjp(low_keep, low_pass)
low_back.defvjp(back_keep, back_low)

def row_scale(source):
    return lax.rsqrt(lax.optimization_barrier(jnp.mean(source * source, axis=1, keepdims=True)) + norm_eps)

def layer_forward(weights, tokens_in):
    mixer_gain, in_weight, conv_weight, out_weight, ffn_gain, gate_weight, up_weight, down_weight = weights
    length = tokens_in.shape[0]
    normed = low(tokens_in * row_scale(tokens_in) * mixer_gain)
    projected = jnp.einsum('ti,ikc->ktc', normed, in_weight, precision=highest_mode)
    b_gate = low_back(projected[0])
    c_gate = low_back(projected[1])
    x_stream = low_back(projected[2])
    mixed_in = b_gate * x_stream
    padded = jnp.pad(mixed_in, ((KERNEL - 1, 0), (0, 0)))
    convolved = conv_weight[0] * padded[0:length]
    for offset in range(1, KERNEL):
        convolved = convolved + conv_weight[offset] * padded[offset:offset + length]
    gated = low(c_gate * convolved)
    mixer_out = low_back(jnp.dot(gated, out_weight.T, precision=highest_mode))
    first = tokens_in + mixer_out
    normed_two = low(first * row_scale(first) * ffn_gain)
    gate_val = low_back(jnp.dot(normed_two, gate_weight, precision=highest_mode))
    up_val = low_back(jnp.dot(normed_two, up_weight, precision=highest_mode))
    hidden = low(jax.nn.silu(gate_val) * up_val)
    ffn_out = low_back(jnp.dot(hidden, down_weight.T, precision=highest_mode))
    return first + ffn_out

def add_pair(left, right):
    return left + right

def reference(tokens, teacher, valid, mixer_gain, in_weight, conv_weight, out_weight, ffn_gain, gate_weight, up_weight, down_weight):
    weights = tuple((weight_arr.astype(jnp.float32) for weight_arr in (mixer_gain, in_weight, conv_weight, out_weight, ffn_gain, gate_weight, up_weight, down_weight)))
    valid_f = valid.astype(jnp.float32)
    valid_total = jnp.sum(valid_f)
    loss_scale = 1.0 / (D * valid_total)
    seq_tokens = tokens.astype(jnp.float32).reshape(SEQS, SEQ_LEN, D)
    seq_teacher = teacher.astype(jnp.float32).reshape(SEQS, SEQ_LEN, D)
    seq_masks = valid_f.reshape(SEQS, SEQ_LEN)

    def one_sequence(carry, block):
        loss_acc, grad_acc = carry
        seq_in, seq_target, seq_mask = block

        def seq_loss(weights_in, tokens_in):
            block_out = layer_forward(weights_in, tokens_in)
            error = block_out - seq_target
            return (jnp.sum(seq_mask[:, None] * error * error), block_out)
        (loss_part, block_out), pullback = jax.vjp(seq_loss, weights, seq_in)
        grad_weights, grad_in = pullback((loss_scale, jnp.zeros_like(block_out)))
        grad_acc = jax.tree.map(add_pair, grad_acc, grad_weights)
        return ((loss_acc + loss_part, grad_acc), (block_out, grad_in))
    start = (jnp.zeros((), jnp.float32), jax.tree.map(jnp.zeros_like, weights))
    (loss_total, grads), (outputs, grads_in) = lax.scan(one_sequence, start, (seq_tokens, seq_teacher, seq_masks))
    loss = loss_total * loss_scale
    return (loss, outputs.reshape(TOKENS, D), grads_in.reshape(TOKENS, D), grads[0], grads[1], grads[2], grads[3], grads[4], grads[5], grads[6], grads[7])
```

```python
import functools
from types import SimpleNamespace

import jax
import jax.numpy as jnp
from jax import lax
from jax.experimental import pallas as pl
from jax.experimental.pallas import tpu as pltpu
from jax.sharding import PartitionSpec as P

MESH = pl.DeviceIdType.MESH
f32 = jnp.float32
bf16 = jnp.bfloat16
norm_eps = 1e-05
LANES = 256
NSUB = 3
VMEM = pl.BlockSpec(memory_space=pltpu.VMEM)
ANY = pl.BlockSpec(memory_space=pl.ANY)


def rows_of(start, size, step=16):
    return pl.ds(pl.multiple_of(start, step), size)


def place(ndp):
    d, x = lax.axis_index("dp"), lax.axis_index("tensor")
    core, y, z = d % 2, (d // 2) % 2, d // 4
    depth = ndp // 4
    at = SimpleNamespace(d=d, x=x, core=core, y=y, z=z, depth=depth, chip=d // 2)
    at.sib = (d + 1 - 2 * core, x)
    at.across = (d, 1 - x)
    at.beside = (d + 2 - 4 * y, x)
    at.lower, at.upper = (d - 4, x), (d + 4, x)
    at.has_lower, at.has_upper = z > 0, z < depth - 1
    at.cube = [at.sib, at.across, at.beside]
    step = 1
    while step < depth:
        at.cube.append((d + 4 * step * (1 - 2 * ((z // step) % 2)), x))
        step *= 2
    at.own = 2 * core + x
    at.own_sib = 2 * (1 - core) + x
    at.own_across = 2 * core + 1 - x
    at.own_far = 2 * (1 - core) + 1 - x
    return at


def meet(at):
    bar = pltpu.get_barrier_semaphore()
    always = [at.sib, at.across, at.beside] + at.cube[4:]
    for dev in always:
        pl.semaphore_signal(bar, 1, device_id=dev, device_id_type=MESH)
    for has, dev in ((at.has_lower, at.lower), (at.has_upper, at.upper)):

        @pl.when(has)
        def _():
            pl.semaphore_signal(bar, 1, device_id=dev, device_id_type=MESH)

    ends = jnp.where(at.has_lower, 1, 0) + jnp.where(at.has_upper, 1, 0)
    pl.semaphore_wait(bar, len(always) + ends)


def remote(src, dst, send, recv, dev):
    return pltpu.make_async_remote_copy(
        src_ref=src, dst_ref=dst, send_sem=send, recv_sem=recv, device_id=dev, device_id_type=MESH
    )


def total_step(at, step, cur, got, send, recv):
    copy = remote(cur.at[step], got.at[step], send.at[step], recv.at[step], at.cube[step])
    copy.start()
    copy.wait()
    cur[step + 1] = cur[step] + got[step]


class Share:
    def __init__(self, at, buf, rows, sems):
        self.at, self.buf, self.rows, self.sems = at, buf, rows, sems
        self.sub = rows // NSUB

    def part(self, slot, j):
        return self.buf.at[rows_of(slot * self.rows + j * self.sub, self.sub), :]

    def copy(self, slot, j, k, dev):
        part = self.part(slot, j)
        return remote(part, part, self.sems.at[2 * k, j], self.sems.at[2 * k + 1, j], dev)

    def start(self, j):
        self.copy(self.at.own, j, 0, self.at.across).start()
        self.copy(self.at.own, j, 1, self.at.sib).start()

    def forward(self, j):
        self.copy(self.at.own_across, j, 0, self.at.across).wait_recv()
        self.copy(self.at.own_across, j, 2, self.at.sib).start()

    def finish(self):
        for j in range(NSUB):
            self.copy(self.at.own_sib, j, 1, self.at.sib).wait_recv()
            self.copy(self.at.own_far, j, 2, self.at.sib).wait_recv()
            self.copy(self.at.own, j, 0, self.at.across).wait_send()
            self.copy(self.at.own, j, 1, self.at.sib).wait_send()
            self.copy(self.at.own_across, j, 2, self.at.sib).wait_send()


class Sums:
    def __init__(self, at, acc, rows, core_out, core_in, far_out, far_in, core_sems, far_sems):
        self.at, self.acc, self.rows = at, acc, rows
        self.core_out, self.core_in, self.far_out, self.far_in = core_out, core_in, far_out, far_in
        self.core_sems, self.far_sems = core_sems, far_sems
        self.sub = rows // NSUB

    def of(self, slot, j):
        return self.acc[rows_of(slot * self.rows + j * self.sub, self.sub), :]

    def core_copy(self, k, j):
        part = rows_of(j * self.sub, self.sub)
        return remote(
            self.core_out.at[k, part, :],
            self.core_in.at[k, part, :],
            self.core_sems.at[0, k, j],
            self.core_sems.at[1, k, j],
            self.at.sib,
        )

    def far_copy(self, j):
        part = rows_of(j * self.sub, self.sub)
        return remote(
            self.far_out.at[part, :],
            self.far_in.at[part, :],
            self.far_sems.at[0, j],
            self.far_sems.at[1, j],
            self.at.across,
        )

    def to_core(self):
        for k, slot in ((0, self.at.own_far), (1, self.at.own_sib)):
            for j in range(NSUB):
                self.core_out[k, rows_of(j * self.sub, self.sub), :] = self.of(slot, j).astype(bf16)
                self.core_copy(k, j).start()

    def to_far(self):
        for j in range(NSUB):
            part = rows_of(j * self.sub, self.sub)
            self.core_copy(0, j).wait_recv()
            both = self.of(self.at.own_across, j) + self.core_in[0, part, :].astype(f32)
            self.far_out[part, :] = both.astype(bf16)
            self.far_copy(j).start()

    def take(self, j):
        part = rows_of(j * self.sub, self.sub)
        self.core_copy(1, j).wait_recv()
        self.far_copy(j).wait_recv()
        return (
            self.of(self.at.own, j)
            + self.core_in[1, part, :].astype(f32)
            + self.far_in[part, :].astype(f32)
        )

    def finish(self):
        for j in range(NSUB):
            self.core_copy(0, j).wait_send()
            self.core_copy(1, j).wait_send()
            self.far_copy(j).wait_send()


def nt(left, right):
    return lax.dot_general(left, right, (((1,), (1,)), ((), ())), preferred_element_type=f32)


def tn(left, right):
    return lax.dot_general(left, right, (((0,), (0,)), ((), ())), preferred_element_type=f32)


def nn(left, right):
    return jnp.dot(left, right, preferred_element_type=f32)


def inverse_of(source):
    return lax.rsqrt(jnp.mean(source * source, axis=1, keepdims=True) + norm_eps)


def shifted(value, by):
    if by == 0:
        return value
    size = value.shape[0]
    row = lax.broadcasted_iota(jnp.int32, value.shape, 0)
    inside = row >= by if by > 0 else row < size + by
    return jnp.where(inside, pltpu.roll(value, by % size, 0), 0.0)


def convolve(mixed, taps):
    return taps[0:1] * shifted(mixed, 2) + taps[1:2] * shifted(mixed, 1) + taps[2:3] * mixed


class Gather:
    def __init__(self, at, held, chunk, early_y, sems):
        self.at, self.held, self.chunk, self.early_y = at, held, chunk, early_y
        self.recv, self.own_send, self.send = sems

    def block(self, p, chip, count=1):
        return self.held.at[p, rows_of(chip * self.chunk, count * self.chunk), :]

    def copy(self, p, chip, count, send, dev):
        block = self.block(p, chip, count)
        return remote(block, block, send, self.recv.at[p, chip], dev)

    def arrived(self, p, chip, count=1):
        self.copy(p, chip, count, self.own_send.at[0, 0], self.at.beside).wait_recv()

    def own(self, p, act):
        at = self.at
        act(self.copy(p, at.chip, 1, self.own_send.at[0, p], at.beside))
        if p not in self.early_y:
            self.own_z(p, at.chip, 1, act)

    def own_z(self, p, chip, count, act):
        at = self.at

        @pl.when(at.has_upper)
        def _():
            act(self.copy(p, chip, count, self.own_send.at[1, p], at.upper))

        @pl.when(at.has_lower)
        def _():
            act(self.copy(p, chip, count, self.own_send.at[2, p], at.lower))

    def passing(self, p, pairs, parity, wait, act):
        at = self.at

        def step(s, carry):
            for from_z, goes_on, dev, way in (
                (at.z - 1 - s, at.has_upper, at.upper, 0),
                (at.z + 1 + s, at.has_lower, at.lower, 1),
            ):

                @pl.when(jnp.logical_and(from_z >= 0, from_z < at.depth))
                def _():
                    chip = 2 * from_z if pairs else 2 * from_z + at.y
                    count = 2 if pairs else 1
                    if wait:
                        self.arrived(p, chip, count)

                    @pl.when(goes_on)
                    def _():
                        act(self.copy(p, chip, count, self.send.at[way, parity, from_z], dev))

                    if not pairs:
                        act(self.copy(p, chip, count, self.send.at[2, parity, from_z], at.beside))

            return carry

        lax.fori_loop(0, at.depth - 1, step, 0)

    def relay(self, p, parity, drop):
        if drop is not None:
            self.passing(drop[0], drop[1], parity, False, lambda copy: copy.wait_send())
        pairs = isinstance(p, int) and p in self.early_y
        if pairs:
            self.arrived(p, 2 * self.at.z + 1 - self.at.y)
            self.own_z(p, 2 * self.at.z, 2, lambda copy: copy.start())
        self.passing(p, pairs, parity, True, lambda copy: copy.start())

    def whole(self, p):
        def step(z, carry):
            self.arrived(p, 2 * z + 1 - self.at.y)
            return carry

        lax.fori_loop(0, self.at.depth, step, 0)


def forward_kernel(
    ndp,
    early_y,
    shards,
    tokens,
    teacher,
    valid,
    small,
    held_out,
    normed_out,
    normed_two_out,
    grad_rows_out,
    streams_out,
    gates_out,
    first_out,
    block_out,
    grad_out,
    small_out,
    loss_out,
    held,
    landed,
    mine,
    rows_a,
    rows_b,
    acc,
    streams,
    gates,
    core_out,
    core_in,
    far_out,
    far_in,
    first,
    result,
    error_grad,
    cur,
    got,
    chip_sems,
    recv_sems,
    own_sems,
    send_sems,
    share_sems,
    core_sems,
    far_sems,
    cube_sems,
    out_sems,
    held_sems,
    gate_sems,
):
    at = place(ndp)
    pieces, width, piece = held.shape
    part_rows = shards.shape[2]
    chunk = 2 * part_rows
    rows = tokens.shape[0]
    sub = rows // NSUB
    channels = streams.shape[1] // 3
    aligned = part_rows % 16 == 0
    go = lambda copy: copy.start()
    gather = Gather(at, held, chunk, early_y, (recv_sems, own_sems, send_sems))
    share_a = Share(at, rows_a, rows, share_sems)
    share_b = Share(at, rows_b, rows, share_sems)
    sums = Sums(at, acc, rows, core_out, core_in, far_out, far_in, core_sems, far_sems)

    def half(p, core):
        return held.at[p, rows_of(at.chip * chunk + core * part_rows, part_rows), :]

    def to_sib(p):
        dst = half(p, at.core) if aligned else landed.at[p]
        return remote(shards.at[1 - at.core, p], dst, chip_sems.at[0, p], chip_sems.at[1, p], at.sib)

    def from_sib(p):
        dst = half(p, 1 - at.core) if aligned else landed.at[p]
        return remote(dst, dst, chip_sems.at[0, p], chip_sems.at[1, p], at.sib)

    def keep(p):
        dst = half(p, at.core) if aligned else mine.at[p]
        return pltpu.make_async_copy(shards.at[at.core, p], dst, chip_sems.at[2, p])

    def own_block(p):
        keep(p).wait()
        from_sib(p).wait_recv()
        if not aligned:
            a, b = mine[p].astype(f32), landed[p].astype(f32)
            lower = jnp.where(at.core == 0, a, b)
            upper = jnp.where(at.core == 0, b, a)
            both = jnp.concatenate([lower, upper], axis=0).astype(bf16)
            held[p, rows_of(at.chip * chunk, chunk), :] = both
        gather.own(p, go)

    meet(at)
    for j in range(NSUB):
        rows_a[rows_of(at.own * rows + j * sub, sub), :] = tokens[pl.ds(j * sub, sub), :]
        share_a.start(j)
    for p in range(pieces):
        to_sib(p).start()
        keep(p).start()
    own_block(0)
    own_block(1)
    cur[0] = small[...]
    for step in range(len(at.cube)):
        total_step(at, step, cur, got, cube_sems.at[0], cube_sems.at[1])
    last = len(at.cube)
    small_out[...] = cur[last]
    own_block(2)
    for j in range(NSUB):
        share_a.forward(j)
    gain_one, gain_two = cur[last, 0:1, :], cur[last, 1:2, :]
    share_a.finish()

    def norm_rows(i, carry):
        part = rows_of(i * sub, sub)
        source = rows_a[part, :].astype(f32)
        rows_a[part, :] = (source * inverse_of(source) * gain_one).astype(bf16)
        return carry

    lax.fori_loop(0, 4 * NSUB, norm_rows, 0)
    normed_copy = pltpu.make_async_copy(rows_a, normed_out, out_sems.at[0])
    normed_copy.start()

    def save(p):
        return pltpu.make_async_copy(held.at[p], held_out.at[p], held_sems.at[p])

    gather.relay(0, 0, None)
    own_block(3)
    gather.relay(1, 1, None)
    own_block(4)
    for p in (0, 1):
        gather.whole(p)
        save(p).start()
    lane = at.x * 2 * channels + at.core * channels
    taps = cur[last, 2:5, rows_of(lane, channels, 128)]

    def mix(r, carry):
        part = rows_of(((r + 1 - at.core) % 2) * 2 * rows, 2 * rows)
        both = nn(rows_a[part, :], held[0])
        x_stream = nn(rows_a[part, :], held[1, :, 0:channels])
        streams[part, 0 : 2 * channels] = both
        streams[part, 2 * channels :] = x_stream
        convolved = convolve(both[:, 0:channels] * x_stream, taps)
        gated = (both[:, channels:] * convolved).astype(bf16)
        acc[part, :] = nt(gated, held[1, :, channels:])
        return carry

    lax.fori_loop(0, 2, mix, 0)
    streams_copy = pltpu.make_async_copy(streams, streams_out, out_sems.at[1])
    streams_copy.start()
    sums.to_core()
    gather.relay(2, 0, (0, 0 in early_y))
    own_block(5)
    sums.to_far()
    own_block(6)
    gather.relay(3, 1, (1, 1 in early_y))
    own_block(7)
    own_block(8)
    for p in range(9, pieces):
        own_block(p)
    for j in range(NSUB):
        part = rows_of(j * sub, sub)
        value = tokens[part, :].astype(f32) + sums.take(j)
        first[part, :] = value
        normed_two = (value * inverse_of(value) * gain_two).astype(bf16)
        rows_b[rows_of(at.own * rows + j * sub, sub), :] = normed_two
        share_b.start(j)
    sums.finish()
    first_copy = pltpu.make_async_copy(first, first_out, out_sems.at[2])
    first_copy.start()
    gather.relay(4, 0, (2, 2 in early_y))
    for j in range(NSUB):
        share_b.forward(j)
    share_b.finish()
    normed_two_copy = pltpu.make_async_copy(rows_b, normed_two_out, out_sems.at[3])
    normed_two_copy.start()
    acc[...] = jnp.zeros_like(acc)

    def gates_copy(p):
        slot = p % 2
        return pltpu.make_async_copy(gates.at[slot], gates_out.at[p - 2], gate_sems.at[slot])

    def feed(p, carry):
        @pl.when(p >= 5)
        def _():
            parity = p % 2

            @pl.when(p == 5)
            def _():
                gather.relay(p, parity, (3, 3 in early_y))

            @pl.when(p > 5)
            def _():
                gather.relay(p, parity, (p - 2, False))

        for q in range(2, pieces):
            if q not in early_y:

                @pl.when(p == q)
                def _():
                    gather.whole(q)

        save(p).start()

        @pl.when(p >= 4)
        def _():
            gates_copy(p - 2).wait()

        def some(r, inner):
            part = rows_of(((r + 1 - at.core) % 2) * 2 * rows, 2 * rows)
            both = nn(rows_b[part, :], held[p, :, 0 : 2 * LANES])
            gate, up = both[:, 0:LANES], both[:, LANES:]
            gates[p % 2, part, :] = both.astype(bf16)
            hidden = (gate * jax.nn.sigmoid(gate) * up).astype(bf16)
            acc[part, :] += nt(hidden, held[p, :, 2 * LANES :])
            return inner

        lax.fori_loop(0, 2, some, 0)
        gates_copy(p).start()
        return carry

    normed_copy.wait()
    lax.fori_loop(2, pieces, feed, 0)
    sums.to_core()
    sums.to_far()
    scale = 1.0 / (width * cur[last, 5:6, 0:1])
    loss = jnp.zeros((1, width), f32)
    for j in range(NSUB):
        part = rows_of(j * sub, sub)
        value = first[part, :] + sums.take(j)
        result[part, :] = value
        error = value - teacher[part, :].astype(f32)
        weighted = valid[part, :] * error
        loss = loss + jnp.sum(weighted * error, axis=0, keepdims=True)
        grad = (2.0 * scale) * weighted
        error_grad[part, :] = grad
        rows_a[rows_of(at.own * rows + j * sub, sub), :] = grad.astype(bf16)
        share_a.start(j)
    loss_out[...] = jnp.broadcast_to(jnp.sum(loss, axis=1, keepdims=True), loss_out.shape)
    sums.finish()
    result_copy = pltpu.make_async_copy(result, block_out, out_sems.at[4])
    result_copy.start()
    grad_copy = pltpu.make_async_copy(error_grad, grad_out, out_sems.at[5])
    grad_copy.start()
    for j in range(NSUB):
        share_a.forward(j)
    share_a.finish()
    rows_copy = pltpu.make_async_copy(rows_a, grad_rows_out, out_sems.at[6])
    rows_copy.start()
    for p in range(pieces):
        save(p).wait()
        to_sib(p).wait_send()
        gather.own(p, lambda copy: copy.wait_send())
        if p in early_y:
            gather.own_z(p, 2 * at.z, 2, lambda copy: copy.wait_send())
    for p in (pieces - 2, pieces - 1):
        gather.passing(p, p in early_y, p % 2, False, lambda copy: copy.wait_send())
        gates_copy(p).wait()
    for copy in (streams_copy, first_copy, normed_two_copy, result_copy, grad_copy, rows_copy):
        copy.wait()


def forward(ndp, shards, tokens, teacher, valid, small):
    _, pieces, part_rows, piece = shards.shape
    rows, width = tokens.shape
    channels = (2 * piece - piece // 2) // 3
    cube = small_steps(ndp)
    early_y = (3,)
    dma = pltpu.SemaphoreType.DMA
    landing = (pieces, part_rows, piece) if part_rows % 16 else (1, 16, 128)
    shape = jax.ShapeDtypeStruct
    outs = (
        shape((pieces, width, piece), bf16),
        shape((4 * rows, width), bf16),
        shape((4 * rows, width), bf16),
        shape((4 * rows, width), bf16),
        shape((4 * rows, 3 * channels), f32),
        shape((pieces - 2, 4 * rows, 2 * LANES), bf16),
        shape((rows, width), f32),
        shape((rows, width), f32),
        shape((rows, width), f32),
        shape((8, width), f32),
        shape((8, 128), f32),
    )
    scratch = [
        pltpu.VMEM((pieces, width, piece), bf16),
        pltpu.VMEM(landing, bf16),
        pltpu.VMEM(landing, bf16),
        pltpu.VMEM((4 * rows, width), bf16),
        pltpu.VMEM((4 * rows, width), bf16),
        pltpu.VMEM((4 * rows, width), f32),
        pltpu.VMEM((4 * rows, 3 * channels), f32),
        pltpu.VMEM((2, 4 * rows, 2 * LANES), bf16),
        pltpu.VMEM((2, rows, width), bf16),
        pltpu.VMEM((2, rows, width), bf16),
        pltpu.VMEM((rows, width), bf16),
        pltpu.VMEM((rows, width), bf16),
        pltpu.VMEM((rows, width), f32),
        pltpu.VMEM((rows, width), f32),
        pltpu.VMEM((rows, width), f32),
        pltpu.VMEM((cube + 1, 8, width), f32),
        pltpu.VMEM((cube, 8, width), f32),
        dma((3, pieces)),
        dma((pieces, ndp // 2)),
        dma((3, pieces)),
        dma((3, 2, ndp // 4)),
        dma((6, NSUB)),
        dma((2, 2, NSUB)),
        dma((2, NSUB)),
        dma((2, cube)),
        dma((7,)),
        dma((pieces,)),
        dma((2,)),
    ]
    return pl.pallas_call(
        functools.partial(forward_kernel, ndp, early_y),
        out_shape=outs,
        in_specs=[ANY, VMEM, VMEM, VMEM, VMEM],
        out_specs=[ANY] * 9 + [VMEM] * 2,
        scratch_shapes=scratch,
        compiler_params=pltpu.CompilerParams(
            collective_id=0, has_side_effects=True, vmem_limit_bytes=63 << 20
        ),
    )(shards, tokens, teacher, valid, small)


def small_steps(ndp):
    return 3 + (ndp // 4 - 1).bit_length()


def shard_pieces(in_weight, out_weight, gate_weight, up_weight, down_weight):
    part_rows, _, channels = in_weight.shape
    channels //= 2
    taps = in_weight.reshape(part_rows, 3, 2, channels).transpose(2, 0, 1, 3)
    taps = taps.reshape(2, part_rows, 3 * channels)
    outs = out_weight.reshape(part_rows, 2, channels).transpose(1, 0, 2)
    mixer = jnp.concatenate([taps, outs], axis=2)
    mixer = mixer.reshape(2, part_rows, 2, 2 * channels).transpose(0, 2, 1, 3)
    units = gate_weight.shape[1]
    count = -(-units // (2 * LANES))

    def cut(weight):
        weight = jnp.pad(weight, ((0, 0), (0, 2 * count * LANES - units)))
        return weight.reshape(part_rows, 2, count, LANES).transpose(1, 2, 0, 3)

    ffn = jnp.concatenate([cut(gate_weight), cut(up_weight), cut(down_weight)], axis=3)
    return jnp.concatenate([mixer, ffn], axis=1)


class Scatter:
    def __init__(self, at, held, chunk, count, beside_in, line_in, pair_in, pair_beside, total, sems, credits):
        self.at, self.held, self.chunk, self.count = at, held, chunk, count
        self.beside_in, self.line_in, self.pair_in, self.pair_beside = beside_in, line_in, pair_in, pair_beside
        self.total, self.credits = total, credits
        self.beside_sems, self.line_sems, self.pair_sems, self.pair_y_sems = sems

    def block(self, p, chip, count=1):
        return self.held.at[p, rows_of(chip * self.chunk, count * self.chunk), :]

    def beside_copy(self, p, m, z):
        slot = m % 2
        return remote(
            self.block(p, 2 * z + 1 - self.at.y),
            self.beside_in.at[slot, z],
            self.beside_sems.at[0, slot, z],
            self.beside_sems.at[1, slot, z],
            self.at.beside,
        )

    def line_copy(self, p, m, z, up):
        slot, way = m % 2, 0 if up else 1
        into = z + 1 if up else z
        return remote(
            self.block(p, 2 * z + self.at.y),
            self.line_in.at[slot, into],
            self.line_sems.at[way, slot, z],
            self.line_sems.at[2, slot, into],
            self.at.upper if up else self.at.lower,
        )

    def pair_copy(self, p, z, up):
        into = z + 1 if up else z
        return remote(
            self.block(p, 2 * z, 2),
            self.pair_in.at[into],
            self.pair_sems.at[0 if up else 1, z],
            self.pair_sems.at[2, into],
            self.at.upper if up else self.at.lower,
        )

    def send_beside(self, p, m, dropped):
        if m >= 2:
            pl.semaphore_wait(self.credits.at[0], 1)

        def step(s, carry):
            z = (s % 2) * (s // 2) + (1 - s % 2) * (self.at.depth - 1 - s // 2)
            if dropped is not None:
                self.beside_copy(dropped, m, z).wait_send()
            self.beside_copy(p, m, z).start()
            return carry

        lax.fori_loop(0, self.at.depth, step, 0)

    def line(self, p, m, dropped):
        at, chunk = self.at, self.chunk
        total = self.total.at[pl.ds(0, chunk), :]
        if m >= 2:
            for has, credit in ((at.has_upper, 1), (at.has_lower, 2)):

                @pl.when(has)
                def _():
                    pl.semaphore_wait(self.credits.at[credit], 1)

            self.drop(dropped, m)

        def gather(z, behind, up):
            own = self.block(p, 2 * z + at.y)
            self.beside_copy(p, m, z).wait_recv()
            total[...] = own[...].astype(f32) + self.beside_in[m % 2, z].astype(f32)
            for has, goes_up in behind:

                @pl.when(has)
                def _():
                    self.line_copy(p, m, z, goes_up).wait_recv()
                    total[...] += self.line_in[m % 2, z + 1 if goes_up else z].astype(f32)

            return own

        def step(s, carry):
            for z, wanted, has, up in (
                (at.depth - 1 - s, at.depth - 1 - s > at.z, at.has_lower, True),
                (s, s < at.z, at.has_upper, False),
            ):

                @pl.when(wanted)
                def _():
                    own = gather(z, ((has, up),), up)
                    own[...] = total[...].astype(bf16)
                    self.line_copy(p, m, z, up).start()

            return carry

        lax.fori_loop(0, at.depth - 1, step, 0)
        gather(at.z, ((at.has_lower, True), (at.has_upper, False)), True)
        if m + 2 < self.count:
            pl.semaphore_signal(self.credits.at[0], 1, device_id=at.beside, device_id_type=MESH)

            @pl.when(at.has_lower)
            def _():
                pl.semaphore_signal(self.credits.at[1], 1, device_id=at.lower, device_id_type=MESH)

            @pl.when(at.has_upper)
            def _():
                pl.semaphore_signal(self.credits.at[2], 1, device_id=at.upper, device_id_type=MESH)

    def drop(self, p, m):
        at = self.at

        def step(s, carry):
            for z, wanted, up in (
                (at.depth - 1 - s, at.depth - 1 - s > at.z, True),
                (s, s < at.z, False),
            ):

                @pl.when(wanted)
                def _():
                    self.line_copy(p, m, z, up).wait_send()

            return carry

        lax.fori_loop(0, at.depth - 1, step, 0)

    def drop_beside(self, p, m):
        def step(z, carry):
            self.beside_copy(p, m, z).wait_send()
            return carry

        lax.fori_loop(0, self.at.depth, step, 0)

    def pair_steps(self, p, at_ends, act):
        at = self.at

        def step(s, carry):
            for z, wanted, behind, up in (
                (at.depth - 1 - s, at.depth - 1 - s > at.z, at.has_lower, True),
                (s, s < at.z, at.has_upper, False),
            ):
                ok = wanted
                if at_ends is True:
                    ok = jnp.logical_and(wanted, jnp.logical_not(behind))
                elif at_ends is False:
                    ok = jnp.logical_and(wanted, behind)

                @pl.when(ok)
                def _():
                    act(z, up)

            return carry

        lax.fori_loop(0, at.depth - 1, step, 0)

    def pairs_open(self, p):
        self.pair_steps(p, True, lambda z, up: self.pair_copy(p, z, up).start())

    def pair_y_copy(self, p):
        at = self.at
        return remote(
            self.block(p, 2 * at.z + 1 - at.y),
            self.pair_beside,
            self.pair_y_sems.at[0],
            self.pair_y_sems.at[1],
            at.beside,
        )

    def pairs(self, p):
        at, total, chunk = self.at, self.total, self.chunk

        def add(z, up):
            self.pair_copy(p, z, up).wait_recv()
            total[...] += self.pair_in[z + 1 if up else z].astype(f32)

        def on(z, up):
            own = self.block(p, 2 * z, 2)
            total[...] = own[...].astype(f32)
            add(z, up)
            own[...] = total[...].astype(bf16)
            self.pair_copy(p, z, up).start()

        self.pair_steps(p, False, on)
        total[...] = self.block(p, 2 * at.z, 2)[...].astype(f32)
        for has, up in ((at.has_lower, True), (at.has_upper, False)):

            @pl.when(has)
            def _():
                add(at.z, up)

        other = self.block(p, 2 * at.z + 1 - at.y)
        other[...] = total[rows_of((1 - at.y) * chunk, chunk), :].astype(bf16)
        self.pair_y_copy(p).start()

    def pairs_close(self, p):
        at, total, chunk = self.at, self.total, self.chunk
        self.pair_y_copy(p).wait()
        mine = total[rows_of(at.y * chunk, chunk), :] + self.pair_beside[...].astype(f32)
        total[pl.ds(0, chunk), :] = mine
        self.pair_steps(p, None, lambda z, up: self.pair_copy(p, z, up).wait_send())


def backward_kernel(
    ndp,
    held_in,
    normed_in,
    normed_two_in,
    grad_rows_in,
    streams_in,
    gates_in,
    first_in,
    grad_in,
    small,
    loss,
    tokens,
    grads_out,
    tokens_grad,
    small_out,
    held,
    rows_a,
    rows_b,
    acc,
    gates,
    streams,
    core_out,
    core_in,
    far_out,
    far_in,
    first,
    grad,
    back,
    gated,
    beside_in,
    line_in,
    pair_in,
    pair_beside,
    total,
    done,
    cur,
    got,
    share_sems,
    core_sems,
    far_sems,
    cube_sems,
    load_sems,
    held_sems,
    gate_sems,
    beside_sems,
    line_sems,
    pair_sems,
    pair_y_sems,
    done_sems,
    credits,
):
    at = place(ndp)
    pieces, width, piece = held.shape
    rows = tokens.shape[0]
    sub = rows // NSUB
    chunk = 2 * width // ndp
    half = chunk // 2
    channels = piece // 2
    order = list(range(2, pieces)) + [0, 1]
    share = Share(at, rows_a, rows, share_sems)
    sums = Sums(at, acc, rows, core_out, core_in, far_out, far_in, core_sems, far_sems)
    scatter = Scatter(
        at,
        held,
        chunk,
        pieces - 1,
        beside_in,
        line_in,
        pair_in,
        pair_beside,
        total,
        (beside_sems, line_sems, pair_sems, pair_y_sems),
        credits,
    )

    def load(src, dst, k):
        return pltpu.make_async_copy(src, dst, load_sems.at[k])

    def load_held(p):
        return pltpu.make_async_copy(held_in.at[p], held.at[p], held_sems.at[p])

    def load_gates(p):
        return pltpu.make_async_copy(gates_in.at[p - 2], gates.at[p % 2], gate_sems.at[p % 2])

    def load_streams(r):
        return load(streams_in.at[pl.ds(r * 2 * rows, 2 * rows), :], streams, 5)

    opening = (
        load(grad_rows_in, rows_a, 0),
        load_gates(2),
        load_held(2),
        load(normed_two_in, rows_b, 1),
    )
    for copy in opening:
        copy.start()
    load_gates(3).start()
    for p in order[1:]:
        load_held(p).start()
    load_first, load_grad = load(first_in, first, 2), load(grad_in, grad, 3)
    load_first.start()
    load_grad.start()
    load_streams(0).start()
    meet(at)
    acc[...] = jnp.zeros_like(acc)
    opening[0].wait()
    opening[3].wait()

    def ffn(p):
        load_gates(p).wait()
        load_held(p).wait()

        def some(r, carry):
            part = rows_of(((r + 1 - at.core) % 2) * 2 * rows, 2 * rows)
            grad_hidden = nn(rows_a[part, :], held[p, :, 2 * LANES :])
            gate = gates[p % 2, part, 0:LANES].astype(f32)
            up = gates[p % 2, part, LANES:].astype(f32)
            sig = jax.nn.sigmoid(gate)
            active = gate * sig
            back[part, 2 * LANES : 3 * LANES] = (active * up).astype(bf16)
            grad_gate = grad_hidden * up * sig * (1.0 + gate * (1.0 - sig))
            back[part, 0:LANES] = grad_gate.astype(bf16)
            back[part, LANES : 2 * LANES] = (grad_hidden * active).astype(bf16)
            acc[part, :] += nt(back[part, 0 : 2 * LANES], held[p, :, 0 : 2 * LANES])
            return carry

        lax.fori_loop(0, 2, some, 0)

        def weights(i, carry):
            part = rows_of(i * piece // 2, piece // 2, 128)
            held[p, part, 0 : 2 * LANES] = tn(rows_b[:, part], back[:, 0 : 2 * LANES]).astype(bf16)
            held[p, part, 2 * LANES :] = tn(rows_a[:, part], back[:, 2 * LANES : 3 * LANES]).astype(bf16)
            return carry

        lax.fori_loop(0, 2 * width // piece, weights, 0)

    def ffn_at(k):
        p = order[k]
        ffn(p)
        if p + 2 < pieces:
            load_gates(p + 2).start()

    def out_local(k):
        src = done.at[k % 2, rows_of(at.core * half, half, 8), :]
        return pltpu.make_async_copy(src, grads_out.at[at.core, order[k]], done_sems.at[0, order[k]])

    def out_sib(k):
        src = done.at[k % 2, rows_of((1 - at.core) * half, half, 8), :]
        dst = grads_out.at[at.core, order[k]]
        return remote(src, dst, done_sems.at[1, order[k]], done_sems.at[2, order[k]], at.sib)

    def from_sib(k):
        src = done.at[k % 2, rows_of((1 - at.core) * half, half, 8), :]
        dst = grads_out.at[1 - at.core, order[k]]
        return remote(src, dst, done_sems.at[1, order[k]], done_sems.at[2, order[k]], at.sib)

    def give(k):
        if k >= 2:
            out_local(k - 2).wait()
            out_sib(k - 2).wait_send()
        done[k % 2] = total[pl.ds(0, chunk), :]
        out_local(k).start()
        out_sib(k).start()

    def beside(k):
        scatter.send_beside(order[k], k - 1, order[k - 2] if k >= 3 else None)

    def line(k):
        scatter.line(order[k], k - 1, order[k - 2] if k >= 3 else None)
        give(k)

    gain_one, gain_two = small[0:1, :], small[1:2, :]
    ffn_at(0)
    scatter.pairs_open(order[0])
    ffn_at(1)
    beside(1)
    scatter.pairs(order[0])
    ffn_at(2)
    beside(2)
    scatter.pairs_close(order[0])
    give(0)
    ffn_pieces = pieces - 2
    for k in range(3, ffn_pieces):
        ffn_at(k)
        if k == ffn_pieces - 1:
            sums.to_core()
            load_normed = load(normed_in, rows_b, 4)
            load_normed.start()
        line(k - 2)
        beside(k)
    sums.to_far()
    line(ffn_pieces - 2)
    load_first.wait()
    load_grad.wait()
    gain_two_grad = jnp.zeros((1, width), f32)
    for j in range(NSUB):
        part = rows_of(j * sub, sub)
        coming = sums.take(j)
        source = first[part, :]
        inverse = inverse_of(source)
        weighted = coming * gain_two
        inner = jnp.mean(weighted * source, axis=1, keepdims=True)
        value = grad[part, :] + inverse * weighted - source * (inverse * inverse * inverse * inner)
        grad[part, :] = value
        gain_two_grad += jnp.sum(coming * source * inverse, axis=0, keepdims=True)
        rows_a[rows_of(at.own * rows + j * sub, sub), :] = value.astype(bf16)
        share.start(j)
    sums.finish()
    for j in range(NSUB):
        share.forward(j)
    share.finish()
    lane = at.x * 2 * channels + at.core * channels
    cur[0] = jnp.zeros(cur.shape[1:], f32)
    cur[0, 1:2, :] = gain_two_grad
    cur[0, 5:6, :] = jnp.broadcast_to(loss[0:1, 0:1], (1, width))
    taps = small[2:5, rows_of(lane, channels, 128)]
    load_held(0).wait()
    load_held(1).wait()
    for r in range(2):
        load_streams(r).wait()
        part = pl.ds(r * 2 * rows, 2 * rows)
        b_gate, c_gate = streams[:, 0:channels], streams[:, channels : 2 * channels]
        x_stream = streams[:, 2 * channels :]
        mixed = b_gate * x_stream
        convolved = convolve(mixed, taps)
        grad_gated = nn(rows_a[part, :], held[1, :, channels:])
        gated[part, :] = (c_gate * convolved).astype(bf16)
        back[part, channels : 2 * channels] = (grad_gated * convolved).astype(bf16)
        grad_conv = grad_gated * c_gate
        grad_mixed = taps[2:3] * grad_conv
        grad_mixed += taps[1:2] * shifted(grad_conv, -1) + taps[0:1] * shifted(grad_conv, -2)
        for k in range(3):
            tap = jnp.sum(grad_conv * shifted(mixed, 2 - k), axis=0, keepdims=True)
            cur[0, 2 + k : 3 + k, rows_of(lane, channels, 128)] += tap
        back[part, 0:channels] = (grad_mixed * x_stream).astype(bf16)
        back[part, 2 * channels :] = (grad_mixed * b_gate).astype(bf16)
        if r == 0:
            load_streams(1).start()
        value = nt(back[part, 0 : 2 * channels], held[0])
        acc[part, :] = value + nt(back[part, 2 * channels :], held[1, :, 0:channels])
    sums.to_core()
    load_normed.wait()

    def mixer_weights(i, carry):
        part = rows_of(i * channels, channels, 128)
        left = rows_b[:, part]
        held[0, part, :] = tn(left, back[:, 0 : 2 * channels]).astype(bf16)
        held[1, part, 0:channels] = tn(left, back[:, 2 * channels :]).astype(bf16)
        held[1, part, channels:] = tn(rows_a[:, part], gated[...]).astype(bf16)
        return carry

    lax.fori_loop(0, width // channels, mixer_weights, 0)
    beside(pieces - 2)
    sums.to_far()
    line(pieces - 3)
    beside(pieces - 1)
    gain_one_grad = jnp.zeros((1, width), f32)
    for j in range(NSUB):
        part = rows_of(j * sub, sub)
        coming = sums.take(j)
        source = tokens[part, :].astype(f32)
        inverse = inverse_of(source)
        weighted = coming * gain_one
        inner = jnp.mean(weighted * source, axis=1, keepdims=True)
        grad[part, :] += inverse * weighted - source * (inverse * inverse * inverse * inner)
        gain_one_grad += jnp.sum(coming * source * inverse, axis=0, keepdims=True)
    sums.finish()
    tokens_copy = load(grad, tokens_grad, 6)
    tokens_copy.start()
    cur[0, 0:1, :] = gain_one_grad
    line(pieces - 2)
    for step in range(len(at.cube)):
        total_step(at, step, cur, got, cube_sems.at[0], cube_sems.at[1])
    small_out[...] = cur[len(at.cube)]
    line(pieces - 1)
    for k in (pieces - 2, pieces - 1):
        scatter.drop_beside(order[k], k - 1)
        scatter.drop(order[k], k - 1)
        out_local(k).wait()
        out_sib(k).wait_send()
    for k in range(pieces):
        from_sib(k).wait_recv()
    tokens_copy.wait()


def backward(ndp, held, normed, normed_two, grad_rows, streams, gates, first, grad, small, loss, tokens):
    pieces, width, piece = held.shape
    rows = tokens.shape[0]
    chunk = 2 * width // ndp
    depth = ndp // 4
    channels = piece // 2
    cube = small_steps(ndp)
    dma = pltpu.SemaphoreType.DMA
    shape = jax.ShapeDtypeStruct
    outs = (
        shape((2, pieces, chunk // 2, piece), f32),
        shape((rows, width), f32),
        shape((8, width), f32),
    )
    scratch = [
        pltpu.VMEM((pieces, width, piece), bf16),
        pltpu.VMEM((4 * rows, width), bf16),
        pltpu.VMEM((4 * rows, width), bf16),
        pltpu.VMEM((4 * rows, width), f32),
        pltpu.VMEM((2, 4 * rows, 2 * LANES), bf16),
        pltpu.VMEM((2 * rows, 3 * channels), f32),
        pltpu.VMEM((2, rows, width), bf16),
        pltpu.VMEM((2, rows, width), bf16),
        pltpu.VMEM((rows, width), bf16),
        pltpu.VMEM((rows, width), bf16),
        pltpu.VMEM((rows, width), f32),
        pltpu.VMEM((rows, width), f32),
        pltpu.VMEM((4 * rows, 3 * channels), bf16),
        pltpu.VMEM((4 * rows, channels), bf16),
        pltpu.VMEM((2, depth, chunk, piece), bf16),
        pltpu.VMEM((2, depth + 1, chunk, piece), bf16),
        pltpu.VMEM((depth + 1, 2 * chunk, piece), bf16),
        pltpu.VMEM((chunk, piece), bf16),
        pltpu.VMEM((2 * chunk, piece), f32),
        pltpu.VMEM((2, chunk, piece), f32),
        pltpu.VMEM((cube + 1, 8, width), f32),
        pltpu.VMEM((cube, 8, width), f32),
        dma((6, NSUB)),
        dma((2, 2, NSUB)),
        dma((2, NSUB)),
        dma((2, cube)),
        dma((7,)),
        dma((pieces,)),
        dma((2,)),
        dma((2, 2, depth)),
        dma((3, 2, depth + 1)),
        dma((3, depth + 1)),
        dma((2,)),
        dma((3, pieces)),
        pltpu.SemaphoreType.REGULAR((3,)),
    ]
    return pl.pallas_call(
        functools.partial(backward_kernel, ndp),
        out_shape=outs,
        in_specs=[ANY] * 8 + [VMEM] * 3,
        out_specs=[ANY, ANY, VMEM],
        scratch_shapes=scratch,
        compiler_params=pltpu.CompilerParams(
            collective_id=1, has_side_effects=True, vmem_limit_bytes=63 << 20
        ),
    )(held, normed, normed_two, grad_rows, streams, gates, first, grad, small, loss, tokens)


def body(
    tokens,
    teacher,
    valid,
    mixer_gain,
    in_weight,
    conv_weight,
    out_weight,
    ffn_gain,
    gate_weight,
    up_weight,
    down_weight,
):
    ndp = lax.axis_size("dp")
    place_of = lax.axis_index("dp") * 2 + lax.axis_index("tensor")
    width = tokens.shape[1]
    valid_f = valid.astype(f32)
    vectors = jnp.concatenate([mixer_gain[None], ffn_gain[None], conv_weight], axis=0).astype(f32)
    share = vectors.shape[1]
    small = jnp.zeros((5, width), f32)
    small = lax.dynamic_update_slice(small, vectors, (0, place_of * share))
    small = jnp.concatenate([small, jnp.full((3, width), jnp.sum(valid_f), f32)], axis=0)
    shards = shard_pieces(in_weight, out_weight, gate_weight, up_weight, down_weight)
    held, normed, normed_two, grad_rows, streams, gates, first, block_out, grad, small, loss = forward(
        ndp, shards, tokens, teacher, valid_f[:, None], small
    )
    grads, tokens_grad, small_grads = backward(
        ndp, held, normed, normed_two, grad_rows, streams, gates, first, grad, small, loss, tokens
    )
    part_rows, _, channels = in_weight.shape
    channels //= 2
    units = gate_weight.shape[1]
    mixer = grads[:, 0:2].transpose(0, 2, 1, 3).reshape(2, part_rows, 4 * channels)
    in_grad = mixer[:, :, 0 : 3 * channels].reshape(2, part_rows, 3, channels)
    in_grad = in_grad.transpose(1, 2, 0, 3).reshape(part_rows, 3, 2 * channels)
    out_grad = mixer[:, :, 3 * channels :].transpose(1, 0, 2).reshape(part_rows, 2 * channels)

    def joined(k):
        cut = grads[:, 2:, :, k * LANES : (k + 1) * LANES]
        return cut.transpose(2, 0, 1, 3).reshape(part_rows, -1)[:, 0:units]

    own = lax.dynamic_slice(small_grads, (0, place_of * share), (5, share))
    return (
        small_grads[5, 0] / (width * small[5, 0]),
        block_out,
        tokens_grad,
        own[0],
        in_grad,
        own[2:5],
        out_grad,
        own[1],
        joined(0),
        joined(1),
        joined(2),
    )


def solution(mesh):
    rows = P(("dp", "tensor"), None)
    vector = P(("dp", "tensor"))
    weight = P("dp", "tensor")
    streams = P("dp", None, "tensor")
    taps = P(None, ("dp", "tensor"))
    return jax.shard_map(
        body,
        mesh=mesh,
        in_specs=(rows, rows, vector, vector, streams, taps, weight, vector, weight, weight, weight),
        out_specs=(P(), rows, rows, vector, streams, taps, weight, vector, weight, weight, weight),
        check_vma=False,
    )
```

```python
import functools
from types import SimpleNamespace

import jax
import jax.numpy as jnp
from jax import lax
from jax.experimental import pallas as pl
from jax.experimental.pallas import tpu as pltpu
from jax.sharding import PartitionSpec as P

MESH = pl.DeviceIdType.MESH
f32 = jnp.float32
bf16 = jnp.bfloat16
norm_eps = 1e-05
LANES = 256
NSUB = 3
YDEPTH, ZDEPTH = 3, 4
AHEAD = 4
VMEM = pl.BlockSpec(memory_space=pltpu.VMEM)
ANY = pl.BlockSpec(memory_space=pl.ANY)


def rows_of(start, size, step=16):
    return pl.ds(pl.multiple_of(start, step), size)


def place(ndp):
    d, x = lax.axis_index("dp"), lax.axis_index("tensor")
    core, y, z = d % 2, (d // 2) % 2, d // 4
    depth = ndp // 4
    at = SimpleNamespace(d=d, x=x, core=core, y=y, z=z, depth=depth, chip=d // 2)
    at.sib = (d + 1 - 2 * core, x)
    at.across = (d, 1 - x)
    at.beside = (d + 2 - 4 * y, x)
    at.lower, at.upper = (d - 4, x), (d + 4, x)
    at.has_lower, at.has_upper = z > 0, z < depth - 1
    at.cube = [at.sib, at.across, at.beside]
    step = 1
    while step < depth:
        at.cube.append((d + 4 * step * (1 - 2 * ((z // step) % 2)), x))
        step *= 2
    at.own = 2 * core + x
    at.own_sib = 2 * (1 - core) + x
    at.own_across = 2 * core + 1 - x
    at.own_far = 2 * (1 - core) + 1 - x
    return at


def meet(at):
    bar = pltpu.get_barrier_semaphore()
    always = [at.sib, at.across, at.beside] + at.cube[4:]
    for dev in always:
        pl.semaphore_signal(bar, 1, device_id=dev, device_id_type=MESH)
    for has, dev in ((at.has_lower, at.lower), (at.has_upper, at.upper)):

        @pl.when(has)
        def _():
            pl.semaphore_signal(bar, 1, device_id=dev, device_id_type=MESH)

    ends = jnp.where(at.has_lower, 1, 0) + jnp.where(at.has_upper, 1, 0)
    pl.semaphore_wait(bar, len(always) + ends)


def remote(src, dst, send, recv, dev):
    return pltpu.make_async_remote_copy(
        src_ref=src, dst_ref=dst, send_sem=send, recv_sem=recv, device_id=dev, device_id_type=MESH
    )


def total_copy(at, step, cur, got, send, recv):
    return remote(cur.at[step], got.at[step], send.at[step], recv.at[step], at.cube[step])


def total_end(at, step, cur, got, copy):
    copy.wait()
    cur[step + 1] = cur[step] + got[step]


def total_step(at, step, cur, got, send, recv):
    copy = total_copy(at, step, cur, got, send, recv)
    copy.start()
    total_end(at, step, cur, got, copy)


class Share:
    def __init__(self, at, buf, rows, sems):
        self.at, self.buf, self.rows, self.sems = at, buf, rows, sems
        self.sub = rows // NSUB

    def part(self, slot, j):
        return self.buf.at[rows_of(slot * self.rows + j * self.sub, self.sub), :]

    def copy(self, slot, j, k, dev):
        part = self.part(slot, j)
        return remote(part, part, self.sems.at[2 * k, j], self.sems.at[2 * k + 1, j], dev)

    def start(self, j):
        self.copy(self.at.own, j, 0, self.at.across).start()
        self.copy(self.at.own, j, 1, self.at.sib).start()

    def forward(self, j):
        self.copy(self.at.own_across, j, 0, self.at.across).wait_recv()
        self.copy(self.at.own_across, j, 2, self.at.sib).start()

    def finish(self):
        for j in range(NSUB):
            self.copy(self.at.own_sib, j, 1, self.at.sib).wait_recv()
            self.copy(self.at.own_far, j, 2, self.at.sib).wait_recv()
            self.copy(self.at.own, j, 0, self.at.across).wait_send()
            self.copy(self.at.own, j, 1, self.at.sib).wait_send()
            self.copy(self.at.own_across, j, 2, self.at.sib).wait_send()


class Sums:
    def __init__(self, at, acc, rows, core_out, core_in, far_in, core_sems, far_sems):
        self.at, self.acc, self.rows = at, acc, rows
        self.core_out, self.core_in, self.far_in = core_out, core_in, far_in
        self.core_sems, self.far_sems = core_sems, far_sems
        self.sub = rows // NSUB

    def of(self, slot, j):
        return self.acc[rows_of(slot * self.rows + j * self.sub, self.sub), :]

    def core_copy(self, k, j):
        part = rows_of(j * self.sub, self.sub)
        return remote(
            self.core_out.at[k, part, :],
            self.core_in.at[k, part, :],
            self.core_sems.at[0, k, j],
            self.core_sems.at[1, k, j],
            self.at.sib,
        )

    def far_copy(self, j):
        part = rows_of(j * self.sub, self.sub)
        return remote(
            self.core_in.at[0, part, :],
            self.far_in.at[part, :],
            self.far_sems.at[0, j],
            self.far_sems.at[1, j],
            self.at.across,
        )

    def to_core(self):
        for k, slot in ((0, self.at.own_far), (1, self.at.own_sib)):
            for j in range(NSUB):
                self.core_out[k, rows_of(j * self.sub, self.sub), :] = self.of(slot, j).astype(bf16)
                self.core_copy(k, j).start()

    def to_far(self):
        for j in range(NSUB):
            part = rows_of(j * self.sub, self.sub)
            self.core_copy(0, j).wait_recv()
            both = self.of(self.at.own_across, j) + self.core_in[0, part, :].astype(f32)
            self.core_in[0, part, :] = both.astype(bf16)
            self.far_copy(j).start()

    def take(self, j):
        part = rows_of(j * self.sub, self.sub)
        self.core_copy(1, j).wait_recv()
        self.far_copy(j).wait_recv()
        return (
            self.of(self.at.own, j)
            + self.core_in[1, part, :].astype(f32)
            + self.far_in[part, :].astype(f32)
        )

    def finish(self):
        for j in range(NSUB):
            self.core_copy(0, j).wait_send()
            self.core_copy(1, j).wait_send()
            self.far_copy(j).wait_send()


def nt(left, right):
    return lax.dot_general(left, right, (((1,), (1,)), ((), ())), preferred_element_type=f32)


def tn(left, right):
    return lax.dot_general(left, right, (((0,), (0,)), ((), ())), preferred_element_type=f32)


def nn(left, right):
    return jnp.dot(left, right, preferred_element_type=f32)


def inverse_of(source):
    return lax.rsqrt(jnp.mean(source * source, axis=1, keepdims=True) + norm_eps)


def shifted(value, by):
    if by == 0:
        return value
    size = value.shape[0]
    row = lax.broadcasted_iota(jnp.int32, value.shape, 0)
    inside = row >= by if by > 0 else row < size + by
    return jnp.where(inside, pltpu.roll(value, by % size, 0), 0.0)


def convolve(mixed, taps):
    return taps[0:1] * shifted(mixed, 2) + taps[1:2] * shifted(mixed, 1) + taps[2:3] * mixed


class Gather:
    def __init__(self, at, held, chunk, early_y, sems):
        self.at, self.held, self.chunk, self.early_y = at, held, chunk, early_y
        self.recv, self.own_send, self.send = sems

    def block(self, p, chip, count=1):
        return self.held.at[p, rows_of(chip * self.chunk, count * self.chunk), :]

    def copy(self, p, chip, count, send, dev):
        block = self.block(p, chip, count)
        return remote(block, block, send, self.recv.at[p, chip], dev)

    def arrived(self, p, chip, count=1):
        self.copy(p, chip, count, self.own_send.at[0, 0], self.at.beside).wait_recv()

    def own(self, p, act):
        at = self.at
        act(self.copy(p, at.chip, 1, self.own_send.at[0, p], at.beside))
        if p not in self.early_y:
            self.own_z(p, at.chip, 1, act)

    def own_z(self, p, chip, count, act):
        at = self.at

        @pl.when(at.has_upper)
        def _():
            act(self.copy(p, chip, count, self.own_send.at[1, p], at.upper))

        @pl.when(at.has_lower)
        def _():
            act(self.copy(p, chip, count, self.own_send.at[2, p], at.lower))

    def passing(self, p, pairs, parity, wait, act):
        at = self.at

        def step(s, carry):
            for from_z, goes_on, dev, way in (
                (at.z - 1 - s, at.has_upper, at.upper, 0),
                (at.z + 1 + s, at.has_lower, at.lower, 1),
            ):

                @pl.when(jnp.logical_and(from_z >= 0, from_z < at.depth))
                def _():
                    chip = 2 * from_z if pairs else 2 * from_z + at.y
                    count = 2 if pairs else 1
                    if wait:
                        self.arrived(p, chip, count)

                    @pl.when(goes_on)
                    def _():
                        act(self.copy(p, chip, count, self.send.at[way, parity, from_z], dev))

                    if not pairs:
                        act(self.copy(p, chip, count, self.send.at[2, parity, from_z], at.beside))

            return carry

        lax.fori_loop(0, at.depth - 1, step, 0)

    def relay(self, p, parity, drop):
        if drop is not None:
            self.passing(drop[0], drop[1], parity, False, lambda copy: copy.wait_send())
        pairs = isinstance(p, int) and p in self.early_y
        if pairs:
            self.arrived(p, 2 * self.at.z + 1 - self.at.y)
            self.own_z(p, 2 * self.at.z, 2, lambda copy: copy.start())
        self.passing(p, pairs, parity, True, lambda copy: copy.start())

    def whole(self, p):
        def step(z, carry):
            self.arrived(p, 2 * z + 1 - self.at.y)
            return carry

        lax.fori_loop(0, self.at.depth, step, 0)


def forward_kernel(
    ndp,
    early_y,
    shards,
    tokens,
    teacher,
    valid,
    small,
    held_out,
    normed_out,
    normed_two_out,
    grad_rows_out,
    streams_out,
    gates_out,
    first_out,
    block_out,
    grad_out,
    small_out,
    loss_out,
    held,
    landed,
    mine,
    rows_a,
    rows_b,
    acc,
    streams,
    gates,
    core_out,
    core_in,
    far_in,
    first,
    result,
    error_grad,
    cur,
    got,
    chip_sems,
    recv_sems,
    own_sems,
    send_sems,
    share_sems,
    core_sems,
    far_sems,
    cube_sems,
    out_sems,
    held_sems,
    gate_sems,
):
    at = place(ndp)
    pieces, width, piece = held.shape
    part_rows = shards.shape[2]
    chunk = 2 * part_rows
    rows = tokens.shape[0]
    sub = rows // NSUB
    channels = streams.shape[1] // 3
    aligned = part_rows % 16 == 0
    go = lambda copy: copy.start()
    gather = Gather(at, held, chunk, early_y, (recv_sems, own_sems, send_sems))
    share_a = Share(at, rows_a, rows, share_sems)
    share_b = Share(at, rows_b, rows, share_sems)
    sums = Sums(at, acc, rows, core_out, core_in, far_in, core_sems, far_sems)

    def half(p, core):
        return held.at[p, rows_of(at.chip * chunk + core * part_rows, part_rows), :]

    def to_sib(p):
        dst = half(p, at.core) if aligned else landed.at[p]
        return remote(shards.at[1 - at.core, p], dst, chip_sems.at[0, p], chip_sems.at[1, p], at.sib)

    def from_sib(p):
        dst = half(p, 1 - at.core) if aligned else landed.at[p]
        return remote(dst, dst, chip_sems.at[0, p], chip_sems.at[1, p], at.sib)

    def keep(p):
        dst = half(p, at.core) if aligned else mine.at[p]
        return pltpu.make_async_copy(shards.at[at.core, p], dst, chip_sems.at[2, p])

    def own_block(p):
        keep(p).wait()
        from_sib(p).wait_recv()
        if not aligned:
            a, b = mine[p].astype(f32), landed[p].astype(f32)
            lower = jnp.where(at.core == 0, a, b)
            upper = jnp.where(at.core == 0, b, a)
            both = jnp.concatenate([lower, upper], axis=0).astype(bf16)
            held[p, rows_of(at.chip * chunk, chunk), :] = both
        gather.own(p, go)

    meet(at)
    to_sib(0).start()
    keep(0).start()
    cur[0] = small[...]
    total_step(at, 0, cur, got, cube_sems.at[0], cube_sems.at[1])
    own_block(0)
    total_step(at, 1, cur, got, cube_sems.at[0], cube_sems.at[1])
    for j in range(NSUB):
        rows_a[rows_of(at.own * rows + j * sub, sub), :] = tokens[pl.ds(j * sub, sub), :]
        share_a.start(j)
    for p in range(1, pieces):
        to_sib(p).start()
        keep(p).start()
    for step in range(2, len(at.cube)):
        total_step(at, step, cur, got, cube_sems.at[0], cube_sems.at[1])
        if step < 4:
            own_block(step - 1)
    last = len(at.cube)
    small_out[...] = cur[last]
    for j in range(NSUB):
        share_a.forward(j)
    gain_one, gain_two = cur[last, 0:1, :], cur[last, 1:2, :]
    relay = lambda p: gather.relay(p, p % AHEAD, (p - AHEAD, p - AHEAD in early_y) if p >= AHEAD else None)
    relay(0)
    share_a.finish()

    def norm_rows(i, carry):
        part = rows_of(i * sub, sub)
        source = rows_a[part, :].astype(f32)
        rows_a[part, :] = (source * inverse_of(source) * gain_one).astype(bf16)
        return carry

    lax.fori_loop(0, 4 * NSUB, norm_rows, 0)
    normed_copy = pltpu.make_async_copy(rows_a, normed_out, out_sems.at[0])
    normed_copy.start()

    def save(p):
        return pltpu.make_async_copy(held.at[p], held_out.at[p], held_sems.at[p])

    own_block(3)
    relay(1)
    own_block(4)
    relay(2)
    own_block(5)
    for p in (0, 1):
        gather.whole(p)
        save(p).start()
    lane = at.x * 2 * channels + at.core * channels
    taps = cur[last, 2:5, rows_of(lane, channels, 128)]

    def mix(r, carry):
        part = rows_of(((r + 1 - at.core) % 2) * 2 * rows, 2 * rows)
        both = nn(rows_a[part, :], held[0])
        x_stream = nn(rows_a[part, :], held[1, :, 0:channels])
        streams[part, 0 : 2 * channels] = both
        streams[part, 2 * channels :] = x_stream
        convolved = convolve(both[:, 0:channels] * x_stream, taps)
        gated = (both[:, channels:] * convolved).astype(bf16)
        acc[part, :] = nt(gated, held[1, :, channels:])
        return carry

    lax.fori_loop(0, 2, mix, 0)
    streams_copy = pltpu.make_async_copy(streams, streams_out, out_sems.at[1])
    streams_copy.start()
    sums.to_core()
    own_block(6)
    own_block(7)
    sums.to_far()
    relay(3)
    for p in range(8, pieces):
        own_block(p)
    for j in range(NSUB):
        part = rows_of(j * sub, sub)
        value = tokens[part, :].astype(f32) + sums.take(j)
        first[part, :] = value
        normed_two = (value * inverse_of(value) * gain_two).astype(bf16)
        rows_b[rows_of(at.own * rows + j * sub, sub), :] = normed_two
        share_b.start(j)
    sums.finish()
    first_copy = pltpu.make_async_copy(first, first_out, out_sems.at[2])
    first_copy.start()
    relay(4)
    for j in range(NSUB):
        share_b.forward(j)
    share_b.finish()
    normed_two_copy = pltpu.make_async_copy(rows_b, normed_two_out, out_sems.at[3])
    normed_two_copy.start()
    acc[...] = jnp.zeros_like(acc)

    def gates_copy(p):
        slot = p % 2
        return pltpu.make_async_copy(gates.at[slot], gates_out.at[p - 2], gate_sems.at[slot])

    def feed(p, carry):
        for q in range(5, pieces):

            @pl.when(p == q - 3)
            def _():
                relay(q)

        for q in range(2, pieces):
            if q not in early_y:

                @pl.when(p == q)
                def _():
                    gather.whole(q)

        save(p).start()

        @pl.when(p >= 4)
        def _():
            gates_copy(p - 2).wait()

        def some(r, inner):
            part = rows_of(((r + 1 - at.core) % 2) * 2 * rows, 2 * rows)
            both = nn(rows_b[part, :], held[p, :, 0 : 2 * LANES])
            gate, up = both[:, 0:LANES], both[:, LANES:]
            gates[p % 2, part, :] = both.astype(bf16)
            hidden = (gate * jax.nn.sigmoid(gate) * up).astype(bf16)
            acc[part, :] += nt(hidden, held[p, :, 2 * LANES :])
            return inner

        lax.fori_loop(0, 2, some, 0)
        gates_copy(p).start()
        return carry

    normed_copy.wait()
    lax.fori_loop(2, pieces, feed, 0)
    sums.to_core()
    sums.to_far()
    scale = 1.0 / (width * cur[last, 5:6, 0:1])
    loss = jnp.zeros((1, width), f32)
    for j in range(NSUB):
        part = rows_of(j * sub, sub)
        value = first[part, :] + sums.take(j)
        result[part, :] = value
        error = value - teacher[part, :].astype(f32)
        weighted = valid[part, :] * error
        loss = loss + jnp.sum(weighted * error, axis=0, keepdims=True)
        grad = (2.0 * scale) * weighted
        error_grad[part, :] = grad
        rows_a[rows_of(at.own * rows + j * sub, sub), :] = grad.astype(bf16)
        share_a.start(j)
    loss_out[...] = jnp.broadcast_to(jnp.sum(loss, axis=1, keepdims=True), loss_out.shape)
    sums.finish()
    result_copy = pltpu.make_async_copy(result, block_out, out_sems.at[4])
    result_copy.start()
    grad_copy = pltpu.make_async_copy(error_grad, grad_out, out_sems.at[5])
    grad_copy.start()
    for j in range(NSUB):
        share_a.forward(j)
    share_a.finish()
    rows_copy = pltpu.make_async_copy(rows_a, grad_rows_out, out_sems.at[6])
    rows_copy.start()
    for p in range(pieces):
        save(p).wait()
        to_sib(p).wait_send()
        gather.own(p, lambda copy: copy.wait_send())
        if p in early_y:
            gather.own_z(p, 2 * at.z, 2, lambda copy: copy.wait_send())
    for p in range(pieces - AHEAD, pieces):
        gather.passing(p, p in early_y, p % AHEAD, False, lambda copy: copy.wait_send())
    for p in (pieces - 2, pieces - 1):
        gates_copy(p).wait()
    for copy in (streams_copy, first_copy, normed_two_copy, result_copy, grad_copy, rows_copy):
        copy.wait()


def forward(ndp, shards, tokens, teacher, valid, small):
    _, pieces, part_rows, piece = shards.shape
    rows, width = tokens.shape
    channels = (2 * piece - piece // 2) // 3
    cube = small_steps(ndp)
    early_y = (3,)
    dma = pltpu.SemaphoreType.DMA
    landing = (pieces, part_rows, piece) if part_rows % 16 else (1, 16, 128)
    shape = jax.ShapeDtypeStruct
    outs = (
        shape((pieces, width, piece), bf16),
        shape((4 * rows, width), bf16),
        shape((4 * rows, width), bf16),
        shape((4 * rows, width), bf16),
        shape((4 * rows, 3 * channels), f32),
        shape((pieces - 2, 4 * rows, 2 * LANES), bf16),
        shape((rows, width), f32),
        shape((rows, width), f32),
        shape((rows, width), f32),
        shape((8, width), f32),
        shape((8, 128), f32),
    )
    scratch = [
        pltpu.VMEM((pieces, width, piece), bf16),
        pltpu.VMEM(landing, bf16),
        pltpu.VMEM(landing, bf16),
        pltpu.VMEM((4 * rows, width), bf16),
        pltpu.VMEM((4 * rows, width), bf16),
        pltpu.VMEM((4 * rows, width), f32),
        pltpu.VMEM((4 * rows, 3 * channels), f32),
        pltpu.VMEM((2, 4 * rows, 2 * LANES), bf16),
        pltpu.VMEM((2, rows, width), bf16),
        pltpu.VMEM((2, rows, width), bf16),
        pltpu.VMEM((rows, width), bf16),
        pltpu.VMEM((rows, width), f32),
        pltpu.VMEM((rows, width), f32),
        pltpu.VMEM((rows, width), f32),
        pltpu.VMEM((cube + 1, 8, width), f32),
        pltpu.VMEM((cube, 8, width), f32),
        dma((3, pieces)),
        dma((pieces, ndp // 2)),
        dma((3, pieces)),
        dma((3, AHEAD, ndp // 4)),
        dma((6, NSUB)),
        dma((2, 2, NSUB)),
        dma((2, NSUB)),
        dma((2, cube)),
        dma((7,)),
        dma((pieces,)),
        dma((2,)),
    ]
    return pl.pallas_call(
        functools.partial(forward_kernel, ndp, early_y),
        out_shape=outs,
        in_specs=[ANY, VMEM, VMEM, VMEM, VMEM],
        out_specs=[ANY] * 9 + [VMEM] * 2,
        scratch_shapes=scratch,
        compiler_params=pltpu.CompilerParams(
            collective_id=0, has_side_effects=True, vmem_limit_bytes=63 << 20
        ),
    )(shards, tokens, teacher, valid, small)


def small_steps(ndp):
    return 3 + (ndp // 4 - 1).bit_length()


def shard_pieces(in_weight, out_weight, gate_weight, up_weight, down_weight):
    part_rows, _, channels = in_weight.shape
    channels //= 2
    taps = in_weight.reshape(part_rows, 3, 2, channels).transpose(2, 0, 1, 3)
    taps = taps.reshape(2, part_rows, 3 * channels)
    outs = out_weight.reshape(part_rows, 2, channels).transpose(1, 0, 2)
    mixer = jnp.concatenate([taps, outs], axis=2)
    mixer = mixer.reshape(2, part_rows, 2, 2 * channels).transpose(0, 2, 1, 3)
    units = gate_weight.shape[1]
    count = -(-units // (2 * LANES))

    def cut(weight):
        weight = jnp.pad(weight, ((0, 0), (0, 2 * count * LANES - units)))
        return weight.reshape(part_rows, 2, count, LANES).transpose(1, 2, 0, 3)

    ffn = jnp.concatenate([cut(gate_weight), cut(up_weight), cut(down_weight)], axis=3)
    return jnp.concatenate([mixer, ffn], axis=1)


class Scatter:
    def __init__(self, at, held, chunk, count, beside_in, line_in, pair_in, pair_beside, total, sems, credits):
        self.at, self.held, self.chunk, self.count = at, held, chunk, count
        self.beside_in, self.line_in, self.pair_in, self.pair_beside = beside_in, line_in, pair_in, pair_beside
        self.total, self.credits = total, credits
        self.beside_sems, self.line_sems, self.pair_sems, self.pair_y_sems = sems
        self.ydepth, self.zdepth = beside_in.shape[0], line_in.shape[0]

    def block(self, p, chip, count=1):
        return self.held.at[p, rows_of(chip * self.chunk, count * self.chunk), :]

    def beside_copy(self, p, m, z):
        slot = m % self.ydepth
        return remote(
            self.block(p, 2 * z + 1 - self.at.y),
            self.beside_in.at[slot, z],
            self.beside_sems.at[0, slot, z],
            self.beside_sems.at[1, slot, z],
            self.at.beside,
        )

    def line_copy(self, p, m, z, up):
        slot, way = m % self.zdepth, 0 if up else 1
        into = z + 1 if up else z
        return remote(
            self.block(p, 2 * z + self.at.y),
            self.line_in.at[slot, into],
            self.line_sems.at[way, slot, z],
            self.line_sems.at[2, slot, into],
            self.at.upper if up else self.at.lower,
        )

    def pair_copy(self, p, z, up):
        into = z + 1 if up else z
        return remote(
            self.block(p, 2 * z, 2),
            self.pair_in.at[into],
            self.pair_sems.at[0 if up else 1, z],
            self.pair_sems.at[2, into],
            self.at.upper if up else self.at.lower,
        )

    def turn(self, s):
        return (s % 2) * (s // 2) + (1 - s % 2) * (self.at.depth - 1 - s // 2)

    def free_beside(self, p, m, before):
        if m >= self.ydepth:
            pl.semaphore_wait(self.credits.at[0], 1)
            self.drop_beside(before, m)

    def drop_beside(self, p, m):
        def step(z, carry):
            self.beside_copy(p, m, z).wait_send()
            return carry

        lax.fori_loop(0, self.at.depth, step, 0)

    def send_beside(self, p, m, before):
        self.free_beside(p, m, before)

        def step(s, carry):
            self.beside_copy(p, m, self.turn(s)).start()
            return carry

        lax.fori_loop(0, self.at.depth, step, 0)

    def ways(self, has, act):
        at = self.at

        def step(s, carry):
            for z, wanted, up in (
                (at.depth - 1 - s, at.depth - 1 - s > at.z, True),
                (s, s < at.z, False),
            ):

                @pl.when(jnp.logical_and(wanted, has(up)))
                def _():
                    act(z, up)

            return carry

        lax.fori_loop(0, at.depth - 1, step, 0)

    def behind(self, up):
        return self.at.has_lower if up else self.at.has_upper

    def opens(self, up):
        return jnp.logical_not(self.behind(up))

    def near(self, up):
        low = self.at.z < self.at.depth // 2
        return jnp.logical_and(self.behind(up), low if up else jnp.logical_not(low))

    def far(self, up):
        low = self.at.z < self.at.depth // 2
        return jnp.logical_and(self.behind(up), jnp.logical_not(low) if up else low)

    def add_beside(self, p, m, before):
        at = self.at
        if m >= self.zdepth:
            for has, credit in ((at.has_upper, 1), (at.has_lower, 2)):

                @pl.when(has)
                def _():
                    pl.semaphore_wait(self.credits.at[credit], 1)

            self.drop(before, m)

        def step(s, carry):
            z = self.turn(s)
            own = self.block(p, 2 * z + at.y)
            self.beside_copy(p, m, z).wait_recv()
            own[...] = (own[...].astype(f32) + self.beside_in[m % self.ydepth, z].astype(f32)).astype(bf16)
            for up in (True, False):

                @pl.when(jnp.logical_and(z > at.z if up else z < at.z, self.opens(up)))
                def _():
                    self.line_copy(p, m, z, up).start()

            return carry

        lax.fori_loop(0, at.depth, step, 0)
        if m + self.ydepth < self.count:
            pl.semaphore_signal(self.credits.at[0], 1, device_id=at.beside, device_id_type=MESH)

    def hop(self, p, m, has):
        def act(z, up):
            self.line_copy(p, m, z, up).wait_recv()
            own = self.block(p, 2 * z + self.at.y)
            came = self.line_in[m % self.zdepth, z + 1 if up else z].astype(f32)
            own[...] = (own[...].astype(f32) + came).astype(bf16)
            self.line_copy(p, m, z, up).start()

        self.ways(has, act)

    def collect(self, p, m, slot):
        at = self.at
        total = self.total.at[slot]
        total[...] = self.block(p, 2 * at.z + at.y)[...].astype(f32)
        for up in (True, False):

            @pl.when(self.behind(up))
            def _():
                self.line_copy(p, m, at.z, up).wait_recv()
                total[...] += self.line_in[m % self.zdepth, at.z + 1 if up else at.z].astype(f32)
                if m + self.zdepth < self.count:
                    pl.semaphore_signal(
                        self.credits.at[1 if up else 2],
                        1,
                        device_id=at.lower if up else at.upper,
                        device_id_type=MESH,
                    )

    def drop(self, p, m):
        self.ways(lambda up: True, lambda z, up: self.line_copy(p, m, z, up).wait_send())

    def pairs_open(self, p):
        self.ways(self.opens, lambda z, up: self.pair_copy(p, z, up).start())

    def pair_hop(self, p, has):
        def act(z, up):
            self.pair_copy(p, z, up).wait_recv()
            own = self.block(p, 2 * z, 2)
            own[...] = (own[...].astype(f32) + self.pair_in[z + 1 if up else z].astype(f32)).astype(bf16)
            self.pair_copy(p, z, up).start()

        self.ways(has, act)

    def pair_y_copy(self, p):
        at = self.at
        return remote(
            self.block(p, 2 * at.z + 1 - at.y),
            self.pair_beside,
            self.pair_y_sems.at[0],
            self.pair_y_sems.at[1],
            at.beside,
        )

    def pairs_cross(self, p):
        at = self.at
        own = self.block(p, 2 * at.z, 2)
        for up in (True, False):

            @pl.when(self.behind(up))
            def _():
                self.pair_copy(p, at.z, up).wait_recv()
                came = self.pair_in[at.z + 1 if up else at.z].astype(f32)
                own[...] = (own[...].astype(f32) + came).astype(bf16)

        self.pair_y_copy(p).start()

    def pairs_close(self, p, slot):
        at = self.at
        self.pair_y_copy(p).wait()
        mine = self.block(p, 2 * at.z + at.y)[...].astype(f32)
        self.total[slot] = mine + self.pair_beside[...].astype(f32)
        self.ways(lambda up: True, lambda z, up: self.pair_copy(p, z, up).wait_send())


def backward_kernel(
    ndp,
    held_in,
    normed_in,
    normed_two_in,
    grad_rows_in,
    streams_in,
    gates_in,
    first_in,
    grad_in,
    small,
    loss,
    tokens,
    grads_out,
    tokens_grad,
    small_out,
    held,
    rows_a,
    rows_b,
    acc,
    gates,
    streams,
    core_out,
    core_in,
    far_in,
    first,
    grad,
    back,
    beside_in,
    line_in,
    pair_in,
    pair_beside,
    total,
    cur,
    got,
    share_sems,
    core_sems,
    far_sems,
    cube_sems,
    load_sems,
    held_sems,
    gate_sems,
    beside_sems,
    line_sems,
    pair_sems,
    pair_y_sems,
    done_sems,
    credits,
):
    at = place(ndp)
    pieces, width, piece = held.shape
    rows = tokens.shape[0]
    sub = rows // NSUB
    chunk = 2 * width // ndp
    half = chunk // 2
    channels = piece // 2
    order = [2] + list(range(4, pieces)) + [0, 1]
    paired = 3
    share = Share(at, rows_a, rows, share_sems)
    sums = Sums(at, acc, rows, core_out, core_in, far_in, core_sems, far_sems)
    scatter = Scatter(
        at,
        held,
        chunk,
        len(order),
        beside_in,
        line_in,
        pair_in,
        pair_beside,
        total,
        (beside_sems, line_sems, pair_sems, pair_y_sems),
        credits,
    )

    def load(src, dst, k):
        return pltpu.make_async_copy(src, dst, load_sems.at[k])

    def load_held(p):
        return pltpu.make_async_copy(held_in.at[p], held.at[p], held_sems.at[p])

    def load_gates(p):
        return pltpu.make_async_copy(gates_in.at[p - 2], gates.at[p % 2], gate_sems.at[p % 2])

    def load_streams(r):
        return load(streams_in.at[pl.ds(r * 2 * rows, 2 * rows), :], streams, 5)

    opening = (
        load(grad_rows_in, rows_a, 0),
        load_gates(2),
        load_held(2),
        load(normed_two_in, rows_b, 1),
    )
    for copy in opening:
        copy.start()
    load_gates(3).start()
    for p in list(range(3, pieces)) + [0, 1]:
        load_held(p).start()
    load_first, load_grad = load(first_in, first, 2), load(grad_in, grad, 3)
    load_first.start()
    load_grad.start()
    load_streams(0).start()
    meet(at)
    acc[...] = jnp.zeros_like(acc)
    opening[0].wait()
    opening[3].wait()

    def ffn(p, m=None):
        load_gates(p).wait()
        load_held(p).wait()

        def some(r, carry):
            part = rows_of(((r + 1 - at.core) % 2) * 2 * rows, 2 * rows)
            grad_hidden = nn(rows_a[part, :], held[p, :, 2 * LANES :])
            gate = gates[p % 2, part, 0:LANES].astype(f32)
            up = gates[p % 2, part, LANES:].astype(f32)
            sig = jax.nn.sigmoid(gate)
            active = gate * sig
            back[part, 2 * LANES : 3 * LANES] = (active * up).astype(bf16)
            grad_gate = grad_hidden * up * sig * (1.0 + gate * (1.0 - sig))
            back[part, 0:LANES] = grad_gate.astype(bf16)
            back[part, LANES : 2 * LANES] = (grad_hidden * active).astype(bf16)
            acc[part, :] += nt(back[part, 0 : 2 * LANES], held[p, :, 0 : 2 * LANES])
            return carry

        lax.fori_loop(0, 2, some, 0)

        blocks = 2 * width // piece
        each = at.depth // blocks

        def weights(s, carry):
            i = (s % 2) * (s // 2) + (1 - s % 2) * (blocks - 1 - s // 2)
            part = rows_of(i * piece // 2, piece // 2, 128)
            held[p, part, 0 : 2 * LANES] = tn(rows_b[:, part], back[:, 0 : 2 * LANES]).astype(bf16)
            held[p, part, 2 * LANES :] = tn(rows_a[:, part], back[:, 2 * LANES : 3 * LANES]).astype(bf16)
            if m is not None:
                for e in range(each):
                    scatter.beside_copy(p, m, i * each + e).start()
            return carry

        lax.fori_loop(0, blocks, weights, 0)
        if p + 2 < pieces:
            load_gates(p + 2).start()

    given = []

    def out_local(p):
        src = total.at[given.index(p) % 2, rows_of(at.core * half, half, 8), :]
        return pltpu.make_async_copy(src, grads_out.at[at.core, p], done_sems.at[0, p])

    def out_sib(p):
        src = total.at[given.index(p) % 2, rows_of((1 - at.core) * half, half, 8), :]
        return remote(src, grads_out.at[at.core, p], done_sems.at[1, p], done_sems.at[2, p], at.sib)

    def from_sib(p):
        src = total.at[0, rows_of((1 - at.core) * half, half, 8), :]
        return remote(src, grads_out.at[1 - at.core, p], done_sems.at[1, p], done_sems.at[2, p], at.sib)

    def give(p, fill):
        if len(given) > 1:
            out_local(given[-2]).wait()
            out_sib(given[-2]).wait_send()
        given.append(p)
        fill((len(given) - 1) % 2)
        out_local(p).start()
        out_sib(p).start()

    def beside(m):
        scatter.send_beside(order[m], m, order[m - YDEPTH] if m >= YDEPTH else None)

    def finish(m):
        give(order[m], functools.partial(scatter.collect, order[m], m))

    def advance(m):
        scatter.add_beside(order[m], m, order[m - ZDEPTH] if m >= ZDEPTH else None)
        scatter.hop(order[m], m, scatter.near)
        if m == 0:
            scatter.pair_hop(paired, scatter.near)
        if m >= 1:
            scatter.hop(order[m - 1], m - 1, scatter.far)
        if m == 2:
            scatter.pair_hop(paired, scatter.far)
        if m >= 2:
            finish(m - 2)
        if m == 3:
            scatter.pairs_cross(paired)
        if m == 4:
            give(paired, functools.partial(scatter.pairs_close, paired))

    gain_one, gain_two = small[0:1, :], small[1:2, :]
    ffn(2, 0)
    ffn(3)
    scatter.pairs_open(paired)
    ffn(4, 1)
    ffn(5, 2)
    advance(0)
    ffn(6)
    beside(3)
    for p in range(7, pieces):
        ffn(p)
    sums.to_core()
    load_normed = load(normed_in, rows_b, 4)
    load_normed.start()
    advance(1)
    beside(4)
    sums.to_far()
    load_first.wait()
    load_grad.wait()
    gain_two_grad = jnp.zeros((1, width), f32)
    for j in range(NSUB):
        part = rows_of(j * sub, sub)
        coming = sums.take(j)
        source = first[part, :]
        inverse = inverse_of(source)
        weighted = coming * gain_two
        inner = jnp.mean(weighted * source, axis=1, keepdims=True)
        value = grad[part, :] + inverse * weighted - source * (inverse * inverse * inverse * inner)
        grad[part, :] = value
        gain_two_grad += jnp.sum(coming * source * inverse, axis=0, keepdims=True)
        rows_a[rows_of(at.own * rows + j * sub, sub), :] = value.astype(bf16)
        share.start(j)
    sums.finish()
    advance(2)
    beside(5)
    for j in range(NSUB):
        share.forward(j)
    share.finish()
    shift = at.x * 2 * channels + at.core * channels
    cur[0] = jnp.zeros(cur.shape[1:], f32)
    cur[0, 1:2, :] = gain_two_grad
    cur[0, 5:6, :] = jnp.broadcast_to(loss[0:1, 0:1], (1, width))
    load_held(0).wait()
    load_held(1).wait()
    for r in range(2):
        load_streams(r).wait()
        part = pl.ds(r * 2 * rows, 2 * rows)
        acc[part, 0:channels] = nn(rows_a[part, :], held[1, :, channels:])

        def mix(q, carry):
            lanes = [rows_of(k * channels + q * 128, 128, 128) for k in range(3)]
            b_gate, c_gate, x_stream = (streams[:, lane] for lane in lanes)
            tap = small[2:5, rows_of(shift + q * 128, 128, 128)]
            mixed = b_gate * x_stream
            convolved = convolve(mixed, tap)
            grad_gated = acc[part, lanes[0]]
            gates[0, part, lanes[0]] = (c_gate * convolved).astype(bf16)
            back[part, lanes[1]] = (grad_gated * convolved).astype(bf16)
            grad_conv = grad_gated * c_gate
            grad_mixed = tap[2:3] * grad_conv
            grad_mixed += tap[1:2] * shifted(grad_conv, -1) + tap[0:1] * shifted(grad_conv, -2)
            for k in range(3):
                term = jnp.sum(grad_conv * shifted(mixed, 2 - k), axis=0, keepdims=True)
                cur[0, 2 + k : 3 + k, rows_of(shift + q * 128, 128, 128)] += term
            back[part, lanes[0]] = (grad_mixed * x_stream).astype(bf16)
            back[part, lanes[2]] = (grad_mixed * b_gate).astype(bf16)
            return carry

        lax.fori_loop(0, channels // 128, mix, 0)
        if r == 0:
            load_streams(1).start()
        acc[part, :] = nt(back[part, 0 : 2 * channels], held[0])
        acc[part, :] += nt(back[part, 2 * channels :], held[1, :, 0:channels])
    sums.to_core()
    load_normed.wait()

    def mixer_weights(i, carry):
        part = rows_of(i * channels, channels, 128)
        left = rows_b[:, part]
        held[0, part, :] = tn(left, back[:, 0 : 2 * channels]).astype(bf16)
        held[1, part, 0:channels] = tn(left, back[:, 2 * channels :]).astype(bf16)
        held[1, part, channels:] = tn(rows_a[:, part], gates[0, :, 0:channels]).astype(bf16)
        return carry

    lax.fori_loop(0, width // channels, mixer_weights, 0)
    advance(3)
    beside(6)
    sums.to_far()
    advance(4)
    beside(7)
    gain_one_grad = jnp.zeros((1, width), f32)
    for j in range(NSUB):
        part = rows_of(j * sub, sub)
        coming = sums.take(j)
        source = tokens[part, :].astype(f32)
        inverse = inverse_of(source)
        weighted = coming * gain_one
        inner = jnp.mean(weighted * source, axis=1, keepdims=True)
        grad[part, :] += inverse * weighted - source * (inverse * inverse * inverse * inner)
        gain_one_grad += jnp.sum(coming * source * inverse, axis=0, keepdims=True)
    sums.finish()
    tokens_copy = load(grad, tokens_grad, 6)
    tokens_copy.start()
    cur[0, 0:1, :] = gain_one_grad
    tally = lambda step: total_copy(at, step, cur, got, cube_sems.at[0], cube_sems.at[1])
    for step in range(3):
        tally(step).start()
        if step < 2:
            total_end(at, step, cur, got, tally(step))
    steps = len(at.cube)
    count = len(order)
    for m in range(5, count):
        advance(m)
        step = m - 3
        if step < steps:
            total_end(at, step, cur, got, tally(step))
            if step + 1 < steps:
                tally(step + 1).start()
    scatter.hop(order[count - 1], count - 1, scatter.far)
    finish(count - 2)
    finish(count - 1)
    for step in range(count - 3, steps):
        total_end(at, step, cur, got, tally(step))
        if step + 1 < steps:
            tally(step + 1).start()
    small_out[...] = cur[steps]
    for m in range(count - YDEPTH, count):
        scatter.drop_beside(order[m], m)
    for m in range(count - ZDEPTH, count):
        scatter.drop(order[m], m)
    for p in given[-2:]:
        out_local(p).wait()
        out_sib(p).wait_send()
    for p in given:
        from_sib(p).wait_recv()
    tokens_copy.wait()


def backward(ndp, held, normed, normed_two, grad_rows, streams, gates, first, grad, small, loss, tokens):
    pieces, width, piece = held.shape
    rows = tokens.shape[0]
    chunk = 2 * width // ndp
    depth = ndp // 4
    channels = piece // 2
    cube = small_steps(ndp)
    dma = pltpu.SemaphoreType.DMA
    shape = jax.ShapeDtypeStruct
    outs = (
        shape((2, pieces, chunk // 2, piece), f32),
        shape((rows, width), f32),
        shape((8, width), f32),
    )
    scratch = [
        pltpu.VMEM((pieces, width, piece), bf16),
        pltpu.VMEM((4 * rows, width), bf16),
        pltpu.VMEM((4 * rows, width), bf16),
        pltpu.VMEM((4 * rows, width), f32),
        pltpu.VMEM((2, 4 * rows, 2 * LANES), bf16),
        pltpu.VMEM((2 * rows, 3 * channels), f32),
        pltpu.VMEM((2, rows, width), bf16),
        pltpu.VMEM((2, rows, width), bf16),
        pltpu.VMEM((rows, width), bf16),
        pltpu.VMEM((rows, width), f32),
        pltpu.VMEM((rows, width), f32),
        pltpu.VMEM((4 * rows, 3 * channels), bf16),
        pltpu.VMEM((YDEPTH, depth, chunk, piece), bf16),
        pltpu.VMEM((ZDEPTH, depth + 1, chunk, piece), bf16),
        pltpu.VMEM((depth + 1, 2 * chunk, piece), bf16),
        pltpu.VMEM((chunk, piece), bf16),
        pltpu.VMEM((2, chunk, piece), f32),
        pltpu.VMEM((cube + 1, 8, width), f32),
        pltpu.VMEM((cube, 8, width), f32),
        dma((6, NSUB)),
        dma((2, 2, NSUB)),
        dma((2, NSUB)),
        dma((2, cube)),
        dma((7,)),
        dma((pieces,)),
        dma((2,)),
        dma((2, YDEPTH, depth)),
        dma((3, ZDEPTH, depth + 1)),
        dma((3, depth + 1)),
        dma((2,)),
        dma((3, pieces)),
        pltpu.SemaphoreType.REGULAR((3,)),
    ]
    return pl.pallas_call(
        functools.partial(backward_kernel, ndp),
        out_shape=outs,
        in_specs=[ANY] * 8 + [VMEM] * 3,
        out_specs=[ANY, ANY, VMEM],
        scratch_shapes=scratch,
        compiler_params=pltpu.CompilerParams(
            collective_id=1, has_side_effects=True, vmem_limit_bytes=127 << 19
        ),
    )(held, normed, normed_two, grad_rows, streams, gates, first, grad, small, loss, tokens)


def body(
    tokens,
    teacher,
    valid,
    mixer_gain,
    in_weight,
    conv_weight,
    out_weight,
    ffn_gain,
    gate_weight,
    up_weight,
    down_weight,
):
    ndp = lax.axis_size("dp")
    place_of = lax.axis_index("dp") * 2 + lax.axis_index("tensor")
    width = tokens.shape[1]
    valid_f = valid.astype(f32)
    vectors = jnp.concatenate([mixer_gain[None], ffn_gain[None], conv_weight], axis=0).astype(f32)
    share = vectors.shape[1]
    small = jnp.zeros((5, width), f32)
    small = lax.dynamic_update_slice(small, vectors, (0, place_of * share))
    small = jnp.concatenate([small, jnp.full((3, width), jnp.sum(valid_f), f32)], axis=0)
    shards = shard_pieces(in_weight, out_weight, gate_weight, up_weight, down_weight)
    held, normed, normed_two, grad_rows, streams, gates, first, block_out, grad, small, loss = forward(
        ndp, shards, tokens, teacher, valid_f[:, None], small
    )
    grads, tokens_grad, small_grads = backward(
        ndp, held, normed, normed_two, grad_rows, streams, gates, first, grad, small, loss, tokens
    )
    part_rows, _, channels = in_weight.shape
    channels //= 2
    units = gate_weight.shape[1]
    mixer = grads[:, 0:2].transpose(0, 2, 1, 3).reshape(2, part_rows, 4 * channels)
    in_grad = mixer[:, :, 0 : 3 * channels].reshape(2, part_rows, 3, channels)
    in_grad = in_grad.transpose(1, 2, 0, 3).reshape(part_rows, 3, 2 * channels)
    out_grad = mixer[:, :, 3 * channels :].transpose(1, 0, 2).reshape(part_rows, 2 * channels)

    def joined(k):
        cut = grads[:, 2:, :, k * LANES : (k + 1) * LANES]
        return cut.transpose(2, 0, 1, 3).reshape(part_rows, -1)[:, 0:units]

    own = lax.dynamic_slice(small_grads, (0, place_of * share), (5, share))
    return (
        small_grads[5, 0] / (width * small[5, 0]),
        block_out,
        tokens_grad,
        own[0],
        in_grad,
        own[2:5],
        out_grad,
        own[1],
        joined(0),
        joined(1),
        joined(2),
    )


def solution(mesh):
    rows = P(("dp", "tensor"), None)
    vector = P(("dp", "tensor"))
    weight = P("dp", "tensor")
    streams = P("dp", None, "tensor")
    taps = P(None, ("dp", "tensor"))
    return jax.shard_map(
        body,
        mesh=mesh,
        in_specs=(rows, rows, vector, vector, streams, taps, weight, vector, weight, weight, weight),
        out_specs=(P(), rows, rows, vector, streams, taps, weight, vector, weight, weight, weight),
        check_vma=False,
    )
```

```python
import functools
from types import SimpleNamespace

import jax
import jax.numpy as jnp
from jax import lax
from jax.experimental import pallas as pl
from jax.experimental.pallas import tpu as pltpu
from jax.sharding import PartitionSpec as P

MESH = pl.DeviceIdType.MESH
f32 = jnp.float32
bf16 = jnp.bfloat16
norm_eps = 1e-05
LANES = 256
NSUB = 3
YDEPTH, ZDEPTH = 3, 4
AHEAD = 4
VMEM = pl.BlockSpec(memory_space=pltpu.VMEM)
ANY = pl.BlockSpec(memory_space=pl.ANY)


def rows_of(start, size, step=16):
    return pl.ds(pl.multiple_of(start, step), size)


def place(ndp):
    d, x = lax.axis_index("dp"), lax.axis_index("tensor")
    core, y, z = d % 2, (d // 2) % 2, d // 4
    depth = ndp // 4
    at = SimpleNamespace(d=d, x=x, core=core, y=y, z=z, depth=depth, chip=d // 2)
    at.sib = (d + 1 - 2 * core, x)
    at.across = (d, 1 - x)
    at.beside = (d + 2 - 4 * y, x)
    at.lower, at.upper = (d - 4, x), (d + 4, x)
    at.has_lower, at.has_upper = z > 0, z < depth - 1
    at.cube = [at.sib, at.across, at.beside]
    step = 1
    while step < depth:
        at.cube.append((d + 4 * step * (1 - 2 * ((z // step) % 2)), x))
        step *= 2
    at.own = 2 * core + x
    at.own_sib = 2 * (1 - core) + x
    at.own_across = 2 * core + 1 - x
    at.own_far = 2 * (1 - core) + 1 - x
    return at


def meet(at):
    bar = pltpu.get_barrier_semaphore()
    always = [at.sib, at.across, at.beside] + at.cube[4:]
    for dev in always:
        pl.semaphore_signal(bar, 1, device_id=dev, device_id_type=MESH)
    for has, dev in ((at.has_lower, at.lower), (at.has_upper, at.upper)):

        @pl.when(has)
        def _():
            pl.semaphore_signal(bar, 1, device_id=dev, device_id_type=MESH)

    ends = jnp.where(at.has_lower, 1, 0) + jnp.where(at.has_upper, 1, 0)
    pl.semaphore_wait(bar, len(always) + ends)


def remote(src, dst, send, recv, dev):
    return pltpu.make_async_remote_copy(
        src_ref=src, dst_ref=dst, send_sem=send, recv_sem=recv, device_id=dev, device_id_type=MESH
    )


def total_copy(at, step, cur, got, send, recv):
    return remote(cur.at[step], got.at[step], send.at[step], recv.at[step], at.cube[step])


def total_end(at, step, cur, got, copy):
    copy.wait()
    cur[step + 1] = cur[step] + got[step]


def total_step(at, step, cur, got, send, recv):
    copy = total_copy(at, step, cur, got, send, recv)
    copy.start()
    total_end(at, step, cur, got, copy)


class Share:
    def __init__(self, at, buf, rows, sems):
        self.at, self.buf, self.rows, self.sems = at, buf, rows, sems
        self.sub = rows // NSUB

    def part(self, slot, j):
        return self.buf.at[rows_of(slot * self.rows + j * self.sub, self.sub), :]

    def copy(self, slot, j, k, dev):
        part = self.part(slot, j)
        return remote(part, part, self.sems.at[2 * k, j], self.sems.at[2 * k + 1, j], dev)

    def start(self, j):
        self.copy(self.at.own, j, 0, self.at.across).start()
        self.copy(self.at.own, j, 1, self.at.sib).start()

    def forward(self, j):
        self.copy(self.at.own_across, j, 0, self.at.across).wait_recv()
        self.copy(self.at.own_across, j, 2, self.at.sib).start()

    def finish(self):
        for j in range(NSUB):
            self.copy(self.at.own_sib, j, 1, self.at.sib).wait_recv()
            self.copy(self.at.own_far, j, 2, self.at.sib).wait_recv()
            self.copy(self.at.own, j, 0, self.at.across).wait_send()
            self.copy(self.at.own, j, 1, self.at.sib).wait_send()
            self.copy(self.at.own_across, j, 2, self.at.sib).wait_send()


class Sums:
    def __init__(self, at, acc, rows, core_out, core_in, far_in, core_sems, far_sems):
        self.at, self.acc, self.rows = at, acc, rows
        self.core_out, self.core_in, self.far_in = core_out, core_in, far_in
        self.core_sems, self.far_sems = core_sems, far_sems
        self.sub = rows // NSUB

    def of(self, slot, j):
        return self.acc[rows_of(slot * self.rows + j * self.sub, self.sub), :]

    def core_copy(self, k, j):
        part = rows_of(j * self.sub, self.sub)
        return remote(
            self.core_out.at[k, part, :],
            self.core_in.at[k, part, :],
            self.core_sems.at[0, k, j],
            self.core_sems.at[1, k, j],
            self.at.sib,
        )

    def far_copy(self, j):
        part = rows_of(j * self.sub, self.sub)
        return remote(
            self.core_in.at[0, part, :],
            self.far_in.at[part, :],
            self.far_sems.at[0, j],
            self.far_sems.at[1, j],
            self.at.across,
        )

    def to_core(self):
        for k, slot in ((0, self.at.own_far), (1, self.at.own_sib)):
            for j in range(NSUB):
                self.core_out[k, rows_of(j * self.sub, self.sub), :] = self.of(slot, j).astype(bf16)
                self.core_copy(k, j).start()

    def to_far(self):
        for j in range(NSUB):
            part = rows_of(j * self.sub, self.sub)
            self.core_copy(0, j).wait_recv()
            both = self.of(self.at.own_across, j) + self.core_in[0, part, :].astype(f32)
            self.core_in[0, part, :] = both.astype(bf16)
            self.far_copy(j).start()

    def take(self, j):
        part = rows_of(j * self.sub, self.sub)
        self.core_copy(1, j).wait_recv()
        self.far_copy(j).wait_recv()
        return (
            self.of(self.at.own, j)
            + self.core_in[1, part, :].astype(f32)
            + self.far_in[part, :].astype(f32)
        )

    def finish(self):
        for j in range(NSUB):
            self.core_copy(0, j).wait_send()
            self.core_copy(1, j).wait_send()
            self.far_copy(j).wait_send()


def nt(left, right):
    return lax.dot_general(left, right, (((1,), (1,)), ((), ())), preferred_element_type=f32)


def tn(left, right):
    return lax.dot_general(left, right, (((0,), (0,)), ((), ())), preferred_element_type=f32)


def nn(left, right):
    return jnp.dot(left, right, preferred_element_type=f32)


def inverse_of(source):
    return lax.rsqrt(jnp.mean(source * source, axis=1, keepdims=True) + norm_eps)


def shifted(value, by):
    if by == 0:
        return value
    size = value.shape[0]
    row = lax.broadcasted_iota(jnp.int32, value.shape, 0)
    inside = row >= by if by > 0 else row < size + by
    return jnp.where(inside, pltpu.roll(value, by % size, 0), 0.0)


def convolve(mixed, taps):
    return taps[0:1] * shifted(mixed, 2) + taps[1:2] * shifted(mixed, 1) + taps[2:3] * mixed


class Gather:
    def __init__(self, at, held, chunk, early_y, sems):
        self.at, self.held, self.chunk, self.early_y = at, held, chunk, early_y
        self.recv, self.own_send, self.send = sems

    def by_kind(self, p, act):
        kind = self.early_y.get(p)
        if kind != "half":
            act(kind == "both")
            return
        for core in (0, 1):

            @pl.when(self.at.core == core)
            def _():
                act(core == 1)

    def block(self, p, chip, count=1):
        return self.held.at[p, rows_of(chip * self.chunk, count * self.chunk), :]

    def copy(self, p, chip, count, send, dev):
        block = self.block(p, chip, count)
        return remote(block, block, send, self.recv.at[p, chip], dev)

    def arrived(self, p, chip, count=1):
        self.copy(p, chip, count, self.own_send.at[0, 0], self.at.beside).wait_recv()

    def own(self, p, act):
        at = self.at
        act(self.copy(p, at.chip, 1, self.own_send.at[0, p], at.beside))
        self.by_kind(p, lambda pairs: None if pairs else self.own_z(p, at.chip, 1, act))

    def own_z(self, p, chip, count, act):
        at = self.at

        @pl.when(at.has_upper)
        def _():
            act(self.copy(p, chip, count, self.own_send.at[1, p], at.upper))

        @pl.when(at.has_lower)
        def _():
            act(self.copy(p, chip, count, self.own_send.at[2, p], at.lower))

    def passing(self, p, pairs, parity, wait, act):
        at = self.at

        def step(s, carry):
            for from_z, goes_on, dev, way in (
                (at.z - 1 - s, at.has_upper, at.upper, 0),
                (at.z + 1 + s, at.has_lower, at.lower, 1),
            ):

                @pl.when(jnp.logical_and(from_z >= 0, from_z < at.depth))
                def _():
                    chip = 2 * from_z if pairs else 2 * from_z + at.y
                    count = 2 if pairs else 1
                    if wait:
                        self.arrived(p, chip, count)

                    @pl.when(goes_on)
                    def _():
                        act(self.copy(p, chip, count, self.send.at[way, parity, from_z], dev))

                    if not pairs:
                        act(self.copy(p, chip, count, self.send.at[2, parity, from_z], at.beside))

            return carry

        lax.fori_loop(0, at.depth - 1, step, 0)

    def sent(self, p):
        self.by_kind(p, lambda pairs: self.passing(p, pairs, p % AHEAD, False, lambda copy: copy.wait_send()))

    def relay(self, p):
        go = lambda copy: copy.start()
        if p >= AHEAD:
            self.sent(p - AHEAD)

        def hand_on(pairs):
            if pairs:
                self.arrived(p, 2 * self.at.z + 1 - self.at.y)
                self.own_z(p, 2 * self.at.z, 2, go)
            self.passing(p, pairs, p % AHEAD, True, go)

        self.by_kind(p, hand_on)

    def whole(self, p):
        def step(z, carry):
            self.arrived(p, 2 * z + 1 - self.at.y)
            return carry

        self.by_kind(p, lambda pairs: None if pairs else lax.fori_loop(0, self.at.depth, step, 0))

    def own_done(self, p):
        done = lambda copy: copy.wait_send()
        self.own(p, done)
        self.by_kind(p, lambda pairs: self.own_z(p, 2 * self.at.z, 2, done) if pairs else None)


def forward_kernel(
    ndp,
    early_y,
    shards,
    tokens,
    teacher,
    valid,
    small,
    held_out,
    normed_out,
    normed_two_out,
    grad_rows_out,
    streams_out,
    gates_out,
    first_out,
    block_out,
    grad_out,
    small_out,
    loss_out,
    held,
    landed,
    mine,
    rows_a,
    rows_b,
    acc,
    streams,
    gates,
    core_out,
    core_in,
    far_in,
    first,
    result,
    error_grad,
    cur,
    got,
    chip_sems,
    recv_sems,
    own_sems,
    send_sems,
    share_sems,
    core_sems,
    far_sems,
    cube_sems,
    out_sems,
    held_sems,
    gate_sems,
):
    at = place(ndp)
    pieces, width, piece = held.shape
    part_rows = shards.shape[2]
    chunk = 2 * part_rows
    rows = tokens.shape[0]
    sub = rows // NSUB
    channels = streams.shape[1] // 3
    aligned = part_rows % 16 == 0
    go = lambda copy: copy.start()
    gather = Gather(at, held, chunk, early_y, (recv_sems, own_sems, send_sems))
    share_a = Share(at, rows_a, rows, share_sems)
    share_b = Share(at, rows_b, rows, share_sems)
    sums = Sums(at, acc, rows, core_out, core_in, far_in, core_sems, far_sems)

    def half(p, core):
        return held.at[p, rows_of(at.chip * chunk + core * part_rows, part_rows), :]

    def to_sib(p):
        dst = half(p, at.core) if aligned else landed.at[p]
        return remote(shards.at[1 - at.core, p], dst, chip_sems.at[0, p], chip_sems.at[1, p], at.sib)

    def from_sib(p):
        dst = half(p, 1 - at.core) if aligned else landed.at[p]
        return remote(dst, dst, chip_sems.at[0, p], chip_sems.at[1, p], at.sib)

    def keep(p):
        dst = half(p, at.core) if aligned else mine.at[p]
        return pltpu.make_async_copy(shards.at[at.core, p], dst, chip_sems.at[2, p])

    def own_block(p):
        keep(p).wait()
        from_sib(p).wait_recv()
        if not aligned:
            a, b = mine[p].astype(f32), landed[p].astype(f32)
            lower = jnp.where(at.core == 0, a, b)
            upper = jnp.where(at.core == 0, b, a)
            both = jnp.concatenate([lower, upper], axis=0).astype(bf16)
            held[p, rows_of(at.chip * chunk, chunk), :] = both
        gather.own(p, go)

    meet(at)
    to_sib(0).start()
    keep(0).start()
    cur[0] = small[...]
    total_step(at, 0, cur, got, cube_sems.at[0], cube_sems.at[1])
    own_block(0)
    total_step(at, 1, cur, got, cube_sems.at[0], cube_sems.at[1])
    for j in range(NSUB):
        rows_a[rows_of(at.own * rows + j * sub, sub), :] = tokens[pl.ds(j * sub, sub), :]
        share_a.start(j)
    for p in range(1, pieces):
        to_sib(p).start()
        keep(p).start()
    for step in range(2, len(at.cube)):
        total_step(at, step, cur, got, cube_sems.at[0], cube_sems.at[1])
        if step < 4:
            own_block(step - 1)
    last = len(at.cube)
    small_out[...] = cur[last]
    for j in range(NSUB):
        share_a.forward(j)
    gain_one, gain_two = cur[last, 0:1, :], cur[last, 1:2, :]
    relay = gather.relay
    relay(0)
    share_a.finish()

    def norm_rows(i, carry):
        part = rows_of(i * sub, sub)
        source = rows_a[part, :].astype(f32)
        rows_a[part, :] = (source * inverse_of(source) * gain_one).astype(bf16)
        return carry

    lax.fori_loop(0, 4 * NSUB, norm_rows, 0)
    normed_copy = pltpu.make_async_copy(rows_a, normed_out, out_sems.at[0])
    normed_copy.start()

    def save(p):
        return pltpu.make_async_copy(held.at[p], held_out.at[p], held_sems.at[p])

    own_block(3)
    relay(1)
    own_block(4)
    relay(2)
    own_block(5)
    for p in (0, 1):
        gather.whole(p)
        save(p).start()
    lane = at.x * 2 * channels + at.core * channels
    taps = cur[last, 2:5, rows_of(lane, channels, 128)]

    def mix(r, carry):
        part = rows_of(((r + 1 - at.core) % 2) * 2 * rows, 2 * rows)
        both = nn(rows_a[part, :], held[0])
        x_stream = nn(rows_a[part, :], held[1, :, 0:channels])
        streams[part, 0 : 2 * channels] = both
        streams[part, 2 * channels :] = x_stream
        convolved = convolve(both[:, 0:channels] * x_stream, taps)
        gated = (both[:, channels:] * convolved).astype(bf16)
        acc[part, :] = nt(gated, held[1, :, channels:])
        return carry

    lax.fori_loop(0, 2, mix, 0)
    streams_copy = pltpu.make_async_copy(streams, streams_out, out_sems.at[1])
    streams_copy.start()
    sums.to_core()
    own_block(6)
    own_block(7)
    sums.to_far()
    relay(3)
    for p in range(8, pieces):
        own_block(p)
    for j in range(NSUB):
        part = rows_of(j * sub, sub)
        value = tokens[part, :].astype(f32) + sums.take(j)
        first[part, :] = value
        normed_two = (value * inverse_of(value) * gain_two).astype(bf16)
        rows_b[rows_of(at.own * rows + j * sub, sub), :] = normed_two
        share_b.start(j)
    sums.finish()
    first_copy = pltpu.make_async_copy(first, first_out, out_sems.at[2])
    first_copy.start()
    relay(4)
    for j in range(NSUB):
        share_b.forward(j)
    share_b.finish()
    normed_two_copy = pltpu.make_async_copy(rows_b, normed_two_out, out_sems.at[3])
    normed_two_copy.start()
    acc[...] = jnp.zeros_like(acc)

    def gates_copy(p):
        slot = p % 2
        return pltpu.make_async_copy(gates.at[slot], gates_out.at[p - 2], gate_sems.at[slot])

    def feed(p, carry):
        for q in range(5, pieces):

            @pl.when(p == q - 3)
            def _():
                relay(q)

        for q in range(2, pieces):

            @pl.when(p == q)
            def _():
                gather.whole(q)

        save(p).start()

        @pl.when(p >= 4)
        def _():
            gates_copy(p - 2).wait()

        def some(r, inner):
            part = rows_of(((r + 1 - at.core) % 2) * 2 * rows, 2 * rows)
            both = nn(rows_b[part, :], held[p, :, 0 : 2 * LANES])
            gate, up = both[:, 0:LANES], both[:, LANES:]
            gates[p % 2, part, :] = both.astype(bf16)
            hidden = (gate * jax.nn.sigmoid(gate) * up).astype(bf16)
            acc[part, :] += nt(hidden, held[p, :, 2 * LANES :])
            return inner

        lax.fori_loop(0, 2, some, 0)
        gates_copy(p).start()
        return carry

    normed_copy.wait()
    lax.fori_loop(2, pieces, feed, 0)
    sums.to_core()
    sums.to_far()
    scale = 1.0 / (width * cur[last, 5:6, 0:1])
    loss = jnp.zeros((1, width), f32)
    for j in range(NSUB):
        part = rows_of(j * sub, sub)
        value = first[part, :] + sums.take(j)
        result[part, :] = value
        error = value - teacher[part, :].astype(f32)
        weighted = valid[part, :] * error
        loss = loss + jnp.sum(weighted * error, axis=0, keepdims=True)
        grad = (2.0 * scale) * weighted
        error_grad[part, :] = grad
        rows_a[rows_of(at.own * rows + j * sub, sub), :] = grad.astype(bf16)
        share_a.start(j)
    loss_out[...] = jnp.broadcast_to(jnp.sum(loss, axis=1, keepdims=True), loss_out.shape)
    sums.finish()
    result_copy = pltpu.make_async_copy(result, block_out, out_sems.at[4])
    result_copy.start()
    grad_copy = pltpu.make_async_copy(error_grad, grad_out, out_sems.at[5])
    grad_copy.start()
    for j in range(NSUB):
        share_a.forward(j)
    share_a.finish()
    rows_copy = pltpu.make_async_copy(rows_a, grad_rows_out, out_sems.at[6])
    rows_copy.start()
    for p in range(pieces):
        save(p).wait()
        to_sib(p).wait_send()
        gather.own_done(p)
    for p in range(pieces - AHEAD, pieces):
        gather.sent(p)
    for p in (pieces - 2, pieces - 1):
        gates_copy(p).wait()
    for copy in (streams_copy, first_copy, normed_two_copy, result_copy, grad_copy, rows_copy):
        copy.wait()


def forward(ndp, shards, tokens, teacher, valid, small):
    _, pieces, part_rows, piece = shards.shape
    rows, width = tokens.shape
    channels = (2 * piece - piece // 2) // 3
    cube = small_steps(ndp)
    early_y = {3: "both", 6: "half"}
    dma = pltpu.SemaphoreType.DMA
    landing = (pieces, part_rows, piece) if part_rows % 16 else (1, 16, 128)
    shape = jax.ShapeDtypeStruct
    outs = (
        shape((pieces, width, piece), bf16),
        shape((4 * rows, width), bf16),
        shape((4 * rows, width), bf16),
        shape((4 * rows, width), bf16),
        shape((4 * rows, 3 * channels), f32),
        shape((pieces - 2, 4 * rows, 2 * LANES), bf16),
        shape((rows, width), f32),
        shape((rows, width), f32),
        shape((rows, width), f32),
        shape((8, width), f32),
        shape((8, 128), f32),
    )
    scratch = [
        pltpu.VMEM((pieces, width, piece), bf16),
        pltpu.VMEM(landing, bf16),
        pltpu.VMEM(landing, bf16),
        pltpu.VMEM((4 * rows, width), bf16),
        pltpu.VMEM((4 * rows, width), bf16),
        pltpu.VMEM((4 * rows, width), f32),
        pltpu.VMEM((4 * rows, 3 * channels), f32),
        pltpu.VMEM((2, 4 * rows, 2 * LANES), bf16),
        pltpu.VMEM((2, rows, width), bf16),
        pltpu.VMEM((2, rows, width), bf16),
        pltpu.VMEM((rows, width), bf16),
        pltpu.VMEM((rows, width), f32),
        pltpu.VMEM((rows, width), f32),
        pltpu.VMEM((rows, width), f32),
        pltpu.VMEM((cube + 1, 8, width), f32),
        pltpu.VMEM((cube, 8, width), f32),
        dma((3, pieces)),
        dma((pieces, ndp // 2)),
        dma((3, pieces)),
        dma((3, AHEAD, ndp // 4)),
        dma((6, NSUB)),
        dma((2, 2, NSUB)),
        dma((2, NSUB)),
        dma((2, cube)),
        dma((7,)),
        dma((pieces,)),
        dma((2,)),
    ]
    return pl.pallas_call(
        functools.partial(forward_kernel, ndp, early_y),
        out_shape=outs,
        in_specs=[ANY, VMEM, VMEM, VMEM, VMEM],
        out_specs=[ANY] * 9 + [VMEM] * 2,
        scratch_shapes=scratch,
        compiler_params=pltpu.CompilerParams(
            collective_id=0, has_side_effects=True, vmem_limit_bytes=63 << 20
        ),
    )(shards, tokens, teacher, valid, small)


def small_steps(ndp):
    return 3 + (ndp // 4 - 1).bit_length()


def shard_pieces(in_weight, out_weight, gate_weight, up_weight, down_weight):
    part_rows, _, channels = in_weight.shape
    channels //= 2
    taps = in_weight.reshape(part_rows, 3, 2, channels).transpose(2, 0, 1, 3)
    taps = taps.reshape(2, part_rows, 3 * channels)
    outs = out_weight.reshape(part_rows, 2, channels).transpose(1, 0, 2)
    mixer = jnp.concatenate([taps, outs], axis=2)
    mixer = mixer.reshape(2, part_rows, 2, 2 * channels).transpose(0, 2, 1, 3)
    units = gate_weight.shape[1]
    count = -(-units // (2 * LANES))

    def cut(weight):
        weight = jnp.pad(weight, ((0, 0), (0, 2 * count * LANES - units)))
        return weight.reshape(part_rows, 2, count, LANES).transpose(1, 2, 0, 3)

    ffn = jnp.concatenate([cut(gate_weight), cut(up_weight), cut(down_weight)], axis=3)
    return jnp.concatenate([mixer, ffn], axis=1)


class Scatter:
    def __init__(self, at, held, chunk, count, beside_in, line_in, pair_in, pair_beside, total, sems, credits):
        self.at, self.held, self.chunk, self.count = at, held, chunk, count
        self.beside_in, self.line_in, self.pair_in, self.pair_beside = beside_in, line_in, pair_in, pair_beside
        self.total, self.credits = total, credits
        self.beside_sems, self.line_sems, self.pair_sems, self.pair_y_sems = sems
        self.ydepth, self.zdepth = beside_in.shape[0], line_in.shape[0]

    def block(self, p, chip, count=1):
        return self.held.at[p, rows_of(chip * self.chunk, count * self.chunk), :]

    def beside_copy(self, p, m, z):
        slot = m % self.ydepth
        return remote(
            self.block(p, 2 * z + 1 - self.at.y),
            self.beside_in.at[slot, z],
            self.beside_sems.at[0, slot, z],
            self.beside_sems.at[1, slot, z],
            self.at.beside,
        )

    def line_copy(self, p, m, z, up):
        slot, way = m % self.zdepth, 0 if up else 1
        into = z + 1 if up else z
        return remote(
            self.block(p, 2 * z + self.at.y),
            self.line_in.at[slot, into],
            self.line_sems.at[way, slot, z],
            self.line_sems.at[2, slot, into],
            self.at.upper if up else self.at.lower,
        )

    def pair_copy(self, p, z, up):
        into = z + 1 if up else z
        return remote(
            self.block(p, 2 * z, 2),
            self.pair_in.at[into],
            self.pair_sems.at[0 if up else 1, z],
            self.pair_sems.at[2, into],
            self.at.upper if up else self.at.lower,
        )

    def turn(self, s):
        z, last = self.at.z, self.at.depth - 1
        low = jnp.where(z < self.at.depth // 2, 1, 0)
        down, up = last - s, s
        other = low * (down - jnp.where(down <= z, 1, 0)) + (1 - low) * (up + jnp.where(up >= z, 1, 0))
        mine = jnp.where(s == last, 1, 0)
        return mine * z + (1 - mine) * other

    def free_beside(self, p, m, before):
        if m >= self.ydepth:
            pl.semaphore_wait(self.credits.at[0], 1)
            self.drop_beside(before, m)

    def drop_beside(self, p, m):
        def step(z, carry):
            self.beside_copy(p, m, z).wait_send()
            return carry

        lax.fori_loop(0, self.at.depth, step, 0)

    def send_beside(self, p, m, before):
        self.free_beside(p, m, before)

        def step(s, carry):
            self.beside_copy(p, m, self.turn(s)).start()
            return carry

        lax.fori_loop(0, self.at.depth, step, 0)

    def ways(self, has, act):
        at = self.at

        def step(s, carry):
            for z, wanted, up in (
                (at.depth - 1 - s, at.depth - 1 - s > at.z, True),
                (s, s < at.z, False),
            ):

                @pl.when(jnp.logical_and(wanted, has(up)))
                def _():
                    act(z, up)

            return carry

        lax.fori_loop(0, at.depth - 1, step, 0)

    def behind(self, up):
        return self.at.has_lower if up else self.at.has_upper

    def opens(self, up):
        return jnp.logical_not(self.behind(up))

    def near(self, up):
        low = self.at.z < self.at.depth // 2
        return jnp.logical_and(self.behind(up), low if up else jnp.logical_not(low))

    def far(self, up):
        low = self.at.z < self.at.depth // 2
        return jnp.logical_and(self.behind(up), jnp.logical_not(low) if up else low)

    def add_beside(self, p, m, before, onward):
        at = self.at
        if m >= self.zdepth:
            for has, credit in ((at.has_upper, 1), (at.has_lower, 2)):

                @pl.when(has)
                def _():
                    pl.semaphore_wait(self.credits.at[credit], 1)

            self.drop(before, m)

        def step(s, carry):
            z = self.turn(s)
            own = self.block(p, 2 * z + at.y)
            self.beside_copy(p, m, z).wait_recv()
            own[...] = (own[...].astype(f32) + self.beside_in[m % self.ydepth, z].astype(f32)).astype(bf16)
            for up in (True, False):

                @pl.when(jnp.logical_and(z > at.z if up else z < at.z, self.opens(up)))
                def _():
                    self.line_copy(p, m, z, up).start()

                if onward:

                    @pl.when(jnp.logical_and(z > at.z if up else z < at.z, self.behind(up)))
                    def _():
                        self.pass_on(p, m, z, up)

            return carry

        lax.fori_loop(0, at.depth, step, 0)
        if m + self.ydepth < self.count:
            pl.semaphore_signal(self.credits.at[0], 1, device_id=at.beside, device_id_type=MESH)

    def pass_on(self, p, m, z, up):
        self.line_copy(p, m, z, up).wait_recv()
        own = self.block(p, 2 * z + self.at.y)
        came = self.line_in[m % self.zdepth, z + 1 if up else z].astype(f32)
        own[...] = (own[...].astype(f32) + came).astype(bf16)
        self.line_copy(p, m, z, up).start()

    def hop(self, p, m, has):
        self.ways(has, functools.partial(self.pass_on, p, m))

    def collect(self, p, m, slot):
        at = self.at
        total = self.total.at[slot]
        total[...] = self.block(p, 2 * at.z + at.y)[...].astype(f32)
        for up in (True, False):

            @pl.when(self.behind(up))
            def _():
                self.line_copy(p, m, at.z, up).wait_recv()
                total[...] += self.line_in[m % self.zdepth, at.z + 1 if up else at.z].astype(f32)
                if m + self.zdepth < self.count:
                    pl.semaphore_signal(
                        self.credits.at[1 if up else 2],
                        1,
                        device_id=at.lower if up else at.upper,
                        device_id_type=MESH,
                    )

    def drop(self, p, m):
        self.ways(lambda up: True, lambda z, up: self.line_copy(p, m, z, up).wait_send())

    def pairs_open(self, p):
        self.ways(self.opens, lambda z, up: self.pair_copy(p, z, up).start())

    def pair_hop(self, p, has):
        def act(z, up):
            self.pair_copy(p, z, up).wait_recv()
            own = self.block(p, 2 * z, 2)
            own[...] = (own[...].astype(f32) + self.pair_in[z + 1 if up else z].astype(f32)).astype(bf16)
            self.pair_copy(p, z, up).start()

        self.ways(has, act)

    def pair_y_copy(self, p):
        at = self.at
        return remote(
            self.block(p, 2 * at.z + 1 - at.y),
            self.pair_beside,
            self.pair_y_sems.at[0],
            self.pair_y_sems.at[1],
            at.beside,
        )

    def pairs_cross(self, p):
        at = self.at
        own = self.block(p, 2 * at.z, 2)
        for up in (True, False):

            @pl.when(self.behind(up))
            def _():
                self.pair_copy(p, at.z, up).wait_recv()
                came = self.pair_in[at.z + 1 if up else at.z].astype(f32)
                own[...] = (own[...].astype(f32) + came).astype(bf16)

        self.pair_y_copy(p).start()

    def pairs_close(self, p, slot):
        at = self.at
        self.pair_y_copy(p).wait()
        mine = self.block(p, 2 * at.z + at.y)[...].astype(f32)
        self.total[slot] = mine + self.pair_beside[...].astype(f32)
        self.ways(lambda up: True, lambda z, up: self.pair_copy(p, z, up).wait_send())


def backward_kernel(
    ndp,
    held_in,
    normed_in,
    normed_two_in,
    grad_rows_in,
    streams_in,
    gates_in,
    first_in,
    grad_in,
    small,
    loss,
    tokens,
    streams_grad,
    out_grad,
    gate_grad,
    up_grad,
    down_grad,
    tokens_grad,
    small_out,
    held,
    rows_a,
    rows_b,
    acc,
    gates,
    streams,
    core_out,
    core_in,
    far_in,
    first,
    grad,
    back,
    beside_in,
    line_in,
    pair_in,
    pair_beside,
    total,
    cur,
    got,
    share_sems,
    core_sems,
    far_sems,
    cube_sems,
    load_sems,
    held_sems,
    gate_sems,
    beside_sems,
    line_sems,
    pair_sems,
    pair_y_sems,
    done_sems,
    credits,
):
    at = place(ndp)
    pieces, width, piece = held.shape
    rows = tokens.shape[0]
    sub = rows // NSUB
    chunk = 2 * width // ndp
    half = chunk // 2
    channels = piece // 2
    order = [2] + list(range(4, pieces)) + [0, 1]
    paired = 3
    share = Share(at, rows_a, rows, share_sems)
    sums = Sums(at, acc, rows, core_out, core_in, far_in, core_sems, far_sems)
    scatter = Scatter(
        at,
        held,
        chunk,
        len(order),
        beside_in,
        line_in,
        pair_in,
        pair_beside,
        total,
        (beside_sems, line_sems, pair_sems, pair_y_sems),
        credits,
    )

    def load(src, dst, k):
        return pltpu.make_async_copy(src, dst, load_sems.at[k])

    def load_held(p):
        return pltpu.make_async_copy(held_in.at[p], held.at[p], held_sems.at[p])

    def load_gates(p):
        return pltpu.make_async_copy(gates_in.at[p - 2], gates.at[p % 2], gate_sems.at[p % 2])

    def load_streams(r):
        return load(streams_in.at[pl.ds(r * 2 * rows, 2 * rows), :], streams, 5)

    opening = (
        load(grad_rows_in, rows_a, 0),
        load_gates(2),
        load_held(2),
        load(normed_two_in, rows_b, 1),
    )
    for copy in opening:
        copy.start()
    load_gates(3).start()
    for p in list(range(3, pieces)) + [0, 1]:
        load_held(p).start()
    load_first, load_grad = load(first_in, first, 2), load(grad_in, grad, 3)
    load_first.start()
    load_grad.start()
    load_streams(0).start()
    meet(at)
    acc[...] = jnp.zeros_like(acc)
    opening[0].wait()
    opening[3].wait()

    def ffn(p, m=None):
        load_gates(p).wait()
        load_held(p).wait()

        def some(r, carry):
            part = rows_of(((r + 1 - at.core) % 2) * 2 * rows, 2 * rows)
            grad_hidden = nn(rows_a[part, :], held[p, :, 2 * LANES :])
            gate = gates[p % 2, part, 0:LANES].astype(f32)
            up = gates[p % 2, part, LANES:].astype(f32)
            sig = jax.nn.sigmoid(gate)
            active = gate * sig
            back[part, 2 * LANES : 3 * LANES] = (active * up).astype(bf16)
            grad_gate = grad_hidden * up * sig * (1.0 + gate * (1.0 - sig))
            back[part, 0:LANES] = grad_gate.astype(bf16)
            back[part, LANES : 2 * LANES] = (grad_hidden * active).astype(bf16)
            acc[part, :] += nt(back[part, 0 : 2 * LANES], held[p, :, 0 : 2 * LANES])
            return carry

        lax.fori_loop(0, 2, some, 0)

        blocks = 2 * width // piece
        matched = blocks == at.depth

        def weights(s, carry):
            i = scatter.turn(s) if matched else s
            part = rows_of(i * (piece // 2), piece // 2, 128)
            held[p, part, 0 : 2 * LANES] = tn(rows_b[:, part], back[:, 0 : 2 * LANES]).astype(bf16)
            held[p, part, 2 * LANES :] = tn(rows_a[:, part], back[:, 2 * LANES : 3 * LANES]).astype(bf16)
            if m is not None and matched:
                scatter.beside_copy(p, m, i).start()
            return carry

        lax.fori_loop(0, blocks, weights, 0)
        if m is not None and not matched:
            scatter.send_beside(p, m, None)
        if p + 2 < pieces:
            load_gates(p + 2).start()

    given = []

    span = (pieces - 2) * LANES
    short = gate_grad.shape[1] - 2 * span + LANES

    def parts(p, core):
        if p == 0:
            at_columns = rows_of(core * channels, channels, 128)
            return [(k * channels, channels, streams_grad.at[k, :, at_columns]) for k in range(2)]
        if p == 1:
            at_columns = rows_of(core * channels, channels, 128)
            return [
                (0, channels, streams_grad.at[2, :, at_columns]),
                (channels, channels, out_grad.at[:, at_columns]),
            ]
        found = []
        for k, out in enumerate((gate_grad, up_grad, down_grad)):
            found.append((k * LANES, LANES, out.at[:, rows_of(core * span + (p - 2) * LANES, LANES, 128)]))
        return found

    def narrow(p, core):
        found = []
        for k, out in enumerate((gate_grad, up_grad, down_grad)):
            found.append((k * LANES, short, out.at[:, rows_of(core * span + (p - 2) * LANES, short, 128)]))
        return found

    def each_part(p, core, act):
        if p < pieces - 1 or short == LANES:
            for k, (first_column, count, dst) in enumerate(parts(p, core)):
                act(k, first_column, count, dst)
            return

        for is_short, found in ((False, parts), (True, narrow)):

            @pl.when((core == 1) if is_short else (core == 0))
            def _():
                for k, (first_column, count, dst) in enumerate(found(p, 0 if not is_short else 1)):
                    act(k, first_column, count, dst)

    def piece_rows(p, core, first_column, count):
        slot = given.index(p) % 2 if p in given else 0
        return total.at[slot, rows_of(core * half, half, 8), pl.ds(first_column, count)]

    def out_local(p, act):
        def copy(k, first_column, count, dst):
            src = piece_rows(p, at.core, first_column, count)
            act(pltpu.make_async_copy(src, dst, done_sems.at[0, p, k]))

        each_part(p, at.core, copy)

    def out_sib(p, core, act):
        def copy(k, first_column, count, dst):
            src = piece_rows(p, 1 - at.core, first_column, count)
            act(remote(src, dst, done_sems.at[1, p, k], done_sems.at[2, p, k], at.sib))

        each_part(p, core, copy)

    def give(p, fill):
        if len(given) > 1:
            out_local(given[-2], lambda copy: copy.wait())
            out_sib(given[-2], at.core, lambda copy: copy.wait_send())
        given.append(p)
        fill((len(given) - 1) % 2)
        out_local(p, lambda copy: copy.start())
        out_sib(p, at.core, lambda copy: copy.start())

    def beside(m):
        scatter.send_beside(order[m], m, order[m - YDEPTH] if m >= YDEPTH else None)

    def finish(m):
        give(order[m], functools.partial(scatter.collect, order[m], m))

    def advance(m):
        onward = m == len(order) - 1
        if onward:
            scatter.hop(order[m - 1], m - 1, scatter.far)
            finish(m - 2)
        scatter.add_beside(order[m], m, order[m - ZDEPTH] if m >= ZDEPTH else None, onward)
        if onward:
            return
        scatter.hop(order[m], m, scatter.near)
        if m == 0:
            scatter.pair_hop(paired, scatter.near)
        if m >= 1:
            scatter.hop(order[m - 1], m - 1, scatter.far)
        if m == 2:
            scatter.pair_hop(paired, scatter.far)
        if m >= 2:
            finish(m - 2)
        if m == 3:
            scatter.pairs_cross(paired)
        if m == 4:
            give(paired, functools.partial(scatter.pairs_close, paired))

    gain_one, gain_two = small[0:1, :], small[1:2, :]
    ffn(2, 0)
    ffn(3)
    scatter.pairs_open(paired)
    ffn(4, 1)
    ffn(5, 2)
    advance(0)
    ffn(6)
    beside(3)
    for p in range(7, pieces):
        ffn(p)
    sums.to_core()
    load_normed = load(normed_in, rows_b, 4)
    load_normed.start()
    advance(1)
    beside(4)
    sums.to_far()
    load_first.wait()
    load_grad.wait()
    gain_two_grad = jnp.zeros((1, width), f32)
    for j in range(NSUB):
        part = rows_of(j * sub, sub)
        coming = sums.take(j)
        source = first[part, :]
        inverse = inverse_of(source)
        weighted = coming * gain_two
        inner = jnp.mean(weighted * source, axis=1, keepdims=True)
        value = grad[part, :] + inverse * weighted - source * (inverse * inverse * inverse * inner)
        grad[part, :] = value
        gain_two_grad += jnp.sum(coming * source * inverse, axis=0, keepdims=True)
        rows_a[rows_of(at.own * rows + j * sub, sub), :] = value.astype(bf16)
        share.start(j)
    sums.finish()
    advance(2)
    beside(5)
    for j in range(NSUB):
        share.forward(j)
    share.finish()
    shift = at.x * 2 * channels + at.core * channels
    cur[0] = jnp.zeros(cur.shape[1:], f32)
    cur[0, 1:2, :] = gain_two_grad
    cur[0, 5:6, :] = jnp.broadcast_to(loss[0:1, 0:1], (1, width))
    load_held(0).wait()
    load_held(1).wait()
    for r in range(2):
        load_streams(r).wait()
        part = pl.ds(r * 2 * rows, 2 * rows)
        acc[part, 0:channels] = nn(rows_a[part, :], held[1, :, channels:])

        def mix(q, carry):
            lanes = [rows_of(k * channels + q * 128, 128, 128) for k in range(3)]
            b_gate, c_gate, x_stream = (streams[:, lane] for lane in lanes)
            tap = small[2:5, rows_of(shift + q * 128, 128, 128)]
            mixed = b_gate * x_stream
            convolved = convolve(mixed, tap)
            grad_gated = acc[part, lanes[0]]
            gates[0, part, lanes[0]] = (c_gate * convolved).astype(bf16)
            back[part, lanes[1]] = (grad_gated * convolved).astype(bf16)
            grad_conv = grad_gated * c_gate
            grad_mixed = tap[2:3] * grad_conv
            grad_mixed += tap[1:2] * shifted(grad_conv, -1) + tap[0:1] * shifted(grad_conv, -2)
            for k in range(3):
                term = jnp.sum(grad_conv * shifted(mixed, 2 - k), axis=0, keepdims=True)
                cur[0, 2 + k : 3 + k, rows_of(shift + q * 128, 128, 128)] += term
            back[part, lanes[0]] = (grad_mixed * x_stream).astype(bf16)
            back[part, lanes[2]] = (grad_mixed * b_gate).astype(bf16)
            return carry

        lax.fori_loop(0, channels // 128, mix, 0)
        if r == 0:
            load_streams(1).start()
        acc[part, :] = nt(back[part, 0 : 2 * channels], held[0])
        acc[part, :] += nt(back[part, 2 * channels :], held[1, :, 0:channels])
    sums.to_core()
    load_normed.wait()

    def mixer_weights(i, carry):
        part = rows_of(i * channels, channels, 128)
        left = rows_b[:, part]
        held[0, part, :] = tn(left, back[:, 0 : 2 * channels]).astype(bf16)
        held[1, part, 0:channels] = tn(left, back[:, 2 * channels :]).astype(bf16)
        held[1, part, channels:] = tn(rows_a[:, part], gates[0, :, 0:channels]).astype(bf16)
        return carry

    lax.fori_loop(0, width // channels, mixer_weights, 0)
    advance(3)
    beside(6)
    sums.to_far()
    advance(4)
    beside(7)
    gain_one_grad = jnp.zeros((1, width), f32)
    for j in range(NSUB):
        part = rows_of(j * sub, sub)
        coming = sums.take(j)
        source = tokens[part, :].astype(f32)
        inverse = inverse_of(source)
        weighted = coming * gain_one
        inner = jnp.mean(weighted * source, axis=1, keepdims=True)
        grad[part, :] += inverse * weighted - source * (inverse * inverse * inverse * inner)
        gain_one_grad += jnp.sum(coming * source * inverse, axis=0, keepdims=True)
    sums.finish()
    tokens_copy = load(grad, tokens_grad, 6)
    tokens_copy.start()
    cur[0, 0:1, :] = gain_one_grad
    tally = lambda step: total_copy(at, step, cur, got, cube_sems.at[0], cube_sems.at[1])
    for step in range(3):
        tally(step).start()
        if step < 2:
            total_end(at, step, cur, got, tally(step))
    steps = len(at.cube)
    count = len(order)
    for m in range(5, count):
        advance(m)
        step = m - 3
        if step < steps:
            total_end(at, step, cur, got, tally(step))
            if step + 1 < steps:
                tally(step + 1).start()
    finish(count - 2)
    finish(count - 1)
    for step in range(count - 3, steps):
        total_end(at, step, cur, got, tally(step))
        if step + 1 < steps:
            tally(step + 1).start()
    small_out[...] = cur[steps]
    for m in range(count - YDEPTH, count):
        scatter.drop_beside(order[m], m)
    for m in range(count - ZDEPTH, count):
        scatter.drop(order[m], m)
    for p in given[-2:]:
        out_local(p, lambda copy: copy.wait())
        out_sib(p, at.core, lambda copy: copy.wait_send())
    for p in given:
        out_sib(p, 1 - at.core, lambda copy: copy.wait_recv())
    tokens_copy.wait()


def backward(ndp, units, held, normed, normed_two, grad_rows, streams, gates, first, grad, small, loss, tokens):
    pieces, width, piece = held.shape
    rows = tokens.shape[0]
    chunk = 2 * width // ndp
    depth = ndp // 4
    channels = piece // 2
    cube = small_steps(ndp)
    dma = pltpu.SemaphoreType.DMA
    shape = jax.ShapeDtypeStruct
    outs = (
        shape((3, chunk // 2, 2 * channels), f32),
        shape((chunk // 2, 2 * channels), f32),
        shape((chunk // 2, units), f32),
        shape((chunk // 2, units), f32),
        shape((chunk // 2, units), f32),
        shape((rows, width), f32),
        shape((8, width), f32),
    )
    scratch = [
        pltpu.VMEM((pieces, width, piece), bf16),
        pltpu.VMEM((4 * rows, width), bf16),
        pltpu.VMEM((4 * rows, width), bf16),
        pltpu.VMEM((4 * rows, width), f32),
        pltpu.VMEM((2, 4 * rows, 2 * LANES), bf16),
        pltpu.VMEM((2 * rows, 3 * channels), f32),
        pltpu.VMEM((2, rows, width), bf16),
        pltpu.VMEM((2, rows, width), bf16),
        pltpu.VMEM((rows, width), bf16),
        pltpu.VMEM((rows, width), f32),
        pltpu.VMEM((rows, width), f32),
        pltpu.VMEM((4 * rows, 3 * channels), bf16),
        pltpu.VMEM((YDEPTH, depth, chunk, piece), bf16),
        pltpu.VMEM((ZDEPTH, depth + 1, chunk, piece), bf16),
        pltpu.VMEM((depth + 1, 2 * chunk, piece), bf16),
        pltpu.VMEM((chunk, piece), bf16),
        pltpu.VMEM((2, chunk, piece), f32),
        pltpu.VMEM((cube + 1, 8, width), f32),
        pltpu.VMEM((cube, 8, width), f32),
        dma((6, NSUB)),
        dma((2, 2, NSUB)),
        dma((2, NSUB)),
        dma((2, cube)),
        dma((7,)),
        dma((pieces,)),
        dma((2,)),
        dma((2, YDEPTH, depth)),
        dma((3, ZDEPTH, depth + 1)),
        dma((3, depth + 1)),
        dma((2,)),
        dma((3, pieces, 3)),
        pltpu.SemaphoreType.REGULAR((3,)),
    ]
    return pl.pallas_call(
        functools.partial(backward_kernel, ndp),
        out_shape=outs,
        in_specs=[ANY] * 8 + [VMEM] * 3,
        out_specs=[ANY] * 6 + [VMEM],
        scratch_shapes=scratch,
        compiler_params=pltpu.CompilerParams(
            collective_id=1, has_side_effects=True, vmem_limit_bytes=127 << 19
        ),
    )(held, normed, normed_two, grad_rows, streams, gates, first, grad, small, loss, tokens)


def body(
    tokens,
    teacher,
    valid,
    mixer_gain,
    in_weight,
    conv_weight,
    out_weight,
    ffn_gain,
    gate_weight,
    up_weight,
    down_weight,
):
    ndp = lax.axis_size("dp")
    place_of = lax.axis_index("dp") * 2 + lax.axis_index("tensor")
    width = tokens.shape[1]
    valid_f = valid.astype(f32)
    vectors = jnp.concatenate([mixer_gain[None], ffn_gain[None], conv_weight], axis=0).astype(f32)
    share = vectors.shape[1]
    small = jnp.zeros((5, width), f32)
    small = lax.dynamic_update_slice(small, vectors, (0, place_of * share))
    small = jnp.concatenate([small, jnp.full((3, width), jnp.sum(valid_f), f32)], axis=0)
    shards = shard_pieces(in_weight, out_weight, gate_weight, up_weight, down_weight)
    held, normed, normed_two, grad_rows, streams, gates, first, block_out, grad, small, loss = forward(
        ndp, shards, tokens, teacher, valid_f[:, None], small
    )
    streams_grad, out_grad, gate_grad, up_grad, down_grad, tokens_grad, small_grads = backward(
        ndp,
        gate_weight.shape[1],
        held,
        normed,
        normed_two,
        grad_rows,
        streams,
        gates,
        first,
        grad,
        small,
        loss,
        tokens,
    )
    own = lax.dynamic_slice(small_grads, (0, place_of * share), (5, share))
    return (
        small_grads[5, 0] / (width * small[5, 0]),
        block_out,
        tokens_grad,
        own[0],
        streams_grad.transpose(1, 0, 2),
        own[2:5],
        out_grad,
        own[1],
        gate_grad,
        up_grad,
        down_grad,
    )


def solution(mesh):
    rows = P(("dp", "tensor"), None)
    vector = P(("dp", "tensor"))
    weight = P("dp", "tensor")
    streams = P("dp", None, "tensor")
    taps = P(None, ("dp", "tensor"))
    return jax.shard_map(
        body,
        mesh=mesh,
        in_specs=(rows, rows, vector, vector, streams, taps, weight, vector, weight, weight, weight),
        out_specs=(P(), rows, rows, vector, streams, taps, weight, vector, weight, weight, weight),
        check_vma=False,
    )
```

```python
import functools
from types import SimpleNamespace

import jax
import jax.numpy as jnp
from jax import lax
from jax.experimental import pallas as pl
from jax.experimental.pallas import tpu as pltpu
from jax.sharding import PartitionSpec as P

MESH = pl.DeviceIdType.MESH
f32 = jnp.float32
bf16 = jnp.bfloat16
norm_eps = 1e-05
LANES = 256
NSUB = 3
YDEPTH, ZDEPTH = 3, 4
AHEAD = 4
VMEM = pl.BlockSpec(memory_space=pltpu.VMEM)
ANY = pl.BlockSpec(memory_space=pl.ANY)


def rows_of(start, size, step=16):
    return pl.ds(pl.multiple_of(start, step), size)


def place(ndp):
    d, x = lax.axis_index("dp"), lax.axis_index("tensor")
    core, y, z = d % 2, (d // 2) % 2, d // 4
    depth = ndp // 4
    at = SimpleNamespace(d=d, x=x, core=core, y=y, z=z, depth=depth, chip=d // 2)
    at.sib = (d + 1 - 2 * core, x)
    at.across = (d, 1 - x)
    at.beside = (d + 2 - 4 * y, x)
    at.lower, at.upper = (d - 4, x), (d + 4, x)
    at.has_lower, at.has_upper = z > 0, z < depth - 1
    at.cube = [at.sib, at.across, at.beside]
    step = 1
    while step < depth:
        at.cube.append((d + 4 * step * (1 - 2 * ((z // step) % 2)), x))
        step *= 2
    at.own = 2 * core + x
    at.own_sib = 2 * (1 - core) + x
    at.own_across = 2 * core + 1 - x
    at.own_far = 2 * (1 - core) + 1 - x
    return at


def meet(at):
    bar = pltpu.get_barrier_semaphore()
    always = [at.sib, at.across, at.beside] + at.cube[4:]
    for dev in always:
        pl.semaphore_signal(bar, 1, device_id=dev, device_id_type=MESH)
    for has, dev in ((at.has_lower, at.lower), (at.has_upper, at.upper)):

        @pl.when(has)
        def _():
            pl.semaphore_signal(bar, 1, device_id=dev, device_id_type=MESH)

    ends = jnp.where(at.has_lower, 1, 0) + jnp.where(at.has_upper, 1, 0)
    pl.semaphore_wait(bar, len(always) + ends)


def remote(src, dst, send, recv, dev):
    return pltpu.make_async_remote_copy(
        src_ref=src, dst_ref=dst, send_sem=send, recv_sem=recv, device_id=dev, device_id_type=MESH
    )


def total_copy(at, step, cur, got, send, recv):
    return remote(cur.at[step], got.at[step], send.at[step], recv.at[step], at.cube[step])


def total_end(at, step, cur, got, copy):
    copy.wait()
    cur[step + 1] = cur[step] + got[step]


def total_step(at, step, cur, got, send, recv):
    copy = total_copy(at, step, cur, got, send, recv)
    copy.start()
    total_end(at, step, cur, got, copy)


class Share:
    def __init__(self, at, buf, rows, sems):
        self.at, self.buf, self.rows, self.sems = at, buf, rows, sems
        self.sub = rows // NSUB

    def part(self, slot, j):
        return self.buf.at[rows_of(slot * self.rows + j * self.sub, self.sub), :]

    def copy(self, slot, j, k, dev):
        part = self.part(slot, j)
        return remote(part, part, self.sems.at[2 * k, j], self.sems.at[2 * k + 1, j], dev)

    def start(self, j):
        self.copy(self.at.own, j, 0, self.at.across).start()
        self.copy(self.at.own, j, 1, self.at.sib).start()

    def forward(self, j):
        self.copy(self.at.own_across, j, 0, self.at.across).wait_recv()
        self.copy(self.at.own_across, j, 2, self.at.sib).start()

    def finish(self):
        for j in range(NSUB):
            self.copy(self.at.own_sib, j, 1, self.at.sib).wait_recv()
            self.copy(self.at.own_far, j, 2, self.at.sib).wait_recv()
            self.copy(self.at.own, j, 0, self.at.across).wait_send()
            self.copy(self.at.own, j, 1, self.at.sib).wait_send()
            self.copy(self.at.own_across, j, 2, self.at.sib).wait_send()


class Sums:
    def __init__(self, at, acc, rows, core_out, core_in, far_in, core_sems, far_sems):
        self.at, self.acc, self.rows = at, acc, rows
        self.core_out, self.core_in, self.far_in = core_out, core_in, far_in
        self.core_sems, self.far_sems = core_sems, far_sems
        self.sub = rows // NSUB

    def of(self, slot, j):
        return self.acc[rows_of(slot * self.rows + j * self.sub, self.sub), :]

    def core_copy(self, k, j):
        part = rows_of(j * self.sub, self.sub)
        return remote(
            self.core_out.at[k, part, :],
            self.core_in.at[k, part, :],
            self.core_sems.at[0, k, j],
            self.core_sems.at[1, k, j],
            self.at.sib,
        )

    def far_copy(self, j):
        part = rows_of(j * self.sub, self.sub)
        return remote(
            self.core_in.at[0, part, :],
            self.far_in.at[part, :],
            self.far_sems.at[0, j],
            self.far_sems.at[1, j],
            self.at.across,
        )

    def to_core(self):
        for k, slot in ((0, self.at.own_far), (1, self.at.own_sib)):
            for j in range(NSUB):
                self.core_out[k, rows_of(j * self.sub, self.sub), :] = self.of(slot, j).astype(bf16)
                self.core_copy(k, j).start()

    def to_far(self):
        for j in range(NSUB):
            part = rows_of(j * self.sub, self.sub)
            self.core_copy(0, j).wait_recv()
            both = self.of(self.at.own_across, j) + self.core_in[0, part, :].astype(f32)
            self.core_in[0, part, :] = both.astype(bf16)
            self.far_copy(j).start()

    def take(self, j):
        part = rows_of(j * self.sub, self.sub)
        self.core_copy(1, j).wait_recv()
        self.far_copy(j).wait_recv()
        return (
            self.of(self.at.own, j)
            + self.core_in[1, part, :].astype(f32)
            + self.far_in[part, :].astype(f32)
        )

    def finish(self):
        for j in range(NSUB):
            self.core_copy(0, j).wait_send()
            self.core_copy(1, j).wait_send()
            self.far_copy(j).wait_send()


def nt(left, right):
    return lax.dot_general(left, right, (((1,), (1,)), ((), ())), preferred_element_type=f32)


def tn(left, right):
    return lax.dot_general(left, right, (((0,), (0,)), ((), ())), preferred_element_type=f32)


def nn(left, right):
    return jnp.dot(left, right, preferred_element_type=f32)


def inverse_of(source):
    return lax.rsqrt(jnp.mean(source * source, axis=1, keepdims=True) + norm_eps)


def shifted(value, by):
    if by == 0:
        return value
    size = value.shape[0]
    row = lax.broadcasted_iota(jnp.int32, value.shape, 0)
    inside = row >= by if by > 0 else row < size + by
    return jnp.where(inside, pltpu.roll(value, by % size, 0), 0.0)


def convolve(mixed, taps):
    return taps[0:1] * shifted(mixed, 2) + taps[1:2] * shifted(mixed, 1) + taps[2:3] * mixed


class Gather:
    def __init__(self, at, held, chunk, early_y, sems):
        self.at, self.held, self.chunk, self.early_y = at, held, chunk, early_y
        self.recv, self.own_send, self.send = sems

    def by_kind(self, p, act):
        kind = self.early_y.get(p)
        if kind != "half":
            act(kind == "both")
            return
        for core in (0, 1):

            @pl.when(self.at.core == core)
            def _():
                act(core == 1)

    def block(self, p, chip, count=1):
        return self.held.at[p, rows_of(chip * self.chunk, count * self.chunk), :]

    def copy(self, p, chip, count, send, dev):
        block = self.block(p, chip, count)
        return remote(block, block, send, self.recv.at[p, chip], dev)

    def arrived(self, p, chip, count=1):
        self.copy(p, chip, count, self.own_send.at[0, 0], self.at.beside).wait_recv()

    def own(self, p, act):
        at = self.at
        act(self.copy(p, at.chip, 1, self.own_send.at[0, p], at.beside))
        self.by_kind(p, lambda pairs: None if pairs else self.own_z(p, at.chip, 1, act))

    def own_z(self, p, chip, count, act):
        at = self.at

        @pl.when(at.has_upper)
        def _():
            act(self.copy(p, chip, count, self.own_send.at[1, p], at.upper))

        @pl.when(at.has_lower)
        def _():
            act(self.copy(p, chip, count, self.own_send.at[2, p], at.lower))

    def passing(self, p, pairs, parity, wait, act):
        at = self.at

        def step(s, carry):
            for from_z, goes_on, dev, way in (
                (at.z - 1 - s, at.has_upper, at.upper, 0),
                (at.z + 1 + s, at.has_lower, at.lower, 1),
            ):

                @pl.when(jnp.logical_and(from_z >= 0, from_z < at.depth))
                def _():
                    chip = 2 * from_z if pairs else 2 * from_z + at.y
                    count = 2 if pairs else 1
                    if wait:
                        self.arrived(p, chip, count)

                    @pl.when(goes_on)
                    def _():
                        act(self.copy(p, chip, count, self.send.at[way, parity, from_z], dev))

                    if not pairs:
                        act(self.copy(p, chip, count, self.send.at[2, parity, from_z], at.beside))

            return carry

        lax.fori_loop(0, at.depth - 1, step, 0)

    def sent(self, p):
        self.by_kind(p, lambda pairs: self.passing(p, pairs, p % AHEAD, False, lambda copy: copy.wait_send()))

    def relay(self, p):
        go = lambda copy: copy.start()
        if p >= AHEAD:
            self.sent(p - AHEAD)

        def hand_on(pairs):
            if pairs:
                self.arrived(p, 2 * self.at.z + 1 - self.at.y)
                self.own_z(p, 2 * self.at.z, 2, go)
            self.passing(p, pairs, p % AHEAD, True, go)

        self.by_kind(p, hand_on)

    def whole(self, p):
        def step(z, carry):
            self.arrived(p, 2 * z + 1 - self.at.y)
            return carry

        self.by_kind(p, lambda pairs: None if pairs else lax.fori_loop(0, self.at.depth, step, 0))

    def own_done(self, p):
        done = lambda copy: copy.wait_send()
        self.own(p, done)
        self.by_kind(p, lambda pairs: self.own_z(p, 2 * self.at.z, 2, done) if pairs else None)


def forward_kernel(
    ndp,
    early_y,
    in_weight,
    out_weight,
    gate_weight,
    up_weight,
    down_weight,
    tokens,
    teacher,
    valid,
    mixer_gain,
    ffn_gain,
    conv_weight,
    held_out,
    normed_out,
    normed_two_out,
    grad_rows_out,
    streams_out,
    gates_out,
    first_out,
    block_out,
    grad_out,
    small_out,
    loss_out,
    held,
    landed,
    mine,
    rows_a,
    rows_b,
    acc,
    streams,
    gates,
    core_out,
    core_in,
    far_in,
    first,
    result,
    error_grad,
    cur,
    got,
    chip_sems,
    recv_sems,
    own_sems,
    send_sems,
    share_sems,
    core_sems,
    far_sems,
    cube_sems,
    out_sems,
    held_sems,
    gate_sems,
):
    at = place(ndp)
    pieces, width, piece = held.shape
    part_rows = out_weight.shape[0]
    chunk = 2 * part_rows
    rows = tokens.shape[0]
    sub = rows // NSUB
    channels = streams.shape[1] // 3
    aligned = part_rows % 16 == 0
    go = lambda copy: copy.start()
    gather = Gather(at, held, chunk, early_y, (recv_sems, own_sems, send_sems))
    share_a = Share(at, rows_a, rows, share_sems)
    share_b = Share(at, rows_b, rows, share_sems)
    sums = Sums(at, acc, rows, core_out, core_in, far_in, core_sems, far_sems)

    span = (pieces - 2) * LANES
    short = gate_weight.shape[1] - 2 * span + LANES

    def parts(p, core, count=LANES):
        at_columns = rows_of(core * channels, channels, 128)
        if p == 0:
            return [(in_weight.at[k, :, at_columns], k * channels, channels) for k in range(2)]
        if p == 1:
            return [(in_weight.at[2, :, at_columns], 0, channels), (out_weight.at[:, at_columns], channels, channels)]
        at_columns = rows_of(core * span + (p - 2) * LANES, count, 128)
        return [(w.at[:, at_columns], k * LANES, count) for k, w in enumerate((gate_weight, up_weight, down_weight))]

    def each_part(p, core, act):
        if p < pieces - 1 or short == LANES:
            for k, (src, column, count) in enumerate(parts(p, core)):
                act(k, src, column, count)
            return
        for to, count in ((0, LANES), (1, short)):

            @pl.when(core == to)
            def _():
                for k, (src, column, size) in enumerate(parts(p, to, count)):
                    act(k, src, column, size)

    def landing(p, core, column, count, buffer):
        if not aligned:
            return buffer.at[p, :, pl.ds(column, count)]
        rows_there = rows_of(at.chip * chunk + core * part_rows, part_rows)
        return held.at[p, rows_there, pl.ds(column, count)]

    def to_sib(p, act):
        def copy(k, src, column, count):
            dst = landing(p, at.core, column, count, landed)
            act(remote(src, dst, chip_sems.at[0, p, k], chip_sems.at[1, p, k], at.sib))

        each_part(p, 1 - at.core, copy)

    def from_sib(p):
        def copy(k, src, column, count):
            dst = landing(p, 1 - at.core, column, count, landed)
            remote(src, dst, chip_sems.at[0, p, k], chip_sems.at[1, p, k], at.sib).wait_recv()

        each_part(p, at.core, copy)

    def keep(p, act):
        def copy(k, src, column, count):
            dst = landing(p, at.core, column, count, mine)
            act(pltpu.make_async_copy(src, dst, chip_sems.at[2, p, k]))

        each_part(p, at.core, copy)

    def own_block(p):
        keep(p, lambda copy: copy.wait())
        from_sib(p)
        here = rows_of(at.chip * chunk, chunk)
        if not aligned:
            a, b = mine[p].astype(f32), landed[p].astype(f32)
            lower = jnp.where(at.core == 0, a, b)
            upper = jnp.where(at.core == 0, b, a)
            held[p, here, :] = jnp.concatenate([lower, upper], axis=0).astype(bf16)
        if p == pieces - 1 and short < LANES:

            @pl.when(at.core == 1)
            def _():
                for k in range(3):
                    held[p, here, k * LANES + short : (k + 1) * LANES] = jnp.zeros((chunk, LANES - short), bf16)

        gather.own(p, go)

    meet(at)
    to_sib(0, go)
    keep(0, go)
    share = mixer_gain.shape[1]
    cur[0] = jnp.zeros(cur.shape[1:], f32)
    cur[0, 0:1, 0:share] = mixer_gain[...].astype(f32)
    cur[0, 1:2, 0:share] = ffn_gain[...].astype(f32)
    cur[0, 2:5, 0:share] = conv_weight[...].astype(f32)
    placed = pltpu.roll(cur[0], (at.d * 2 + at.x) * share, 1)
    line = lax.broadcasted_iota(jnp.int32, placed.shape, 0)
    cur[0] = jnp.where(line < 5, placed, jnp.sum(valid[...]))
    total_step(at, 0, cur, got, cube_sems.at[0], cube_sems.at[1])
    own_block(0)
    total_step(at, 1, cur, got, cube_sems.at[0], cube_sems.at[1])
    for j in range(NSUB):
        rows_a[rows_of(at.own * rows + j * sub, sub), :] = tokens[pl.ds(j * sub, sub), :]
        share_a.start(j)
    for p in range(1, pieces):
        to_sib(p, go)
        keep(p, go)
    for step in range(2, len(at.cube)):
        total_step(at, step, cur, got, cube_sems.at[0], cube_sems.at[1])
        if step < 4:
            own_block(step - 1)
    last = len(at.cube)
    small_out[...] = cur[last]
    for j in range(NSUB):
        share_a.forward(j)
    gain_one, gain_two = cur[last, 0:1, :], cur[last, 1:2, :]
    relay = gather.relay
    relay(0)
    share_a.finish()

    def norm_rows(i, carry):
        part = rows_of(i * sub, sub)
        source = rows_a[part, :].astype(f32)
        rows_a[part, :] = (source * inverse_of(source) * gain_one).astype(bf16)
        return carry

    lax.fori_loop(0, 4 * NSUB, norm_rows, 0)
    normed_copy = pltpu.make_async_copy(rows_a, normed_out, out_sems.at[0])
    normed_copy.start()

    def save(p):
        return pltpu.make_async_copy(held.at[p], held_out.at[p], held_sems.at[p])

    own_block(3)
    relay(1)
    own_block(4)
    relay(2)
    own_block(5)
    for p in (0, 1):
        gather.whole(p)
        save(p).start()
    lane = at.x * 2 * channels + at.core * channels
    taps = cur[last, 2:5, rows_of(lane, channels, 128)]

    def mix(r, carry):
        part = rows_of(((r + 1 - at.core) % 2) * 2 * rows, 2 * rows)
        both = nn(rows_a[part, :], held[0])
        x_stream = nn(rows_a[part, :], held[1, :, 0:channels])
        streams[part, 0 : 2 * channels] = both
        streams[part, 2 * channels :] = x_stream
        convolved = convolve(both[:, 0:channels] * x_stream, taps)
        gated = (both[:, channels:] * convolved).astype(bf16)
        acc[part, :] = nt(gated, held[1, :, channels:])
        return carry

    lax.fori_loop(0, 2, mix, 0)
    streams_copy = pltpu.make_async_copy(streams, streams_out, out_sems.at[1])
    streams_copy.start()
    sums.to_core()
    own_block(6)
    own_block(7)
    sums.to_far()
    relay(3)
    for p in range(8, pieces):
        own_block(p)
    for j in range(NSUB):
        part = rows_of(j * sub, sub)
        value = tokens[part, :].astype(f32) + sums.take(j)
        first[part, :] = value
        normed_two = (value * inverse_of(value) * gain_two).astype(bf16)
        rows_b[rows_of(at.own * rows + j * sub, sub), :] = normed_two
        share_b.start(j)
    sums.finish()
    first_copy = pltpu.make_async_copy(first, first_out, out_sems.at[2])
    first_copy.start()
    relay(4)
    for j in range(NSUB):
        share_b.forward(j)
    share_b.finish()
    normed_two_copy = pltpu.make_async_copy(rows_b, normed_two_out, out_sems.at[3])
    normed_two_copy.start()
    acc[...] = jnp.zeros_like(acc)

    def gates_copy(p):
        slot = p % 2
        return pltpu.make_async_copy(gates.at[slot], gates_out.at[p - 2], gate_sems.at[slot])

    def feed(p, carry):
        for q in range(5, pieces):

            @pl.when(p == q - 3)
            def _():
                relay(q)

        for q in range(2, pieces):

            @pl.when(p == q)
            def _():
                gather.whole(q)

        save(p).start()

        @pl.when(p >= 4)
        def _():
            gates_copy(p - 2).wait()

        def some(r, inner):
            part = rows_of(((r + 1 - at.core) % 2) * 2 * rows, 2 * rows)
            both = nn(rows_b[part, :], held[p, :, 0 : 2 * LANES])
            gate, up = both[:, 0:LANES], both[:, LANES:]
            gates[p % 2, part, :] = both.astype(bf16)
            hidden = (gate * jax.nn.sigmoid(gate) * up).astype(bf16)
            acc[part, :] += nt(hidden, held[p, :, 2 * LANES :])
            return inner

        lax.fori_loop(0, 2, some, 0)
        gates_copy(p).start()
        return carry

    normed_copy.wait()
    lax.fori_loop(2, pieces, feed, 0)
    sums.to_core()
    sums.to_far()
    scale = 1.0 / (width * cur[last, 5:6, 0:1])
    loss = jnp.zeros((1, width), f32)
    for j in range(NSUB):
        part = rows_of(j * sub, sub)
        value = first[part, :] + sums.take(j)
        result[part, :] = value
        error = value - teacher[part, :].astype(f32)
        weighted = valid[part, :] * error
        loss = loss + jnp.sum(weighted * error, axis=0, keepdims=True)
        grad = (2.0 * scale) * weighted
        error_grad[part, :] = grad
        rows_a[rows_of(at.own * rows + j * sub, sub), :] = grad.astype(bf16)
        share_a.start(j)
    loss_out[...] = jnp.broadcast_to(jnp.sum(loss, axis=1, keepdims=True), loss_out.shape)
    sums.finish()
    result_copy = pltpu.make_async_copy(result, block_out, out_sems.at[4])
    result_copy.start()
    grad_copy = pltpu.make_async_copy(error_grad, grad_out, out_sems.at[5])
    grad_copy.start()
    for j in range(NSUB):
        share_a.forward(j)
    share_a.finish()
    rows_copy = pltpu.make_async_copy(rows_a, grad_rows_out, out_sems.at[6])
    rows_copy.start()
    for p in range(pieces):
        save(p).wait()
        to_sib(p, lambda copy: copy.wait_send())
        gather.own_done(p)
    for p in range(pieces - AHEAD, pieces):
        gather.sent(p)
    for p in (pieces - 2, pieces - 1):
        gates_copy(p).wait()
    for copy in (streams_copy, first_copy, normed_two_copy, result_copy, grad_copy, rows_copy):
        copy.wait()


def forward(ndp, weights, tokens, teacher, valid, vectors):
    part_rows, channels = weights[1].shape
    channels //= 2
    piece = 2 * channels
    pieces = 2 - (-weights[2].shape[1] // (2 * LANES))
    rows, width = tokens.shape
    cube = small_steps(ndp)
    early_y = {3: "both", 6: "half"}
    dma = pltpu.SemaphoreType.DMA
    landing = (pieces, part_rows, piece) if part_rows % 16 else (1, 16, 128)
    shape = jax.ShapeDtypeStruct
    outs = (
        shape((pieces, width, piece), bf16),
        shape((4 * rows, width), bf16),
        shape((4 * rows, width), bf16),
        shape((4 * rows, width), bf16),
        shape((4 * rows, 3 * channels), f32),
        shape((pieces - 2, 4 * rows, 2 * LANES), bf16),
        shape((rows, width), f32),
        shape((rows, width), f32),
        shape((rows, width), f32),
        shape((8, width), f32),
        shape((8, 128), f32),
    )
    scratch = [
        pltpu.VMEM((pieces, width, piece), bf16),
        pltpu.VMEM(landing, bf16),
        pltpu.VMEM(landing, bf16),
        pltpu.VMEM((4 * rows, width), bf16),
        pltpu.VMEM((4 * rows, width), bf16),
        pltpu.VMEM((4 * rows, width), f32),
        pltpu.VMEM((4 * rows, 3 * channels), f32),
        pltpu.VMEM((2, 4 * rows, 2 * LANES), bf16),
        pltpu.VMEM((2, rows, width), bf16),
        pltpu.VMEM((2, rows, width), bf16),
        pltpu.VMEM((rows, width), bf16),
        pltpu.VMEM((rows, width), f32),
        pltpu.VMEM((rows, width), f32),
        pltpu.VMEM((rows, width), f32),
        pltpu.VMEM((cube + 1, 8, width), f32),
        pltpu.VMEM((cube, 8, width), f32),
        dma((3, pieces, 3)),
        dma((pieces, ndp // 2)),
        dma((3, pieces)),
        dma((3, AHEAD, ndp // 4)),
        dma((6, NSUB)),
        dma((2, 2, NSUB)),
        dma((2, NSUB)),
        dma((2, cube)),
        dma((7,)),
        dma((pieces,)),
        dma((2,)),
    ]
    return pl.pallas_call(
        functools.partial(forward_kernel, ndp, early_y),
        out_shape=outs,
        in_specs=[ANY] * 5 + [VMEM] * 6,
        out_specs=[ANY] * 9 + [VMEM] * 2,
        scratch_shapes=scratch,
        compiler_params=pltpu.CompilerParams(
            collective_id=0, has_side_effects=True, vmem_limit_bytes=63 << 20
        ),
    )(*weights, tokens, teacher, valid, *vectors)


def small_steps(ndp):
    return 3 + (ndp // 4 - 1).bit_length()


class Scatter:
    def __init__(self, at, held, chunk, count, beside_in, line_in, pair_in, pair_beside, total, sems, credits):
        self.at, self.held, self.chunk, self.count = at, held, chunk, count
        self.beside_in, self.line_in, self.pair_in, self.pair_beside = beside_in, line_in, pair_in, pair_beside
        self.total, self.credits = total, credits
        self.beside_sems, self.line_sems, self.pair_sems, self.pair_y_sems = sems
        self.ydepth, self.zdepth = beside_in.shape[0], line_in.shape[0]

    def block(self, p, chip, count=1):
        return self.held.at[p, rows_of(chip * self.chunk, count * self.chunk), :]

    def beside_copy(self, p, m, z):
        slot = m % self.ydepth
        return remote(
            self.block(p, 2 * z + 1 - self.at.y),
            self.beside_in.at[slot, z],
            self.beside_sems.at[0, slot, z],
            self.beside_sems.at[1, slot, z],
            self.at.beside,
        )

    def line_copy(self, p, m, z, up):
        slot, way = m % self.zdepth, 0 if up else 1
        into = z + 1 if up else z
        return remote(
            self.block(p, 2 * z + self.at.y),
            self.line_in.at[slot, into],
            self.line_sems.at[way, slot, z],
            self.line_sems.at[2, slot, into],
            self.at.upper if up else self.at.lower,
        )

    def pair_copy(self, p, z, up):
        into = z + 1 if up else z
        return remote(
            self.block(p, 2 * z, 2),
            self.pair_in.at[into],
            self.pair_sems.at[0 if up else 1, z],
            self.pair_sems.at[2, into],
            self.at.upper if up else self.at.lower,
        )

    def turn(self, s):
        z, last = self.at.z, self.at.depth - 1
        low = jnp.where(z < self.at.depth // 2, 1, 0)
        down, up = last - s, s
        other = low * (down - jnp.where(down <= z, 1, 0)) + (1 - low) * (up + jnp.where(up >= z, 1, 0))
        mine = jnp.where(s == last, 1, 0)
        return mine * z + (1 - mine) * other

    def free_beside(self, p, m, before):
        if m >= self.ydepth:
            pl.semaphore_wait(self.credits.at[0], 1)
            self.drop_beside(before, m)

    def drop_beside(self, p, m):
        def step(z, carry):
            self.beside_copy(p, m, z).wait_send()
            return carry

        lax.fori_loop(0, self.at.depth, step, 0)

    def send_beside(self, p, m, before):
        self.free_beside(p, m, before)

        def step(s, carry):
            self.beside_copy(p, m, self.turn(s)).start()
            return carry

        lax.fori_loop(0, self.at.depth, step, 0)

    def ways(self, has, act):
        at = self.at

        def step(s, carry):
            for z, wanted, up in (
                (at.depth - 1 - s, at.depth - 1 - s > at.z, True),
                (s, s < at.z, False),
            ):

                @pl.when(jnp.logical_and(wanted, has(up)))
                def _():
                    act(z, up)

            return carry

        lax.fori_loop(0, at.depth - 1, step, 0)

    def behind(self, up):
        return self.at.has_lower if up else self.at.has_upper

    def opens(self, up):
        return jnp.logical_not(self.behind(up))

    def near(self, up):
        low = self.at.z < self.at.depth // 2
        return jnp.logical_and(self.behind(up), low if up else jnp.logical_not(low))

    def far(self, up):
        low = self.at.z < self.at.depth // 2
        return jnp.logical_and(self.behind(up), jnp.logical_not(low) if up else low)

    def add_beside(self, p, m, before, onward):
        at = self.at
        if m >= self.zdepth:
            for has, credit in ((at.has_upper, 1), (at.has_lower, 2)):

                @pl.when(has)
                def _():
                    pl.semaphore_wait(self.credits.at[credit], 1)

            self.drop(before, m)

        def step(s, carry):
            z = self.turn(s)
            own = self.block(p, 2 * z + at.y)
            self.beside_copy(p, m, z).wait_recv()
            own[...] = (own[...].astype(f32) + self.beside_in[m % self.ydepth, z].astype(f32)).astype(bf16)
            for up in (True, False):

                @pl.when(jnp.logical_and(z > at.z if up else z < at.z, self.opens(up)))
                def _():
                    self.line_copy(p, m, z, up).start()

                if onward:

                    @pl.when(jnp.logical_and(z > at.z if up else z < at.z, self.behind(up)))
                    def _():
                        self.pass_on(p, m, z, up)

            return carry

        lax.fori_loop(0, at.depth, step, 0)
        if m + self.ydepth < self.count:
            pl.semaphore_signal(self.credits.at[0], 1, device_id=at.beside, device_id_type=MESH)

    def pass_on(self, p, m, z, up):
        self.line_copy(p, m, z, up).wait_recv()
        own = self.block(p, 2 * z + self.at.y)
        came = self.line_in[m % self.zdepth, z + 1 if up else z].astype(f32)
        own[...] = (own[...].astype(f32) + came).astype(bf16)
        self.line_copy(p, m, z, up).start()

    def hop(self, p, m, has):
        self.ways(has, functools.partial(self.pass_on, p, m))

    def collect(self, p, m, slot):
        at = self.at
        total = self.total.at[slot]
        total[...] = self.block(p, 2 * at.z + at.y)[...].astype(f32)
        for up in (True, False):

            @pl.when(self.behind(up))
            def _():
                self.line_copy(p, m, at.z, up).wait_recv()
                total[...] += self.line_in[m % self.zdepth, at.z + 1 if up else at.z].astype(f32)
                if m + self.zdepth < self.count:
                    pl.semaphore_signal(
                        self.credits.at[1 if up else 2],
                        1,
                        device_id=at.lower if up else at.upper,
                        device_id_type=MESH,
                    )

    def drop(self, p, m):
        self.ways(lambda up: True, lambda z, up: self.line_copy(p, m, z, up).wait_send())

    def pairs_open(self, p):
        self.ways(self.opens, lambda z, up: self.pair_copy(p, z, up).start())

    def pair_hop(self, p, has):
        def act(z, up):
            self.pair_copy(p, z, up).wait_recv()
            own = self.block(p, 2 * z, 2)
            own[...] = (own[...].astype(f32) + self.pair_in[z + 1 if up else z].astype(f32)).astype(bf16)
            self.pair_copy(p, z, up).start()

        self.ways(has, act)

    def pair_y_copy(self, p):
        at = self.at
        return remote(
            self.block(p, 2 * at.z + 1 - at.y),
            self.pair_beside,
            self.pair_y_sems.at[0],
            self.pair_y_sems.at[1],
            at.beside,
        )

    def pairs_cross(self, p):
        at = self.at
        own = self.block(p, 2 * at.z, 2)
        for up in (True, False):

            @pl.when(self.behind(up))
            def _():
                self.pair_copy(p, at.z, up).wait_recv()
                came = self.pair_in[at.z + 1 if up else at.z].astype(f32)
                own[...] = (own[...].astype(f32) + came).astype(bf16)

        self.pair_y_copy(p).start()

    def pairs_close(self, p, slot):
        at = self.at
        self.pair_y_copy(p).wait()
        mine = self.block(p, 2 * at.z + at.y)[...].astype(f32)
        self.total[slot] = mine + self.pair_beside[...].astype(f32)
        self.ways(lambda up: True, lambda z, up: self.pair_copy(p, z, up).wait_send())


def backward_kernel(
    ndp,
    held_in,
    normed_in,
    normed_two_in,
    grad_rows_in,
    streams_in,
    gates_in,
    first_in,
    grad_in,
    small,
    loss,
    tokens,
    streams_grad,
    out_grad,
    gate_grad,
    up_grad,
    down_grad,
    tokens_grad,
    mixer_gain_grad,
    ffn_gain_grad,
    conv_grad,
    loss_out,
    held,
    rows_a,
    rows_b,
    acc,
    gates,
    streams,
    core_out,
    core_in,
    far_in,
    first,
    grad,
    back,
    beside_in,
    line_in,
    pair_in,
    pair_beside,
    total,
    cur,
    got,
    share_sems,
    core_sems,
    far_sems,
    cube_sems,
    load_sems,
    held_sems,
    gate_sems,
    beside_sems,
    line_sems,
    pair_sems,
    pair_y_sems,
    done_sems,
    credits,
):
    at = place(ndp)
    pieces, width, piece = held.shape
    rows = tokens.shape[0]
    sub = rows // NSUB
    chunk = 2 * width // ndp
    half = chunk // 2
    channels = piece // 2
    order = [2] + list(range(4, pieces)) + [0, 1]
    paired = 3
    share = Share(at, rows_a, rows, share_sems)
    sums = Sums(at, acc, rows, core_out, core_in, far_in, core_sems, far_sems)
    scatter = Scatter(
        at,
        held,
        chunk,
        len(order),
        beside_in,
        line_in,
        pair_in,
        pair_beside,
        total,
        (beside_sems, line_sems, pair_sems, pair_y_sems),
        credits,
    )

    def load(src, dst, k):
        return pltpu.make_async_copy(src, dst, load_sems.at[k])

    def load_held(p):
        return pltpu.make_async_copy(held_in.at[p], held.at[p], held_sems.at[p])

    def load_gates(p):
        return pltpu.make_async_copy(gates_in.at[p - 2], gates.at[p % 2], gate_sems.at[p % 2])

    def load_streams(r):
        return load(streams_in.at[pl.ds(r * 2 * rows, 2 * rows), :], streams, 5)

    opening = (
        load(grad_rows_in, rows_a, 0),
        load_gates(2),
        load_held(2),
        load(normed_two_in, rows_b, 1),
    )
    for copy in opening:
        copy.start()
    load_gates(3).start()
    for p in list(range(3, pieces)) + [0, 1]:
        load_held(p).start()
    load_first, load_grad = load(first_in, first, 2), load(grad_in, grad, 3)
    load_first.start()
    load_grad.start()
    load_streams(0).start()
    meet(at)
    acc[...] = jnp.zeros_like(acc)
    opening[0].wait()
    opening[3].wait()

    def ffn(p, m=None):
        load_gates(p).wait()
        load_held(p).wait()

        def some(r, carry):
            part = rows_of(((r + 1 - at.core) % 2) * 2 * rows, 2 * rows)
            grad_hidden = nn(rows_a[part, :], held[p, :, 2 * LANES :])
            gate = gates[p % 2, part, 0:LANES].astype(f32)
            up = gates[p % 2, part, LANES:].astype(f32)
            sig = jax.nn.sigmoid(gate)
            active = gate * sig
            back[part, 2 * LANES : 3 * LANES] = (active * up).astype(bf16)
            grad_gate = grad_hidden * up * sig * (1.0 + gate * (1.0 - sig))
            back[part, 0:LANES] = grad_gate.astype(bf16)
            back[part, LANES : 2 * LANES] = (grad_hidden * active).astype(bf16)
            acc[part, :] += nt(back[part, 0 : 2 * LANES], held[p, :, 0 : 2 * LANES])
            return carry

        lax.fori_loop(0, 2, some, 0)

        blocks = 2 * width // piece
        matched = blocks == at.depth

        def weights(s, carry):
            i = scatter.turn(s) if matched else s
            part = rows_of(i * (piece // 2), piece // 2, 128)
            held[p, part, 0 : 2 * LANES] = tn(rows_b[:, part], back[:, 0 : 2 * LANES]).astype(bf16)
            held[p, part, 2 * LANES :] = tn(rows_a[:, part], back[:, 2 * LANES : 3 * LANES]).astype(bf16)
            if m is not None and matched:
                scatter.beside_copy(p, m, i).start()
            return carry

        lax.fori_loop(0, blocks, weights, 0)
        if m is not None and not matched:
            scatter.send_beside(p, m, None)
        if p + 2 < pieces:
            load_gates(p + 2).start()

    given = []

    span = (pieces - 2) * LANES
    short = gate_grad.shape[1] - 2 * span + LANES

    def parts(p, core):
        if p == 0:
            at_columns = rows_of(core * channels, channels, 128)
            return [(k * channels, channels, streams_grad.at[k, :, at_columns]) for k in range(2)]
        if p == 1:
            at_columns = rows_of(core * channels, channels, 128)
            return [
                (0, channels, streams_grad.at[2, :, at_columns]),
                (channels, channels, out_grad.at[:, at_columns]),
            ]
        found = []
        for k, out in enumerate((gate_grad, up_grad, down_grad)):
            found.append((k * LANES, LANES, out.at[:, rows_of(core * span + (p - 2) * LANES, LANES, 128)]))
        return found

    def narrow(p, core):
        found = []
        for k, out in enumerate((gate_grad, up_grad, down_grad)):
            found.append((k * LANES, short, out.at[:, rows_of(core * span + (p - 2) * LANES, short, 128)]))
        return found

    def each_part(p, core, act):
        if p < pieces - 1 or short == LANES:
            for k, (first_column, count, dst) in enumerate(parts(p, core)):
                act(k, first_column, count, dst)
            return

        for is_short, found in ((False, parts), (True, narrow)):

            @pl.when((core == 1) if is_short else (core == 0))
            def _():
                for k, (first_column, count, dst) in enumerate(found(p, 0 if not is_short else 1)):
                    act(k, first_column, count, dst)

    def piece_rows(p, core, first_column, count):
        slot = given.index(p) % 2 if p in given else 0
        return total.at[slot, rows_of(core * half, half, 8), pl.ds(first_column, count)]

    def out_local(p, act):
        def copy(k, first_column, count, dst):
            src = piece_rows(p, at.core, first_column, count)
            act(pltpu.make_async_copy(src, dst, done_sems.at[0, p, k]))

        each_part(p, at.core, copy)

    def out_sib(p, core, act):
        def copy(k, first_column, count, dst):
            src = piece_rows(p, 1 - at.core, first_column, count)
            act(remote(src, dst, done_sems.at[1, p, k], done_sems.at[2, p, k], at.sib))

        each_part(p, core, copy)

    def give(p, fill):
        if len(given) > 1:
            out_local(given[-2], lambda copy: copy.wait())
            out_sib(given[-2], at.core, lambda copy: copy.wait_send())
        given.append(p)
        fill((len(given) - 1) % 2)
        out_local(p, lambda copy: copy.start())
        out_sib(p, at.core, lambda copy: copy.start())

    def beside(m):
        scatter.send_beside(order[m], m, order[m - YDEPTH] if m >= YDEPTH else None)

    def finish(m):
        give(order[m], functools.partial(scatter.collect, order[m], m))

    def advance(m):
        onward = m == len(order) - 1
        if onward:
            scatter.hop(order[m - 1], m - 1, scatter.far)
            finish(m - 2)
        scatter.add_beside(order[m], m, order[m - ZDEPTH] if m >= ZDEPTH else None, onward)
        if onward:
            return
        scatter.hop(order[m], m, scatter.near)
        if m == 0:
            scatter.pair_hop(paired, scatter.near)
        if m >= 1:
            scatter.hop(order[m - 1], m - 1, scatter.far)
        if m == 2:
            scatter.pair_hop(paired, scatter.far)
        if m >= 2:
            finish(m - 2)
        if m == 3:
            scatter.pairs_cross(paired)
        if m == 4:
            give(paired, functools.partial(scatter.pairs_close, paired))

    gain_one, gain_two = small[0:1, :], small[1:2, :]
    ffn(2, 0)
    ffn(3)
    scatter.pairs_open(paired)
    ffn(4, 1)
    ffn(5, 2)
    advance(0)
    ffn(6)
    beside(3)
    for p in range(7, pieces):
        ffn(p)
    sums.to_core()
    load_normed = load(normed_in, rows_b, 4)
    load_normed.start()
    advance(1)
    beside(4)
    sums.to_far()
    load_first.wait()
    load_grad.wait()
    gain_two_grad = jnp.zeros((1, width), f32)
    for j in range(NSUB):
        part = rows_of(j * sub, sub)
        coming = sums.take(j)
        source = first[part, :]
        inverse = inverse_of(source)
        weighted = coming * gain_two
        inner = jnp.mean(weighted * source, axis=1, keepdims=True)
        value = grad[part, :] + inverse * weighted - source * (inverse * inverse * inverse * inner)
        grad[part, :] = value
        gain_two_grad += jnp.sum(coming * source * inverse, axis=0, keepdims=True)
        rows_a[rows_of(at.own * rows + j * sub, sub), :] = value.astype(bf16)
        share.start(j)
    sums.finish()
    advance(2)
    beside(5)
    for j in range(NSUB):
        share.forward(j)
    share.finish()
    shift = at.x * 2 * channels + at.core * channels
    cur[0] = jnp.zeros(cur.shape[1:], f32)
    cur[0, 1:2, :] = gain_two_grad
    cur[0, 5:6, :] = jnp.broadcast_to(loss[0:1, 0:1], (1, width))
    load_held(0).wait()
    load_held(1).wait()
    for r in range(2):
        load_streams(r).wait()
        part = pl.ds(r * 2 * rows, 2 * rows)
        acc[part, 0:channels] = nn(rows_a[part, :], held[1, :, channels:])

        def mix(q, carry):
            lanes = [rows_of(k * channels + q * 128, 128, 128) for k in range(3)]
            b_gate, c_gate, x_stream = (streams[:, lane] for lane in lanes)
            tap = small[2:5, rows_of(shift + q * 128, 128, 128)]
            mixed = b_gate * x_stream
            convolved = convolve(mixed, tap)
            grad_gated = acc[part, lanes[0]]
            gates[0, part, lanes[0]] = (c_gate * convolved).astype(bf16)
            back[part, lanes[1]] = (grad_gated * convolved).astype(bf16)
            grad_conv = grad_gated * c_gate
            grad_mixed = tap[2:3] * grad_conv
            grad_mixed += tap[1:2] * shifted(grad_conv, -1) + tap[0:1] * shifted(grad_conv, -2)
            for k in range(3):
                term = jnp.sum(grad_conv * shifted(mixed, 2 - k), axis=0, keepdims=True)
                cur[0, 2 + k : 3 + k, rows_of(shift + q * 128, 128, 128)] += term
            back[part, lanes[0]] = (grad_mixed * x_stream).astype(bf16)
            back[part, lanes[2]] = (grad_mixed * b_gate).astype(bf16)
            return carry

        lax.fori_loop(0, channels // 128, mix, 0)
        if r == 0:
            load_streams(1).start()
        acc[part, :] = nt(back[part, 0 : 2 * channels], held[0])
        acc[part, :] += nt(back[part, 2 * channels :], held[1, :, 0:channels])
    sums.to_core()
    load_normed.wait()

    def mixer_weights(i, carry):
        part = rows_of(i * channels, channels, 128)
        left = rows_b[:, part]
        held[0, part, :] = tn(left, back[:, 0 : 2 * channels]).astype(bf16)
        held[1, part, 0:channels] = tn(left, back[:, 2 * channels :]).astype(bf16)
        held[1, part, channels:] = tn(rows_a[:, part], gates[0, :, 0:channels]).astype(bf16)
        return carry

    lax.fori_loop(0, width // channels, mixer_weights, 0)
    advance(3)
    beside(6)
    sums.to_far()
    advance(4)
    gain_one_grad = jnp.zeros((1, width), f32)
    for j in range(NSUB):
        part = rows_of(j * sub, sub)
        coming = sums.take(j)
        source = tokens[part, :].astype(f32)
        inverse = inverse_of(source)
        weighted = coming * gain_one
        inner = jnp.mean(weighted * source, axis=1, keepdims=True)
        grad[part, :] += inverse * weighted - source * (inverse * inverse * inverse * inner)
        gain_one_grad += jnp.sum(coming * source * inverse, axis=0, keepdims=True)
    sums.finish()
    tokens_copy = load(grad, tokens_grad, 6)
    tokens_copy.start()
    cur[0, 0:1, :] = gain_one_grad
    tally = lambda step: total_copy(at, step, cur, got, cube_sems.at[0], cube_sems.at[1])
    for step in range(2):
        tally(step).start()
        total_end(at, step, cur, got, tally(step))
    tally(2).start()
    beside(7)
    steps = len(at.cube)
    count = len(order)
    advance(5)
    advance(6)
    total_end(at, 2, cur, got, tally(2))
    tally(3).start()
    advance(7)
    for step in range(3, steps):
        total_end(at, step, cur, got, tally(step))
        if step + 1 < steps:
            tally(step + 1).start()
        if step == 3:
            finish(count - 2)
    finish(count - 1)
    share_lanes = mixer_gain_grad.shape[1]
    own = pltpu.roll(cur[steps], (width - (at.d * 2 + at.x) * share_lanes) % width, 1)
    mixer_gain_grad[...] = own[0:1, 0:share_lanes]
    ffn_gain_grad[...] = own[1:2, 0:share_lanes]
    conv_grad[...] = own[2:5, 0:share_lanes]
    loss_out[...] = cur[steps, 5:6, 0:1] / (width * small[5:6, 0:1])
    for m in range(count - YDEPTH, count):
        scatter.drop_beside(order[m], m)
    for m in range(count - ZDEPTH, count):
        scatter.drop(order[m], m)
    for p in given[-2:]:
        out_local(p, lambda copy: copy.wait())
        out_sib(p, at.core, lambda copy: copy.wait_send())
    for p in given:
        out_sib(p, 1 - at.core, lambda copy: copy.wait_recv())
    tokens_copy.wait()


def backward(ndp, units, held, normed, normed_two, grad_rows, streams, gates, first, grad, small, loss, tokens):
    pieces, width, piece = held.shape
    rows = tokens.shape[0]
    chunk = 2 * width // ndp
    depth = ndp // 4
    channels = piece // 2
    cube = small_steps(ndp)
    dma = pltpu.SemaphoreType.DMA
    shape = jax.ShapeDtypeStruct
    outs = (
        shape((3, chunk // 2, 2 * channels), f32),
        shape((chunk // 2, 2 * channels), f32),
        shape((chunk // 2, units), f32),
        shape((chunk // 2, units), f32),
        shape((chunk // 2, units), f32),
        shape((rows, width), f32),
        shape((1, width // (2 * ndp)), f32),
        shape((1, width // (2 * ndp)), f32),
        shape((3, width // (2 * ndp)), f32),
        shape((1, 1), f32),
    )
    scratch = [
        pltpu.VMEM((pieces, width, piece), bf16),
        pltpu.VMEM((4 * rows, width), bf16),
        pltpu.VMEM((4 * rows, width), bf16),
        pltpu.VMEM((4 * rows, width), f32),
        pltpu.VMEM((2, 4 * rows, 2 * LANES), bf16),
        pltpu.VMEM((2 * rows, 3 * channels), f32),
        pltpu.VMEM((2, rows, width), bf16),
        pltpu.VMEM((2, rows, width), bf16),
        pltpu.VMEM((rows, width), bf16),
        pltpu.VMEM((rows, width), f32),
        pltpu.VMEM((rows, width), f32),
        pltpu.VMEM((4 * rows, 3 * channels), bf16),
        pltpu.VMEM((YDEPTH, depth, chunk, piece), bf16),
        pltpu.VMEM((ZDEPTH, depth + 1, chunk, piece), bf16),
        pltpu.VMEM((depth + 1, 2 * chunk, piece), bf16),
        pltpu.VMEM((chunk, piece), bf16),
        pltpu.VMEM((2, chunk, piece), f32),
        pltpu.VMEM((cube + 1, 8, width), f32),
        pltpu.VMEM((cube, 8, width), f32),
        dma((6, NSUB)),
        dma((2, 2, NSUB)),
        dma((2, NSUB)),
        dma((2, cube)),
        dma((7,)),
        dma((pieces,)),
        dma((2,)),
        dma((2, YDEPTH, depth)),
        dma((3, ZDEPTH, depth + 1)),
        dma((3, depth + 1)),
        dma((2,)),
        dma((3, pieces, 3)),
        pltpu.SemaphoreType.REGULAR((3,)),
    ]
    return pl.pallas_call(
        functools.partial(backward_kernel, ndp),
        out_shape=outs,
        in_specs=[ANY] * 8 + [VMEM] * 3,
        out_specs=[ANY] * 6 + [VMEM] * 4,
        scratch_shapes=scratch,
        compiler_params=pltpu.CompilerParams(
            collective_id=1, has_side_effects=True, vmem_limit_bytes=127 << 19
        ),
    )(held, normed, normed_two, grad_rows, streams, gates, first, grad, small, loss, tokens)


def body(
    tokens,
    teacher,
    valid,
    mixer_gain,
    in_weight,
    conv_weight,
    out_weight,
    ffn_gain,
    gate_weight,
    up_weight,
    down_weight,
):
    ndp = lax.axis_size("dp")
    held, normed, normed_two, grad_rows, streams, gates, first, block_out, grad, small, loss = forward(
        ndp,
        (in_weight.transpose(1, 0, 2), out_weight, gate_weight, up_weight, down_weight),
        tokens,
        teacher,
        valid.astype(f32)[:, None],
        (mixer_gain[None], ffn_gain[None], conv_weight),
    )
    streams_grad, out_grad, gate_grad, up_grad, down_grad, tokens_grad, *small_grads = backward(
        ndp,
        gate_weight.shape[1],
        held,
        normed,
        normed_two,
        grad_rows,
        streams,
        gates,
        first,
        grad,
        small,
        loss,
        tokens,
    )
    mixer_gain_grad, ffn_gain_grad, conv_grad, loss = small_grads
    return (
        loss[0, 0],
        block_out,
        tokens_grad,
        mixer_gain_grad[0],
        streams_grad.transpose(1, 0, 2),
        conv_grad,
        out_grad,
        ffn_gain_grad[0],
        gate_grad,
        up_grad,
        down_grad,
    )


def solution(mesh):
    rows = P(("dp", "tensor"), None)
    vector = P(("dp", "tensor"))
    weight = P("dp", "tensor")
    streams = P("dp", None, "tensor")
    taps = P(None, ("dp", "tensor"))
    return jax.shard_map(
        body,
        mesh=mesh,
        in_specs=(rows, rows, vector, vector, streams, taps, weight, vector, weight, weight, weight),
        out_specs=(P(), rows, rows, vector, streams, taps, weight, vector, weight, weight, weight),
        check_vma=False,
    )
```

```python
import functools
from types import SimpleNamespace

import jax
import jax.numpy as jnp
from jax import lax
from jax.experimental import pallas as pl
from jax.experimental.pallas import tpu as pltpu
from jax.sharding import PartitionSpec as P

MESH = pl.DeviceIdType.MESH
f32 = jnp.float32
bf16 = jnp.bfloat16
norm_eps = 1e-05
LANES = 256
NSUB = 3
YDEPTH, ZDEPTH = 3, 4
AHEAD = 4
VMEM = pl.BlockSpec(memory_space=pltpu.VMEM)
ANY = pl.BlockSpec(memory_space=pl.ANY)


def rows_of(start, size, step=16):
    return pl.ds(pl.multiple_of(start, step), size)


def place(ndp):
    d, x = lax.axis_index("dp"), lax.axis_index("tensor")
    core, y, z = d % 2, (d // 2) % 2, d // 4
    depth = ndp // 4
    at = SimpleNamespace(d=d, x=x, core=core, y=y, z=z, depth=depth, chip=d // 2)
    at.sib = (d + 1 - 2 * core, x)
    at.across = (d, 1 - x)
    at.beside = (d + 2 - 4 * y, x)
    at.lower, at.upper = (d - 4, x), (d + 4, x)
    at.has_lower, at.has_upper = z > 0, z < depth - 1
    at.cube = [at.sib, at.across, at.beside]
    step = 1
    while step < depth:
        at.cube.append((d + 4 * step * (1 - 2 * ((z // step) % 2)), x))
        step *= 2
    at.own = 2 * core + x
    at.own_sib = 2 * (1 - core) + x
    at.own_across = 2 * core + 1 - x
    at.own_far = 2 * (1 - core) + 1 - x
    return at


def meet(at):
    bar = pltpu.get_barrier_semaphore()
    always = [at.sib, at.across, at.beside] + at.cube[4:]
    for dev in always:
        pl.semaphore_signal(bar, 1, device_id=dev, device_id_type=MESH)
    for has, dev in ((at.has_lower, at.lower), (at.has_upper, at.upper)):

        @pl.when(has)
        def _():
            pl.semaphore_signal(bar, 1, device_id=dev, device_id_type=MESH)

    ends = jnp.where(at.has_lower, 1, 0) + jnp.where(at.has_upper, 1, 0)
    pl.semaphore_wait(bar, len(always) + ends)


def remote(src, dst, send, recv, dev):
    return pltpu.make_async_remote_copy(
        src_ref=src, dst_ref=dst, send_sem=send, recv_sem=recv, device_id=dev, device_id_type=MESH
    )


def total_copy(at, step, cur, got, send, recv):
    return remote(cur.at[step], got.at[step], send.at[step], recv.at[step], at.cube[step])


def total_end(at, step, cur, got, copy):
    copy.wait()
    cur[step + 1] = cur[step] + got[step]


def start(copy):
    copy.start()


def wait(copy):
    copy.wait()


def wait_send(copy):
    copy.wait_send()


def wait_recv(copy):
    copy.wait_recv()


def by_core(at, p, short, width, act):
    if p != short:
        act(width)
        return
    for core, count in ((0, width), (1, width // 2)):

        @pl.when(at.core == core)
        def _():
            act(count)


class Share:
    def __init__(self, at, buf, rows, sems):
        self.at, self.buf, self.rows, self.sems = at, buf, rows, sems
        self.sub = rows // NSUB

    def part(self, slot, j):
        return self.buf.at[rows_of(slot * self.rows + j * self.sub, self.sub), :]

    def copy(self, slot, j, k, dev):
        part = self.part(slot, j)
        return remote(part, part, self.sems.at[2 * k, j], self.sems.at[2 * k + 1, j], dev)

    def start(self, j):
        self.copy(self.at.own, j, 0, self.at.across).start()
        self.copy(self.at.own, j, 1, self.at.sib).start()

    def forward(self, j):
        self.copy(self.at.own_across, j, 0, self.at.across).wait_recv()
        self.copy(self.at.own_across, j, 2, self.at.sib).start()

    def finish(self):
        for j in range(NSUB):
            self.copy(self.at.own_sib, j, 1, self.at.sib).wait_recv()
            self.copy(self.at.own_far, j, 2, self.at.sib).wait_recv()
            self.copy(self.at.own, j, 0, self.at.across).wait_send()
            self.copy(self.at.own, j, 1, self.at.sib).wait_send()
            self.copy(self.at.own_across, j, 2, self.at.sib).wait_send()


class Sums:
    def __init__(self, at, acc, rows, core_out, core_in, far_in, core_sems, far_sems):
        self.at, self.acc, self.rows = at, acc, rows
        self.core_out, self.core_in, self.far_in = core_out, core_in, far_in
        self.core_sems, self.far_sems = core_sems, far_sems
        self.sub = rows // NSUB

    def of(self, slot, j):
        return self.acc[rows_of(slot * self.rows + j * self.sub, self.sub), :]

    def core_copy(self, k, j):
        part = rows_of(j * self.sub, self.sub)
        return remote(
            self.core_out.at[k, part, :],
            self.core_in.at[k, part, :],
            self.core_sems.at[0, k, j],
            self.core_sems.at[1, k, j],
            self.at.sib,
        )

    def far_copy(self, j):
        part = rows_of(j * self.sub, self.sub)
        return remote(
            self.core_in.at[0, part, :],
            self.far_in.at[part, :],
            self.far_sems.at[0, j],
            self.far_sems.at[1, j],
            self.at.across,
        )

    def to_core(self):
        for k, slot in ((0, self.at.own_far), (1, self.at.own_sib)):
            for j in range(NSUB):
                self.core_out[k, rows_of(j * self.sub, self.sub), :] = self.of(slot, j).astype(bf16)
                self.core_copy(k, j).start()

    def to_far(self):
        for j in range(NSUB):
            part = rows_of(j * self.sub, self.sub)
            self.core_copy(0, j).wait_recv()
            both = self.of(self.at.own_across, j) + self.core_in[0, part, :].astype(f32)
            self.core_in[0, part, :] = both.astype(bf16)
            self.far_copy(j).start()

    def take(self, j):
        part = rows_of(j * self.sub, self.sub)
        self.core_copy(1, j).wait_recv()
        self.far_copy(j).wait_recv()
        return (
            self.of(self.at.own, j)
            + self.core_in[1, part, :].astype(f32)
            + self.far_in[part, :].astype(f32)
        )

    def finish(self):
        for j in range(NSUB):
            self.core_copy(0, j).wait_send()
            self.core_copy(1, j).wait_send()
            self.far_copy(j).wait_send()


def nt(left, right):
    return lax.dot_general(left, right, (((1,), (1,)), ((), ())), preferred_element_type=f32)


def tn(left, right):
    return lax.dot_general(left, right, (((0,), (0,)), ((), ())), preferred_element_type=f32)


def nn(left, right):
    return jnp.dot(left, right, preferred_element_type=f32)


def inverse_of(source):
    return lax.rsqrt(jnp.mean(source * source, axis=1, keepdims=True) + norm_eps)


def shifted(value, by):
    if by == 0:
        return value
    size = value.shape[0]
    row = lax.broadcasted_iota(jnp.int32, value.shape, 0)
    inside = row >= by if by > 0 else row < size + by
    return jnp.where(inside, pltpu.roll(value, by % size, 0), 0.0)


def convolve(mixed, taps):
    return taps[0:1] * shifted(mixed, 2) + taps[1:2] * shifted(mixed, 1) + taps[2:3] * mixed


def ffn_columns(p, pieces, core):
    if p < pieces - 1:
        return [(k * LANES, LANES, 0, k) for k in range(3)]
    half = LANES // 2
    return [((3 * h + k) * half, half, h * half, k) for h in range(2 - core) for k in range(3)]


def ffn_blocks(p, pieces):
    last = isinstance(p, int) and p == pieces - 1
    return [(0, LANES // 2), (3 * LANES // 2, LANES // 2)] if last else [(0, LANES)]


class Gather:
    def __init__(self, at, held, chunk, early_y, sems):
        self.at, self.held, self.chunk, self.early_y = at, held, chunk, early_y
        self.recv, self.own_send, self.send = sems
        self.short = held.shape[0] - 1

    def by_kind(self, p, act):
        kind = self.early_y.get(p)
        if kind != "half":
            act(kind == "both")
            return
        for core in (0, 1):

            @pl.when(self.at.core == core)
            def _():
                act(core == 1)

    def run(self, act, p, chip, count, send, dev):
        def of(width):
            block = self.held.at[p, rows_of(chip * self.chunk, count * self.chunk), pl.ds(0, width)]
            act(remote(block, block, send, self.recv.at[p, chip], dev))

        by_core(self.at, p, self.short, self.held.shape[2], of)

    def arrived(self, p, chip, count=1):
        self.run(wait_recv, p, chip, count, self.own_send.at[0, 0], self.at.beside)

    def own(self, p, act):
        at = self.at
        self.run(act, p, at.chip, 1, self.own_send.at[0, p], at.beside)
        self.by_kind(p, lambda pairs: None if pairs else self.own_z(p, at.chip, 1, act))

    def own_z(self, p, chip, count, act):
        at = self.at

        @pl.when(at.has_upper)
        def _():
            self.run(act, p, chip, count, self.own_send.at[1, p], at.upper)

        @pl.when(at.has_lower)
        def _():
            self.run(act, p, chip, count, self.own_send.at[2, p], at.lower)

    def passing(self, p, pairs, parity, wait, act):
        at = self.at

        def step(s, carry):
            for from_z, goes_on, dev, way in (
                (at.z - 1 - s, at.has_upper, at.upper, 0),
                (at.z + 1 + s, at.has_lower, at.lower, 1),
            ):

                @pl.when(jnp.logical_and(from_z >= 0, from_z < at.depth))
                def _():
                    chip = 2 * from_z if pairs else 2 * from_z + at.y
                    count = 2 if pairs else 1
                    if wait:
                        self.arrived(p, chip, count)

                    @pl.when(goes_on)
                    def _():
                        self.run(act, p, chip, count, self.send.at[way, parity, from_z], dev)

                    if not pairs:
                        self.run(act, p, chip, count, self.send.at[2, parity, from_z], at.beside)

            return carry

        lax.fori_loop(0, at.depth - 1, step, 0)

    def sent(self, p):
        self.by_kind(p, lambda pairs: self.passing(p, pairs, p % AHEAD, False, wait_send))

    def relay(self, p):
        if p >= AHEAD:
            self.sent(p - AHEAD)

        def hand_on(pairs):
            if pairs:
                self.arrived(p, 2 * self.at.z + 1 - self.at.y)
                self.own_z(p, 2 * self.at.z, 2, start)
            self.passing(p, pairs, p % AHEAD, True, start)

        self.by_kind(p, hand_on)

    def whole(self, p):
        def step(z, carry):
            self.arrived(p, 2 * z + 1 - self.at.y)
            return carry

        self.by_kind(p, lambda pairs: None if pairs else lax.fori_loop(0, self.at.depth, step, 0))

    def own_done(self, p):
        self.own(p, wait_send)
        self.by_kind(p, lambda pairs: self.own_z(p, 2 * self.at.z, 2, wait_send) if pairs else None)


def forward_kernel(
    ndp,
    early_y,
    in_weight,
    out_weight,
    gate_weight,
    up_weight,
    down_weight,
    tokens,
    teacher,
    valid,
    mixer_gain,
    ffn_gain,
    conv_weight,
    held_out,
    normed_out,
    normed_two_out,
    grad_rows_out,
    streams_out,
    gates_out,
    first_out,
    block_out,
    grad_out,
    small_out,
    loss_out,
    held,
    landed,
    mine,
    rows_a,
    rows_b,
    acc,
    streams,
    gates,
    core_out,
    core_in,
    far_in,
    first,
    result,
    error_grad,
    cur,
    got,
    chip_sems,
    recv_sems,
    own_sems,
    send_sems,
    share_sems,
    core_sems,
    far_sems,
    cube_sems,
    out_sems,
    held_sems,
    gate_sems,
):
    at = place(ndp)
    pieces, width, piece = held.shape
    part_rows = out_weight.shape[0]
    chunk = 2 * part_rows
    rows = tokens.shape[0]
    sub = rows // NSUB
    channels = streams.shape[1] // 3
    aligned = part_rows % 16 == 0
    gather = Gather(at, held, chunk, early_y, (recv_sems, own_sems, send_sems))
    share_a = Share(at, rows_a, rows, share_sems)
    share_b = Share(at, rows_b, rows, share_sems)
    sums = Sums(at, acc, rows, core_out, core_in, far_in, core_sems, far_sems)

    span = (pieces - 2) * LANES
    assert gate_weight.shape[1] == 2 * span - LANES // 2

    def parts(p, core):
        at_columns = rows_of(core * channels, channels, 128)
        if p == 0:
            return [(in_weight.at[k, :, at_columns], k * channels, channels) for k in range(2)]
        if p == 1:
            return [(in_weight.at[2, :, at_columns], 0, channels), (out_weight.at[:, at_columns], channels, channels)]
        found = []
        for column, count, unit, k in ffn_columns(p, pieces, core):
            at_columns = rows_of(core * span + (p - 2) * LANES + unit, count, 128)
            found.append(((gate_weight, up_weight, down_weight)[k].at[:, at_columns], column, count))
        return found

    def each_part(p, core, act):
        if p < pieces - 1:
            for k, part in enumerate(parts(p, core)):
                act(k, *part)
            return
        for to in (0, 1):

            @pl.when(core == to)
            def _():
                for k, part in enumerate(parts(p, to)):
                    act(k, *part)

    def landing(p, core, column, count, buffer):
        if not aligned:
            return buffer.at[p, :, pl.ds(column, count)]
        rows_there = rows_of(at.chip * chunk + core * part_rows, part_rows)
        return held.at[p, rows_there, pl.ds(column, count)]

    def to_sib(p, act):
        def copy(k, src, column, count):
            dst = landing(p, at.core, column, count, landed)
            act(remote(src, dst, chip_sems.at[0, p, k], chip_sems.at[1, p, k], at.sib))

        each_part(p, 1 - at.core, copy)

    def from_sib(p):
        def copy(k, src, column, count):
            dst = landing(p, 1 - at.core, column, count, landed)
            remote(src, dst, chip_sems.at[0, p, k], chip_sems.at[1, p, k], at.sib).wait_recv()

        each_part(p, at.core, copy)

    def keep(p, act):
        def copy(k, src, column, count):
            dst = landing(p, at.core, column, count, mine)
            act(pltpu.make_async_copy(src, dst, chip_sems.at[2, p, k]))

        each_part(p, at.core, copy)

    def own_block(p):
        keep(p, wait)
        from_sib(p)
        here = rows_of(at.chip * chunk, chunk)
        if not aligned:
            a, b = mine[p].astype(f32), landed[p].astype(f32)
            lower = jnp.where(at.core == 0, a, b)
            upper = jnp.where(at.core == 0, b, a)
            held[p, here, :] = jnp.concatenate([lower, upper], axis=0).astype(bf16)
        gather.own(p, start)

    meet(at)
    to_sib(0, start)
    keep(0, start)

    @pl.when(at.core == 1)
    def _():
        held[pieces - 1, :, piece // 2 :] = jnp.zeros((width, piece - piece // 2), bf16)

    share = mixer_gain.shape[1]
    cur[0] = jnp.zeros(cur.shape[1:], f32)
    cur[0, 0:1, 0:share] = mixer_gain[...].astype(f32)
    cur[0, 1:2, 0:share] = ffn_gain[...].astype(f32)
    cur[0, 2:5, 0:share] = conv_weight[...].astype(f32)
    placed = pltpu.roll(cur[0], (at.d * 2 + at.x) * share, 1)
    line = lax.broadcasted_iota(jnp.int32, placed.shape, 0)
    cur[0] = jnp.where(line < 5, placed, jnp.sum(valid[...]))
    tally = lambda step: total_copy(at, step, cur, got, cube_sems.at[0], cube_sems.at[1])
    tallied = lambda step: total_end(at, step, cur, got, tally(step))
    last = len(at.cube)
    tally(0).start()
    for j in range(NSUB):
        rows_a[rows_of(at.own * rows + j * sub, sub), :] = tokens[pl.ds(j * sub, sub), :]
    own_block(0)
    tallied(0)
    tally(1).start()
    for p in range(1, pieces):
        to_sib(p, start)
        keep(p, start)
    tallied(1)
    for j in range(NSUB):
        share_a.start(j)
    tally(2).start()
    own_block(1)
    tallied(2)
    tally(3).start()
    own_block(2)
    tallied(3)
    if last > 4:
        tally(4).start()
    relay = gather.relay
    relay(0)
    for step in range(4, last):
        tallied(step)
        if step + 1 < last:
            tally(step + 1).start()
    for j in range(NSUB):
        share_a.forward(j)
    small_out[...] = cur[last]
    gain_one, gain_two = cur[last, 0:1, :], cur[last, 1:2, :]
    share_a.finish()

    def norm_rows(i, carry):
        part = rows_of(i * sub, sub)
        source = rows_a[part, :].astype(f32)
        rows_a[part, :] = (source * inverse_of(source) * gain_one).astype(bf16)
        return carry

    lax.fori_loop(0, 4 * NSUB, norm_rows, 0)
    normed_copy = pltpu.make_async_copy(rows_a, normed_out, out_sems.at[0])
    normed_copy.start()

    def save(p):
        return pltpu.make_async_copy(held.at[p], held_out.at[p], held_sems.at[p])

    own_block(3)
    relay(1)
    own_block(4)
    relay(2)
    own_block(5)
    for p in (0, 1):
        gather.whole(p)
        save(p).start()
    lane = at.x * 2 * channels + at.core * channels
    taps = cur[last, 2:5, rows_of(lane, channels, 128)]

    def mix(r, carry):
        part = rows_of(((r + 1 - at.core) % 2) * 2 * rows, 2 * rows)
        both = nn(rows_a[part, :], held[0])
        x_stream = nn(rows_a[part, :], held[1, :, 0:channels])
        streams[part, 0 : 2 * channels] = both
        streams[part, 2 * channels :] = x_stream
        convolved = convolve(both[:, 0:channels] * x_stream, taps)
        gated = (both[:, channels:] * convolved).astype(bf16)
        acc[part, :] = nt(gated, held[1, :, channels:])
        return carry

    lax.fori_loop(0, 2, mix, 0)
    streams_copy = pltpu.make_async_copy(streams, streams_out, out_sems.at[1])
    streams_copy.start()
    sums.to_core()
    own_block(6)
    own_block(7)
    sums.to_far()
    relay(3)
    for p in range(8, pieces):
        own_block(p)
    for j in range(NSUB):
        part = rows_of(j * sub, sub)
        value = tokens[part, :].astype(f32) + sums.take(j)
        first[part, :] = value
        normed_two = (value * inverse_of(value) * gain_two).astype(bf16)
        rows_b[rows_of(at.own * rows + j * sub, sub), :] = normed_two
        share_b.start(j)
    sums.finish()
    first_copy = pltpu.make_async_copy(first, first_out, out_sems.at[2])
    first_copy.start()
    relay(4)
    for j in range(NSUB):
        share_b.forward(j)
    share_b.finish()
    normed_two_copy = pltpu.make_async_copy(rows_b, normed_two_out, out_sems.at[3])
    normed_two_copy.start()
    acc[...] = jnp.zeros_like(acc)

    def gates_copy(p):
        slot = p % 2
        return pltpu.make_async_copy(gates.at[slot], gates_out.at[p - 2], gate_sems.at[slot])

    def some(p, r):
        part = rows_of(((r + 1 - at.core) % 2) * 2 * rows, 2 * rows)
        for column, units in ffn_blocks(p, pieces):
            both = nn(rows_b[part, :], held[p, :, column : column + 2 * units])
            gate, up = both[:, 0:units], both[:, units:]
            kept = 2 * column // 3
            gates[p % 2, part, kept : kept + 2 * units] = both.astype(bf16)
            hidden = (gate * jax.nn.sigmoid(gate) * up).astype(bf16)
            acc[part, :] += nt(hidden, held[p, :, column + 2 * units : column + 3 * units])

    def feed(p, carry):
        for q in range(5, pieces):

            @pl.when(p == q - 3)
            def _():
                relay(q)

        for q in range(2, pieces - 1):

            @pl.when(p == q)
            def _():
                gather.whole(q)

        save(p).start()

        @pl.when(p >= 4)
        def _():
            gates_copy(p - 2).wait()

        def rows_part(r, inner):
            some(p, r)
            return inner

        lax.fori_loop(0, 2, rows_part, 0)
        gates_copy(p).start()
        return carry

    normed_copy.wait()
    lax.fori_loop(2, pieces - 1, feed, 0)
    final = pieces - 1
    gather.whole(final)
    gates_copy(final - 2).wait()
    some(final, 0)
    sums.to_core()
    some(final, 1)
    sums.to_far()
    save(final).start()
    gates_copy(final).start()
    scale = 1.0 / (width * cur[last, 5:6, 0:1])
    loss = jnp.zeros((1, width), f32)
    for j in range(NSUB):
        part = rows_of(j * sub, sub)
        value = first[part, :] + sums.take(j)
        result[part, :] = value
        error = value - teacher[part, :].astype(f32)
        weighted = valid[part, :] * error
        loss = loss + jnp.sum(weighted * error, axis=0, keepdims=True)
        grad = (2.0 * scale) * weighted
        error_grad[part, :] = grad
        rows_a[rows_of(at.own * rows + j * sub, sub), :] = grad.astype(bf16)
        share_a.start(j)
    loss_out[...] = jnp.broadcast_to(jnp.sum(loss, axis=1, keepdims=True), loss_out.shape)
    sums.finish()
    result_copy = pltpu.make_async_copy(result, block_out, out_sems.at[4])
    result_copy.start()
    grad_copy = pltpu.make_async_copy(error_grad, grad_out, out_sems.at[5])
    grad_copy.start()
    for j in range(NSUB):
        share_a.forward(j)
    share_a.finish()
    rows_copy = pltpu.make_async_copy(rows_a, grad_rows_out, out_sems.at[6])
    rows_copy.start()
    for p in range(pieces):
        save(p).wait()
        to_sib(p, wait_send)
        gather.own_done(p)
    for p in range(pieces - AHEAD, pieces):
        gather.sent(p)
    for p in (pieces - 2, pieces - 1):
        gates_copy(p).wait()
    for copy in (streams_copy, first_copy, normed_two_copy, result_copy, grad_copy, rows_copy):
        copy.wait()


def forward(ndp, weights, tokens, teacher, valid, vectors):
    part_rows, channels = weights[1].shape
    channels //= 2
    piece = 2 * channels
    pieces = 2 - (-weights[2].shape[1] // (2 * LANES))
    rows, width = tokens.shape
    cube = small_steps(ndp)
    early_y = {3: "both", 6: "half"}
    dma = pltpu.SemaphoreType.DMA
    landing = (pieces, part_rows, piece) if part_rows % 16 else (1, 16, 128)
    shape = jax.ShapeDtypeStruct
    outs = (
        shape((pieces, width, piece), bf16),
        shape((4 * rows, width), bf16),
        shape((4 * rows, width), bf16),
        shape((4 * rows, width), bf16),
        shape((4 * rows, 3 * channels), f32),
        shape((pieces - 2, 4 * rows, 2 * LANES), bf16),
        shape((rows, width), f32),
        shape((rows, width), f32),
        shape((rows, width), f32),
        shape((8, width), f32),
        shape((8, 128), f32),
    )
    scratch = [
        pltpu.VMEM((pieces, width, piece), bf16),
        pltpu.VMEM(landing, bf16),
        pltpu.VMEM(landing, bf16),
        pltpu.VMEM((4 * rows, width), bf16),
        pltpu.VMEM((4 * rows, width), bf16),
        pltpu.VMEM((4 * rows, width), f32),
        pltpu.VMEM((4 * rows, 3 * channels), f32),
        pltpu.VMEM((2, 4 * rows, 2 * LANES), bf16),
        pltpu.VMEM((2, rows, width), bf16),
        pltpu.VMEM((2, rows, width), bf16),
        pltpu.VMEM((rows, width), bf16),
        pltpu.VMEM((rows, width), f32),
        pltpu.VMEM((rows, width), f32),
        pltpu.VMEM((rows, width), f32),
        pltpu.VMEM((cube + 1, 8, width), f32),
        pltpu.VMEM((cube, 8, width), f32),
        dma((3, pieces, 6)),
        dma((pieces, ndp // 2)),
        dma((3, pieces)),
        dma((3, AHEAD, ndp // 4)),
        dma((6, NSUB)),
        dma((2, 2, NSUB)),
        dma((2, NSUB)),
        dma((2, cube)),
        dma((7,)),
        dma((pieces,)),
        dma((2,)),
    ]
    return pl.pallas_call(
        functools.partial(forward_kernel, ndp, early_y),
        out_shape=outs,
        in_specs=[ANY] * 5 + [VMEM] * 6,
        out_specs=[ANY] * 9 + [VMEM] * 2,
        scratch_shapes=scratch,
        compiler_params=pltpu.CompilerParams(
            collective_id=0, has_side_effects=True, vmem_limit_bytes=63 << 20
        ),
    )(*weights, tokens, teacher, valid, *vectors)


def small_steps(ndp):
    return 3 + (ndp // 4 - 1).bit_length()


class Scatter:
    def __init__(self, at, held, chunk, count, beside_in, line_in, pair_in, pair_beside, total, sems, credits):
        self.at, self.held, self.chunk, self.count = at, held, chunk, count
        self.beside_in, self.line_in, self.pair_in, self.pair_beside = beside_in, line_in, pair_in, pair_beside
        self.total, self.credits = total, credits
        self.beside_sems, self.line_sems, self.pair_sems, self.pair_y_sems = sems
        self.short, self.width = held.shape[0] - 1, held.shape[2]
        self.ydepth, self.zdepth = beside_in.shape[0], line_in.shape[0]

    def block(self, p, chip, count=1, width=None):
        here = rows_of(chip * self.chunk, count * self.chunk)
        return self.held.at[p, here, pl.ds(0, width or self.width)]

    def run(self, act, copy, p, *rest):
        by_core(self.at, p, self.short, self.width, lambda width: act(copy(p, *rest, width)))

    def beside_copy(self, p, m, z, width):
        slot = m % self.ydepth
        return remote(
            self.block(p, 2 * z + 1 - self.at.y, 1, width),
            self.beside_in.at[slot, z, :, pl.ds(0, width)],
            self.beside_sems.at[0, slot, z],
            self.beside_sems.at[1, slot, z],
            self.at.beside,
        )

    def line_copy(self, p, m, z, up, width):
        slot, way = m % self.zdepth, 0 if up else 1
        into = z + 1 if up else z
        return remote(
            self.block(p, 2 * z + self.at.y, 1, width),
            self.line_in.at[slot, into, :, pl.ds(0, width)],
            self.line_sems.at[way, slot, z],
            self.line_sems.at[2, slot, into],
            self.at.upper if up else self.at.lower,
        )

    def pair_copy(self, p, z, up):
        into = z + 1 if up else z
        return remote(
            self.block(p, 2 * z, 2),
            self.pair_in.at[into],
            self.pair_sems.at[0 if up else 1, z],
            self.pair_sems.at[2, into],
            self.at.upper if up else self.at.lower,
        )

    def turn(self, s):
        z, last = self.at.z, self.at.depth - 1
        low = jnp.where(z < self.at.depth // 2, 1, 0)
        down, up = last - s, s
        other = low * (down - jnp.where(down <= z, 1, 0)) + (1 - low) * (up + jnp.where(up >= z, 1, 0))
        mine = jnp.where(s == last, 1, 0)
        return mine * z + (1 - mine) * other

    def free_beside(self, p, m, before):
        if m >= self.ydepth:
            pl.semaphore_wait(self.credits.at[0], 1)
            self.drop_beside(before, m)

    def drop_beside(self, p, m):
        def step(z, carry):
            self.run(wait_send, self.beside_copy, p, m, z)
            return carry

        lax.fori_loop(0, self.at.depth, step, 0)

    def send_beside(self, p, m, before):
        self.free_beside(p, m, before)

        def step(s, carry):
            self.run(start, self.beside_copy, p, m, self.turn(s))
            return carry

        lax.fori_loop(0, self.at.depth, step, 0)

    def ways(self, has, act):
        at = self.at

        def step(s, carry):
            for z, wanted, up in (
                (at.depth - 1 - s, at.depth - 1 - s > at.z, True),
                (s, s < at.z, False),
            ):

                @pl.when(jnp.logical_and(wanted, has(up)))
                def _():
                    act(z, up)

            return carry

        lax.fori_loop(0, at.depth - 1, step, 0)

    def behind(self, up):
        return self.at.has_lower if up else self.at.has_upper

    def opens(self, up):
        return jnp.logical_not(self.behind(up))

    def near(self, up):
        low = self.at.z < self.at.depth // 2
        return jnp.logical_and(self.behind(up), low if up else jnp.logical_not(low))

    def far(self, up):
        low = self.at.z < self.at.depth // 2
        return jnp.logical_and(self.behind(up), jnp.logical_not(low) if up else low)

    def add_beside(self, p, m, before, onward):
        at = self.at
        if m >= self.zdepth:
            for has, credit in ((at.has_upper, 1), (at.has_lower, 2)):

                @pl.when(has)
                def _():
                    pl.semaphore_wait(self.credits.at[credit], 1)

            self.drop(before, m)

        def step(s, carry):
            z = self.turn(s)
            own = self.block(p, 2 * z + at.y)
            self.run(wait_recv, self.beside_copy, p, m, z)
            own[...] = (own[...].astype(f32) + self.beside_in[m % self.ydepth, z].astype(f32)).astype(bf16)
            for up in (True, False):

                @pl.when(jnp.logical_and(z > at.z if up else z < at.z, self.opens(up)))
                def _():
                    self.run(start, self.line_copy, p, m, z, up)

                if onward:

                    @pl.when(jnp.logical_and(z > at.z if up else z < at.z, self.behind(up)))
                    def _():
                        self.pass_on(p, m, z, up)

            return carry

        lax.fori_loop(0, at.depth, step, 0)
        if m + self.ydepth < self.count:
            pl.semaphore_signal(self.credits.at[0], 1, device_id=at.beside, device_id_type=MESH)

    def pass_on(self, p, m, z, up):
        self.run(wait_recv, self.line_copy, p, m, z, up)
        own = self.block(p, 2 * z + self.at.y)
        came = self.line_in[m % self.zdepth, z + 1 if up else z].astype(f32)
        own[...] = (own[...].astype(f32) + came).astype(bf16)
        self.run(start, self.line_copy, p, m, z, up)

    def hop(self, p, m, has):
        self.ways(has, functools.partial(self.pass_on, p, m))

    def collect(self, p, m, slot):
        at = self.at
        total = self.total.at[slot]
        total[...] = self.block(p, 2 * at.z + at.y)[...].astype(f32)
        for up in (True, False):

            @pl.when(self.behind(up))
            def _():
                self.run(wait_recv, self.line_copy, p, m, at.z, up)
                total[...] += self.line_in[m % self.zdepth, at.z + 1 if up else at.z].astype(f32)
                if m + self.zdepth < self.count:
                    pl.semaphore_signal(
                        self.credits.at[1 if up else 2],
                        1,
                        device_id=at.lower if up else at.upper,
                        device_id_type=MESH,
                    )

    def drop(self, p, m):
        self.ways(lambda up: True, lambda z, up: self.run(wait_send, self.line_copy, p, m, z, up))

    def pairs_open(self, p):
        self.ways(self.opens, lambda z, up: self.pair_copy(p, z, up).start())

    def pair_hop(self, p, has):
        def act(z, up):
            self.pair_copy(p, z, up).wait_recv()
            own = self.block(p, 2 * z, 2)
            own[...] = (own[...].astype(f32) + self.pair_in[z + 1 if up else z].astype(f32)).astype(bf16)
            self.pair_copy(p, z, up).start()

        self.ways(has, act)

    def pair_y_copy(self, p):
        at = self.at
        return remote(
            self.block(p, 2 * at.z + 1 - at.y),
            self.pair_beside,
            self.pair_y_sems.at[0],
            self.pair_y_sems.at[1],
            at.beside,
        )

    def pairs_cross(self, p):
        at = self.at
        own = self.block(p, 2 * at.z, 2)
        for up in (True, False):

            @pl.when(self.behind(up))
            def _():
                self.pair_copy(p, at.z, up).wait_recv()
                came = self.pair_in[at.z + 1 if up else at.z].astype(f32)
                own[...] = (own[...].astype(f32) + came).astype(bf16)

        self.pair_y_copy(p).start()

    def pairs_close(self, p, slot):
        at = self.at
        self.pair_y_copy(p).wait()
        mine = self.block(p, 2 * at.z + at.y)[...].astype(f32)
        self.total[slot] = mine + self.pair_beside[...].astype(f32)
        self.ways(lambda up: True, lambda z, up: self.pair_copy(p, z, up).wait_send())


def backward_kernel(
    ndp,
    held_in,
    normed_in,
    normed_two_in,
    grad_rows_in,
    streams_in,
    gates_in,
    first_in,
    grad_in,
    small,
    loss,
    tokens,
    streams_grad,
    out_grad,
    gate_grad,
    up_grad,
    down_grad,
    tokens_grad,
    mixer_gain_grad,
    ffn_gain_grad,
    conv_grad,
    loss_out,
    held,
    rows_a,
    rows_b,
    acc,
    gates,
    streams,
    core_out,
    core_in,
    far_in,
    first,
    grad,
    back,
    beside_in,
    line_in,
    pair_in,
    pair_beside,
    total,
    cur,
    got,
    share_sems,
    core_sems,
    far_sems,
    cube_sems,
    load_sems,
    held_sems,
    gate_sems,
    beside_sems,
    line_sems,
    pair_sems,
    pair_y_sems,
    done_sems,
    credits,
):
    at = place(ndp)
    pieces, width, piece = held.shape
    rows = tokens.shape[0]
    sub = rows // NSUB
    chunk = 2 * width // ndp
    half = chunk // 2
    channels = piece // 2
    order = [2] + list(range(4, pieces)) + [0, 1]
    paired = 3
    share = Share(at, rows_a, rows, share_sems)
    sums = Sums(at, acc, rows, core_out, core_in, far_in, core_sems, far_sems)
    scatter = Scatter(
        at,
        held,
        chunk,
        len(order),
        beside_in,
        line_in,
        pair_in,
        pair_beside,
        total,
        (beside_sems, line_sems, pair_sems, pair_y_sems),
        credits,
    )

    def load(src, dst, k):
        return pltpu.make_async_copy(src, dst, load_sems.at[k])

    def load_held(p):
        return pltpu.make_async_copy(held_in.at[p], held.at[p], held_sems.at[p])

    def load_gates(p):
        return pltpu.make_async_copy(gates_in.at[p - 2], gates.at[p % 2], gate_sems.at[p % 2])

    def load_streams(r):
        return load(streams_in.at[pl.ds(r * 2 * rows, 2 * rows), :], streams, 5)

    opening = (
        load(grad_rows_in, rows_a, 0),
        load_gates(2),
        load_held(2),
        load(normed_two_in, rows_b, 1),
    )
    for copy in opening:
        copy.start()
    load_gates(3).start()
    for p in list(range(3, pieces)) + [0, 1]:
        load_held(p).start()
    load_first, load_grad = load(first_in, first, 2), load(grad_in, grad, 3)
    load_first.start()
    load_grad.start()
    load_streams(0).start()
    meet(at)
    acc[...] = jnp.zeros_like(acc)
    opening[0].wait()

    def ffn(p, m=None):
        load_gates(p).wait()
        load_held(p).wait()

        def some(r, carry):
            part = rows_of(((r + 1 - at.core) % 2) * 2 * rows, 2 * rows)
            for column, units in ffn_blocks(p, pieces):
                ends = [column + k * units for k in range(4)]
                grad_hidden = nn(rows_a[part, :], held[p, :, ends[2] : ends[3]])
                kept = 2 * column // 3
                gate = gates[p % 2, part, kept : kept + units].astype(f32)
                up = gates[p % 2, part, kept + units : kept + 2 * units].astype(f32)
                sig = jax.nn.sigmoid(gate)
                active = gate * sig
                back[part, ends[2] : ends[3]] = (active * up).astype(bf16)
                grad_gate = grad_hidden * up * sig * (1.0 + gate * (1.0 - sig))
                back[part, ends[0] : ends[1]] = grad_gate.astype(bf16)
                back[part, ends[1] : ends[2]] = (grad_hidden * active).astype(bf16)
                acc[part, :] += nt(back[part, ends[0] : ends[2]], held[p, :, ends[0] : ends[2]])
            return carry

        lax.fori_loop(0, 2, some, 0)

        if p == 2:
            opening[3].wait()
        blocks = 2 * width // piece
        matched = blocks == at.depth

        def weights(s, carry):
            i = scatter.turn(s) if matched else s
            part = rows_of(i * (piece // 2), piece // 2, 128)
            for column, units in ffn_blocks(p, pieces):
                ends = [column + k * units for k in range(4)]
                held[p, part, ends[0] : ends[2]] = tn(rows_b[:, part], back[:, ends[0] : ends[2]]).astype(bf16)
                held[p, part, ends[2] : ends[3]] = tn(rows_a[:, part], back[:, ends[2] : ends[3]]).astype(bf16)
            if m is not None and matched:
                scatter.run(start, scatter.beside_copy, p, m, i)
            return carry

        lax.fori_loop(0, blocks, weights, 0)
        if m is not None and not matched:
            scatter.send_beside(p, m, None)
        if p + 2 < pieces:
            load_gates(p + 2).start()

    given = []

    span = (pieces - 2) * LANES

    def parts(p, core):
        at_columns = rows_of(core * channels, channels, 128)
        if p == 0:
            return [(k * channels, channels, streams_grad.at[k, :, at_columns]) for k in range(2)]
        if p == 1:
            return [
                (0, channels, streams_grad.at[2, :, at_columns]),
                (channels, channels, out_grad.at[:, at_columns]),
            ]
        found = []
        for column, count, unit, k in ffn_columns(p, pieces, core):
            at_columns = rows_of(core * span + (p - 2) * LANES + unit, count, 128)
            found.append((column, count, (gate_grad, up_grad, down_grad)[k].at[:, at_columns]))
        return found

    def each_part(p, core, act):
        if p < pieces - 1:
            for k, part in enumerate(parts(p, core)):
                act(k, *part)
            return
        for to in (0, 1):

            @pl.when(core == to)
            def _():
                for k, part in enumerate(parts(p, to)):
                    act(k, *part)

    def piece_rows(p, core, first_column, count):
        slot = given.index(p) % 2 if p in given else 0
        return total.at[slot, rows_of(core * half, half, 8), pl.ds(first_column, count)]

    def out_local(p, act):
        def copy(k, first_column, count, dst):
            src = piece_rows(p, at.core, first_column, count)
            act(pltpu.make_async_copy(src, dst, done_sems.at[0, p, k]))

        each_part(p, at.core, copy)

    def out_sib(p, core, act):
        def copy(k, first_column, count, dst):
            src = piece_rows(p, 1 - at.core, first_column, count)
            act(remote(src, dst, done_sems.at[1, p, k], done_sems.at[2, p, k], at.sib))

        each_part(p, core, copy)

    def give(p, fill):
        if len(given) > 1:
            out_local(given[-2], wait)
            out_sib(given[-2], at.core, wait_send)
        given.append(p)
        fill((len(given) - 1) % 2)
        out_local(p, start)
        out_sib(p, at.core, start)

    def beside(m):
        scatter.send_beside(order[m], m, order[m - YDEPTH] if m >= YDEPTH else None)

    def finish(m):
        give(order[m], functools.partial(scatter.collect, order[m], m))

    def advance(m):
        onward = m == len(order) - 1
        if onward:
            scatter.hop(order[m - 1], m - 1, scatter.far)
            finish(m - 2)
        scatter.add_beside(order[m], m, order[m - ZDEPTH] if m >= ZDEPTH else None, onward)
        if onward:
            return
        scatter.hop(order[m], m, scatter.near)
        if m == 0:
            scatter.pair_hop(paired, scatter.near)
        if m >= 1:
            scatter.hop(order[m - 1], m - 1, scatter.far)
        if m == 2:
            scatter.pair_hop(paired, scatter.far)
        if m >= 2:
            finish(m - 2)
        if m == 3:
            scatter.pairs_cross(paired)
        if m == 4:
            give(paired, functools.partial(scatter.pairs_close, paired))

    gain_one, gain_two = small[0:1, :], small[1:2, :]
    ffn(2, 0)
    ffn(3)
    scatter.pairs_open(paired)
    ffn(4, 1)
    ffn(5, 2)
    advance(0)
    ffn(6)
    beside(3)
    for p in range(7, pieces):
        ffn(p)
    sums.to_core()
    load_normed = load(normed_in, rows_b, 4)
    load_normed.start()
    advance(1)
    beside(4)
    sums.to_far()
    load_first.wait()
    load_grad.wait()
    gain_two_grad = jnp.zeros((1, width), f32)
    for j in range(NSUB):
        part = rows_of(j * sub, sub)
        coming = sums.take(j)
        source = first[part, :]
        inverse = inverse_of(source)
        weighted = coming * gain_two
        inner = jnp.mean(weighted * source, axis=1, keepdims=True)
        value = grad[part, :] + inverse * weighted - source * (inverse * inverse * inverse * inner)
        grad[part, :] = value
        gain_two_grad += jnp.sum(coming * source * inverse, axis=0, keepdims=True)
        rows_a[rows_of(at.own * rows + j * sub, sub), :] = value.astype(bf16)
        share.start(j)
    sums.finish()
    advance(2)
    beside(5)
    for j in range(NSUB):
        share.forward(j)
    share.finish()
    shift = at.x * 2 * channels + at.core * channels
    cur[0] = jnp.zeros(cur.shape[1:], f32)
    cur[0, 1:2, :] = gain_two_grad
    cur[0, 5:6, :] = jnp.broadcast_to(loss[0:1, 0:1], (1, width))
    load_held(0).wait()
    load_held(1).wait()
    for r in range(2):
        load_streams(r).wait()
        part = pl.ds(r * 2 * rows, 2 * rows)
        acc[part, 0:channels] = nn(rows_a[part, :], held[1, :, channels:])

        def mix(q, carry):
            lanes = [rows_of(k * channels + q * 128, 128, 128) for k in range(3)]
            b_gate, c_gate, x_stream = (streams[:, lane] for lane in lanes)
            tap = small[2:5, rows_of(shift + q * 128, 128, 128)]
            mixed = b_gate * x_stream
            convolved = convolve(mixed, tap)
            grad_gated = acc[part, lanes[0]]
            gates[0, part, lanes[0]] = (c_gate * convolved).astype(bf16)
            back[part, lanes[1]] = (grad_gated * convolved).astype(bf16)
            grad_conv = grad_gated * c_gate
            grad_mixed = tap[2:3] * grad_conv
            grad_mixed += tap[1:2] * shifted(grad_conv, -1) + tap[0:1] * shifted(grad_conv, -2)
            for k in range(3):
                term = jnp.sum(grad_conv * shifted(mixed, 2 - k), axis=0, keepdims=True)
                cur[0, 2 + k : 3 + k, rows_of(shift + q * 128, 128, 128)] += term
            back[part, lanes[0]] = (grad_mixed * x_stream).astype(bf16)
            back[part, lanes[2]] = (grad_mixed * b_gate).astype(bf16)
            return carry

        lax.fori_loop(0, channels // 128, mix, 0)
        if r == 0:
            load_streams(1).start()
        acc[part, :] = nt(back[part, 0 : 2 * channels], held[0])
        acc[part, :] += nt(back[part, 2 * channels :], held[1, :, 0:channels])
    sums.to_core()
    load_normed.wait()

    def mixer_weights(i, carry):
        part = rows_of(i * channels, channels, 128)
        left = rows_b[:, part]
        held[0, part, :] = tn(left, back[:, 0 : 2 * channels]).astype(bf16)
        held[1, part, 0:channels] = tn(left, back[:, 2 * channels :]).astype(bf16)
        held[1, part, channels:] = tn(rows_a[:, part], gates[0, :, 0:channels]).astype(bf16)
        return carry

    lax.fori_loop(0, width // channels, mixer_weights, 0)
    advance(3)
    beside(6)
    sums.to_far()
    advance(4)
    gain_one_grad = jnp.zeros((1, width), f32)
    for j in range(NSUB):
        part = rows_of(j * sub, sub)
        coming = sums.take(j)
        source = tokens[part, :].astype(f32)
        inverse = inverse_of(source)
        weighted = coming * gain_one
        inner = jnp.mean(weighted * source, axis=1, keepdims=True)
        grad[part, :] += inverse * weighted - source * (inverse * inverse * inverse * inner)
        gain_one_grad += jnp.sum(coming * source * inverse, axis=0, keepdims=True)
    sums.finish()
    tokens_copy = load(grad, tokens_grad, 6)
    tokens_copy.start()
    cur[0, 0:1, :] = gain_one_grad
    tally = lambda step: total_copy(at, step, cur, got, cube_sems.at[0], cube_sems.at[1])
    for step in range(2):
        tally(step).start()
        total_end(at, step, cur, got, tally(step))
    tally(2).start()
    beside(7)
    steps = len(at.cube)
    count = len(order)
    advance(5)
    advance(6)
    total_end(at, 2, cur, got, tally(2))
    tally(3).start()
    advance(7)
    for step in range(3, steps):
        total_end(at, step, cur, got, tally(step))
        if step + 1 < steps:
            tally(step + 1).start()
        if step == 3:
            finish(count - 2)
    finish(count - 1)
    share_lanes = mixer_gain_grad.shape[1]
    own = pltpu.roll(cur[steps], (width - (at.d * 2 + at.x) * share_lanes) % width, 1)
    mixer_gain_grad[...] = own[0:1, 0:share_lanes]
    ffn_gain_grad[...] = own[1:2, 0:share_lanes]
    conv_grad[...] = own[2:5, 0:share_lanes]
    loss_out[...] = cur[steps, 5:6, 0:1] / (width * small[5:6, 0:1])
    for m in range(count - YDEPTH, count):
        scatter.drop_beside(order[m], m)
    for m in range(count - ZDEPTH, count):
        scatter.drop(order[m], m)
    for p in given[-2:]:
        out_local(p, wait)
        out_sib(p, at.core, wait_send)
    for p in given:
        out_sib(p, 1 - at.core, wait_recv)
    tokens_copy.wait()


def backward(ndp, units, held, normed, normed_two, grad_rows, streams, gates, first, grad, small, loss, tokens):
    pieces, width, piece = held.shape
    rows = tokens.shape[0]
    chunk = 2 * width // ndp
    depth = ndp // 4
    channels = piece // 2
    cube = small_steps(ndp)
    dma = pltpu.SemaphoreType.DMA
    shape = jax.ShapeDtypeStruct
    outs = (
        shape((3, chunk // 2, 2 * channels), f32),
        shape((chunk // 2, 2 * channels), f32),
        shape((chunk // 2, units), f32),
        shape((chunk // 2, units), f32),
        shape((chunk // 2, units), f32),
        shape((rows, width), f32),
        shape((1, width // (2 * ndp)), f32),
        shape((1, width // (2 * ndp)), f32),
        shape((3, width // (2 * ndp)), f32),
        shape((1, 1), f32),
    )
    scratch = [
        pltpu.VMEM((pieces, width, piece), bf16),
        pltpu.VMEM((4 * rows, width), bf16),
        pltpu.VMEM((4 * rows, width), bf16),
        pltpu.VMEM((4 * rows, width), f32),
        pltpu.VMEM((2, 4 * rows, 2 * LANES), bf16),
        pltpu.VMEM((2 * rows, 3 * channels), f32),
        pltpu.VMEM((2, rows, width), bf16),
        pltpu.VMEM((2, rows, width), bf16),
        pltpu.VMEM((rows, width), bf16),
        pltpu.VMEM((rows, width), f32),
        pltpu.VMEM((rows, width), f32),
        pltpu.VMEM((4 * rows, 3 * channels), bf16),
        pltpu.VMEM((YDEPTH, depth, chunk, piece), bf16),
        pltpu.VMEM((ZDEPTH, depth + 1, chunk, piece), bf16),
        pltpu.VMEM((depth + 1, 2 * chunk, piece), bf16),
        pltpu.VMEM((chunk, piece), bf16),
        pltpu.VMEM((2, chunk, piece), f32),
        pltpu.VMEM((cube + 1, 8, width), f32),
        pltpu.VMEM((cube, 8, width), f32),
        dma((6, NSUB)),
        dma((2, 2, NSUB)),
        dma((2, NSUB)),
        dma((2, cube)),
        dma((7,)),
        dma((pieces,)),
        dma((2,)),
        dma((2, YDEPTH, depth)),
        dma((3, ZDEPTH, depth + 1)),
        dma((3, depth + 1)),
        dma((2,)),
        dma((3, pieces, 6)),
        pltpu.SemaphoreType.REGULAR((3,)),
    ]
    return pl.pallas_call(
        functools.partial(backward_kernel, ndp),
        out_shape=outs,
        in_specs=[ANY] * 8 + [VMEM] * 3,
        out_specs=[ANY] * 6 + [VMEM] * 4,
        scratch_shapes=scratch,
        compiler_params=pltpu.CompilerParams(
            collective_id=1, has_side_effects=True, vmem_limit_bytes=127 << 19
        ),
    )(held, normed, normed_two, grad_rows, streams, gates, first, grad, small, loss, tokens)


def body(
    tokens,
    teacher,
    valid,
    mixer_gain,
    in_weight,
    conv_weight,
    out_weight,
    ffn_gain,
    gate_weight,
    up_weight,
    down_weight,
):
    ndp = lax.axis_size("dp")
    held, normed, normed_two, grad_rows, streams, gates, first, block_out, grad, small, loss = forward(
        ndp,
        (in_weight.transpose(1, 0, 2), out_weight, gate_weight, up_weight, down_weight),
        tokens,
        teacher,
        valid.astype(f32)[:, None],
        (mixer_gain[None], ffn_gain[None], conv_weight),
    )
    streams_grad, out_grad, gate_grad, up_grad, down_grad, tokens_grad, *small_grads = backward(
        ndp,
        gate_weight.shape[1],
        held,
        normed,
        normed_two,
        grad_rows,
        streams,
        gates,
        first,
        grad,
        small,
        loss,
        tokens,
    )
    mixer_gain_grad, ffn_gain_grad, conv_grad, loss = small_grads
    return (
        loss[0, 0],
        block_out,
        tokens_grad,
        mixer_gain_grad[0],
        streams_grad.transpose(1, 0, 2),
        conv_grad,
        out_grad,
        ffn_gain_grad[0],
        gate_grad,
        up_grad,
        down_grad,
    )


def solution(mesh):
    rows = P(("dp", "tensor"), None)
    vector = P(("dp", "tensor"))
    weight = P("dp", "tensor")
    streams = P("dp", None, "tensor")
    taps = P(None, ("dp", "tensor"))
    return jax.shard_map(
        body,
        mesh=mesh,
        in_specs=(rows, rows, vector, vector, streams, taps, weight, vector, weight, weight, weight),
        out_specs=(P(), rows, rows, vector, streams, taps, weight, vector, weight, weight, weight),
        check_vma=False,
    )
```

```python
import functools
from types import SimpleNamespace

import jax
import jax.numpy as jnp
from jax import lax
from jax.experimental import pallas as pl
from jax.experimental.pallas import tpu as pltpu
from jax.sharding import PartitionSpec as P

MESH = pl.DeviceIdType.MESH
f32 = jnp.float32
bf16 = jnp.bfloat16
norm_eps = 1e-05
LANES = 256
NSUB = 3
YDEPTH, ZDEPTH = 3, 4
AHEAD = 4
VMEM = pl.BlockSpec(memory_space=pltpu.VMEM)
ANY = pl.BlockSpec(memory_space=pl.ANY)


def rows_of(start, size, step=16):
    return pl.ds(pl.multiple_of(start, step), size)


def place(ndp):
    d, x = lax.axis_index("dp"), lax.axis_index("tensor")
    core, y, z = d % 2, (d // 2) % 2, d // 4
    depth = ndp // 4
    at = SimpleNamespace(d=d, x=x, core=core, y=y, z=z, depth=depth, chip=d // 2)
    at.sib = (d + 1 - 2 * core, x)
    at.across = (d, 1 - x)
    at.beside = (d + 2 - 4 * y, x)
    at.lower, at.upper = (d - 4, x), (d + 4, x)
    at.has_lower, at.has_upper = z > 0, z < depth - 1
    at.cube = [at.sib, at.across, at.beside]
    step = 1
    while step < depth:
        at.cube.append((d + 4 * step * (1 - 2 * ((z // step) % 2)), x))
        step *= 2
    at.own = 2 * core + x
    at.own_sib = 2 * (1 - core) + x
    at.own_across = 2 * core + 1 - x
    at.own_far = 2 * (1 - core) + 1 - x
    return at


def meet(at):
    bar = pltpu.get_barrier_semaphore()
    always = [at.sib, at.across, at.beside] + at.cube[4:]
    for dev in always:
        pl.semaphore_signal(bar, 1, device_id=dev, device_id_type=MESH)
    for has, dev in ((at.has_lower, at.lower), (at.has_upper, at.upper)):

        @pl.when(has)
        def _():
            pl.semaphore_signal(bar, 1, device_id=dev, device_id_type=MESH)

    ends = jnp.where(at.has_lower, 1, 0) + jnp.where(at.has_upper, 1, 0)
    pl.semaphore_wait(bar, len(always) + ends)


def remote(src, dst, send, recv, dev):
    return pltpu.make_async_remote_copy(
        src_ref=src, dst_ref=dst, send_sem=send, recv_sem=recv, device_id=dev, device_id_type=MESH
    )


def total_copy(at, step, cur, got, send, recv):
    return remote(cur.at[step], got.at[step], send.at[step], recv.at[step], at.cube[step])


def total_end(at, step, cur, got, copy):
    copy.wait()
    cur[step + 1] = cur[step] + got[step]


def start(copy):
    copy.start()


def wait(copy):
    copy.wait()


def wait_send(copy):
    copy.wait_send()


def wait_recv(copy):
    copy.wait_recv()


def by_core(at, p, short, width, act):
    if p != short:
        act(width)
        return
    for core, count in ((0, width), (1, width // 2)):

        @pl.when(at.core == core)
        def _():
            act(count)


class Share:
    def __init__(self, at, buf, rows, sems):
        self.at, self.buf, self.rows, self.sems = at, buf, rows, sems
        self.sub = rows // NSUB

    def part(self, slot, j):
        return self.buf.at[rows_of(slot * self.rows + j * self.sub, self.sub), :]

    def copy(self, slot, j, k, dev):
        part = self.part(slot, j)
        return remote(part, part, self.sems.at[2 * k, j], self.sems.at[2 * k + 1, j], dev)

    def start(self, j):
        self.copy(self.at.own, j, 0, self.at.across).start()
        self.copy(self.at.own, j, 1, self.at.sib).start()

    def forward(self, j):
        self.copy(self.at.own_across, j, 0, self.at.across).wait_recv()
        self.copy(self.at.own_across, j, 2, self.at.sib).start()

    def finish(self):
        for j in range(NSUB):
            self.copy(self.at.own_sib, j, 1, self.at.sib).wait_recv()
            self.copy(self.at.own_far, j, 2, self.at.sib).wait_recv()
            self.copy(self.at.own, j, 0, self.at.across).wait_send()
            self.copy(self.at.own, j, 1, self.at.sib).wait_send()
            self.copy(self.at.own_across, j, 2, self.at.sib).wait_send()


class Sums:
    def __init__(self, at, acc, rows, core_out, core_in, far_in, core_sems, far_sems):
        self.at, self.acc, self.rows = at, acc, rows
        self.core_out, self.core_in, self.far_in = core_out, core_in, far_in
        self.core_sems, self.far_sems = core_sems, far_sems
        self.sub = rows // NSUB

    def of(self, slot, j):
        return self.acc[rows_of(slot * self.rows + j * self.sub, self.sub), :]

    def core_copy(self, k, j):
        part = rows_of(j * self.sub, self.sub)
        return remote(
            self.core_out.at[k, part, :],
            self.core_in.at[k, part, :],
            self.core_sems.at[0, k, j],
            self.core_sems.at[1, k, j],
            self.at.sib,
        )

    def far_copy(self, j):
        part = rows_of(j * self.sub, self.sub)
        return remote(
            self.core_in.at[0, part, :],
            self.far_in.at[part, :],
            self.far_sems.at[0, j],
            self.far_sems.at[1, j],
            self.at.across,
        )

    def to_core(self):
        for k, slot in ((0, self.at.own_far), (1, self.at.own_sib)):
            for j in range(NSUB):
                self.core_out[k, rows_of(j * self.sub, self.sub), :] = self.of(slot, j).astype(bf16)
                self.core_copy(k, j).start()

    def to_far(self):
        for j in range(NSUB):
            part = rows_of(j * self.sub, self.sub)
            self.core_copy(0, j).wait_recv()
            both = self.of(self.at.own_across, j) + self.core_in[0, part, :].astype(f32)
            self.core_in[0, part, :] = both.astype(bf16)
            self.far_copy(j).start()

    def take(self, j):
        part = rows_of(j * self.sub, self.sub)
        self.core_copy(1, j).wait_recv()
        self.far_copy(j).wait_recv()
        return (
            self.of(self.at.own, j)
            + self.core_in[1, part, :].astype(f32)
            + self.far_in[part, :].astype(f32)
        )

    def finish(self):
        for j in range(NSUB):
            self.core_copy(0, j).wait_send()
            self.core_copy(1, j).wait_send()
            self.far_copy(j).wait_send()


def nt(left, right):
    return lax.dot_general(left, right, (((1,), (1,)), ((), ())), preferred_element_type=f32)


def tn(left, right):
    return lax.dot_general(left, right, (((0,), (0,)), ((), ())), preferred_element_type=f32)


def nn(left, right):
    return jnp.dot(left, right, preferred_element_type=f32)


def inverse_of(source):
    return lax.rsqrt(jnp.mean(source * source, axis=1, keepdims=True) + norm_eps)


def shifted(value, by):
    if by == 0:
        return value
    size = value.shape[0]
    row = lax.broadcasted_iota(jnp.int32, value.shape, 0)
    inside = row >= by if by > 0 else row < size + by
    return jnp.where(inside, pltpu.roll(value, by % size, 0), 0.0)


def convolve(mixed, taps):
    return taps[0:1] * shifted(mixed, 2) + taps[1:2] * shifted(mixed, 1) + taps[2:3] * mixed


def ffn_columns(p, pieces, core):
    if p < pieces - 1:
        return [(k * LANES, LANES, 0, k) for k in range(3)]
    half = LANES // 2
    return [((3 * h + k) * half, half, h * half, k) for h in range(2 - core) for k in range(3)]


def ffn_blocks(p, pieces):
    last = isinstance(p, int) and p == pieces - 1
    return [(0, LANES // 2), (3 * LANES // 2, LANES // 2)] if last else [(0, LANES)]


class Gather:
    def __init__(self, at, held, chunk, early_y, sems):
        self.at, self.held, self.chunk, self.early_y = at, held, chunk, early_y
        self.recv, self.own_send, self.send = sems
        self.short = held.shape[0] - 1

    def by_kind(self, p, act):
        kind = self.early_y.get(p)
        if kind != "half":
            act(kind == "both")
            return
        for core in (0, 1):

            @pl.when(self.at.core == core)
            def _():
                act(core == 1)

    def run(self, act, p, chip, count, send, dev):
        def of(width):
            block = self.held.at[p, rows_of(chip * self.chunk, count * self.chunk), pl.ds(0, width)]
            act(remote(block, block, send, self.recv.at[p, chip], dev))

        by_core(self.at, p, self.short, self.held.shape[2], of)

    def arrived(self, p, chip, count=1):
        self.run(wait_recv, p, chip, count, self.own_send.at[0, 0], self.at.beside)

    def own(self, p, act):
        at = self.at
        self.run(act, p, at.chip, 1, self.own_send.at[0, p], at.beside)
        self.by_kind(p, lambda pairs: None if pairs else self.own_z(p, at.chip, 1, act))

    def own_z(self, p, chip, count, act):
        at = self.at

        @pl.when(at.has_upper)
        def _():
            self.run(act, p, chip, count, self.own_send.at[1, p], at.upper)

        @pl.when(at.has_lower)
        def _():
            self.run(act, p, chip, count, self.own_send.at[2, p], at.lower)

    def passing(self, p, pairs, parity, wait, act):
        at = self.at

        def step(s, carry):
            for from_z, goes_on, dev, way in (
                (at.z - 1 - s, at.has_upper, at.upper, 0),
                (at.z + 1 + s, at.has_lower, at.lower, 1),
            ):

                @pl.when(jnp.logical_and(from_z >= 0, from_z < at.depth))
                def _():
                    chip = 2 * from_z if pairs else 2 * from_z + at.y
                    count = 2 if pairs else 1
                    if wait:
                        self.arrived(p, chip, count)

                    @pl.when(goes_on)
                    def _():
                        self.run(act, p, chip, count, self.send.at[way, parity, from_z], dev)

                    if not pairs:
                        self.run(act, p, chip, count, self.send.at[2, parity, from_z], at.beside)

            return carry

        lax.fori_loop(0, at.depth - 1, step, 0)

    def sent(self, p):
        self.by_kind(p, lambda pairs: self.passing(p, pairs, p % AHEAD, False, wait_send))

    def relay(self, p):
        if p >= AHEAD:
            self.sent(p - AHEAD)

        def hand_on(pairs):
            if pairs:
                self.arrived(p, 2 * self.at.z + 1 - self.at.y)
                self.own_z(p, 2 * self.at.z, 2, start)
            self.passing(p, pairs, p % AHEAD, True, start)

        self.by_kind(p, hand_on)

    def whole(self, p):
        def step(z, carry):
            self.arrived(p, 2 * z + 1 - self.at.y)
            return carry

        self.by_kind(p, lambda pairs: None if pairs else lax.fori_loop(0, self.at.depth, step, 0))

    def own_done(self, p):
        self.own(p, wait_send)
        self.by_kind(p, lambda pairs: self.own_z(p, 2 * self.at.z, 2, wait_send) if pairs else None)


def forward_kernel(
    ndp,
    early_y,
    in_weight,
    out_weight,
    gate_weight,
    up_weight,
    down_weight,
    tokens,
    teacher,
    valid,
    mixer_gain,
    ffn_gain,
    conv_weight,
    held_out,
    normed_out,
    normed_two_out,
    grad_rows_out,
    streams_out,
    gates_out,
    first_out,
    block_out,
    grad_out,
    small_out,
    loss_out,
    held,
    landed,
    mine,
    rows_a,
    rows_b,
    acc,
    streams,
    gates,
    core_out,
    core_in,
    far_in,
    first,
    result,
    error_grad,
    cur,
    got,
    chip_sems,
    recv_sems,
    own_sems,
    send_sems,
    share_sems,
    core_sems,
    far_sems,
    cube_sems,
    out_sems,
    held_sems,
    gate_sems,
):
    at = place(ndp)
    pieces, width, piece = held.shape
    part_rows = out_weight.shape[0]
    chunk = 2 * part_rows
    rows = tokens.shape[0]
    sub = rows // NSUB
    channels = streams.shape[1] // 3
    aligned = part_rows % 16 == 0
    gather = Gather(at, held, chunk, early_y, (recv_sems, own_sems, send_sems))
    share_a = Share(at, rows_a, rows, share_sems)
    share_b = Share(at, rows_b, rows, share_sems)
    sums = Sums(at, acc, rows, core_out, core_in, far_in, core_sems, far_sems)

    span = (pieces - 2) * LANES
    assert gate_weight.shape[1] == 2 * span - LANES // 2

    def parts(p, core):
        at_columns = rows_of(core * channels, channels, 128)
        if p == 0:
            return [(in_weight.at[k, :, at_columns], k * channels, channels) for k in range(2)]
        if p == 1:
            return [(in_weight.at[2, :, at_columns], 0, channels), (out_weight.at[:, at_columns], channels, channels)]
        found = []
        for column, count, unit, k in ffn_columns(p, pieces, core):
            at_columns = rows_of(core * span + (p - 2) * LANES + unit, count, 128)
            found.append(((gate_weight, up_weight, down_weight)[k].at[:, at_columns], column, count))
        return found

    def each_part(p, core, act):
        if p < pieces - 1:
            for k, part in enumerate(parts(p, core)):
                act(k, *part)
            return
        for to in (0, 1):

            @pl.when(core == to)
            def _():
                for k, part in enumerate(parts(p, to)):
                    act(k, *part)

    def landing(p, core, column, count, buffer):
        if not aligned:
            return buffer.at[p, :, pl.ds(column, count)]
        rows_there = rows_of(at.chip * chunk + core * part_rows, part_rows)
        return held.at[p, rows_there, pl.ds(column, count)]

    def to_sib(p, act):
        def copy(k, src, column, count):
            dst = landing(p, at.core, column, count, landed)
            act(remote(src, dst, chip_sems.at[0, p, k], chip_sems.at[1, p, k], at.sib))

        each_part(p, 1 - at.core, copy)

    def from_sib(p):
        def copy(k, src, column, count):
            dst = landing(p, 1 - at.core, column, count, landed)
            remote(src, dst, chip_sems.at[0, p, k], chip_sems.at[1, p, k], at.sib).wait_recv()

        each_part(p, at.core, copy)

    def keep(p, act):
        def copy(k, src, column, count):
            dst = landing(p, at.core, column, count, mine)
            act(pltpu.make_async_copy(src, dst, chip_sems.at[2, p, k]))

        each_part(p, at.core, copy)

    def own_block(p):
        keep(p, wait)
        from_sib(p)
        here = rows_of(at.chip * chunk, chunk)
        if not aligned:
            a, b = mine[p].astype(f32), landed[p].astype(f32)
            lower = jnp.where(at.core == 0, a, b)
            upper = jnp.where(at.core == 0, b, a)
            held[p, here, :] = jnp.concatenate([lower, upper], axis=0).astype(bf16)
        gather.own(p, start)

    meet(at)
    to_sib(0, start)
    keep(0, start)

    @pl.when(at.core == 1)
    def _():
        held[pieces - 1, :, piece // 2 :] = jnp.zeros((width, piece - piece // 2), bf16)

    share = mixer_gain.shape[1]
    cur[0] = jnp.zeros(cur.shape[1:], f32)
    cur[0, 0:1, 0:share] = mixer_gain[...].astype(f32)
    cur[0, 1:2, 0:share] = ffn_gain[...].astype(f32)
    cur[0, 2:5, 0:share] = conv_weight[...].astype(f32)
    placed = pltpu.roll(cur[0], (at.d * 2 + at.x) * share, 1)
    line = lax.broadcasted_iota(jnp.int32, placed.shape, 0)
    cur[0] = jnp.where(line < 5, placed, jnp.sum(valid[...]))
    tally = lambda step: total_copy(at, step, cur, got, cube_sems.at[0], cube_sems.at[1])
    tallied = lambda step: total_end(at, step, cur, got, tally(step))
    last = len(at.cube)
    tally(0).start()
    for j in range(NSUB):
        rows_a[rows_of(at.own * rows + j * sub, sub), :] = tokens[pl.ds(j * sub, sub), :]
    own_block(0)
    tallied(0)
    tally(1).start()
    for p in range(1, pieces):
        to_sib(p, start)
        keep(p, start)
    tallied(1)
    for j in range(NSUB):
        share_a.start(j)
    tally(2).start()
    own_block(1)
    tallied(2)
    tally(3).start()
    own_block(2)
    tallied(3)
    if last > 4:
        tally(4).start()
    relay = gather.relay
    relay(0)
    for step in range(4, last):
        tallied(step)
        if step + 1 < last:
            tally(step + 1).start()
    for j in range(NSUB):
        share_a.forward(j)
    small_out[...] = cur[last]
    gain_one, gain_two = cur[last, 0:1, :], cur[last, 1:2, :]
    share_a.finish()

    def norm_rows(i, carry):
        part = rows_of(i * sub, sub)
        source = rows_a[part, :].astype(f32)
        rows_a[part, :] = (source * inverse_of(source) * gain_one).astype(bf16)
        return carry

    lax.fori_loop(0, 4 * NSUB, norm_rows, 0)
    normed_copy = pltpu.make_async_copy(rows_a, normed_out, out_sems.at[0])
    normed_copy.start()

    def save(p):
        return pltpu.make_async_copy(held.at[p], held_out.at[p], held_sems.at[p])

    own_block(3)
    relay(1)
    own_block(4)
    relay(2)
    own_block(5)
    for p in (0, 1):
        gather.whole(p)
        save(p).start()
    lane = at.x * 2 * channels + at.core * channels
    taps = cur[last, 2:5, rows_of(lane, channels, 128)]

    def mix(r, carry):
        part = rows_of(((r + 1 - at.core) % 2) * 2 * rows, 2 * rows)
        both = nn(rows_a[part, :], held[0])
        x_stream = nn(rows_a[part, :], held[1, :, 0:channels])
        streams[part, 0 : 2 * channels] = both
        streams[part, 2 * channels :] = x_stream
        convolved = convolve(both[:, 0:channels] * x_stream, taps)
        gated = (both[:, channels:] * convolved).astype(bf16)
        acc[part, :] = nt(gated, held[1, :, channels:])
        return carry

    lax.fori_loop(0, 2, mix, 0)
    streams_copy = pltpu.make_async_copy(streams, streams_out, out_sems.at[1])
    streams_copy.start()
    sums.to_core()
    own_block(6)
    own_block(7)
    sums.to_far()
    relay(3)
    for p in range(8, pieces):
        own_block(p)
    for j in range(NSUB):
        part = rows_of(j * sub, sub)
        value = tokens[part, :].astype(f32) + sums.take(j)
        first[part, :] = value
        normed_two = (value * inverse_of(value) * gain_two).astype(bf16)
        rows_b[rows_of(at.own * rows + j * sub, sub), :] = normed_two
        share_b.start(j)
    sums.finish()
    first_copy = pltpu.make_async_copy(first, first_out, out_sems.at[2])
    first_copy.start()
    relay(4)
    for j in range(NSUB):
        share_b.forward(j)
    share_b.finish()
    normed_two_copy = pltpu.make_async_copy(rows_b, normed_two_out, out_sems.at[3])
    normed_two_copy.start()
    acc[...] = jnp.zeros_like(acc)

    def gates_copy(p):
        slot = p % 2
        return pltpu.make_async_copy(gates.at[slot], gates_out.at[p - 2], gate_sems.at[slot])

    def some(p, r):
        part = rows_of(((r + 1 - at.core) % 2) * 2 * rows, 2 * rows)
        for column, units in ffn_blocks(p, pieces):
            both = nn(rows_b[part, :], held[p, :, column : column + 2 * units])
            gate, up = both[:, 0:units], both[:, units:]
            kept = 2 * column // 3
            gates[p % 2, part, kept : kept + 2 * units] = both.astype(bf16)
            hidden = (gate * jax.nn.sigmoid(gate) * up).astype(bf16)
            acc[part, :] += nt(hidden, held[p, :, column + 2 * units : column + 3 * units])

    def feed(p, carry):
        for q in range(5, pieces):

            @pl.when(p == q - 3)
            def _():
                relay(q)

        for q in range(2, pieces - 1):

            @pl.when(p == q)
            def _():
                gather.whole(q)

        save(p).start()

        @pl.when(p >= 4)
        def _():
            gates_copy(p - 2).wait()

        def rows_part(r, inner):
            some(p, r)
            return inner

        lax.fori_loop(0, 2, rows_part, 0)
        gates_copy(p).start()
        return carry

    normed_copy.wait()
    lax.fori_loop(2, pieces - 1, feed, 0)
    final = pieces - 1
    gather.whole(final)
    gates_copy(final - 2).wait()
    some(final, 0)
    sums.to_core()
    some(final, 1)
    sums.to_far()
    save(final).start()
    gates_copy(final).start()
    scale = 1.0 / (width * cur[last, 5:6, 0:1])
    loss = jnp.zeros((1, width), f32)
    for j in range(NSUB):
        part = rows_of(j * sub, sub)
        value = first[part, :] + sums.take(j)
        result[part, :] = value
        error = value - teacher[part, :].astype(f32)
        weighted = valid[part, :] * error
        loss = loss + jnp.sum(weighted * error, axis=0, keepdims=True)
        grad = (2.0 * scale) * weighted
        error_grad[part, :] = grad
        rows_a[rows_of(at.own * rows + j * sub, sub), :] = grad.astype(bf16)
        share_a.start(j)
    loss_out[...] = jnp.broadcast_to(jnp.sum(loss, axis=1, keepdims=True), loss_out.shape)
    sums.finish()
    result_copy = pltpu.make_async_copy(result, block_out, out_sems.at[4])
    result_copy.start()
    grad_copy = pltpu.make_async_copy(error_grad, grad_out, out_sems.at[5])
    grad_copy.start()
    for j in range(NSUB):
        share_a.forward(j)
    share_a.finish()
    rows_copy = pltpu.make_async_copy(rows_a, grad_rows_out, out_sems.at[6])
    rows_copy.start()
    for p in range(pieces):
        save(p).wait()
        to_sib(p, wait_send)
        gather.own_done(p)
    for p in range(pieces - AHEAD, pieces):
        gather.sent(p)
    for p in (pieces - 2, pieces - 1):
        gates_copy(p).wait()
    for copy in (streams_copy, first_copy, normed_two_copy, result_copy, grad_copy, rows_copy):
        copy.wait()


def forward(ndp, weights, tokens, teacher, valid, vectors):
    part_rows, channels = weights[1].shape
    channels //= 2
    piece = 2 * channels
    pieces = 2 - (-weights[2].shape[1] // (2 * LANES))
    rows, width = tokens.shape
    cube = small_steps(ndp)
    early_y = {3: "both", 6: "half"}
    dma = pltpu.SemaphoreType.DMA
    landing = (pieces, part_rows, piece) if part_rows % 16 else (1, 16, 128)
    shape = jax.ShapeDtypeStruct
    outs = (
        shape((pieces, width, piece), bf16),
        shape((4 * rows, width), bf16),
        shape((4 * rows, width), bf16),
        shape((4 * rows, width), bf16),
        shape((4 * rows, 3 * channels), f32),
        shape((pieces - 2, 4 * rows, 2 * LANES), bf16),
        shape((rows, width), f32),
        shape((rows, width), f32),
        shape((rows, width), f32),
        shape((8, width), f32),
        shape((8, 128), f32),
    )
    scratch = [
        pltpu.VMEM((pieces, width, piece), bf16),
        pltpu.VMEM(landing, bf16),
        pltpu.VMEM(landing, bf16),
        pltpu.VMEM((4 * rows, width), bf16),
        pltpu.VMEM((4 * rows, width), bf16),
        pltpu.VMEM((4 * rows, width), f32),
        pltpu.VMEM((4 * rows, 3 * channels), f32),
        pltpu.VMEM((2, 4 * rows, 2 * LANES), bf16),
        pltpu.VMEM((2, rows, width), bf16),
        pltpu.VMEM((2, rows, width), bf16),
        pltpu.VMEM((rows, width), bf16),
        pltpu.VMEM((rows, width), f32),
        pltpu.VMEM((rows, width), f32),
        pltpu.VMEM((rows, width), f32),
        pltpu.VMEM((cube + 1, 8, width), f32),
        pltpu.VMEM((cube, 8, width), f32),
        dma((3, pieces, 6)),
        dma((pieces, ndp // 2)),
        dma((3, pieces)),
        dma((3, AHEAD, ndp // 4)),
        dma((6, NSUB)),
        dma((2, 2, NSUB)),
        dma((2, NSUB)),
        dma((2, cube)),
        dma((7,)),
        dma((pieces,)),
        dma((2,)),
    ]
    return pl.pallas_call(
        functools.partial(forward_kernel, ndp, early_y),
        out_shape=outs,
        in_specs=[ANY] * 5 + [VMEM] * 6,
        out_specs=[ANY] * 9 + [VMEM] * 2,
        scratch_shapes=scratch,
        compiler_params=pltpu.CompilerParams(
            collective_id=0, has_side_effects=True, vmem_limit_bytes=63 << 20
        ),
    )(*weights, tokens, teacher, valid, *vectors)


def small_steps(ndp):
    return 3 + (ndp // 4 - 1).bit_length()


class Scatter:
    def __init__(self, at, held, chunk, count, mixed, beside_in, line_in, pair_in, pair_beside, total, sems, credits):
        self.mixed = mixed
        self.at, self.held, self.chunk, self.count = at, held, chunk, count
        self.beside_in, self.line_in, self.pair_in, self.pair_beside = beside_in, line_in, pair_in, pair_beside
        self.total, self.credits = total, credits
        self.beside_sems, self.line_sems, self.pair_sems, self.pair_y_sems = sems
        self.short, self.width = held.shape[0] - 1, held.shape[2]
        self.ydepth, self.zdepth = beside_in.shape[0], line_in.shape[0]

    def block(self, p, chip, count=1, width=None):
        here = rows_of(chip * self.chunk, count * self.chunk)
        return self.held.at[p, here, pl.ds(0, width or self.width)]

    def where_it_crosses(self, p, act):
        if p == self.mixed:
            pl.when(self.at.core == 0)(act)
        else:
            act()

    def run(self, act, copy, p, *rest):
        each = lambda width: act(copy(p, *rest, width))
        self.where_it_crosses(p, lambda: by_core(self.at, p, self.short, self.width, each))

    def beside_copy(self, p, m, z, width):
        slot = m % self.ydepth
        return remote(
            self.block(p, 2 * z + 1 - self.at.y, 1, width),
            self.beside_in.at[slot, z, :, pl.ds(0, width)],
            self.beside_sems.at[0, slot, z],
            self.beside_sems.at[1, slot, z],
            self.at.beside,
        )

    def line_copy(self, p, m, z, up, width):
        slot, way = m % self.zdepth, 0 if up else 1
        into = z + 1 if up else z
        return remote(
            self.block(p, 2 * z + self.at.y, 1, width),
            self.line_in.at[slot, into, :, pl.ds(0, width)],
            self.line_sems.at[way, slot, z],
            self.line_sems.at[2, slot, into],
            self.at.upper if up else self.at.lower,
        )

    def pair_copy(self, p, z, up):
        second = 1 if p == self.mixed else 0
        into = z + 1 if up else z
        return remote(
            self.block(p, 2 * z, 2),
            self.pair_in.at[into],
            self.pair_sems.at[3 * second + (0 if up else 1), z],
            self.pair_sems.at[3 * second + 2, into],
            self.at.upper if up else self.at.lower,
        )

    def turn(self, s):
        z, last = self.at.z, self.at.depth - 1
        low = jnp.where(z < self.at.depth // 2, 1, 0)
        down, up = last - s, s
        other = low * (down - jnp.where(down <= z, 1, 0)) + (1 - low) * (up + jnp.where(up >= z, 1, 0))
        mine = jnp.where(s == last, 1, 0)
        return mine * z + (1 - mine) * other

    def free_beside(self, p, m, before):
        if m >= self.ydepth:
            pl.semaphore_wait(self.credits.at[0], 1)
            self.drop_beside(before, m)

    def drop_beside(self, p, m):
        def step(z, carry):
            self.run(wait_send, self.beside_copy, p, m, z)
            return carry

        lax.fori_loop(0, self.at.depth, step, 0)

    def send_beside(self, p, m, before):
        self.free_beside(p, m, before)

        def step(s, carry):
            self.run(start, self.beside_copy, p, m, self.turn(s))
            return carry

        lax.fori_loop(0, self.at.depth, step, 0)

    def ways(self, has, act):
        at = self.at

        def step(s, carry):
            for z, wanted, up in (
                (at.depth - 1 - s, at.depth - 1 - s > at.z, True),
                (s, s < at.z, False),
            ):

                @pl.when(jnp.logical_and(wanted, has(up)))
                def _():
                    act(z, up)

            return carry

        lax.fori_loop(0, at.depth - 1, step, 0)

    def behind(self, up):
        return self.at.has_lower if up else self.at.has_upper

    def opens(self, up):
        return jnp.logical_not(self.behind(up))

    def near(self, up):
        low = self.at.z < self.at.depth // 2
        return jnp.logical_and(self.behind(up), low if up else jnp.logical_not(low))

    def far(self, up):
        low = self.at.z < self.at.depth // 2
        return jnp.logical_and(self.behind(up), jnp.logical_not(low) if up else low)

    def add_beside(self, p, m, before, onward):
        at = self.at
        if m >= self.zdepth:
            for has, credit in ((at.has_upper, 1), (at.has_lower, 2)):

                @pl.when(has)
                def _():
                    pl.semaphore_wait(self.credits.at[credit], 1)

            self.drop(before, m)

        def step(s, carry):
            z = self.turn(s)
            own = self.block(p, 2 * z + at.y)
            self.run(wait_recv, self.beside_copy, p, m, z)

            def add():
                came = self.beside_in[m % self.ydepth, z].astype(f32)
                own[...] = (own[...].astype(f32) + came).astype(bf16)

            self.where_it_crosses(p, add)
            for up in (True, False):

                @pl.when(jnp.logical_and(z > at.z if up else z < at.z, self.opens(up)))
                def _():
                    self.run(start, self.line_copy, p, m, z, up)

                if onward:

                    @pl.when(jnp.logical_and(z > at.z if up else z < at.z, self.behind(up)))
                    def _():
                        self.pass_on(p, m, z, up)

            return carry

        lax.fori_loop(0, at.depth, step, 0)
        if m + self.ydepth < self.count:
            pl.semaphore_signal(self.credits.at[0], 1, device_id=at.beside, device_id_type=MESH)

    def pass_on(self, p, m, z, up):
        self.run(wait_recv, self.line_copy, p, m, z, up)
        own = self.block(p, 2 * z + self.at.y)

        def add():
            came = self.line_in[m % self.zdepth, z + 1 if up else z].astype(f32)
            own[...] = (own[...].astype(f32) + came).astype(bf16)

        self.where_it_crosses(p, add)
        self.run(start, self.line_copy, p, m, z, up)

    def hop(self, p, m, has):
        self.ways(has, functools.partial(self.pass_on, p, m))

    def collect(self, p, m, slot):
        at = self.at
        total = self.total.at[slot]
        total[...] = self.block(p, 2 * at.z + at.y)[...].astype(f32)
        for up in (True, False):

            @pl.when(self.behind(up))
            def _():
                self.run(wait_recv, self.line_copy, p, m, at.z, up)
                total[...] += self.line_in[m % self.zdepth, at.z + 1 if up else at.z].astype(f32)
                if m + self.zdepth < self.count:
                    pl.semaphore_signal(
                        self.credits.at[1 if up else 2],
                        1,
                        device_id=at.lower if up else at.upper,
                        device_id_type=MESH,
                    )

    def drop(self, p, m):
        self.ways(lambda up: True, lambda z, up: self.run(wait_send, self.line_copy, p, m, z, up))

    def pairs_open(self, p):
        self.ways(self.opens, lambda z, up: self.pair_copy(p, z, up).start())

    def pair_hop(self, p, has):
        def act(z, up):
            self.pair_copy(p, z, up).wait_recv()
            own = self.block(p, 2 * z, 2)
            own[...] = (own[...].astype(f32) + self.pair_in[z + 1 if up else z].astype(f32)).astype(bf16)
            self.pair_copy(p, z, up).start()

        self.ways(has, act)

    def pair_y_copy(self, p):
        at = self.at
        second = 1 if p == self.mixed else 0
        return remote(
            self.block(p, 2 * at.z + 1 - at.y),
            self.pair_beside.at[second],
            self.pair_y_sems.at[2 * second],
            self.pair_y_sems.at[2 * second + 1],
            at.beside,
        )

    def pairs_free(self):
        at = self.at
        for has, dev, credit in ((at.has_lower, at.lower, 3), (at.has_upper, at.upper, 4)):

            @pl.when(has)
            def _():
                pl.semaphore_signal(self.credits.at[credit], 1, device_id=dev, device_id_type=MESH)

    def pairs_wait(self):
        for has, credit in ((self.at.has_upper, 3), (self.at.has_lower, 4)):

            @pl.when(has)
            def _():
                pl.semaphore_wait(self.credits.at[credit], 1)

    def pairs_cross(self, p):
        at = self.at
        own = self.block(p, 2 * at.z, 2)
        for up in (True, False):

            @pl.when(self.behind(up))
            def _():
                self.pair_copy(p, at.z, up).wait_recv()
                came = self.pair_in[at.z + 1 if up else at.z].astype(f32)
                own[...] = (own[...].astype(f32) + came).astype(bf16)

        self.pair_y_copy(p).start()

    def pairs_close(self, p, slot):
        at = self.at
        self.pair_y_copy(p).wait()
        mine = self.block(p, 2 * at.z + at.y)[...].astype(f32)
        self.total[slot] = mine + self.pair_beside[1 if p == self.mixed else 0].astype(f32)
        self.ways(lambda up: True, lambda z, up: self.pair_copy(p, z, up).wait_send())


def backward_kernel(
    ndp,
    held_in,
    normed_in,
    normed_two_in,
    grad_rows_in,
    streams_in,
    gates_in,
    first_in,
    grad_in,
    small,
    loss,
    tokens,
    streams_grad,
    out_grad,
    gate_grad,
    up_grad,
    down_grad,
    tokens_grad,
    mixer_gain_grad,
    ffn_gain_grad,
    conv_grad,
    loss_out,
    held,
    rows_a,
    rows_b,
    acc,
    gates,
    streams,
    core_out,
    core_in,
    far_in,
    first,
    grad,
    back,
    beside_in,
    line_in,
    pair_in,
    pair_beside,
    total,
    cur,
    got,
    share_sems,
    core_sems,
    far_sems,
    cube_sems,
    load_sems,
    held_sems,
    gate_sems,
    beside_sems,
    line_sems,
    pair_sems,
    pair_y_sems,
    done_sems,
    credits,
):
    at = place(ndp)
    pieces, width, piece = held.shape
    rows = tokens.shape[0]
    sub = rows // NSUB
    chunk = 2 * width // ndp
    half = chunk // 2
    channels = piece // 2
    order = [2] + list(range(4, pieces)) + [0, 1]
    paired = 3
    mixed = 0
    share = Share(at, rows_a, rows, share_sems)
    sums = Sums(at, acc, rows, core_out, core_in, far_in, core_sems, far_sems)
    scatter = Scatter(
        at,
        held,
        chunk,
        len(order),
        mixed,
        beside_in,
        line_in,
        pair_in,
        pair_beside,
        total,
        (beside_sems, line_sems, pair_sems, pair_y_sems),
        credits,
    )

    def load(src, dst, k):
        return pltpu.make_async_copy(src, dst, load_sems.at[k])

    def load_held(p):
        return pltpu.make_async_copy(held_in.at[p], held.at[p], held_sems.at[p])

    def load_gates(p):
        return pltpu.make_async_copy(gates_in.at[p - 2], gates.at[p % 2], gate_sems.at[p % 2])

    def load_streams(r):
        return load(streams_in.at[pl.ds(r * 2 * rows, 2 * rows), :], streams, 5)

    opening = (
        load(grad_rows_in, rows_a, 0),
        load_gates(2),
        load_held(2),
        load(normed_two_in, rows_b, 1),
    )
    for copy in opening:
        copy.start()
    load_gates(3).start()
    for p in list(range(3, pieces)) + [0, 1]:
        load_held(p).start()
    load_first, load_grad = load(first_in, first, 2), load(grad_in, grad, 3)
    load_first.start()
    load_grad.start()
    load_streams(0).start()
    meet(at)
    acc[...] = jnp.zeros_like(acc)
    opening[0].wait()

    def ffn(p, m=None):
        load_gates(p).wait()
        load_held(p).wait()

        def some(r, carry):
            part = rows_of(((r + 1 - at.core) % 2) * 2 * rows, 2 * rows)
            for column, units in ffn_blocks(p, pieces):
                ends = [column + k * units for k in range(4)]
                grad_hidden = nn(rows_a[part, :], held[p, :, ends[2] : ends[3]])
                kept = 2 * column // 3
                gate = gates[p % 2, part, kept : kept + units].astype(f32)
                up = gates[p % 2, part, kept + units : kept + 2 * units].astype(f32)
                sig = jax.nn.sigmoid(gate)
                active = gate * sig
                back[part, ends[2] : ends[3]] = (active * up).astype(bf16)
                grad_gate = grad_hidden * up * sig * (1.0 + gate * (1.0 - sig))
                back[part, ends[0] : ends[1]] = grad_gate.astype(bf16)
                back[part, ends[1] : ends[2]] = (grad_hidden * active).astype(bf16)
                acc[part, :] += nt(back[part, ends[0] : ends[2]], held[p, :, ends[0] : ends[2]])
            return carry

        lax.fori_loop(0, 2, some, 0)

        if p == 2:
            opening[3].wait()
        blocks = 2 * width // piece
        matched = blocks == at.depth

        def weights(s, carry):
            i = scatter.turn(s) if matched else s
            part = rows_of(i * (piece // 2), piece // 2, 128)
            for column, units in ffn_blocks(p, pieces):
                ends = [column + k * units for k in range(4)]
                held[p, part, ends[0] : ends[2]] = tn(rows_b[:, part], back[:, ends[0] : ends[2]]).astype(bf16)
                held[p, part, ends[2] : ends[3]] = tn(rows_a[:, part], back[:, ends[2] : ends[3]]).astype(bf16)
            if m is not None and matched:
                scatter.run(start, scatter.beside_copy, p, m, i)
            return carry

        lax.fori_loop(0, blocks, weights, 0)
        if m is not None and not matched:
            scatter.send_beside(p, m, None)
        if p + 2 < pieces:
            load_gates(p + 2).start()

    given = []

    span = (pieces - 2) * LANES

    def parts(p, core):
        at_columns = rows_of(core * channels, channels, 128)
        if p == 0:
            return [(k * channels, channels, streams_grad.at[k, :, at_columns]) for k in range(2)]
        if p == 1:
            return [
                (0, channels, streams_grad.at[2, :, at_columns]),
                (channels, channels, out_grad.at[:, at_columns]),
            ]
        found = []
        for column, count, unit, k in ffn_columns(p, pieces, core):
            at_columns = rows_of(core * span + (p - 2) * LANES + unit, count, 128)
            found.append((column, count, (gate_grad, up_grad, down_grad)[k].at[:, at_columns]))
        return found

    def each_part(p, core, act):
        if p < pieces - 1:
            for k, part in enumerate(parts(p, core)):
                act(k, *part)
            return
        for to in (0, 1):

            @pl.when(core == to)
            def _():
                for k, part in enumerate(parts(p, to)):
                    act(k, *part)

    def piece_rows(p, core, first_column, count):
        slot = given.index(p) % 2 if p in given else 0
        return total.at[slot, rows_of(core * half, half, 8), pl.ds(first_column, count)]

    def out_local(p, act):
        def copy(k, first_column, count, dst):
            src = piece_rows(p, at.core, first_column, count)
            act(pltpu.make_async_copy(src, dst, done_sems.at[0, p, k]))

        each_part(p, at.core, copy)

    def out_sib(p, core, act):
        def copy(k, first_column, count, dst):
            src = piece_rows(p, 1 - at.core, first_column, count)
            act(remote(src, dst, done_sems.at[1, p, k], done_sems.at[2, p, k], at.sib))

        each_part(p, core, copy)

    def give(p, fill):
        if len(given) > 1:
            out_local(given[-2], wait)
            out_sib(given[-2], at.core, wait_send)
        given.append(p)
        fill((len(given) - 1) % 2)
        out_local(p, start)
        out_sib(p, at.core, start)

    def beside(m):
        scatter.send_beside(order[m], m, order[m - YDEPTH] if m >= YDEPTH else None)

    on_core_one = pl.when(at.core == 1)

    def finish(m):
        def fill(slot):
            scatter.where_it_crosses(order[m], lambda: scatter.collect(order[m], m, slot))
            if order[m] == mixed:
                on_core_one(lambda: scatter.pairs_close(mixed, slot))

        give(order[m], fill)

    def advance(m):
        onward = m == len(order) - 1
        if onward:
            scatter.hop(order[m - 1], m - 1, scatter.far)
            finish(m - 2)
        scatter.add_beside(order[m], m, order[m - ZDEPTH] if m >= ZDEPTH else None, onward)
        if onward:
            return
        for k in (0, 1) if m == 1 else (m,) if m > 1 else ():
            scatter.hop(order[k], k, scatter.near)
        for k in (0, 1) if m == 2 else (m - 1,) if m > 2 else ():
            scatter.hop(order[k], k, scatter.far)
        if m == 2:
            scatter.pair_hop(paired, scatter.far)
        for k in (0, 1) if m == 3 else (m - 2,) if m > 3 else ():
            finish(k)
        if m == 3:
            scatter.pairs_cross(paired)
            on_core_one(scatter.pairs_free)
        if m == 4:
            give(paired, functools.partial(scatter.pairs_close, paired))

    gain_one, gain_two = small[0:1, :], small[1:2, :]
    ffn(2, 0)
    ffn(3)
    scatter.pairs_open(paired)
    ffn(4, 1)
    ffn(5, 2)
    advance(0)
    ffn(6)
    beside(3)
    scatter.pair_hop(paired, scatter.near)
    for p in range(7, pieces):
        ffn(p)
    sums.to_core()
    load_normed = load(normed_in, rows_b, 4)
    load_normed.start()
    sums.to_far()
    advance(1)
    beside(4)
    load_first.wait()
    load_grad.wait()
    gain_two_grad = jnp.zeros((1, width), f32)
    for j in range(NSUB):
        part = rows_of(j * sub, sub)
        coming = sums.take(j)
        source = first[part, :]
        inverse = inverse_of(source)
        weighted = coming * gain_two
        inner = jnp.mean(weighted * source, axis=1, keepdims=True)
        value = grad[part, :] + inverse * weighted - source * (inverse * inverse * inverse * inner)
        grad[part, :] = value
        gain_two_grad += jnp.sum(coming * source * inverse, axis=0, keepdims=True)
        rows_a[rows_of(at.own * rows + j * sub, sub), :] = value.astype(bf16)
        share.start(j)
    sums.finish()
    advance(2)
    beside(5)
    for j in range(NSUB):
        share.forward(j)
    share.finish()
    shift = at.x * 2 * channels + at.core * channels
    cur[0] = jnp.zeros(cur.shape[1:], f32)
    cur[0, 1:2, :] = gain_two_grad
    cur[0, 5:6, :] = jnp.broadcast_to(loss[0:1, 0:1], (1, width))
    load_held(0).wait()
    load_held(1).wait()
    for r in range(2):
        load_streams(r).wait()
        part = pl.ds(r * 2 * rows, 2 * rows)
        acc[part, 0:channels] = nn(rows_a[part, :], held[1, :, channels:])

        def mix(q, carry):
            lanes = [rows_of(k * channels + q * 128, 128, 128) for k in range(3)]
            b_gate, c_gate, x_stream = (streams[:, lane] for lane in lanes)
            tap = small[2:5, rows_of(shift + q * 128, 128, 128)]
            mixed = b_gate * x_stream
            convolved = convolve(mixed, tap)
            grad_gated = acc[part, lanes[0]]
            gates[0, part, lanes[0]] = (c_gate * convolved).astype(bf16)
            back[part, lanes[1]] = (grad_gated * convolved).astype(bf16)
            grad_conv = grad_gated * c_gate
            grad_mixed = tap[2:3] * grad_conv
            grad_mixed += tap[1:2] * shifted(grad_conv, -1) + tap[0:1] * shifted(grad_conv, -2)
            for k in range(3):
                term = jnp.sum(grad_conv * shifted(mixed, 2 - k), axis=0, keepdims=True)
                cur[0, 2 + k : 3 + k, rows_of(shift + q * 128, 128, 128)] += term
            back[part, lanes[0]] = (grad_mixed * x_stream).astype(bf16)
            back[part, lanes[2]] = (grad_mixed * b_gate).astype(bf16)
            return carry

        lax.fori_loop(0, channels // 128, mix, 0)
        if r == 0:
            load_streams(1).start()
        acc[part, :] = nt(back[part, 0 : 2 * channels], held[0])
        acc[part, :] += nt(back[part, 2 * channels :], held[1, :, 0:channels])
    sums.to_core()
    load_normed.wait()

    def mixer_weights(i, carry):
        part = rows_of(i * channels, channels, 128)
        left = rows_b[:, part]
        held[0, part, :] = tn(left, back[:, 0 : 2 * channels]).astype(bf16)
        held[1, part, 0:channels] = tn(left, back[:, 2 * channels :]).astype(bf16)
        held[1, part, channels:] = tn(rows_a[:, part], gates[0, :, 0:channels]).astype(bf16)
        return carry

    lax.fori_loop(0, width // channels, mixer_weights, 0)
    advance(3)
    beside(6)

    @on_core_one
    def _():
        scatter.pairs_wait()
        scatter.pairs_open(mixed)

    sums.to_far()
    advance(4)
    on_core_one(lambda: scatter.pair_hop(mixed, scatter.near))
    gain_one_grad = jnp.zeros((1, width), f32)
    for j in range(NSUB):
        part = rows_of(j * sub, sub)
        coming = sums.take(j)
        source = tokens[part, :].astype(f32)
        inverse = inverse_of(source)
        weighted = coming * gain_one
        inner = jnp.mean(weighted * source, axis=1, keepdims=True)
        grad[part, :] += inverse * weighted - source * (inverse * inverse * inverse * inner)
        gain_one_grad += jnp.sum(coming * source * inverse, axis=0, keepdims=True)
    sums.finish()
    tokens_copy = load(grad, tokens_grad, 6)
    tokens_copy.start()
    cur[0, 0:1, :] = gain_one_grad
    tally = lambda step: total_copy(at, step, cur, got, cube_sems.at[0], cube_sems.at[1])
    for step in range(2):
        tally(step).start()
        total_end(at, step, cur, got, tally(step))
    tally(2).start()
    beside(7)
    steps = len(at.cube)
    count = len(order)
    advance(5)
    on_core_one(lambda: scatter.pair_hop(mixed, scatter.far))
    advance(6)
    on_core_one(lambda: scatter.pairs_cross(mixed))
    total_end(at, 2, cur, got, tally(2))
    tally(3).start()
    advance(7)
    for step in range(3, steps):
        total_end(at, step, cur, got, tally(step))
        if step + 1 < steps:
            tally(step + 1).start()
        if step == 3:
            finish(count - 2)
    finish(count - 1)
    share_lanes = mixer_gain_grad.shape[1]
    own = pltpu.roll(cur[steps], (width - (at.d * 2 + at.x) * share_lanes) % width, 1)
    mixer_gain_grad[...] = own[0:1, 0:share_lanes]
    ffn_gain_grad[...] = own[1:2, 0:share_lanes]
    conv_grad[...] = own[2:5, 0:share_lanes]
    loss_out[...] = cur[steps, 5:6, 0:1] / (width * small[5:6, 0:1])
    for m in range(count - YDEPTH, count):
        scatter.drop_beside(order[m], m)
    for m in range(count - ZDEPTH, count):
        scatter.drop(order[m], m)
    for p in given[-2:]:
        out_local(p, wait)
        out_sib(p, at.core, wait_send)
    for p in given:
        out_sib(p, 1 - at.core, wait_recv)
    tokens_copy.wait()


def backward(ndp, units, held, normed, normed_two, grad_rows, streams, gates, first, grad, small, loss, tokens):
    pieces, width, piece = held.shape
    rows = tokens.shape[0]
    chunk = 2 * width // ndp
    depth = ndp // 4
    channels = piece // 2
    cube = small_steps(ndp)
    dma = pltpu.SemaphoreType.DMA
    shape = jax.ShapeDtypeStruct
    outs = (
        shape((3, chunk // 2, 2 * channels), f32),
        shape((chunk // 2, 2 * channels), f32),
        shape((chunk // 2, units), f32),
        shape((chunk // 2, units), f32),
        shape((chunk // 2, units), f32),
        shape((rows, width), f32),
        shape((1, width // (2 * ndp)), f32),
        shape((1, width // (2 * ndp)), f32),
        shape((3, width // (2 * ndp)), f32),
        shape((1, 1), f32),
    )
    scratch = [
        pltpu.VMEM((pieces, width, piece), bf16),
        pltpu.VMEM((4 * rows, width), bf16),
        pltpu.VMEM((4 * rows, width), bf16),
        pltpu.VMEM((4 * rows, width), f32),
        pltpu.VMEM((2, 4 * rows, 2 * LANES), bf16),
        pltpu.VMEM((2 * rows, 3 * channels), f32),
        pltpu.VMEM((2, rows, width), bf16),
        pltpu.VMEM((2, rows, width), bf16),
        pltpu.VMEM((rows, width), bf16),
        pltpu.VMEM((rows, width), f32),
        pltpu.VMEM((rows, width), f32),
        pltpu.VMEM((4 * rows, 3 * channels), bf16),
        pltpu.VMEM((YDEPTH, depth, chunk, piece), bf16),
        pltpu.VMEM((ZDEPTH, depth + 1, chunk, piece), bf16),
        pltpu.VMEM((depth + 1, 2 * chunk, piece), bf16),
        pltpu.VMEM((2, chunk, piece), bf16),
        pltpu.VMEM((2, chunk, piece), f32),
        pltpu.VMEM((cube + 1, 8, width), f32),
        pltpu.VMEM((cube, 8, width), f32),
        dma((6, NSUB)),
        dma((2, 2, NSUB)),
        dma((2, NSUB)),
        dma((2, cube)),
        dma((7,)),
        dma((pieces,)),
        dma((2,)),
        dma((2, YDEPTH, depth)),
        dma((3, ZDEPTH, depth + 1)),
        dma((6, depth + 1)),
        dma((4,)),
        dma((3, pieces, 6)),
        pltpu.SemaphoreType.REGULAR((5,)),
    ]
    return pl.pallas_call(
        functools.partial(backward_kernel, ndp),
        out_shape=outs,
        in_specs=[ANY] * 8 + [VMEM] * 3,
        out_specs=[ANY] * 6 + [VMEM] * 4,
        scratch_shapes=scratch,
        compiler_params=pltpu.CompilerParams(
            collective_id=1, has_side_effects=True, vmem_limit_bytes=127 << 19
        ),
    )(held, normed, normed_two, grad_rows, streams, gates, first, grad, small, loss, tokens)


def body(
    tokens,
    teacher,
    valid,
    mixer_gain,
    in_weight,
    conv_weight,
    out_weight,
    ffn_gain,
    gate_weight,
    up_weight,
    down_weight,
):
    ndp = lax.axis_size("dp")
    held, normed, normed_two, grad_rows, streams, gates, first, block_out, grad, small, loss = forward(
        ndp,
        (in_weight.transpose(1, 0, 2), out_weight, gate_weight, up_weight, down_weight),
        tokens,
        teacher,
        valid.astype(f32)[:, None],
        (mixer_gain[None], ffn_gain[None], conv_weight),
    )
    streams_grad, out_grad, gate_grad, up_grad, down_grad, tokens_grad, *small_grads = backward(
        ndp,
        gate_weight.shape[1],
        held,
        normed,
        normed_two,
        grad_rows,
        streams,
        gates,
        first,
        grad,
        small,
        loss,
        tokens,
    )
    mixer_gain_grad, ffn_gain_grad, conv_grad, loss = small_grads
    return (
        loss[0, 0],
        block_out,
        tokens_grad,
        mixer_gain_grad[0],
        streams_grad.transpose(1, 0, 2),
        conv_grad,
        out_grad,
        ffn_gain_grad[0],
        gate_grad,
        up_grad,
        down_grad,
    )


def solution(mesh):
    rows = P(("dp", "tensor"), None)
    vector = P(("dp", "tensor"))
    weight = P("dp", "tensor")
    streams = P("dp", None, "tensor")
    taps = P(None, ("dp", "tensor"))
    return jax.shard_map(
        body,
        mesh=mesh,
        in_specs=(rows, rows, vector, vector, streams, taps, weight, vector, weight, weight, weight),
        out_specs=(P(), rows, rows, vector, streams, taps, weight, vector, weight, weight, weight),
        check_vma=False,
    )
```

```python
import functools
from types import SimpleNamespace

import jax
import jax.numpy as jnp
from jax import lax
from jax.experimental import pallas as pl
from jax.experimental.pallas import tpu as pltpu
from jax.sharding import PartitionSpec as P

MESH = pl.DeviceIdType.MESH
f32 = jnp.float32
bf16 = jnp.bfloat16
norm_eps = 1e-05
LANES = 256
NSUB = 3
YDEPTH, ZDEPTH = 3, 4
AHEAD = 4
VMEM = pl.BlockSpec(memory_space=pltpu.VMEM)
ANY = pl.BlockSpec(memory_space=pl.ANY)


def rows_of(start, size, step=16):
    return pl.ds(pl.multiple_of(start, step), size)


def place(ndp):
    d, x = lax.axis_index("dp"), lax.axis_index("tensor")
    core, y, z = d % 2, (d // 2) % 2, d // 4
    depth = ndp // 4
    at = SimpleNamespace(d=d, x=x, core=core, y=y, z=z, depth=depth, chip=d // 2)
    at.sib = (d + 1 - 2 * core, x)
    at.across = (d, 1 - x)
    at.beside = (d + 2 - 4 * y, x)
    at.lower, at.upper = (d - 4, x), (d + 4, x)
    at.has_lower, at.has_upper = z > 0, z < depth - 1
    at.cube = [at.sib, at.across, at.beside]
    step = 1
    while step < depth:
        at.cube.append((d + 4 * step * (1 - 2 * ((z // step) % 2)), x))
        step *= 2
    at.own = 2 * core + x
    at.own_sib = 2 * (1 - core) + x
    at.own_across = 2 * core + 1 - x
    at.own_far = 2 * (1 - core) + 1 - x
    return at


def meet(at):
    bar = pltpu.get_barrier_semaphore()
    always = [at.sib, at.across, at.beside] + at.cube[4:]
    for dev in always:
        pl.semaphore_signal(bar, 1, device_id=dev, device_id_type=MESH)
    for has, dev in ((at.has_lower, at.lower), (at.has_upper, at.upper)):

        @pl.when(has)
        def _():
            pl.semaphore_signal(bar, 1, device_id=dev, device_id_type=MESH)

    ends = jnp.where(at.has_lower, 1, 0) + jnp.where(at.has_upper, 1, 0)
    pl.semaphore_wait(bar, len(always) + ends)


def remote(src, dst, send, recv, dev):
    return pltpu.make_async_remote_copy(
        src_ref=src, dst_ref=dst, send_sem=send, recv_sem=recv, device_id=dev, device_id_type=MESH
    )


def total_copy(at, step, cur, got, send, recv):
    return remote(cur.at[step], got.at[step], send.at[step], recv.at[step], at.cube[step])


def total_end(at, step, cur, got, copy):
    copy.wait()
    cur[step + 1] = cur[step] + got[step]


def start(copy):
    copy.start()


def wait(copy):
    copy.wait()


def wait_send(copy):
    copy.wait_send()


def wait_recv(copy):
    copy.wait_recv()


def by_core(at, p, short, width, act):
    if p != short:
        act(width)
        return
    for core, count in ((0, width), (1, width // 2)):

        @pl.when(at.core == core)
        def _():
            act(count)


class Share:
    def __init__(self, at, buf, rows, sems):
        self.at, self.buf, self.rows, self.sems = at, buf, rows, sems
        self.sub = rows // NSUB

    def part(self, slot, j):
        return self.buf.at[rows_of(slot * self.rows + j * self.sub, self.sub), :]

    def copy(self, slot, j, k, dev):
        part = self.part(slot, j)
        return remote(part, part, self.sems.at[2 * k, j], self.sems.at[2 * k + 1, j], dev)

    def start(self, j):
        self.copy(self.at.own, j, 0, self.at.across).start()
        self.copy(self.at.own, j, 1, self.at.sib).start()

    def forward(self, j):
        self.copy(self.at.own_across, j, 0, self.at.across).wait_recv()
        self.copy(self.at.own_across, j, 2, self.at.sib).start()

    def finish(self):
        for j in range(NSUB):
            self.copy(self.at.own_sib, j, 1, self.at.sib).wait_recv()
            self.copy(self.at.own_far, j, 2, self.at.sib).wait_recv()
            self.copy(self.at.own, j, 0, self.at.across).wait_send()
            self.copy(self.at.own, j, 1, self.at.sib).wait_send()
            self.copy(self.at.own_across, j, 2, self.at.sib).wait_send()


class Sums:
    def __init__(self, at, acc, rows, core_out, core_in, far_in, core_sems, far_sems):
        self.at, self.acc, self.rows = at, acc, rows
        self.core_out, self.core_in, self.far_in = core_out, core_in, far_in
        self.core_sems, self.far_sems = core_sems, far_sems
        self.sub = rows // NSUB

    def of(self, slot, j):
        return self.acc[rows_of(slot * self.rows + j * self.sub, self.sub), :]

    def core_copy(self, k, j):
        part = rows_of(j * self.sub, self.sub)
        return remote(
            self.core_out.at[k, part, :],
            self.core_in.at[k, part, :],
            self.core_sems.at[0, k, j],
            self.core_sems.at[1, k, j],
            self.at.sib,
        )

    def far_copy(self, j):
        part = rows_of(j * self.sub, self.sub)
        return remote(
            self.core_in.at[0, part, :],
            self.far_in.at[part, :],
            self.far_sems.at[0, j],
            self.far_sems.at[1, j],
            self.at.across,
        )

    def to_core(self):
        for k, slot in ((0, self.at.own_far), (1, self.at.own_sib)):
            for j in range(NSUB):
                self.core_out[k, rows_of(j * self.sub, self.sub), :] = self.of(slot, j).astype(bf16)
                self.core_copy(k, j).start()

    def to_far(self):
        for j in range(NSUB):
            part = rows_of(j * self.sub, self.sub)
            self.core_copy(0, j).wait_recv()
            both = self.of(self.at.own_across, j) + self.core_in[0, part, :].astype(f32)
            self.core_in[0, part, :] = both.astype(bf16)
            self.far_copy(j).start()

    def take(self, j):
        part = rows_of(j * self.sub, self.sub)
        self.core_copy(1, j).wait_recv()
        self.far_copy(j).wait_recv()
        return (
            self.of(self.at.own, j)
            + self.core_in[1, part, :].astype(f32)
            + self.far_in[part, :].astype(f32)
        )

    def finish(self):
        for j in range(NSUB):
            self.core_copy(0, j).wait_send()
            self.core_copy(1, j).wait_send()
            self.far_copy(j).wait_send()


def nt(left, right):
    return lax.dot_general(left, right, (((1,), (1,)), ((), ())), preferred_element_type=f32)


def tn(left, right):
    return lax.dot_general(left, right, (((0,), (0,)), ((), ())), preferred_element_type=f32)


def nn(left, right):
    return jnp.dot(left, right, preferred_element_type=f32)


def inverse_of(source):
    return lax.rsqrt(jnp.mean(source * source, axis=1, keepdims=True) + norm_eps)


def shifted(value, by):
    if by == 0:
        return value
    size = value.shape[0]
    row = lax.broadcasted_iota(jnp.int32, value.shape, 0)
    inside = row >= by if by > 0 else row < size + by
    return jnp.where(inside, pltpu.roll(value, by % size, 0), 0.0)


def convolve(mixed, taps):
    return taps[0:1] * shifted(mixed, 2) + taps[1:2] * shifted(mixed, 1) + taps[2:3] * mixed


def ffn_columns(p, pieces, core):
    if p < pieces - 1:
        return [(k * LANES, LANES, 0, k) for k in range(3)]
    half = LANES // 2
    return [((3 * h + k) * half, half, h * half, k) for h in range(2 - core) for k in range(3)]


def ffn_blocks(p, pieces):
    last = isinstance(p, int) and p == pieces - 1
    return [(0, LANES // 2), (3 * LANES // 2, LANES // 2)] if last else [(0, LANES)]


class Gather:
    def __init__(self, at, held, chunk, early_y, sems):
        self.at, self.held, self.chunk, self.early_y = at, held, chunk, early_y
        self.recv, self.own_send, self.send = sems
        self.short = held.shape[0] - 1

    def by_kind(self, p, act):
        kind = self.early_y.get(p)
        if kind != "half":
            act(kind == "both")
            return
        for core in (0, 1):

            @pl.when(self.at.core == core)
            def _():
                act(core == 1)

    def run(self, act, p, chip, count, send, dev):
        def of(width):
            block = self.held.at[p, rows_of(chip * self.chunk, count * self.chunk), pl.ds(0, width)]
            act(remote(block, block, send, self.recv.at[p, chip], dev))

        by_core(self.at, p, self.short, self.held.shape[2], of)

    def arrived(self, p, chip, count=1):
        self.run(wait_recv, p, chip, count, self.own_send.at[0, 0], self.at.beside)

    def own(self, p, act):
        at = self.at
        self.run(act, p, at.chip, 1, self.own_send.at[0, p], at.beside)
        self.by_kind(p, lambda pairs: None if pairs else self.own_z(p, at.chip, 1, act))

    def own_z(self, p, chip, count, act):
        at = self.at

        @pl.when(at.has_upper)
        def _():
            self.run(act, p, chip, count, self.own_send.at[1, p], at.upper)

        @pl.when(at.has_lower)
        def _():
            self.run(act, p, chip, count, self.own_send.at[2, p], at.lower)

    def passing(self, p, pairs, parity, wait, act):
        at = self.at

        def step(s, carry):
            for from_z, goes_on, dev, way in (
                (at.z - 1 - s, at.has_upper, at.upper, 0),
                (at.z + 1 + s, at.has_lower, at.lower, 1),
            ):

                @pl.when(jnp.logical_and(from_z >= 0, from_z < at.depth))
                def _():
                    chip = 2 * from_z if pairs else 2 * from_z + at.y
                    count = 2 if pairs else 1
                    if wait:
                        self.arrived(p, chip, count)

                    @pl.when(goes_on)
                    def _():
                        self.run(act, p, chip, count, self.send.at[way, parity, from_z], dev)

                    if not pairs:
                        self.run(act, p, chip, count, self.send.at[2, parity, from_z], at.beside)

            return carry

        lax.fori_loop(0, at.depth - 1, step, 0)

    def sent(self, p):
        self.by_kind(p, lambda pairs: self.passing(p, pairs, p % AHEAD, False, wait_send))

    def relay(self, p):
        if p >= AHEAD:
            self.sent(p - AHEAD)

        def hand_on(pairs):
            if pairs:
                self.arrived(p, 2 * self.at.z + 1 - self.at.y)
                self.own_z(p, 2 * self.at.z, 2, start)
            self.passing(p, pairs, p % AHEAD, True, start)

        self.by_kind(p, hand_on)

    def whole(self, p):
        def step(z, carry):
            self.arrived(p, 2 * z + 1 - self.at.y)
            return carry

        self.by_kind(p, lambda pairs: None if pairs else lax.fori_loop(0, self.at.depth, step, 0))

    def own_done(self, p):
        self.own(p, wait_send)
        self.by_kind(p, lambda pairs: self.own_z(p, 2 * self.at.z, 2, wait_send) if pairs else None)


def forward_kernel(
    ndp,
    early_y,
    in_weight,
    out_weight,
    gate_weight,
    up_weight,
    down_weight,
    tokens,
    teacher,
    valid,
    mixer_gain,
    ffn_gain,
    conv_weight,
    held_out,
    normed_out,
    normed_two_out,
    grad_rows_out,
    streams_out,
    gates_out,
    first_out,
    block_out,
    grad_out,
    small_out,
    loss_out,
    held,
    landed,
    mine,
    rows_a,
    rows_b,
    acc,
    streams,
    gates,
    core_out,
    core_in,
    far_in,
    first,
    result,
    error_grad,
    cur,
    got,
    chip_sems,
    recv_sems,
    own_sems,
    send_sems,
    share_sems,
    core_sems,
    far_sems,
    cube_sems,
    out_sems,
    held_sems,
    gate_sems,
):
    at = place(ndp)
    pieces, width, piece = held.shape
    part_rows = out_weight.shape[0]
    chunk = 2 * part_rows
    rows = tokens.shape[0]
    sub = rows // NSUB
    channels = streams.shape[1] // 3
    aligned = part_rows % 16 == 0
    gather = Gather(at, held, chunk, early_y, (recv_sems, own_sems, send_sems))
    share_a = Share(at, rows_a, rows, share_sems)
    share_b = Share(at, rows_b, rows, share_sems)
    sums = Sums(at, acc, rows, core_out, core_in, far_in, core_sems, far_sems)

    span = (pieces - 2) * LANES
    assert gate_weight.shape[1] == 2 * span - LANES // 2

    def parts(p, core):
        at_columns = rows_of(core * channels, channels, 128)
        if p == 0:
            return [(in_weight.at[k, :, at_columns], k * channels, channels) for k in range(2)]
        if p == 1:
            return [(in_weight.at[2, :, at_columns], 0, channels), (out_weight.at[:, at_columns], channels, channels)]
        found = []
        for column, count, unit, k in ffn_columns(p, pieces, core):
            at_columns = rows_of(core * span + (p - 2) * LANES + unit, count, 128)
            found.append(((gate_weight, up_weight, down_weight)[k].at[:, at_columns], column, count))
        return found

    def each_part(p, core, act):
        if p < pieces - 1:
            for k, part in enumerate(parts(p, core)):
                act(k, *part)
            return
        for to in (0, 1):

            @pl.when(core == to)
            def _():
                for k, part in enumerate(parts(p, to)):
                    act(k, *part)

    def landing(p, core, column, count, buffer):
        if not aligned:
            return buffer.at[p, :, pl.ds(column, count)]
        rows_there = rows_of(at.chip * chunk + core * part_rows, part_rows)
        return held.at[p, rows_there, pl.ds(column, count)]

    def to_sib(p, act):
        def copy(k, src, column, count):
            dst = landing(p, at.core, column, count, landed)
            act(remote(src, dst, chip_sems.at[0, p, k], chip_sems.at[1, p, k], at.sib))

        each_part(p, 1 - at.core, copy)

    def from_sib(p):
        def copy(k, src, column, count):
            dst = landing(p, 1 - at.core, column, count, landed)
            remote(src, dst, chip_sems.at[0, p, k], chip_sems.at[1, p, k], at.sib).wait_recv()

        each_part(p, at.core, copy)

    def keep(p, act):
        def copy(k, src, column, count):
            dst = landing(p, at.core, column, count, mine)
            act(pltpu.make_async_copy(src, dst, chip_sems.at[2, p, k]))

        each_part(p, at.core, copy)

    def own_block(p):
        keep(p, wait)
        from_sib(p)
        here = rows_of(at.chip * chunk, chunk)
        if not aligned:
            a, b = mine[p].astype(f32), landed[p].astype(f32)
            lower = jnp.where(at.core == 0, a, b)
            upper = jnp.where(at.core == 0, b, a)
            held[p, here, :] = jnp.concatenate([lower, upper], axis=0).astype(bf16)
        gather.own(p, start)

    meet(at)
    to_sib(0, start)
    keep(0, start)

    @pl.when(at.core == 1)
    def _():
        held[pieces - 1, :, piece // 2 :] = jnp.zeros((width, piece - piece // 2), bf16)

    share = mixer_gain.shape[1]
    cur[0] = jnp.zeros(cur.shape[1:], f32)
    cur[0, 0:1, 0:share] = mixer_gain[...].astype(f32)
    cur[0, 1:2, 0:share] = ffn_gain[...].astype(f32)
    cur[0, 2:5, 0:share] = conv_weight[...].astype(f32)
    placed = pltpu.roll(cur[0], (at.d * 2 + at.x) * share, 1)
    line = lax.broadcasted_iota(jnp.int32, placed.shape, 0)
    cur[0] = jnp.where(line < 5, placed, jnp.sum(valid[...]))
    tally = lambda step: total_copy(at, step, cur, got, cube_sems.at[0], cube_sems.at[1])
    tallied = lambda step: total_end(at, step, cur, got, tally(step))
    last = len(at.cube)
    tally(0).start()
    for j in range(NSUB):
        rows_a[rows_of(at.own * rows + j * sub, sub), :] = tokens[pl.ds(j * sub, sub), :]
    own_block(0)
    tallied(0)
    tally(1).start()
    for p in range(1, pieces):
        to_sib(p, start)
        keep(p, start)
    tallied(1)
    for j in range(NSUB):
        share_a.start(j)
    tally(2).start()
    own_block(1)
    tallied(2)
    tally(3).start()
    own_block(2)
    tallied(3)
    if last > 4:
        tally(4).start()
    relay = gather.relay
    relay(0)
    for step in range(4, last):
        tallied(step)
        if step + 1 < last:
            tally(step + 1).start()
    for j in range(NSUB):
        share_a.forward(j)
    small_out[...] = cur[last]
    gain_one, gain_two = cur[last, 0:1, :], cur[last, 1:2, :]
    share_a.finish()

    def norm_rows(i, carry):
        part = rows_of(i * sub, sub)
        source = rows_a[part, :].astype(f32)
        rows_a[part, :] = (source * inverse_of(source) * gain_one).astype(bf16)
        return carry

    lax.fori_loop(0, 4 * NSUB, norm_rows, 0)
    normed_copy = pltpu.make_async_copy(rows_a, normed_out, out_sems.at[0])
    normed_copy.start()

    def save(p):
        return pltpu.make_async_copy(held.at[p], held_out.at[p], held_sems.at[p])

    own_block(3)
    relay(1)
    own_block(4)
    relay(2)
    own_block(5)
    for p in (0, 1):
        gather.whole(p)
        save(p).start()
    lane = at.x * 2 * channels + at.core * channels
    taps = cur[last, 2:5, rows_of(lane, channels, 128)]

    def mix(r, carry):
        part = rows_of(((r + 1 - at.core) % 2) * 2 * rows, 2 * rows)
        both = nn(rows_a[part, :], held[0])
        x_stream = nn(rows_a[part, :], held[1, :, 0:channels])
        streams[part, 0 : 2 * channels] = both
        streams[part, 2 * channels :] = x_stream
        convolved = convolve(both[:, 0:channels] * x_stream, taps)
        gated = (both[:, channels:] * convolved).astype(bf16)
        acc[part, :] = nt(gated, held[1, :, channels:])
        return carry

    lax.fori_loop(0, 2, mix, 0)
    streams_copy = pltpu.make_async_copy(streams, streams_out, out_sems.at[1])
    streams_copy.start()
    sums.to_core()
    own_block(6)
    own_block(7)
    sums.to_far()
    relay(3)
    for p in range(8, pieces):
        own_block(p)
    for j in range(NSUB):
        part = rows_of(j * sub, sub)
        value = tokens[part, :].astype(f32) + sums.take(j)
        first[part, :] = value
        normed_two = (value * inverse_of(value) * gain_two).astype(bf16)
        rows_b[rows_of(at.own * rows + j * sub, sub), :] = normed_two
        share_b.start(j)
    sums.finish()
    first_copy = pltpu.make_async_copy(first, first_out, out_sems.at[2])
    first_copy.start()
    relay(4)
    for j in range(NSUB):
        share_b.forward(j)
    share_b.finish()
    normed_two_copy = pltpu.make_async_copy(rows_b, normed_two_out, out_sems.at[3])
    normed_two_copy.start()
    acc[...] = jnp.zeros_like(acc)

    def gates_copy(p):
        slot = p % 2
        return pltpu.make_async_copy(gates.at[slot], gates_out.at[p - 2], gate_sems.at[slot])

    def some(p, r):
        part = rows_of(((r + 1 - at.core) % 2) * 2 * rows, 2 * rows)
        for column, units in ffn_blocks(p, pieces):
            both = nn(rows_b[part, :], held[p, :, column : column + 2 * units])
            gate, up = both[:, 0:units], both[:, units:]
            kept = 2 * column // 3
            gates[p % 2, part, kept : kept + 2 * units] = both.astype(bf16)
            hidden = (gate * jax.nn.sigmoid(gate) * up).astype(bf16)
            acc[part, :] += nt(hidden, held[p, :, column + 2 * units : column + 3 * units])

    def feed(p, carry):
        for q in range(5, pieces):

            @pl.when(p == q - 3)
            def _():
                relay(q)

        for q in range(2, pieces - 1):

            @pl.when(p == q)
            def _():
                gather.whole(q)

        save(p).start()

        @pl.when(p >= 4)
        def _():
            gates_copy(p - 2).wait()

        def rows_part(r, inner):
            some(p, r)
            return inner

        lax.fori_loop(0, 2, rows_part, 0)
        gates_copy(p).start()
        return carry

    normed_copy.wait()
    lax.fori_loop(2, pieces - 1, feed, 0)
    final = pieces - 1
    gather.whole(final)
    gates_copy(final - 2).wait()
    some(final, 0)
    sums.to_core()
    some(final, 1)
    sums.to_far()
    save(final).start()
    gates_copy(final).start()
    scale = 1.0 / (width * cur[last, 5:6, 0:1])
    loss = jnp.zeros((1, width), f32)
    for j in range(NSUB):
        part = rows_of(j * sub, sub)
        value = first[part, :] + sums.take(j)
        result[part, :] = value
        error = value - teacher[part, :].astype(f32)
        weighted = valid[part, :] * error
        loss = loss + jnp.sum(weighted * error, axis=0, keepdims=True)
        grad = (2.0 * scale) * weighted
        error_grad[part, :] = grad
        rows_a[rows_of(at.own * rows + j * sub, sub), :] = grad.astype(bf16)
        share_a.start(j)
    loss_out[...] = jnp.broadcast_to(jnp.sum(loss, axis=1, keepdims=True), loss_out.shape)
    sums.finish()
    result_copy = pltpu.make_async_copy(result, block_out, out_sems.at[4])
    result_copy.start()
    grad_copy = pltpu.make_async_copy(error_grad, grad_out, out_sems.at[5])
    grad_copy.start()
    for j in range(NSUB):
        share_a.forward(j)
    share_a.finish()
    rows_copy = pltpu.make_async_copy(rows_a, grad_rows_out, out_sems.at[6])
    rows_copy.start()
    for p in range(pieces):
        save(p).wait()
        to_sib(p, wait_send)
        gather.own_done(p)
    for p in range(pieces - AHEAD, pieces):
        gather.sent(p)
    for p in (pieces - 2, pieces - 1):
        gates_copy(p).wait()
    for copy in (streams_copy, first_copy, normed_two_copy, result_copy, grad_copy, rows_copy):
        copy.wait()


def forward(ndp, weights, tokens, teacher, valid, vectors):
    part_rows, channels = weights[1].shape
    channels //= 2
    piece = 2 * channels
    pieces = 2 - (-weights[2].shape[1] // (2 * LANES))
    rows, width = tokens.shape
    cube = small_steps(ndp)
    early_y = {3: "both", 6: "half"}
    dma = pltpu.SemaphoreType.DMA
    landing = (pieces, part_rows, piece) if part_rows % 16 else (1, 16, 128)
    shape = jax.ShapeDtypeStruct
    outs = (
        shape((pieces, width, piece), bf16),
        shape((4 * rows, width), bf16),
        shape((4 * rows, width), bf16),
        shape((4 * rows, width), bf16),
        shape((4 * rows, 3 * channels), f32),
        shape((pieces - 2, 4 * rows, 2 * LANES), bf16),
        shape((rows, width), f32),
        shape((rows, width), f32),
        shape((rows, width), f32),
        shape((8, width), f32),
        shape((8, 128), f32),
    )
    scratch = [
        pltpu.VMEM((pieces, width, piece), bf16),
        pltpu.VMEM(landing, bf16),
        pltpu.VMEM(landing, bf16),
        pltpu.VMEM((4 * rows, width), bf16),
        pltpu.VMEM((4 * rows, width), bf16),
        pltpu.VMEM((4 * rows, width), f32),
        pltpu.VMEM((4 * rows, 3 * channels), f32),
        pltpu.VMEM((2, 4 * rows, 2 * LANES), bf16),
        pltpu.VMEM((2, rows, width), bf16),
        pltpu.VMEM((2, rows, width), bf16),
        pltpu.VMEM((rows, width), bf16),
        pltpu.VMEM((rows, width), f32),
        pltpu.VMEM((rows, width), f32),
        pltpu.VMEM((rows, width), f32),
        pltpu.VMEM((cube + 1, 8, width), f32),
        pltpu.VMEM((cube, 8, width), f32),
        dma((3, pieces, 6)),
        dma((pieces, ndp // 2)),
        dma((3, pieces)),
        dma((3, AHEAD, ndp // 4)),
        dma((6, NSUB)),
        dma((2, 2, NSUB)),
        dma((2, NSUB)),
        dma((2, cube)),
        dma((7,)),
        dma((pieces,)),
        dma((2,)),
    ]
    return pl.pallas_call(
        functools.partial(forward_kernel, ndp, early_y),
        out_shape=outs,
        in_specs=[ANY] * 5 + [VMEM] * 6,
        out_specs=[ANY] * 9 + [VMEM] * 2,
        scratch_shapes=scratch,
        compiler_params=pltpu.CompilerParams(
            collective_id=0, has_side_effects=True, vmem_limit_bytes=63 << 20
        ),
    )(*weights, tokens, teacher, valid, *vectors)


def small_steps(ndp):
    return 3 + (ndp // 4 - 1).bit_length()


class Scatter:
    def __init__(self, at, held, chunk, count, mixed, beside_in, line_in, pair_in, pair_beside, total, sems, credits):
        self.mixed = mixed
        self.at, self.held, self.chunk, self.count = at, held, chunk, count
        self.beside_in, self.line_in, self.pair_in, self.pair_beside = beside_in, line_in, pair_in, pair_beside
        self.total, self.credits = total, credits
        self.beside_sems, self.line_sems, self.pair_sems, self.pair_y_sems = sems
        self.short, self.width = held.shape[0] - 1, held.shape[2]
        self.ydepth, self.zdepth = beside_in.shape[0], line_in.shape[0]

    def block(self, p, chip, count=1, width=None):
        here = rows_of(chip * self.chunk, count * self.chunk)
        return self.held.at[p, here, pl.ds(0, width or self.width)]

    def where_it_crosses(self, p, act):
        if p == self.mixed:
            pl.when(self.at.core == 0)(act)
        else:
            act()

    def run(self, act, copy, p, *rest):
        each = lambda width: act(copy(p, *rest, width))
        self.where_it_crosses(p, lambda: by_core(self.at, p, self.short, self.width, each))

    def beside_copy(self, p, m, z, width):
        slot = m % self.ydepth
        return remote(
            self.block(p, 2 * z + 1 - self.at.y, 1, width),
            self.beside_in.at[slot, z, :, pl.ds(0, width)],
            self.beside_sems.at[0, slot, z],
            self.beside_sems.at[1, slot, z],
            self.at.beside,
        )

    def line_copy(self, p, m, z, up, width):
        slot, way = m % self.zdepth, 0 if up else 1
        into = z + 1 if up else z
        return remote(
            self.block(p, 2 * z + self.at.y, 1, width),
            self.line_in.at[slot, into, :, pl.ds(0, width)],
            self.line_sems.at[way, slot, z],
            self.line_sems.at[2, slot, into],
            self.at.upper if up else self.at.lower,
        )

    def pair_copy(self, p, z, up):
        second = 1 if p == self.mixed else 0
        into = z + 1 if up else z
        return remote(
            self.block(p, 2 * z, 2),
            self.pair_in.at[into],
            self.pair_sems.at[3 * second + (0 if up else 1), z],
            self.pair_sems.at[3 * second + 2, into],
            self.at.upper if up else self.at.lower,
        )

    def turn(self, s):
        z, last = self.at.z, self.at.depth - 1
        low = jnp.where(z < self.at.depth // 2, 1, 0)
        down, up = last - s, s
        other = low * (down - jnp.where(down <= z, 1, 0)) + (1 - low) * (up + jnp.where(up >= z, 1, 0))
        mine = jnp.where(s == last, 1, 0)
        return mine * z + (1 - mine) * other

    def free_beside(self, p, m, before):
        if m >= self.ydepth:
            pl.semaphore_wait(self.credits.at[0], 1)
            self.drop_beside(before, m)

    def drop_beside(self, p, m):
        def step(z, carry):
            self.run(wait_send, self.beside_copy, p, m, z)
            return carry

        lax.fori_loop(0, self.at.depth, step, 0)

    def send_beside(self, p, m, before):
        self.free_beside(p, m, before)

        def step(s, carry):
            self.run(start, self.beside_copy, p, m, self.turn(s))
            return carry

        lax.fori_loop(0, self.at.depth, step, 0)

    def ways(self, has, act):
        at = self.at

        def step(s, carry):
            for z, wanted, up in (
                (at.depth - 1 - s, at.depth - 1 - s > at.z, True),
                (s, s < at.z, False),
            ):

                @pl.when(jnp.logical_and(wanted, has(up)))
                def _():
                    act(z, up)

            return carry

        lax.fori_loop(0, at.depth - 1, step, 0)

    def behind(self, up):
        return self.at.has_lower if up else self.at.has_upper

    def opens(self, up):
        return jnp.logical_not(self.behind(up))

    def near(self, up):
        low = self.at.z < self.at.depth // 2
        return jnp.logical_and(self.behind(up), low if up else jnp.logical_not(low))

    def far(self, up):
        low = self.at.z < self.at.depth // 2
        return jnp.logical_and(self.behind(up), jnp.logical_not(low) if up else low)

    def add_beside(self, p, m, before, onward):
        at = self.at
        if m >= self.zdepth:
            for has, credit in ((at.has_upper, 1), (at.has_lower, 2)):

                @pl.when(has)
                def _():
                    pl.semaphore_wait(self.credits.at[credit], 1)

            self.drop(before, m)

        def step(s, carry):
            z = self.turn(s)
            own = self.block(p, 2 * z + at.y)
            self.run(wait_recv, self.beside_copy, p, m, z)

            def add():
                came = self.beside_in[m % self.ydepth, z].astype(f32)
                own[...] = (own[...].astype(f32) + came).astype(bf16)

            self.where_it_crosses(p, add)
            for up in (True, False):

                @pl.when(jnp.logical_and(z > at.z if up else z < at.z, self.opens(up)))
                def _():
                    self.run(start, self.line_copy, p, m, z, up)

                if onward:

                    @pl.when(jnp.logical_and(z > at.z if up else z < at.z, self.behind(up)))
                    def _():
                        self.pass_on(p, m, z, up)

            return carry

        lax.fori_loop(0, at.depth, step, 0)
        if m + self.ydepth < self.count:
            pl.semaphore_signal(self.credits.at[0], 1, device_id=at.beside, device_id_type=MESH)

    def pass_on(self, p, m, z, up):
        self.run(wait_recv, self.line_copy, p, m, z, up)
        own = self.block(p, 2 * z + self.at.y)

        def add():
            came = self.line_in[m % self.zdepth, z + 1 if up else z].astype(f32)
            own[...] = (own[...].astype(f32) + came).astype(bf16)

        self.where_it_crosses(p, add)
        self.run(start, self.line_copy, p, m, z, up)

    def hop(self, p, m, has):
        self.ways(has, functools.partial(self.pass_on, p, m))

    def collect(self, p, m, slot):
        at = self.at
        total = self.total.at[slot]
        total[...] = self.block(p, 2 * at.z + at.y)[...].astype(f32)
        for up in (True, False):

            @pl.when(self.behind(up))
            def _():
                self.run(wait_recv, self.line_copy, p, m, at.z, up)
                total[...] += self.line_in[m % self.zdepth, at.z + 1 if up else at.z].astype(f32)
                if m + self.zdepth < self.count:
                    pl.semaphore_signal(
                        self.credits.at[1 if up else 2],
                        1,
                        device_id=at.lower if up else at.upper,
                        device_id_type=MESH,
                    )

    def drop(self, p, m):
        self.ways(lambda up: True, lambda z, up: self.run(wait_send, self.line_copy, p, m, z, up))

    def pairs_open(self, p):
        self.ways(self.opens, lambda z, up: self.pair_copy(p, z, up).start())

    def pair_hop(self, p, has):
        def act(z, up):
            self.pair_copy(p, z, up).wait_recv()
            own = self.block(p, 2 * z, 2)
            own[...] = (own[...].astype(f32) + self.pair_in[z + 1 if up else z].astype(f32)).astype(bf16)
            self.pair_copy(p, z, up).start()

        self.ways(has, act)

    def pair_y_copy(self, p):
        at = self.at
        second = 1 if p == self.mixed else 0
        return remote(
            self.block(p, 2 * at.z + 1 - at.y),
            self.pair_beside.at[second],
            self.pair_y_sems.at[2 * second],
            self.pair_y_sems.at[2 * second + 1],
            at.beside,
        )

    def pairs_free(self):
        at = self.at
        for has, dev, credit in ((at.has_lower, at.lower, 3), (at.has_upper, at.upper, 4)):

            @pl.when(has)
            def _():
                pl.semaphore_signal(self.credits.at[credit], 1, device_id=dev, device_id_type=MESH)

    def pairs_wait(self):
        for has, credit in ((self.at.has_upper, 3), (self.at.has_lower, 4)):

            @pl.when(has)
            def _():
                pl.semaphore_wait(self.credits.at[credit], 1)

    def pairs_cross(self, p):
        at = self.at
        own = self.block(p, 2 * at.z, 2)
        for up in (True, False):

            @pl.when(self.behind(up))
            def _():
                self.pair_copy(p, at.z, up).wait_recv()
                came = self.pair_in[at.z + 1 if up else at.z].astype(f32)
                own[...] = (own[...].astype(f32) + came).astype(bf16)

        self.pair_y_copy(p).start()

    def pairs_close(self, p, slot):
        at = self.at
        self.pair_y_copy(p).wait()
        mine = self.block(p, 2 * at.z + at.y)[...].astype(f32)
        self.total[slot] = mine + self.pair_beside[1 if p == self.mixed else 0].astype(f32)
        self.ways(lambda up: True, lambda z, up: self.pair_copy(p, z, up).wait_send())


def backward_kernel(
    ndp,
    held_in,
    normed_in,
    normed_two_in,
    grad_rows_in,
    streams_in,
    gates_in,
    first_in,
    grad_in,
    small,
    loss,
    tokens,
    streams_grad,
    out_grad,
    gate_grad,
    up_grad,
    down_grad,
    tokens_grad,
    mixer_gain_grad,
    ffn_gain_grad,
    conv_grad,
    loss_out,
    held,
    rows_a,
    rows_b,
    acc,
    gates,
    streams,
    core_out,
    core_in,
    far_in,
    first,
    grad,
    back,
    beside_in,
    line_in,
    pair_in,
    pair_beside,
    total,
    cur,
    got,
    share_sems,
    core_sems,
    far_sems,
    cube_sems,
    load_sems,
    held_sems,
    gate_sems,
    beside_sems,
    line_sems,
    pair_sems,
    pair_y_sems,
    done_sems,
    credits,
):
    at = place(ndp)
    pieces, width, piece = held.shape
    rows = tokens.shape[0]
    sub = rows // NSUB
    chunk = 2 * width // ndp
    half = chunk // 2
    channels = piece // 2
    order = [2] + list(range(4, pieces)) + [0, 1]
    paired = 3
    mixed = 0
    share = Share(at, rows_a, rows, share_sems)
    sums = Sums(at, acc, rows, core_out, core_in, far_in, core_sems, far_sems)
    scatter = Scatter(
        at,
        held,
        chunk,
        len(order),
        mixed,
        beside_in,
        line_in,
        pair_in,
        pair_beside,
        total,
        (beside_sems, line_sems, pair_sems, pair_y_sems),
        credits,
    )

    def load(src, dst, k):
        return pltpu.make_async_copy(src, dst, load_sems.at[k])

    def load_held(p):
        return pltpu.make_async_copy(held_in.at[p], held.at[p], held_sems.at[p])

    def load_gates(p):
        return pltpu.make_async_copy(gates_in.at[p - 2], gates.at[p % 2], gate_sems.at[p % 2])

    def load_streams(r):
        return load(streams_in.at[pl.ds(r * 2 * rows, 2 * rows), :], streams, 5)

    opening = (
        load(grad_rows_in, rows_a, 0),
        load_gates(2),
        load_held(2),
        load(normed_two_in, rows_b, 1),
    )
    for copy in opening:
        copy.start()
    load_gates(3).start()
    for p in list(range(3, pieces)) + [0, 1]:
        load_held(p).start()
    load_first, load_grad = load(first_in, first, 2), load(grad_in, grad, 3)
    load_first.start()
    load_grad.start()
    load_streams(0).start()
    meet(at)
    acc[...] = jnp.zeros_like(acc)
    opening[0].wait()

    def ffn(p, m=None):
        load_gates(p).wait()
        load_held(p).wait()

        def some(r, carry):
            part = rows_of(((r + 1 - at.core) % 2) * 2 * rows, 2 * rows)
            for column, units in ffn_blocks(p, pieces):
                ends = [column + k * units for k in range(4)]
                grad_hidden = nn(rows_a[part, :], held[p, :, ends[2] : ends[3]])
                kept = 2 * column // 3
                gate = gates[p % 2, part, kept : kept + units].astype(f32)
                up = gates[p % 2, part, kept + units : kept + 2 * units].astype(f32)
                sig = jax.nn.sigmoid(gate)
                active = gate * sig
                back[part, ends[2] : ends[3]] = (active * up).astype(bf16)
                grad_gate = grad_hidden * up * sig * (1.0 + gate * (1.0 - sig))
                back[part, ends[0] : ends[1]] = grad_gate.astype(bf16)
                back[part, ends[1] : ends[2]] = (grad_hidden * active).astype(bf16)
                acc[part, :] += nt(back[part, ends[0] : ends[2]], held[p, :, ends[0] : ends[2]])
            return carry

        lax.fori_loop(0, 2, some, 0)

        if p == 2:
            opening[3].wait()
        blocks = 2 * width // piece
        matched = blocks == at.depth

        def weights(s, carry):
            i = scatter.turn(s) if matched else s
            part = rows_of(i * (piece // 2), piece // 2, 128)
            for column, units in ffn_blocks(p, pieces):
                ends = [column + k * units for k in range(4)]
                held[p, part, ends[0] : ends[2]] = tn(rows_b[:, part], back[:, ends[0] : ends[2]]).astype(bf16)
                held[p, part, ends[2] : ends[3]] = tn(rows_a[:, part], back[:, ends[2] : ends[3]]).astype(bf16)
            if m is not None and matched:
                scatter.run(start, scatter.beside_copy, p, m, i)
            return carry

        lax.fori_loop(0, blocks, weights, 0)
        if m is not None and not matched:
            scatter.send_beside(p, m, None)
        if p + 2 < pieces:
            load_gates(p + 2).start()

    given = []

    span = (pieces - 2) * LANES

    def parts(p, core):
        at_columns = rows_of(core * channels, channels, 128)
        if p == 0:
            return [(k * channels, channels, streams_grad.at[k, :, at_columns]) for k in range(2)]
        if p == 1:
            return [
                (0, channels, streams_grad.at[2, :, at_columns]),
                (channels, channels, out_grad.at[:, at_columns]),
            ]
        found = []
        for column, count, unit, k in ffn_columns(p, pieces, core):
            at_columns = rows_of(core * span + (p - 2) * LANES + unit, count, 128)
            found.append((column, count, (gate_grad, up_grad, down_grad)[k].at[:, at_columns]))
        return found

    def each_part(p, core, act):
        if p < pieces - 1:
            for k, part in enumerate(parts(p, core)):
                act(k, *part)
            return
        for to in (0, 1):

            @pl.when(core == to)
            def _():
                for k, part in enumerate(parts(p, to)):
                    act(k, *part)

    def piece_rows(p, core, first_column, count):
        slot = given.index(p) % 2 if p in given else 0
        return total.at[slot, rows_of(core * half, half, 8), pl.ds(first_column, count)]

    def out_local(p, act):
        def copy(k, first_column, count, dst):
            src = piece_rows(p, at.core, first_column, count)
            act(pltpu.make_async_copy(src, dst, done_sems.at[0, p, k]))

        each_part(p, at.core, copy)

    def out_sib(p, core, act):
        def copy(k, first_column, count, dst):
            src = piece_rows(p, 1 - at.core, first_column, count)
            act(remote(src, dst, done_sems.at[1, p, k], done_sems.at[2, p, k], at.sib))

        each_part(p, core, copy)

    def give(p, fill):
        if len(given) > 1:
            out_local(given[-2], wait)
            out_sib(given[-2], at.core, wait_send)
        given.append(p)
        fill((len(given) - 1) % 2)
        out_local(p, start)
        out_sib(p, at.core, start)

    def beside(m):
        scatter.send_beside(order[m], m, order[m - YDEPTH] if m >= YDEPTH else None)

    on_core_one = pl.when(at.core == 1)

    def finish(m):
        def fill(slot):
            scatter.where_it_crosses(order[m], lambda: scatter.collect(order[m], m, slot))
            if order[m] == mixed:
                on_core_one(lambda: scatter.pairs_close(mixed, slot))

        give(order[m], fill)

    def advance(m):
        onward = m == len(order) - 1
        if onward:
            scatter.hop(order[m - 1], m - 1, scatter.far)
            finish(m - 2)
        scatter.add_beside(order[m], m, order[m - ZDEPTH] if m >= ZDEPTH else None, onward)
        if onward:
            return
        for k in (0, 1) if m == 1 else (m,) if m > 1 else ():
            scatter.hop(order[k], k, scatter.near)
        for k in (0, 1) if m == 2 else (m - 1,) if m > 2 else ():
            scatter.hop(order[k], k, scatter.far)
        if m == 2:
            scatter.pair_hop(paired, scatter.far)
        for k in (0, 1) if m == 3 else (m - 2,) if m > 3 else ():
            finish(k)
        if m == 3:
            scatter.pairs_cross(paired)
            on_core_one(scatter.pairs_free)
        if m == 4:
            give(paired, functools.partial(scatter.pairs_close, paired))

    gain_one, gain_two = small[0:1, :], small[1:2, :]
    ffn(2, 0)
    ffn(3)
    scatter.pairs_open(paired)
    ffn(4, 1)
    ffn(5, 2)
    advance(0)
    ffn(6)
    beside(3)
    scatter.pair_hop(paired, scatter.near)
    for p in range(7, pieces):
        ffn(p)
    sums.to_core()
    load_normed = load(normed_in, rows_b, 4)
    load_normed.start()
    sums.to_far()
    advance(1)
    beside(4)
    load_first.wait()
    load_grad.wait()
    gain_two_grad = jnp.zeros((1, width), f32)
    for j in range(NSUB):
        part = rows_of(j * sub, sub)
        coming = sums.take(j)
        source = first[part, :]
        inverse = inverse_of(source)
        weighted = coming * gain_two
        inner = jnp.mean(weighted * source, axis=1, keepdims=True)
        value = grad[part, :] + inverse * weighted - source * (inverse * inverse * inverse * inner)
        grad[part, :] = value
        gain_two_grad += jnp.sum(coming * source * inverse, axis=0, keepdims=True)
        rows_a[rows_of(at.own * rows + j * sub, sub), :] = value.astype(bf16)
        share.start(j)
    sums.finish()
    advance(2)
    beside(5)
    for j in range(NSUB):
        share.forward(j)
    share.finish()
    shift = at.x * 2 * channels + at.core * channels
    cur[0] = jnp.zeros(cur.shape[1:], f32)
    cur[0, 1:2, :] = gain_two_grad
    cur[0, 5:6, :] = jnp.broadcast_to(loss[0:1, 0:1], (1, width))
    load_held(0).wait()
    load_held(1).wait()
    for r in range(2):
        load_streams(r).wait()
        part = pl.ds(r * 2 * rows, 2 * rows)
        acc[part, 0:channels] = nn(rows_a[part, :], held[1, :, channels:])

        def mix(q, carry):
            lanes = [rows_of(k * channels + q * 128, 128, 128) for k in range(3)]
            b_gate, c_gate, x_stream = (streams[:, lane] for lane in lanes)
            tap = small[2:5, rows_of(shift + q * 128, 128, 128)]
            mixed = b_gate * x_stream
            convolved = convolve(mixed, tap)
            grad_gated = acc[part, lanes[0]]
            gates[0, part, lanes[0]] = (c_gate * convolved).astype(bf16)
            back[part, lanes[1]] = (grad_gated * convolved).astype(bf16)
            grad_conv = grad_gated * c_gate
            grad_mixed = tap[2:3] * grad_conv
            grad_mixed += tap[1:2] * shifted(grad_conv, -1) + tap[0:1] * shifted(grad_conv, -2)
            for k in range(3):
                term = jnp.sum(grad_conv * shifted(mixed, 2 - k), axis=0, keepdims=True)
                cur[0, 2 + k : 3 + k, rows_of(shift + q * 128, 128, 128)] += term
            back[part, lanes[0]] = (grad_mixed * x_stream).astype(bf16)
            back[part, lanes[2]] = (grad_mixed * b_gate).astype(bf16)
            return carry

        lax.fori_loop(0, channels // 128, mix, 0)
        if r == 0:
            load_streams(1).start()
        acc[part, :] = nt(back[part, 0 : 2 * channels], held[0])
        acc[part, :] += nt(back[part, 2 * channels :], held[1, :, 0:channels])
    sums.to_core()
    load_normed.wait()

    def mixer_weights(i, carry):
        part = rows_of(i * channels, channels, 128)
        left = rows_b[:, part]
        held[0, part, :] = tn(left, back[:, 0 : 2 * channels]).astype(bf16)
        held[1, part, 0:channels] = tn(left, back[:, 2 * channels :]).astype(bf16)
        held[1, part, channels:] = tn(rows_a[:, part], gates[0, :, 0:channels]).astype(bf16)
        return carry

    lax.fori_loop(0, width // channels, mixer_weights, 0)
    advance(3)
    beside(6)

    @on_core_one
    def _():
        scatter.pairs_wait()
        scatter.pairs_open(mixed)

    sums.to_far()
    advance(4)
    on_core_one(lambda: scatter.pair_hop(mixed, scatter.near))
    gain_one_grad = jnp.zeros((1, width), f32)
    for j in range(NSUB):
        part = rows_of(j * sub, sub)
        coming = sums.take(j)
        source = tokens[part, :].astype(f32)
        inverse = inverse_of(source)
        weighted = coming * gain_one
        inner = jnp.mean(weighted * source, axis=1, keepdims=True)
        grad[part, :] += inverse * weighted - source * (inverse * inverse * inverse * inner)
        gain_one_grad += jnp.sum(coming * source * inverse, axis=0, keepdims=True)
    sums.finish()
    tokens_copy = load(grad, tokens_grad, 6)
    tokens_copy.start()
    cur[0, 0:1, :] = gain_one_grad
    tally = lambda step: total_copy(at, step, cur, got, cube_sems.at[0], cube_sems.at[1])
    for step in range(2):
        tally(step).start()
        total_end(at, step, cur, got, tally(step))
    tally(2).start()
    beside(7)
    steps = len(at.cube)
    count = len(order)
    advance(5)
    on_core_one(lambda: scatter.pair_hop(mixed, scatter.far))
    advance(6)
    on_core_one(lambda: scatter.pairs_cross(mixed))
    total_end(at, 2, cur, got, tally(2))
    tally(3).start()
    advance(7)
    finish(count - 2)
    total_end(at, 3, cur, got, tally(3))
    if steps > 4:
        tally(4).start()
    finish(count - 1)
    for step in range(4, steps):
        total_end(at, step, cur, got, tally(step))
        if step + 1 < steps:
            tally(step + 1).start()
    share_lanes = mixer_gain_grad.shape[1]
    own = pltpu.roll(cur[steps], (width - (at.d * 2 + at.x) * share_lanes) % width, 1)
    mixer_gain_grad[...] = own[0:1, 0:share_lanes]
    ffn_gain_grad[...] = own[1:2, 0:share_lanes]
    conv_grad[...] = own[2:5, 0:share_lanes]
    loss_out[...] = cur[steps, 5:6, 0:1] / (width * small[5:6, 0:1])
    for m in range(count - YDEPTH, count):
        scatter.drop_beside(order[m], m)
    for m in range(count - ZDEPTH, count):
        scatter.drop(order[m], m)
    for p in given[-2:]:
        out_local(p, wait)
        out_sib(p, at.core, wait_send)
    for p in given:
        out_sib(p, 1 - at.core, wait_recv)
    tokens_copy.wait()


def backward(ndp, units, held, normed, normed_two, grad_rows, streams, gates, first, grad, small, loss, tokens):
    pieces, width, piece = held.shape
    rows = tokens.shape[0]
    chunk = 2 * width // ndp
    depth = ndp // 4
    channels = piece // 2
    cube = small_steps(ndp)
    dma = pltpu.SemaphoreType.DMA
    shape = jax.ShapeDtypeStruct
    outs = (
        shape((3, chunk // 2, 2 * channels), f32),
        shape((chunk // 2, 2 * channels), f32),
        shape((chunk // 2, units), f32),
        shape((chunk // 2, units), f32),
        shape((chunk // 2, units), f32),
        shape((rows, width), f32),
        shape((1, width // (2 * ndp)), f32),
        shape((1, width // (2 * ndp)), f32),
        shape((3, width // (2 * ndp)), f32),
        shape((1, 1), f32),
    )
    scratch = [
        pltpu.VMEM((pieces, width, piece), bf16),
        pltpu.VMEM((4 * rows, width), bf16),
        pltpu.VMEM((4 * rows, width), bf16),
        pltpu.VMEM((4 * rows, width), f32),
        pltpu.VMEM((2, 4 * rows, 2 * LANES), bf16),
        pltpu.VMEM((2 * rows, 3 * channels), f32),
        pltpu.VMEM((2, rows, width), bf16),
        pltpu.VMEM((2, rows, width), bf16),
        pltpu.VMEM((rows, width), bf16),
        pltpu.VMEM((rows, width), f32),
        pltpu.VMEM((rows, width), f32),
        pltpu.VMEM((4 * rows, 3 * channels), bf16),
        pltpu.VMEM((YDEPTH, depth, chunk, piece), bf16),
        pltpu.VMEM((ZDEPTH, depth + 1, chunk, piece), bf16),
        pltpu.VMEM((depth + 1, 2 * chunk, piece), bf16),
        pltpu.VMEM((2, chunk, piece), bf16),
        pltpu.VMEM((2, chunk, piece), f32),
        pltpu.VMEM((cube + 1, 8, width), f32),
        pltpu.VMEM((cube, 8, width), f32),
        dma((6, NSUB)),
        dma((2, 2, NSUB)),
        dma((2, NSUB)),
        dma((2, cube)),
        dma((7,)),
        dma((pieces,)),
        dma((2,)),
        dma((2, YDEPTH, depth)),
        dma((3, ZDEPTH, depth + 1)),
        dma((6, depth + 1)),
        dma((4,)),
        dma((3, pieces, 6)),
        pltpu.SemaphoreType.REGULAR((5,)),
    ]
    return pl.pallas_call(
        functools.partial(backward_kernel, ndp),
        out_shape=outs,
        in_specs=[ANY] * 8 + [VMEM] * 3,
        out_specs=[ANY] * 6 + [VMEM] * 4,
        scratch_shapes=scratch,
        compiler_params=pltpu.CompilerParams(
            collective_id=1, has_side_effects=True, vmem_limit_bytes=127 << 19
        ),
    )(held, normed, normed_two, grad_rows, streams, gates, first, grad, small, loss, tokens)


def body(
    tokens,
    teacher,
    valid,
    mixer_gain,
    in_weight,
    conv_weight,
    out_weight,
    ffn_gain,
    gate_weight,
    up_weight,
    down_weight,
):
    ndp = lax.axis_size("dp")
    held, normed, normed_two, grad_rows, streams, gates, first, block_out, grad, small, loss = forward(
        ndp,
        (in_weight.transpose(1, 0, 2), out_weight, gate_weight, up_weight, down_weight),
        tokens,
        teacher,
        valid.astype(f32)[:, None],
        (mixer_gain[None], ffn_gain[None], conv_weight),
    )
    streams_grad, out_grad, gate_grad, up_grad, down_grad, tokens_grad, *small_grads = backward(
        ndp,
        gate_weight.shape[1],
        held,
        normed,
        normed_two,
        grad_rows,
        streams,
        gates,
        first,
        grad,
        small,
        loss,
        tokens,
    )
    mixer_gain_grad, ffn_gain_grad, conv_grad, loss = small_grads
    return (
        loss[0, 0],
        block_out,
        tokens_grad,
        mixer_gain_grad[0],
        streams_grad.transpose(1, 0, 2),
        conv_grad,
        out_grad,
        ffn_gain_grad[0],
        gate_grad,
        up_grad,
        down_grad,
    )


def solution(mesh):
    rows = P(("dp", "tensor"), None)
    vector = P(("dp", "tensor"))
    weight = P("dp", "tensor")
    streams = P("dp", None, "tensor")
    taps = P(None, ("dp", "tensor"))
    return jax.shard_map(
        body,
        mesh=mesh,
        in_specs=(rows, rows, vector, vector, streams, taps, weight, vector, weight, weight, weight),
        out_specs=(P(), rows, rows, vector, streams, taps, weight, vector, weight, weight, weight),
        check_vma=False,
    )
```

```python
import functools
from types import SimpleNamespace

import jax
import jax.numpy as jnp
from jax import lax
from jax.experimental import pallas as pl
from jax.experimental.pallas import tpu as pltpu
from jax.sharding import PartitionSpec as P

MESH = pl.DeviceIdType.MESH
f32 = jnp.float32
bf16 = jnp.bfloat16
norm_eps = 1e-05
LANES = 256
NSUB = 3
YDEPTH, ZDEPTH = 3, 4
AHEAD = 4
VMEM = pl.BlockSpec(memory_space=pltpu.VMEM)
ANY = pl.BlockSpec(memory_space=pl.ANY)


def rows_of(start, size, step=16):
    return pl.ds(pl.multiple_of(start, step), size)


def place(ndp):
    d, x = lax.axis_index("dp"), lax.axis_index("tensor")
    core, y, z = d % 2, (d // 2) % 2, d // 4
    depth = ndp // 4
    at = SimpleNamespace(d=d, x=x, core=core, y=y, z=z, depth=depth, chip=d // 2)
    at.sib = (d + 1 - 2 * core, x)
    at.across = (d, 1 - x)
    at.beside = (d + 2 - 4 * y, x)
    at.lower, at.upper = (d - 4, x), (d + 4, x)
    at.has_lower, at.has_upper = z > 0, z < depth - 1
    at.cube = [at.sib, at.across, at.beside]
    step = 1
    while step < depth:
        at.cube.append((d + 4 * step * (1 - 2 * ((z // step) % 2)), x))
        step *= 2
    at.own = 2 * core + x
    at.own_sib = 2 * (1 - core) + x
    at.own_across = 2 * core + 1 - x
    at.own_far = 2 * (1 - core) + 1 - x
    return at


def meet(at):
    bar = pltpu.get_barrier_semaphore()
    always = [at.sib, at.across, at.beside] + at.cube[4:]
    for dev in always:
        pl.semaphore_signal(bar, 1, device_id=dev, device_id_type=MESH)
    for has, dev in ((at.has_lower, at.lower), (at.has_upper, at.upper)):

        @pl.when(has)
        def _():
            pl.semaphore_signal(bar, 1, device_id=dev, device_id_type=MESH)

    ends = jnp.where(at.has_lower, 1, 0) + jnp.where(at.has_upper, 1, 0)
    pl.semaphore_wait(bar, len(always) + ends)


def remote(src, dst, send, recv, dev):
    return pltpu.make_async_remote_copy(
        src_ref=src, dst_ref=dst, send_sem=send, recv_sem=recv, device_id=dev, device_id_type=MESH
    )


def total_copy(at, step, cur, got, send, recv):
    return remote(cur.at[step], got.at[step], send.at[step], recv.at[step], at.cube[step])


def total_end(at, step, cur, got, copy):
    copy.wait()
    cur[step + 1] = cur[step] + got[step]


def start(copy):
    copy.start()


def wait(copy):
    copy.wait()


def wait_send(copy):
    copy.wait_send()


def wait_recv(copy):
    copy.wait_recv()


def by_core(at, p, short, width, act):
    if p != short:
        act(width)
        return
    for core, count in ((0, width), (1, width // 2)):

        @pl.when(at.core == core)
        def _():
            act(count)


class Share:
    def __init__(self, at, buf, rows, sems):
        self.at, self.buf, self.rows, self.sems = at, buf, rows, sems
        self.sub = rows // NSUB

    def part(self, slot, j):
        return self.buf.at[rows_of(slot * self.rows + j * self.sub, self.sub), :]

    def copy(self, slot, j, k, dev):
        part = self.part(slot, j)
        return remote(part, part, self.sems.at[2 * k, j], self.sems.at[2 * k + 1, j], dev)

    def start(self, j):
        self.copy(self.at.own, j, 0, self.at.across).start()
        self.copy(self.at.own, j, 1, self.at.sib).start()

    def forward(self, j):
        self.copy(self.at.own_across, j, 0, self.at.across).wait_recv()
        self.copy(self.at.own_across, j, 2, self.at.sib).start()

    def finish(self):
        for j in range(NSUB):
            self.copy(self.at.own_sib, j, 1, self.at.sib).wait_recv()
            self.copy(self.at.own_far, j, 2, self.at.sib).wait_recv()
            self.copy(self.at.own, j, 0, self.at.across).wait_send()
            self.copy(self.at.own, j, 1, self.at.sib).wait_send()
            self.copy(self.at.own_across, j, 2, self.at.sib).wait_send()


class Sums:
    def __init__(self, at, acc, rows, core_out, core_in, far_in, core_sems, far_sems):
        self.at, self.acc, self.rows = at, acc, rows
        self.core_out, self.core_in, self.far_in = core_out, core_in, far_in
        self.core_sems, self.far_sems = core_sems, far_sems
        self.sub = rows // NSUB

    def of(self, slot, j):
        return self.acc[rows_of(slot * self.rows + j * self.sub, self.sub), :]

    def core_copy(self, k, j):
        part = rows_of(j * self.sub, self.sub)
        return remote(
            self.core_out.at[k, part, :],
            self.core_in.at[k, part, :],
            self.core_sems.at[0, k, j],
            self.core_sems.at[1, k, j],
            self.at.sib,
        )

    def far_copy(self, j):
        part = rows_of(j * self.sub, self.sub)
        return remote(
            self.core_in.at[0, part, :],
            self.far_in.at[part, :],
            self.far_sems.at[0, j],
            self.far_sems.at[1, j],
            self.at.across,
        )

    def to_core(self):
        for k, slot in ((0, self.at.own_far), (1, self.at.own_sib)):
            for j in range(NSUB):
                self.core_out[k, rows_of(j * self.sub, self.sub), :] = self.of(slot, j).astype(bf16)
                self.core_copy(k, j).start()

    def to_far(self):
        for j in range(NSUB):
            part = rows_of(j * self.sub, self.sub)
            self.core_copy(0, j).wait_recv()
            both = self.of(self.at.own_across, j) + self.core_in[0, part, :].astype(f32)
            self.core_in[0, part, :] = both.astype(bf16)
            self.far_copy(j).start()

    def take(self, j):
        part = rows_of(j * self.sub, self.sub)
        self.core_copy(1, j).wait_recv()
        self.far_copy(j).wait_recv()
        return (
            self.of(self.at.own, j)
            + self.core_in[1, part, :].astype(f32)
            + self.far_in[part, :].astype(f32)
        )

    def finish(self):
        for j in range(NSUB):
            self.core_copy(0, j).wait_send()
            self.core_copy(1, j).wait_send()
            self.far_copy(j).wait_send()


def nt(left, right):
    return lax.dot_general(left, right, (((1,), (1,)), ((), ())), preferred_element_type=f32)


def tn(left, right):
    return lax.dot_general(left, right, (((0,), (0,)), ((), ())), preferred_element_type=f32)


def nn(left, right):
    return jnp.dot(left, right, preferred_element_type=f32)


def inverse_of(source):
    return lax.rsqrt(jnp.mean(source * source, axis=1, keepdims=True) + norm_eps)


def shifted(value, by):
    if by == 0:
        return value
    size = value.shape[0]
    row = lax.broadcasted_iota(jnp.int32, value.shape, 0)
    inside = row >= by if by > 0 else row < size + by
    return jnp.where(inside, pltpu.roll(value, by % size, 0), 0.0)


def convolve(mixed, taps):
    return taps[0:1] * shifted(mixed, 2) + taps[1:2] * shifted(mixed, 1) + taps[2:3] * mixed


def ffn_columns(p, pieces, core):
    if p < pieces - 1:
        return [(k * LANES, LANES, 0, k) for k in range(3)]
    half = LANES // 2
    return [((3 * h + k) * half, half, h * half, k) for h in range(2 - core) for k in range(3)]


def ffn_blocks(p, pieces):
    last = isinstance(p, int) and p == pieces - 1
    return [(0, LANES // 2), (3 * LANES // 2, LANES // 2)] if last else [(0, LANES)]


class Gather:
    def __init__(self, at, held, chunk, early_y, sems):
        self.at, self.held, self.chunk, self.early_y = at, held, chunk, early_y
        self.recv, self.own_send, self.send = sems
        self.short = held.shape[0] - 1

    def by_kind(self, p, act):
        kind = self.early_y.get(p)
        if kind != "half":
            act(kind == "both")
            return
        for core in (0, 1):

            @pl.when(self.at.core == core)
            def _():
                act(core == 1)

    def run(self, act, p, chip, count, send, dev):
        def of(width):
            block = self.held.at[p, rows_of(chip * self.chunk, count * self.chunk), pl.ds(0, width)]
            act(remote(block, block, send, self.recv.at[p, chip], dev))

        by_core(self.at, p, self.short, self.held.shape[2], of)

    def arrived(self, p, chip, count=1):
        self.run(wait_recv, p, chip, count, self.own_send.at[0, 0], self.at.beside)

    def own(self, p, act):
        at = self.at
        self.run(act, p, at.chip, 1, self.own_send.at[0, p], at.beside)
        self.by_kind(p, lambda pairs: None if pairs else self.own_z(p, at.chip, 1, act))

    def own_z(self, p, chip, count, act):
        at = self.at

        @pl.when(at.has_upper)
        def _():
            self.run(act, p, chip, count, self.own_send.at[1, p], at.upper)

        @pl.when(at.has_lower)
        def _():
            self.run(act, p, chip, count, self.own_send.at[2, p], at.lower)

    def passing(self, p, pairs, parity, wait, act):
        at = self.at

        def step(s, carry):
            for from_z, goes_on, dev, way in (
                (at.z - 1 - s, at.has_upper, at.upper, 0),
                (at.z + 1 + s, at.has_lower, at.lower, 1),
            ):

                @pl.when(jnp.logical_and(from_z >= 0, from_z < at.depth))
                def _():
                    chip = 2 * from_z if pairs else 2 * from_z + at.y
                    count = 2 if pairs else 1
                    if wait:
                        self.arrived(p, chip, count)

                    @pl.when(goes_on)
                    def _():
                        self.run(act, p, chip, count, self.send.at[way, parity, from_z], dev)

                    if not pairs:
                        self.run(act, p, chip, count, self.send.at[2, parity, from_z], at.beside)

            return carry

        lax.fori_loop(0, at.depth - 1, step, 0)

    def sent(self, p):
        self.by_kind(p, lambda pairs: self.passing(p, pairs, p % AHEAD, False, wait_send))

    def relay(self, p):
        if p >= AHEAD:
            self.sent(p - AHEAD)

        def hand_on(pairs):
            if pairs:
                self.arrived(p, 2 * self.at.z + 1 - self.at.y)
                self.own_z(p, 2 * self.at.z, 2, start)
            self.passing(p, pairs, p % AHEAD, True, start)

        self.by_kind(p, hand_on)

    def whole(self, p):
        def step(z, carry):
            self.arrived(p, 2 * z + 1 - self.at.y)
            return carry

        self.by_kind(p, lambda pairs: None if pairs else lax.fori_loop(0, self.at.depth, step, 0))

    def own_done(self, p):
        self.own(p, wait_send)
        self.by_kind(p, lambda pairs: self.own_z(p, 2 * self.at.z, 2, wait_send) if pairs else None)


def forward_kernel(
    ndp,
    early_y,
    in_weight,
    out_weight,
    gate_weight,
    up_weight,
    down_weight,
    tokens,
    teacher,
    valid,
    mixer_gain,
    ffn_gain,
    conv_weight,
    held_out,
    normed_out,
    normed_two_out,
    grad_rows_out,
    streams_out,
    gates_out,
    first_out,
    block_out,
    grad_out,
    small_out,
    loss_out,
    held,
    landed,
    mine,
    rows_a,
    rows_b,
    acc,
    streams,
    gates,
    core_out,
    core_in,
    far_in,
    first,
    result,
    error_grad,
    cur,
    got,
    chip_sems,
    recv_sems,
    own_sems,
    send_sems,
    share_sems,
    core_sems,
    far_sems,
    cube_sems,
    out_sems,
    held_sems,
    gate_sems,
):
    at = place(ndp)
    pieces, width, piece = held.shape
    part_rows = out_weight.shape[0]
    chunk = 2 * part_rows
    rows = tokens.shape[0]
    sub = rows // NSUB
    channels = streams.shape[1] // 3
    aligned = part_rows % 16 == 0
    gather = Gather(at, held, chunk, early_y, (recv_sems, own_sems, send_sems))
    share_a = Share(at, rows_a, rows, share_sems)
    share_b = Share(at, rows_b, rows, share_sems)
    sums = Sums(at, acc, rows, core_out, core_in, far_in, core_sems, far_sems)

    span = (pieces - 2) * LANES
    assert gate_weight.shape[1] == 2 * span - LANES // 2

    def parts(p, core):
        at_columns = rows_of(core * channels, channels, 128)
        if p == 0:
            return [(in_weight.at[k, :, at_columns], k * channels, channels) for k in range(2)]
        if p == 1:
            return [(in_weight.at[2, :, at_columns], 0, channels), (out_weight.at[:, at_columns], channels, channels)]
        found = []
        for column, count, unit, k in ffn_columns(p, pieces, core):
            at_columns = rows_of(core * span + (p - 2) * LANES + unit, count, 128)
            found.append(((gate_weight, up_weight, down_weight)[k].at[:, at_columns], column, count))
        return found

    def each_part(p, core, act):
        if p < pieces - 1:
            for k, part in enumerate(parts(p, core)):
                act(k, *part)
            return
        for to in (0, 1):

            @pl.when(core == to)
            def _():
                for k, part in enumerate(parts(p, to)):
                    act(k, *part)

    def landing(p, core, column, count, buffer):
        if not aligned:
            return buffer.at[p, :, pl.ds(column, count)]
        rows_there = rows_of(at.chip * chunk + core * part_rows, part_rows)
        return held.at[p, rows_there, pl.ds(column, count)]

    def to_sib(p, act):
        def copy(k, src, column, count):
            dst = landing(p, at.core, column, count, landed)
            act(remote(src, dst, chip_sems.at[0, p, k], chip_sems.at[1, p, k], at.sib))

        each_part(p, 1 - at.core, copy)

    def from_sib(p):
        def copy(k, src, column, count):
            dst = landing(p, 1 - at.core, column, count, landed)
            remote(src, dst, chip_sems.at[0, p, k], chip_sems.at[1, p, k], at.sib).wait_recv()

        each_part(p, at.core, copy)

    def keep(p, act):
        def copy(k, src, column, count):
            dst = landing(p, at.core, column, count, mine)
            act(pltpu.make_async_copy(src, dst, chip_sems.at[2, p, k]))

        each_part(p, at.core, copy)

    def own_block(p):
        keep(p, wait)
        from_sib(p)
        here = rows_of(at.chip * chunk, chunk)
        if not aligned:
            a, b = mine[p].astype(f32), landed[p].astype(f32)
            lower = jnp.where(at.core == 0, a, b)
            upper = jnp.where(at.core == 0, b, a)
            held[p, here, :] = jnp.concatenate([lower, upper], axis=0).astype(bf16)
        gather.own(p, start)

    meet(at)
    to_sib(0, start)
    keep(0, start)

    @pl.when(at.core == 1)
    def _():
        held[pieces - 1, :, piece // 2 :] = jnp.zeros((width, piece - piece // 2), bf16)

    share = mixer_gain.shape[1]
    cur[0] = jnp.zeros(cur.shape[1:], f32)
    cur[0, 0:1, 0:share] = mixer_gain[...].astype(f32)
    cur[0, 1:2, 0:share] = ffn_gain[...].astype(f32)
    cur[0, 2:5, 0:share] = conv_weight[...].astype(f32)
    placed = pltpu.roll(cur[0], (at.d * 2 + at.x) * share, 1)
    line = lax.broadcasted_iota(jnp.int32, placed.shape, 0)
    cur[0] = jnp.where(line < 5, placed, jnp.sum(valid[...]))
    tally = lambda step: total_copy(at, step, cur, got, cube_sems.at[0], cube_sems.at[1])
    tallied = lambda step: total_end(at, step, cur, got, tally(step))
    last = len(at.cube)
    tally(0).start()
    for j in range(NSUB):
        rows_a[rows_of(at.own * rows + j * sub, sub), :] = tokens[pl.ds(j * sub, sub), :]
    own_block(0)
    tallied(0)
    tally(1).start()
    for p in range(1, pieces):
        to_sib(p, start)
        keep(p, start)
    tallied(1)
    for j in range(NSUB):
        share_a.start(j)
    tally(2).start()
    own_block(1)
    tallied(2)
    tally(3).start()
    own_block(2)
    tallied(3)
    if last > 4:
        tally(4).start()
    relay = gather.relay
    relay(0)
    for step in range(4, last):
        tallied(step)
        if step + 1 < last:
            tally(step + 1).start()
    for j in range(NSUB):
        share_a.forward(j)
    small_out[...] = cur[last]
    gain_one, gain_two = cur[last, 0:1, :], cur[last, 1:2, :]
    share_a.finish()

    def norm_rows(i, carry):
        part = rows_of(i * sub, sub)
        source = rows_a[part, :].astype(f32)
        rows_a[part, :] = (source * inverse_of(source) * gain_one).astype(bf16)
        return carry

    lax.fori_loop(0, 4 * NSUB, norm_rows, 0)
    normed_copy = pltpu.make_async_copy(rows_a, normed_out, out_sems.at[0])
    normed_copy.start()

    def save(p):
        return pltpu.make_async_copy(held.at[p], held_out.at[p], held_sems.at[p])

    own_block(3)
    relay(1)
    own_block(4)
    relay(2)
    own_block(5)
    for p in (0, 1):
        gather.whole(p)
        save(p).start()
    lane = at.x * 2 * channels + at.core * channels
    taps = cur[last, 2:5, rows_of(lane, channels, 128)]

    def mix(r, carry):
        part = rows_of(((r + 1 - at.core) % 2) * 2 * rows, 2 * rows)
        both = nn(rows_a[part, :], held[0])
        x_stream = nn(rows_a[part, :], held[1, :, 0:channels])
        streams[part, 0 : 2 * channels] = both
        streams[part, 2 * channels :] = x_stream
        convolved = convolve(both[:, 0:channels] * x_stream, taps)
        gated = (both[:, channels:] * convolved).astype(bf16)
        acc[part, :] = nt(gated, held[1, :, channels:])
        return carry

    lax.fori_loop(0, 2, mix, 0)
    streams_copy = pltpu.make_async_copy(streams, streams_out, out_sems.at[1])
    streams_copy.start()
    sums.to_core()
    own_block(6)
    own_block(7)
    sums.to_far()
    relay(3)
    for p in range(8, pieces):
        own_block(p)
    for j in range(NSUB):
        part = rows_of(j * sub, sub)
        value = tokens[part, :].astype(f32) + sums.take(j)
        first[part, :] = value
        normed_two = (value * inverse_of(value) * gain_two).astype(bf16)
        rows_b[rows_of(at.own * rows + j * sub, sub), :] = normed_two
        share_b.start(j)
    sums.finish()
    first_copy = pltpu.make_async_copy(first, first_out, out_sems.at[2])
    first_copy.start()
    relay(4)
    for j in range(NSUB):
        share_b.forward(j)
    share_b.finish()
    normed_two_copy = pltpu.make_async_copy(rows_b, normed_two_out, out_sems.at[3])
    normed_two_copy.start()
    acc[...] = jnp.zeros_like(acc)

    def gates_copy(p):
        slot = p % 2
        return pltpu.make_async_copy(gates.at[slot], gates_out.at[p - 2], gate_sems.at[slot])

    def some(p, r):
        part = rows_of(((r + 1 - at.core) % 2) * 2 * rows, 2 * rows)
        for column, units in ffn_blocks(p, pieces):
            both = nn(rows_b[part, :], held[p, :, column : column + 2 * units])
            gate, up = both[:, 0:units], both[:, units:]
            kept = 2 * column // 3
            gates[p % 2, part, kept : kept + 2 * units] = both.astype(bf16)
            hidden = (gate * jax.nn.sigmoid(gate) * up).astype(bf16)
            acc[part, :] += nt(hidden, held[p, :, column + 2 * units : column + 3 * units])

    def feed(p, carry):
        for q in range(5, pieces):

            @pl.when(p == q - 3)
            def _():
                relay(q)

        for q in range(2, pieces - 1):

            @pl.when(p == q)
            def _():
                gather.whole(q)

        save(p).start()

        @pl.when(p >= 4)
        def _():
            gates_copy(p - 2).wait()

        def rows_part(r, inner):
            some(p, r)
            return inner

        lax.fori_loop(0, 2, rows_part, 0)
        gates_copy(p).start()
        return carry

    normed_copy.wait()
    lax.fori_loop(2, pieces - 1, feed, 0)
    final = pieces - 1
    gather.whole(final)
    gates_copy(final - 2).wait()
    some(final, 0)
    sums.to_core()
    some(final, 1)
    sums.to_far()
    save(final).start()
    gates_copy(final).start()
    scale = 1.0 / (width * cur[last, 5:6, 0:1])
    loss = jnp.zeros((1, width), f32)
    for j in range(NSUB):
        part = rows_of(j * sub, sub)
        value = first[part, :] + sums.take(j)
        result[part, :] = value
        error = value - teacher[part, :].astype(f32)
        weighted = valid[part, :] * error
        loss = loss + jnp.sum(weighted * error, axis=0, keepdims=True)
        grad = (2.0 * scale) * weighted
        error_grad[part, :] = grad
        rows_a[rows_of(at.own * rows + j * sub, sub), :] = grad.astype(bf16)
        share_a.start(j)
    loss_out[...] = jnp.broadcast_to(jnp.sum(loss, axis=1, keepdims=True), loss_out.shape)
    sums.finish()
    result_copy = pltpu.make_async_copy(result, block_out, out_sems.at[4])
    result_copy.start()
    grad_copy = pltpu.make_async_copy(error_grad, grad_out, out_sems.at[5])
    grad_copy.start()
    for j in range(NSUB):
        share_a.forward(j)
    share_a.finish()
    rows_copy = pltpu.make_async_copy(rows_a, grad_rows_out, out_sems.at[6])
    rows_copy.start()
    for p in range(pieces):
        save(p).wait()
        to_sib(p, wait_send)
        gather.own_done(p)
    for p in range(pieces - AHEAD, pieces):
        gather.sent(p)
    for p in (pieces - 2, pieces - 1):
        gates_copy(p).wait()
    for copy in (streams_copy, first_copy, normed_two_copy, result_copy, grad_copy, rows_copy):
        copy.wait()


def forward(ndp, weights, tokens, teacher, valid, vectors):
    part_rows, channels = weights[1].shape
    channels //= 2
    piece = 2 * channels
    pieces = 2 - (-weights[2].shape[1] // (2 * LANES))
    rows, width = tokens.shape
    cube = small_steps(ndp)
    early_y = {4: "both", 7: "half"}
    dma = pltpu.SemaphoreType.DMA
    landing = (pieces, part_rows, piece) if part_rows % 16 else (1, 16, 128)
    shape = jax.ShapeDtypeStruct
    outs = (
        shape((pieces, width, piece), bf16),
        shape((4 * rows, width), bf16),
        shape((4 * rows, width), bf16),
        shape((4 * rows, width), bf16),
        shape((4 * rows, 3 * channels), f32),
        shape((pieces - 2, 4 * rows, 2 * LANES), bf16),
        shape((rows, width), f32),
        shape((rows, width), f32),
        shape((rows, width), f32),
        shape((8, width), f32),
        shape((8, 128), f32),
    )
    scratch = [
        pltpu.VMEM((pieces, width, piece), bf16),
        pltpu.VMEM(landing, bf16),
        pltpu.VMEM(landing, bf16),
        pltpu.VMEM((4 * rows, width), bf16),
        pltpu.VMEM((4 * rows, width), bf16),
        pltpu.VMEM((4 * rows, width), f32),
        pltpu.VMEM((4 * rows, 3 * channels), f32),
        pltpu.VMEM((2, 4 * rows, 2 * LANES), bf16),
        pltpu.VMEM((2, rows, width), bf16),
        pltpu.VMEM((2, rows, width), bf16),
        pltpu.VMEM((rows, width), bf16),
        pltpu.VMEM((rows, width), f32),
        pltpu.VMEM((rows, width), f32),
        pltpu.VMEM((rows, width), f32),
        pltpu.VMEM((cube + 1, 8, width), f32),
        pltpu.VMEM((cube, 8, width), f32),
        dma((3, pieces, 6)),
        dma((pieces, ndp // 2)),
        dma((3, pieces)),
        dma((3, AHEAD, ndp // 4)),
        dma((6, NSUB)),
        dma((2, 2, NSUB)),
        dma((2, NSUB)),
        dma((2, cube)),
        dma((7,)),
        dma((pieces,)),
        dma((2,)),
    ]
    return pl.pallas_call(
        functools.partial(forward_kernel, ndp, early_y),
        out_shape=outs,
        in_specs=[ANY] * 5 + [VMEM] * 6,
        out_specs=[ANY] * 9 + [VMEM] * 2,
        scratch_shapes=scratch,
        compiler_params=pltpu.CompilerParams(
            collective_id=0, has_side_effects=True, vmem_limit_bytes=63 << 20
        ),
    )(*weights, tokens, teacher, valid, *vectors)


def small_steps(ndp):
    return 3 + (ndp // 4 - 1).bit_length()


class Scatter:
    def __init__(self, at, held, chunk, count, mixed, beside_in, line_in, pair_in, pair_beside, total, sems, credits):
        self.mixed = mixed
        self.at, self.held, self.chunk, self.count = at, held, chunk, count
        self.beside_in, self.line_in, self.pair_in, self.pair_beside = beside_in, line_in, pair_in, pair_beside
        self.total, self.credits = total, credits
        self.beside_sems, self.line_sems, self.pair_sems, self.pair_y_sems = sems
        self.short, self.width = held.shape[0] - 1, held.shape[2]
        self.ydepth, self.zdepth = beside_in.shape[0], line_in.shape[0]

    def block(self, p, chip, count=1, width=None):
        here = rows_of(chip * self.chunk, count * self.chunk)
        return self.held.at[p, here, pl.ds(0, width or self.width)]

    def where_it_crosses(self, p, act):
        if p == self.mixed:
            pl.when(self.at.core == 0)(act)
        else:
            act()

    def run(self, act, copy, p, *rest):
        each = lambda width: act(copy(p, *rest, width))
        self.where_it_crosses(p, lambda: by_core(self.at, p, self.short, self.width, each))

    def beside_copy(self, p, m, z, width):
        slot = m % self.ydepth
        return remote(
            self.block(p, 2 * z + 1 - self.at.y, 1, width),
            self.beside_in.at[slot, z, :, pl.ds(0, width)],
            self.beside_sems.at[0, slot, z],
            self.beside_sems.at[1, slot, z],
            self.at.beside,
        )

    def line_copy(self, p, m, z, up, width):
        slot, way = m % self.zdepth, 0 if up else 1
        into = z + 1 if up else z
        return remote(
            self.block(p, 2 * z + self.at.y, 1, width),
            self.line_in.at[slot, into, :, pl.ds(0, width)],
            self.line_sems.at[way, slot, z],
            self.line_sems.at[2, slot, into],
            self.at.upper if up else self.at.lower,
        )

    def pair_copy(self, p, z, up):
        second = 1 if p == self.mixed else 0
        into = z + 1 if up else z
        return remote(
            self.block(p, 2 * z, 2),
            self.pair_in.at[into],
            self.pair_sems.at[3 * second + (0 if up else 1), z],
            self.pair_sems.at[3 * second + 2, into],
            self.at.upper if up else self.at.lower,
        )

    def turn(self, s):
        z, last = self.at.z, self.at.depth - 1
        low = jnp.where(z < self.at.depth // 2, 1, 0)
        down, up = last - s, s
        other = low * (down - jnp.where(down <= z, 1, 0)) + (1 - low) * (up + jnp.where(up >= z, 1, 0))
        mine = jnp.where(s == last, 1, 0)
        return mine * z + (1 - mine) * other

    def free_beside(self, p, m, before):
        if m >= self.ydepth:
            pl.semaphore_wait(self.credits.at[0], 1)
            self.drop_beside(before, m)

    def drop_beside(self, p, m):
        def step(z, carry):
            self.run(wait_send, self.beside_copy, p, m, z)
            return carry

        lax.fori_loop(0, self.at.depth, step, 0)

    def send_beside(self, p, m, before):
        self.free_beside(p, m, before)

        def step(s, carry):
            self.run(start, self.beside_copy, p, m, self.turn(s))
            return carry

        lax.fori_loop(0, self.at.depth, step, 0)

    def ways(self, has, act):
        at = self.at

        def step(s, carry):
            for z, wanted, up in (
                (at.depth - 1 - s, at.depth - 1 - s > at.z, True),
                (s, s < at.z, False),
            ):

                @pl.when(jnp.logical_and(wanted, has(up)))
                def _():
                    act(z, up)

            return carry

        lax.fori_loop(0, at.depth - 1, step, 0)

    def behind(self, up):
        return self.at.has_lower if up else self.at.has_upper

    def opens(self, up):
        return jnp.logical_not(self.behind(up))

    def near(self, up):
        low = self.at.z < self.at.depth // 2
        return jnp.logical_and(self.behind(up), low if up else jnp.logical_not(low))

    def far(self, up):
        low = self.at.z < self.at.depth // 2
        return jnp.logical_and(self.behind(up), jnp.logical_not(low) if up else low)

    def add_beside(self, p, m, before, onward):
        at = self.at
        if m >= self.zdepth:
            for has, credit in ((at.has_upper, 1), (at.has_lower, 2)):

                @pl.when(has)
                def _():
                    pl.semaphore_wait(self.credits.at[credit], 1)

            self.drop(before, m)

        def step(s, carry):
            z = self.turn(s)
            own = self.block(p, 2 * z + at.y)
            self.run(wait_recv, self.beside_copy, p, m, z)

            def add():
                came = self.beside_in[m % self.ydepth, z].astype(f32)
                own[...] = (own[...].astype(f32) + came).astype(bf16)

            self.where_it_crosses(p, add)
            for up in (True, False):

                @pl.when(jnp.logical_and(z > at.z if up else z < at.z, self.opens(up)))
                def _():
                    self.run(start, self.line_copy, p, m, z, up)

                if onward:

                    @pl.when(jnp.logical_and(z > at.z if up else z < at.z, self.behind(up)))
                    def _():
                        self.pass_on(p, m, z, up)

            return carry

        lax.fori_loop(0, at.depth, step, 0)
        if m + self.ydepth < self.count:
            pl.semaphore_signal(self.credits.at[0], 1, device_id=at.beside, device_id_type=MESH)

    def pass_on(self, p, m, z, up):
        self.run(wait_recv, self.line_copy, p, m, z, up)
        own = self.block(p, 2 * z + self.at.y)

        def add():
            came = self.line_in[m % self.zdepth, z + 1 if up else z].astype(f32)
            own[...] = (own[...].astype(f32) + came).astype(bf16)

        self.where_it_crosses(p, add)
        self.run(start, self.line_copy, p, m, z, up)

    def hop(self, p, m, has):
        self.ways(has, functools.partial(self.pass_on, p, m))

    def collect(self, p, m, slot):
        at = self.at
        total = self.total.at[slot]
        total[...] = self.block(p, 2 * at.z + at.y)[...].astype(f32)
        for up in (True, False):

            @pl.when(self.behind(up))
            def _():
                self.run(wait_recv, self.line_copy, p, m, at.z, up)
                total[...] += self.line_in[m % self.zdepth, at.z + 1 if up else at.z].astype(f32)
                if m + self.zdepth < self.count:
                    pl.semaphore_signal(
                        self.credits.at[1 if up else 2],
                        1,
                        device_id=at.lower if up else at.upper,
                        device_id_type=MESH,
                    )

    def drop(self, p, m):
        self.ways(lambda up: True, lambda z, up: self.run(wait_send, self.line_copy, p, m, z, up))

    def pairs_open(self, p):
        self.ways(self.opens, lambda z, up: self.pair_copy(p, z, up).start())

    def pair_hop(self, p, has):
        def act(z, up):
            self.pair_copy(p, z, up).wait_recv()
            own = self.block(p, 2 * z, 2)
            own[...] = (own[...].astype(f32) + self.pair_in[z + 1 if up else z].astype(f32)).astype(bf16)
            self.pair_copy(p, z, up).start()

        self.ways(has, act)

    def pair_y_copy(self, p):
        at = self.at
        second = 1 if p == self.mixed else 0
        return remote(
            self.block(p, 2 * at.z + 1 - at.y),
            self.pair_beside.at[second],
            self.pair_y_sems.at[2 * second],
            self.pair_y_sems.at[2 * second + 1],
            at.beside,
        )

    def pairs_free(self):
        at = self.at
        for has, dev, credit in ((at.has_lower, at.lower, 3), (at.has_upper, at.upper, 4)):

            @pl.when(has)
            def _():
                pl.semaphore_signal(self.credits.at[credit], 1, device_id=dev, device_id_type=MESH)

    def pairs_wait(self):
        for has, credit in ((self.at.has_upper, 3), (self.at.has_lower, 4)):

            @pl.when(has)
            def _():
                pl.semaphore_wait(self.credits.at[credit], 1)

    def pairs_cross(self, p):
        at = self.at
        own = self.block(p, 2 * at.z, 2)
        for up in (True, False):

            @pl.when(self.behind(up))
            def _():
                self.pair_copy(p, at.z, up).wait_recv()
                came = self.pair_in[at.z + 1 if up else at.z].astype(f32)
                own[...] = (own[...].astype(f32) + came).astype(bf16)

        self.pair_y_copy(p).start()

    def pairs_close(self, p, slot):
        at = self.at
        self.pair_y_copy(p).wait()
        mine = self.block(p, 2 * at.z + at.y)[...].astype(f32)
        self.total[slot] = mine + self.pair_beside[1 if p == self.mixed else 0].astype(f32)
        self.ways(lambda up: True, lambda z, up: self.pair_copy(p, z, up).wait_send())


def backward_kernel(
    ndp,
    held_in,
    normed_in,
    normed_two_in,
    grad_rows_in,
    streams_in,
    gates_in,
    first_in,
    grad_in,
    small,
    loss,
    tokens,
    streams_grad,
    out_grad,
    gate_grad,
    up_grad,
    down_grad,
    tokens_grad,
    mixer_gain_grad,
    ffn_gain_grad,
    conv_grad,
    loss_out,
    held,
    rows_a,
    rows_b,
    acc,
    gates,
    streams,
    core_out,
    core_in,
    far_in,
    first,
    grad,
    back,
    beside_in,
    line_in,
    pair_in,
    pair_beside,
    total,
    cur,
    got,
    share_sems,
    core_sems,
    far_sems,
    cube_sems,
    load_sems,
    held_sems,
    gate_sems,
    beside_sems,
    line_sems,
    pair_sems,
    pair_y_sems,
    done_sems,
    credits,
):
    at = place(ndp)
    pieces, width, piece = held.shape
    rows = tokens.shape[0]
    sub = rows // NSUB
    chunk = 2 * width // ndp
    half = chunk // 2
    channels = piece // 2
    order = [2] + list(range(4, pieces)) + [0, 1]
    paired = 3
    mixed = 0
    share = Share(at, rows_a, rows, share_sems)
    sums = Sums(at, acc, rows, core_out, core_in, far_in, core_sems, far_sems)
    scatter = Scatter(
        at,
        held,
        chunk,
        len(order),
        mixed,
        beside_in,
        line_in,
        pair_in,
        pair_beside,
        total,
        (beside_sems, line_sems, pair_sems, pair_y_sems),
        credits,
    )

    def load(src, dst, k):
        return pltpu.make_async_copy(src, dst, load_sems.at[k])

    def load_held(p):
        return pltpu.make_async_copy(held_in.at[p], held.at[p], held_sems.at[p])

    def load_gates(p):
        return pltpu.make_async_copy(gates_in.at[p - 2], gates.at[p % 2], gate_sems.at[p % 2])

    def load_streams(r):
        return load(streams_in.at[pl.ds(r * 2 * rows, 2 * rows), :], streams, 5)

    opening = (
        load(grad_rows_in, rows_a, 0),
        load_gates(2),
        load_held(2),
        load(normed_two_in, rows_b, 1),
    )
    for copy in opening:
        copy.start()
    load_gates(3).start()
    for p in list(range(3, pieces)) + [0, 1]:
        load_held(p).start()
    load_first, load_grad = load(first_in, first, 2), load(grad_in, grad, 3)
    load_first.start()
    load_grad.start()
    load_streams(0).start()
    meet(at)
    acc[...] = jnp.zeros_like(acc)
    opening[0].wait()

    def ffn(p, m=None):
        load_gates(p).wait()
        load_held(p).wait()

        def some(r, carry):
            part = rows_of(((r + 1 - at.core) % 2) * 2 * rows, 2 * rows)
            for column, units in ffn_blocks(p, pieces):
                ends = [column + k * units for k in range(4)]
                grad_hidden = nn(rows_a[part, :], held[p, :, ends[2] : ends[3]])
                kept = 2 * column // 3
                gate = gates[p % 2, part, kept : kept + units].astype(f32)
                up = gates[p % 2, part, kept + units : kept + 2 * units].astype(f32)
                sig = jax.nn.sigmoid(gate)
                active = gate * sig
                back[part, ends[2] : ends[3]] = (active * up).astype(bf16)
                grad_gate = grad_hidden * up * sig * (1.0 + gate * (1.0 - sig))
                back[part, ends[0] : ends[1]] = grad_gate.astype(bf16)
                back[part, ends[1] : ends[2]] = (grad_hidden * active).astype(bf16)
                acc[part, :] += nt(back[part, ends[0] : ends[2]], held[p, :, ends[0] : ends[2]])
            return carry

        lax.fori_loop(0, 2, some, 0)

        if p == 2:
            opening[3].wait()
        blocks = 2 * width // piece
        matched = blocks == at.depth

        def weights(s, carry):
            i = scatter.turn(s) if matched else s
            part = rows_of(i * (piece // 2), piece // 2, 128)
            for column, units in ffn_blocks(p, pieces):
                ends = [column + k * units for k in range(4)]
                held[p, part, ends[0] : ends[2]] = tn(rows_b[:, part], back[:, ends[0] : ends[2]]).astype(bf16)
                held[p, part, ends[2] : ends[3]] = tn(rows_a[:, part], back[:, ends[2] : ends[3]]).astype(bf16)
            if m is not None and matched:
                scatter.run(start, scatter.beside_copy, p, m, i)
            return carry

        lax.fori_loop(0, blocks, weights, 0)
        if m is not None and not matched:
            scatter.send_beside(p, m, None)
        if p + 2 < pieces:
            load_gates(p + 2).start()

    given = []

    span = (pieces - 2) * LANES

    def parts(p, core):
        at_columns = rows_of(core * channels, channels, 128)
        if p == 0:
            return [(k * channels, channels, streams_grad.at[k, :, at_columns]) for k in range(2)]
        if p == 1:
            return [
                (0, channels, streams_grad.at[2, :, at_columns]),
                (channels, channels, out_grad.at[:, at_columns]),
            ]
        found = []
        for column, count, unit, k in ffn_columns(p, pieces, core):
            at_columns = rows_of(core * span + (p - 2) * LANES + unit, count, 128)
            found.append((column, count, (gate_grad, up_grad, down_grad)[k].at[:, at_columns]))
        return found

    def each_part(p, core, act):
        if p < pieces - 1:
            for k, part in enumerate(parts(p, core)):
                act(k, *part)
            return
        for to in (0, 1):

            @pl.when(core == to)
            def _():
                for k, part in enumerate(parts(p, to)):
                    act(k, *part)

    def piece_rows(p, core, first_column, count):
        slot = given.index(p) % 2 if p in given else 0
        return total.at[slot, rows_of(core * half, half, 8), pl.ds(first_column, count)]

    def out_local(p, act):
        def copy(k, first_column, count, dst):
            src = piece_rows(p, at.core, first_column, count)
            act(pltpu.make_async_copy(src, dst, done_sems.at[0, p, k]))

        each_part(p, at.core, copy)

    def out_sib(p, core, act):
        def copy(k, first_column, count, dst):
            src = piece_rows(p, 1 - at.core, first_column, count)
            act(remote(src, dst, done_sems.at[1, p, k], done_sems.at[2, p, k], at.sib))

        each_part(p, core, copy)

    def give(p, fill):
        if len(given) > 1:
            out_local(given[-2], wait)
            out_sib(given[-2], at.core, wait_send)
        given.append(p)
        fill((len(given) - 1) % 2)
        out_local(p, start)
        out_sib(p, at.core, start)

    def beside(m):
        scatter.send_beside(order[m], m, order[m - YDEPTH] if m >= YDEPTH else None)

    on_core_one = pl.when(at.core == 1)

    def finish(m):
        def fill(slot):
            scatter.where_it_crosses(order[m], lambda: scatter.collect(order[m], m, slot))
            if order[m] == mixed:
                on_core_one(lambda: scatter.pairs_close(mixed, slot))

        give(order[m], fill)

    def advance(m):
        onward = m == len(order) - 1
        if onward:
            scatter.hop(order[m - 1], m - 1, scatter.far)
            finish(m - 2)
        scatter.add_beside(order[m], m, order[m - ZDEPTH] if m >= ZDEPTH else None, onward)
        if onward:
            return
        for k in (0, 1) if m == 1 else (m,) if m > 1 else ():
            scatter.hop(order[k], k, scatter.near)
        for k in (0, 1) if m == 2 else (m - 1,) if m > 2 else ():
            scatter.hop(order[k], k, scatter.far)
        if m == 2:
            scatter.pair_hop(paired, scatter.far)
        for k in (0, 1) if m == 3 else (m - 2,) if m > 3 else ():
            finish(k)
        if m == 3:
            scatter.pairs_cross(paired)
            on_core_one(scatter.pairs_free)
        if m == 4:
            give(paired, functools.partial(scatter.pairs_close, paired))

    gain_one, gain_two = small[0:1, :], small[1:2, :]
    ffn(2, 0)
    ffn(3)
    scatter.pairs_open(paired)
    ffn(4, 1)
    ffn(5, 2)
    advance(0)
    ffn(6)
    beside(3)
    scatter.pair_hop(paired, scatter.near)
    for p in range(7, pieces):
        ffn(p)
    sums.to_core()
    load_normed = load(normed_in, rows_b, 4)
    load_normed.start()
    sums.to_far()
    advance(1)
    beside(4)
    load_first.wait()
    load_grad.wait()
    gain_two_grad = jnp.zeros((1, width), f32)
    for j in range(NSUB):
        part = rows_of(j * sub, sub)
        coming = sums.take(j)
        source = first[part, :]
        inverse = inverse_of(source)
        weighted = coming * gain_two
        inner = jnp.mean(weighted * source, axis=1, keepdims=True)
        value = grad[part, :] + inverse * weighted - source * (inverse * inverse * inverse * inner)
        grad[part, :] = value
        gain_two_grad += jnp.sum(coming * source * inverse, axis=0, keepdims=True)
        rows_a[rows_of(at.own * rows + j * sub, sub), :] = value.astype(bf16)
        share.start(j)
    sums.finish()
    advance(2)
    beside(5)
    for j in range(NSUB):
        share.forward(j)
    share.finish()
    shift = at.x * 2 * channels + at.core * channels
    cur[0] = jnp.zeros(cur.shape[1:], f32)
    cur[0, 1:2, :] = gain_two_grad
    cur[0, 5:6, :] = jnp.broadcast_to(loss[0:1, 0:1], (1, width))
    load_held(0).wait()
    load_held(1).wait()
    for r in range(2):
        load_streams(r).wait()
        part = pl.ds(r * 2 * rows, 2 * rows)
        acc[part, 0:channels] = nn(rows_a[part, :], held[1, :, channels:])

        def mix(q, carry):
            lanes = [rows_of(k * channels + q * 128, 128, 128) for k in range(3)]
            b_gate, c_gate, x_stream = (streams[:, lane] for lane in lanes)
            tap = small[2:5, rows_of(shift + q * 128, 128, 128)]
            mixed = b_gate * x_stream
            convolved = convolve(mixed, tap)
            grad_gated = acc[part, lanes[0]]
            gates[0, part, lanes[0]] = (c_gate * convolved).astype(bf16)
            back[part, lanes[1]] = (grad_gated * convolved).astype(bf16)
            grad_conv = grad_gated * c_gate
            grad_mixed = tap[2:3] * grad_conv
            grad_mixed += tap[1:2] * shifted(grad_conv, -1) + tap[0:1] * shifted(grad_conv, -2)
            for k in range(3):
                term = jnp.sum(grad_conv * shifted(mixed, 2 - k), axis=0, keepdims=True)
                cur[0, 2 + k : 3 + k, rows_of(shift + q * 128, 128, 128)] += term
            back[part, lanes[0]] = (grad_mixed * x_stream).astype(bf16)
            back[part, lanes[2]] = (grad_mixed * b_gate).astype(bf16)
            return carry

        lax.fori_loop(0, channels // 128, mix, 0)
        if r == 0:
            load_streams(1).start()
        acc[part, :] = nt(back[part, 0 : 2 * channels], held[0])
        acc[part, :] += nt(back[part, 2 * channels :], held[1, :, 0:channels])
    sums.to_core()
    load_normed.wait()

    def mixer_weights(i, carry):
        part = rows_of(i * channels, channels, 128)
        left = rows_b[:, part]
        held[0, part, :] = tn(left, back[:, 0 : 2 * channels]).astype(bf16)
        held[1, part, 0:channels] = tn(left, back[:, 2 * channels :]).astype(bf16)
        held[1, part, channels:] = tn(rows_a[:, part], gates[0, :, 0:channels]).astype(bf16)
        return carry

    lax.fori_loop(0, width // channels, mixer_weights, 0)
    advance(3)
    beside(6)

    @on_core_one
    def _():
        scatter.pairs_wait()
        scatter.pairs_open(mixed)

    sums.to_far()
    advance(4)
    on_core_one(lambda: scatter.pair_hop(mixed, scatter.near))
    gain_one_grad = jnp.zeros((1, width), f32)
    for j in range(NSUB):
        part = rows_of(j * sub, sub)
        coming = sums.take(j)
        source = tokens[part, :].astype(f32)
        inverse = inverse_of(source)
        weighted = coming * gain_one
        inner = jnp.mean(weighted * source, axis=1, keepdims=True)
        grad[part, :] += inverse * weighted - source * (inverse * inverse * inverse * inner)
        gain_one_grad += jnp.sum(coming * source * inverse, axis=0, keepdims=True)
    sums.finish()
    tokens_copy = load(grad, tokens_grad, 6)
    tokens_copy.start()
    cur[0, 0:1, :] = gain_one_grad
    tally = lambda step: total_copy(at, step, cur, got, cube_sems.at[0], cube_sems.at[1])
    for step in range(2):
        tally(step).start()
        total_end(at, step, cur, got, tally(step))
    tally(2).start()
    beside(7)
    steps = len(at.cube)
    count = len(order)
    advance(5)
    on_core_one(lambda: scatter.pair_hop(mixed, scatter.far))
    advance(6)
    on_core_one(lambda: scatter.pairs_cross(mixed))
    total_end(at, 2, cur, got, tally(2))
    tally(3).start()
    advance(7)
    finish(count - 2)
    total_end(at, 3, cur, got, tally(3))
    if steps > 4:
        tally(4).start()
    finish(count - 1)
    for step in range(4, steps):
        total_end(at, step, cur, got, tally(step))
        if step + 1 < steps:
            tally(step + 1).start()
    share_lanes = mixer_gain_grad.shape[1]
    own = pltpu.roll(cur[steps], (width - (at.d * 2 + at.x) * share_lanes) % width, 1)
    mixer_gain_grad[...] = own[0:1, 0:share_lanes]
    ffn_gain_grad[...] = own[1:2, 0:share_lanes]
    conv_grad[...] = own[2:5, 0:share_lanes]
    loss_out[...] = cur[steps, 5:6, 0:1] / (width * small[5:6, 0:1])
    for m in range(count - YDEPTH, count):
        scatter.drop_beside(order[m], m)
    for m in range(count - ZDEPTH, count):
        scatter.drop(order[m], m)
    for p in given[-2:]:
        out_local(p, wait)
        out_sib(p, at.core, wait_send)
    for p in given:
        out_sib(p, 1 - at.core, wait_recv)
    tokens_copy.wait()


def backward(ndp, units, held, normed, normed_two, grad_rows, streams, gates, first, grad, small, loss, tokens):
    pieces, width, piece = held.shape
    rows = tokens.shape[0]
    chunk = 2 * width // ndp
    depth = ndp // 4
    channels = piece // 2
    cube = small_steps(ndp)
    dma = pltpu.SemaphoreType.DMA
    shape = jax.ShapeDtypeStruct
    outs = (
        shape((3, chunk // 2, 2 * channels), f32),
        shape((chunk // 2, 2 * channels), f32),
        shape((chunk // 2, units), f32),
        shape((chunk // 2, units), f32),
        shape((chunk // 2, units), f32),
        shape((rows, width), f32),
        shape((1, width // (2 * ndp)), f32),
        shape((1, width // (2 * ndp)), f32),
        shape((3, width // (2 * ndp)), f32),
        shape((1, 1), f32),
    )
    scratch = [
        pltpu.VMEM((pieces, width, piece), bf16),
        pltpu.VMEM((4 * rows, width), bf16),
        pltpu.VMEM((4 * rows, width), bf16),
        pltpu.VMEM((4 * rows, width), f32),
        pltpu.VMEM((2, 4 * rows, 2 * LANES), bf16),
        pltpu.VMEM((2 * rows, 3 * channels), f32),
        pltpu.VMEM((2, rows, width), bf16),
        pltpu.VMEM((2, rows, width), bf16),
        pltpu.VMEM((rows, width), bf16),
        pltpu.VMEM((rows, width), f32),
        pltpu.VMEM((rows, width), f32),
        pltpu.VMEM((4 * rows, 3 * channels), bf16),
        pltpu.VMEM((YDEPTH, depth, chunk, piece), bf16),
        pltpu.VMEM((ZDEPTH, depth + 1, chunk, piece), bf16),
        pltpu.VMEM((depth + 1, 2 * chunk, piece), bf16),
        pltpu.VMEM((2, chunk, piece), bf16),
        pltpu.VMEM((2, chunk, piece), f32),
        pltpu.VMEM((cube + 1, 8, width), f32),
        pltpu.VMEM((cube, 8, width), f32),
        dma((6, NSUB)),
        dma((2, 2, NSUB)),
        dma((2, NSUB)),
        dma((2, cube)),
        dma((7,)),
        dma((pieces,)),
        dma((2,)),
        dma((2, YDEPTH, depth)),
        dma((3, ZDEPTH, depth + 1)),
        dma((6, depth + 1)),
        dma((4,)),
        dma((3, pieces, 6)),
        pltpu.SemaphoreType.REGULAR((5,)),
    ]
    return pl.pallas_call(
        functools.partial(backward_kernel, ndp),
        out_shape=outs,
        in_specs=[ANY] * 8 + [VMEM] * 3,
        out_specs=[ANY] * 6 + [VMEM] * 4,
        scratch_shapes=scratch,
        compiler_params=pltpu.CompilerParams(
            collective_id=1, has_side_effects=True, vmem_limit_bytes=127 << 19
        ),
    )(held, normed, normed_two, grad_rows, streams, gates, first, grad, small, loss, tokens)


def body(
    tokens,
    teacher,
    valid,
    mixer_gain,
    in_weight,
    conv_weight,
    out_weight,
    ffn_gain,
    gate_weight,
    up_weight,
    down_weight,
):
    ndp = lax.axis_size("dp")
    held, normed, normed_two, grad_rows, streams, gates, first, block_out, grad, small, loss = forward(
        ndp,
        (in_weight.transpose(1, 0, 2), out_weight, gate_weight, up_weight, down_weight),
        tokens,
        teacher,
        valid.astype(f32)[:, None],
        (mixer_gain[None], ffn_gain[None], conv_weight),
    )
    streams_grad, out_grad, gate_grad, up_grad, down_grad, tokens_grad, *small_grads = backward(
        ndp,
        gate_weight.shape[1],
        held,
        normed,
        normed_two,
        grad_rows,
        streams,
        gates,
        first,
        grad,
        small,
        loss,
        tokens,
    )
    mixer_gain_grad, ffn_gain_grad, conv_grad, loss = small_grads
    return (
        loss[0, 0],
        block_out,
        tokens_grad,
        mixer_gain_grad[0],
        streams_grad.transpose(1, 0, 2),
        conv_grad,
        out_grad,
        ffn_gain_grad[0],
        gate_grad,
        up_grad,
        down_grad,
    )


def solution(mesh):
    rows = P(("dp", "tensor"), None)
    vector = P(("dp", "tensor"))
    weight = P("dp", "tensor")
    streams = P("dp", None, "tensor")
    taps = P(None, ("dp", "tensor"))
    return jax.shard_map(
        body,
        mesh=mesh,
        in_specs=(rows, rows, vector, vector, streams, taps, weight, vector, weight, weight, weight),
        out_specs=(P(), rows, rows, vector, streams, taps, weight, vector, weight, weight, weight),
        check_vma=False,
    )
```
